32 devices in a mesh: seq: 4 (over y, x), head: 8 (over z, core).
Axes of the slice: x: 2, y: 2, z: 4, core: 2. Of those that a mesh axis runs over, the one named last changes fastest.
Arguments:
- hidden_in: bfloat16 [2, 2048, 2048], P(None, ('seq', 'head')), may hold values from -6 to 6
- seq_starts: int32 [2, 4], replicated, may hold values from 0 to 2047, as said below
- norm_gain: bfloat16 [2048], P(('seq', 'head')), may hold values from 0.5 to 1.5
- in_weight: bfloat16 [2048, 8512], P(('seq', 'head')), may hold values from -0.125 to 0.125
- conv_weight: bfloat16 [4, 4352], P(None, ('seq', 'head')), may hold values from -3 to 3
- conv_bias: bfloat16 [4352], P(('seq', 'head')), may hold values from -3 to 3
- decay_log: float32 [64], P('head'), may hold values from -7 to 1
- dt_bias: float32 [64], P('head'), may hold values from -6 to -2
- skip_gain: float32 [64], P('head'), may hold values from 0.5 to 1.5
- gate_gain: bfloat16 [4096], P(('seq', 'head')), may hold values from 0.5 to 1.5
- out_weight: bfloat16 [4096, 2048], P(('seq', 'head')), may hold values from -0.09375 to 0.09375
- out_grad: bfloat16 [2, 2048, 2048], P(None, ('seq', 'head')), may hold values from -6 to 6
Outputs:
- hidden_out: bfloat16 [2, 2048, 2048], P(None, ('seq', 'head'))
- grad_in: bfloat16 [2, 2048, 2048], P(None, ('seq', 'head'))
- grad_norm_gain: float32 [2048], P(('seq', 'head'))
- grad_in_weight: float32 [2048, 8512], P(('seq', 'head'))
- grad_conv_weight: float32 [4, 4352], P(None, ('seq', 'head'))
- grad_conv_bias: float32 [4352], P(('seq', 'head'))
- grad_decay_log: float32 [64], P('head')
- grad_dt_bias: float32 [64], P('head')
- grad_skip_gain: float32 [64], P('head')
- grad_gate_gain: float32 [4096], P(('seq', 'head'))
- grad_out_weight: float32 [4096, 2048], P(('seq', 'head'))
The draws below stay inside these ranges and needn't reach their ends.
Inputs may be any that keep to these rules, and one draw needn't show every extreme that they name: `seq_starts`: start offsets of the 4 sequences of each micro-batch: the first is 0 and they rise strictly.
All inputs are finite; a program needn't handle non-finite values.
Results may differ from the reference program's by a relative error of at most 0.0084.
Values may be sent and summed in bfloat16 or wider, within the bound.
No kernel may reach another device: no remote copies, remote signals or barrier semaphores. Data moves between devices by JAX's collectives and lax.ppermute only.
A program may use at most 448 MiB of HBM per device.

```python
import jax
import jax.numpy as jnp
from jax import lax

D = 2048
HEADS = 64
HEADDIM = 64
STATE = 128
CONV_K = 4
SCAN_BLOCK = 256
MICRO = 2
D_INNER = 4096
CONV_CH = 4352
PROJ = 8512
SEQ_SHARD = 512
TOKENS = 2048


def draw_seq_starts(key, part):
    key = jax.random.fold_in(key, 11)
    first_key, middle_key, last_key = jax.random.split(key, 3)
    second = jax.random.randint(first_key, (MICRO,), SEQ_SHARD // 2, SEQ_SHARD)
    third = jax.random.randint(middle_key, (MICRO,), TOKENS - SEQ_SHARD + 1, TOKENS - SEQ_SHARD // 4)
    fourth = jax.random.randint(last_key, (MICRO,), third + 1, TOKENS)
    return jnp.stack([jnp.zeros((MICRO,), jnp.int32), second, third, fourth], axis=-1).astype(jnp.int32)


def shard_levels(rng, extent, cuts, low, largest):
    factor_of, own = 1.0, jax.random.fold_in(rng, 6)
    for position, parts in cuts:
        steps = jnp.exp(jax.random.uniform(jax.random.fold_in(own, position), (parts,), jnp.float32, low / len(cuts), largest / len(cuts)))
        factor_of = factor_of * jnp.repeat(steps, extent[position] // parts).reshape([-1 if axis == position else 1 for axis in range(len(extent))])
    return factor_of


def gaussian(stream_key, shape, width, bound, shards=(), dtype=jnp.bfloat16):
    entries = width * jax.random.normal(stream_key, shape, jnp.float32)
    if shards:
        entries = entries * shard_levels(stream_key, shape, shards, -0.22, 0.18)
    return jnp.clip(entries, -bound, bound).astype(dtype)


def setup_inputs(seed: int = 0) -> dict:
    arg_keys = jax.random.split(jax.random.key(seed), 13)
    hidden_in = gaussian(arg_keys[0], (MICRO, TOKENS, D), 1.0, 6.0, ((1, 32),))
    seq_starts = draw_seq_starts(jax.random.fold_in(arg_keys[12], 71), 0)
    norm_gain = jnp.clip(1.0 + 0.1 * jax.random.normal(arg_keys[2], (D,), jnp.float32), 0.5, 1.5).astype(jnp.bfloat16)
    in_weight = gaussian(arg_keys[3], (D, PROJ), D ** -0.5, 0.125, ((0, 32),))
    conv_weight = gaussian(arg_keys[4], (CONV_K, CONV_CH), CONV_K ** -0.5, 3.0, ((1, 32),))
    conv_bias = gaussian(arg_keys[5], (CONV_CH,), 0.5, 3.0, ((0, 32),))
    decay_log = jnp.clip(-7.0 + 8.0 * jax.random.uniform(arg_keys[6], (HEADS,), jnp.float32) ** shard_levels(arg_keys[6], (HEADS,), ((0, 8),), -0.2, 0.2), -7.0, 1.0)
    dt_bias = jnp.clip(-6.0 + 4.0 * jax.random.uniform(arg_keys[7], (HEADS,), jnp.float32) ** shard_levels(arg_keys[7], (HEADS,), ((0, 8),), -0.2, 0.2), -6.0, -2.0)
    skip_gain = jnp.clip(0.5 + 1.0 * jax.random.uniform(arg_keys[8], (HEADS,), jnp.float32) ** shard_levels(arg_keys[8], (HEADS,), ((0, 8),), -0.2, 0.2), 0.5, 1.5)
    gate_gain = jnp.clip(1.0 + 0.1 * jax.random.normal(arg_keys[9], (D_INNER,), jnp.float32), 0.5, 1.5).astype(jnp.bfloat16)
    out_weight = gaussian(arg_keys[10], (D_INNER, D), D_INNER ** -0.5, 0.09375, ((0, 32),))
    out_grad = gaussian(arg_keys[11], (MICRO, TOKENS, D), 1.0, 6.0, ((1, 32),))
    return dict(hidden_in=hidden_in, seq_starts=seq_starts, norm_gain=norm_gain, in_weight=in_weight, conv_weight=conv_weight, conv_bias=conv_bias, decay_log=decay_log, dt_bias=dt_bias, skip_gain=skip_gain, gate_gain=gate_gain, out_weight=out_weight, out_grad=out_grad)


precise = lax.Precision.HIGHEST
eps = 1e-05

@jax.custom_vjp
def low(v):
    return lax.optimization_barrier(v.astype(jnp.bfloat16)).astype(jnp.float32)

@jax.custom_vjp
def low_back(v):
    return v

def low_keep(v):
    return (low(v), None)

def low_pass(kept, grad):
    return (grad,)

def back_keep(v):
    return (v, None)

def back_low(kept, grad):
    return (low(grad),)
low.defvjp(low_keep, low_pass)
low_back.defvjp(back_keep, back_low)

def seg_ids(starts, positions):
    hits = (starts[None, :] <= positions[:, None]).astype(jnp.int32)
    return lax.optimization_barrier(jnp.sum(hits, axis=1)).astype(jnp.int32) - 1

def start_flags(starts, positions):
    return lax.optimization_barrier(jnp.sum((starts[None, :] == positions[:, None]).astype(jnp.float32), axis=1))

def block_step(state_now, inputs_now, rate, skip_one):
    vals, steps, write_key, read_key, segs, firsts = inputs_now
    log_decay = jnp.cumsum(steps * rate)
    causal = jnp.arange(SCAN_BLOCK)[:, None] >= jnp.arange(SCAN_BLOCK)[None, :]
    same_seq = (segs[:, None] == segs[None, :]) & causal
    spread = log_decay[:, None] - log_decay[None, :]
    within = jnp.where(same_seq, jnp.exp(jnp.where(same_seq, spread, 0.0)), 0.0)
    scores = jnp.dot(read_key, write_key.T, precision=precise)
    result = jnp.dot(scores * within * steps[None, :], vals, precision=precise)
    open_seq = jnp.cumsum(firsts) == 0
    carry_in = jnp.where(open_seq, jnp.exp(log_decay), 0.0)
    result = result + carry_in[:, None] * jnp.dot(read_key, state_now.T, precision=precise)
    tail_seq = segs == segs[-1]
    to_end = jnp.where(tail_seq, jnp.exp(jnp.where(tail_seq, log_decay[-1] - log_decay, 0.0)), 0.0)
    carried = jnp.where(open_seq[-1], jnp.exp(log_decay[-1]), 0.0)
    new_state = carried * state_now + jnp.dot((vals * (to_end * steps)[:, None]).T, write_key, precision=precise)
    return (new_state, result + skip_one * vals)

def one_head(inputs_now, write_key, read_key, segs, firsts):
    vals, steps, rate, skip_one = inputs_now
    blocks_here = TOKENS // SCAN_BLOCK
    pieces = (vals.reshape(blocks_here, SCAN_BLOCK, HEADDIM), steps.reshape(blocks_here, SCAN_BLOCK), write_key.reshape(blocks_here, SCAN_BLOCK, STATE), read_key.reshape(blocks_here, SCAN_BLOCK, STATE), segs.reshape(blocks_here, SCAN_BLOCK), firsts.reshape(blocks_here, SCAN_BLOCK))
    stepper = jax.checkpoint(lambda state_now, piece_now: block_step(state_now, piece_now, rate, skip_one))
    _, results = lax.scan(stepper, jnp.zeros((HEADDIM, STATE), jnp.float32), pieces)
    return results.reshape(TOKENS, HEADDIM)

def micro_forward(inputs, starts, params):
    norm_gain, in_weight, conv_weight, conv_bias, decay_log, dt_bias, skip_gain, gate_gain, out_weight = params
    positions = jnp.arange(TOKENS).astype(jnp.int32)
    segs = seg_ids(starts, positions)
    firsts = start_flags(starts, positions)
    normed = inputs * lax.rsqrt(lax.optimization_barrier(jnp.mean(inputs * inputs, axis=-1, keepdims=True)) + eps) * norm_gain
    proj = low_back(jnp.dot(low(normed), in_weight, precision=precise))
    gate_in = proj[:, :D_INNER]
    conv_low = low(proj[:, D_INNER:D_INNER + CONV_CH])
    step_low = low_back(low(proj[:, D_INNER + CONV_CH:]))
    padded = jnp.concatenate([jnp.zeros((CONV_K - 1, CONV_CH), jnp.float32), conv_low], axis=0)
    seg_pad = jnp.concatenate([jnp.full((CONV_K - 1,), -1, jnp.int32), segs], axis=0)
    total = conv_bias[None, :]
    for offset in range(CONV_K):
        valid = (seg_pad[offset:offset + TOKENS] == segs).astype(jnp.float32)
        total = total + conv_weight[offset][None, :] * padded[offset:offset + TOKENS] * valid[:, None]
    mixed = low_back(low(jax.nn.silu(total)))
    values = mixed[:, :D_INNER].reshape(TOKENS, HEADS, HEADDIM)
    write_key = mixed[:, D_INNER:D_INNER + STATE]
    read_key = mixed[:, D_INNER + STATE:]
    step_size = jax.nn.softplus(step_low + dt_bias[None, :])
    rate = -jnp.exp(decay_log)
    head_fn = jax.checkpoint(lambda inputs_now: one_head(inputs_now, write_key, read_key, segs, firsts))
    results = lax.map(head_fn, (jnp.transpose(values, (1, 0, 2)), step_size.T, rate, skip_gain))
    mixer = low_back(low(jnp.transpose(results, (1, 0, 2)).reshape(TOKENS, D_INNER)))
    gated = mixer * jax.nn.silu(gate_in)
    ynorm = gated * lax.rsqrt(lax.optimization_barrier(jnp.mean(gated * gated, axis=-1, keepdims=True)) + eps) * gate_gain
    return inputs + jnp.dot(low(ynorm), out_weight, precision=precise)

def reference(hidden_in, seq_starts, norm_gain, in_weight, conv_weight, conv_bias, decay_log, dt_bias, skip_gain, gate_gain, out_weight, out_grad):
    params = (norm_gain.astype(jnp.float32), in_weight.astype(jnp.float32), conv_weight.astype(jnp.float32), conv_bias.astype(jnp.float32), decay_log.astype(jnp.float32), dt_bias.astype(jnp.float32), skip_gain.astype(jnp.float32), gate_gain.astype(jnp.float32), out_weight.astype(jnp.float32))
    inputs = hidden_in.astype(jnp.float32)

    def forward(inputs_all, params_all):
        stepper = jax.checkpoint(lambda pair: micro_forward(pair[0], pair[1], params_all))
        return lax.map(stepper, (inputs_all, seq_starts))
    output, pullback = jax.vjp(forward, inputs, params)
    grad_inputs, grads = pullback(out_grad.astype(jnp.float32))
    return (output.astype(jnp.bfloat16), grad_inputs.astype(jnp.bfloat16), grads[0], grads[1], grads[2], grads[3], grads[4], grads[5], grads[6], grads[7], grads[8])
```

```python
import jax
import jax.numpy as jnp
from jax import lax
from jax.sharding import PartitionSpec as P

HEADS = 64
HEADDIM = 64
STATE = 128
CONV_K = 4
SCAN_BLOCK = 256
D_INNER = 4096
CONV_CH = 4352
EDGE = CONV_K - 1
EPS = 1e-05

f32 = jnp.float32
bf16 = jnp.bfloat16
BOTH = ("seq", "head")


def dot(spec, a, b):
    return jnp.einsum(spec, a, b, preferred_element_type=f32)


def halves(v):
    high = lax.reduce_precision(v, 8, 7)
    return high.astype(bf16), (v - high).astype(bf16)


def halved(spec, a, b):
    return dot(spec, a, b[0]) + dot(spec, a, b[1])


def three_parts(v):
    parts = []
    for _ in range(3):
        part = lax.reduce_precision(v, 8, 7)
        parts.append(part.astype(bf16))
        v = v - part
    return parts


def linked(payload, back):
    count = lax.axis_size("seq")
    total, reach = 0.0, 1.0
    for k in range(1, count):
        if back:
            pairs = [(i, i - k) for i in range(k, count)]
        else:
            pairs = [(i, i + k) for i in range(count - k)]
        got = lax.ppermute(payload, "seq", pairs).astype(f32)
        total = total + reach * got[:, :, :STATE]
        reach = reach * got[:, :, STATE : STATE + 1]
    return total


def silu_parts(v):
    sig = jax.nn.sigmoid(v)
    return v * sig, sig * (1.0 + v * (1.0 - sig))


def body(
    hidden_in,
    seq_starts,
    norm_gain,
    in_weight,
    conv_weight,
    conv_bias,
    decay_log,
    dt_bias,
    skip_gain,
    gate_gain,
    out_weight,
    out_grad,
):
    seqs, heads = lax.axis_size("seq"), lax.axis_size("head")
    s_i, h_i = lax.axis_index("seq"), lax.axis_index("head")
    micro, tok, width = hidden_in.shape
    rows = in_weight.shape[0]
    shard = tok * heads
    runs = seqs if HEADS % (seqs * heads) == 0 else 1
    run_ch = D_INNER // (runs * heads)
    run_heads = HEADS // (runs * heads)
    chans, n_heads = runs * run_ch, runs * run_heads
    key_ch = 2 * STATE // heads
    conv_share, gate_share, head_share = conv_bias.shape[0], gate_gain.shape[0], decay_log.shape[0]

    def mine(x, size):
        lead = x.shape[:-1]
        x = x.reshape(lead + (runs, heads, size))
        x = lax.dynamic_index_in_dim(x, h_i, len(lead) + 1, False)
        return x.reshape(lead + (runs * size,))

    def columns(x, size):
        x = x.reshape(rows, runs, heads, size)
        return jnp.transpose(x, (2, 0, 1, 3)).reshape(heads, rows, runs * size)

    extras = jnp.concatenate(
        [norm_gain, conv_weight.reshape(-1), conv_bias, gate_gain]
        + three_parts(decay_log)
        + three_parts(dt_bias)
        + three_parts(skip_gain)
    )
    extra_cols = -(-extras.shape[0] // rows)
    extras = jnp.pad(extras, (0, extra_cols * rows - extras.shape[0])).reshape(extra_cols, rows)
    key_p = jnp.transpose(
        in_weight[:, 2 * D_INNER : 2 * D_INNER + 2 * STATE].reshape(rows, heads, key_ch), (1, 2, 0)
    )
    step_p = jnp.transpose(
        in_weight[:, 2 * D_INNER + 2 * STATE :].reshape(rows, runs, heads, run_heads), (2, 1, 3, 0)
    ).reshape(heads, n_heads, rows)
    small_p = jnp.concatenate(
        [key_p, step_p, jnp.broadcast_to(extras[None], (heads,) + extras.shape)], axis=1
    )

    def spread(x):
        x = lax.all_to_all(x, "head", split_axis=0, concat_axis=0, tiled=True)
        return lax.all_gather(x, "seq", axis=0, tiled=False)

    w_val = spread(columns(in_weight[:, D_INNER : 2 * D_INNER], run_ch)).reshape(width, chans)
    small = spread(small_p)
    w_gate = spread(columns(in_weight[:, :D_INNER], run_ch)).reshape(width, chans)
    n_small = key_ch + n_heads
    w_small = jnp.transpose(small[:, :, :n_small], (2, 0, 1, 3)).reshape(n_small, width)
    extras = small[:, :, n_small:].reshape(seqs * heads, -1)
    at = 0

    def take(size):
        nonlocal at
        at += size
        return extras[:, at - size : at]

    gain = take(rows).reshape(width).astype(f32)
    conv_w = jnp.transpose(take(CONV_K * conv_share).reshape(-1, CONV_K, conv_share), (1, 0, 2))
    conv_w = conv_w.reshape(CONV_K, CONV_CH).astype(f32)
    conv_b = take(conv_share).reshape(1, CONV_CH).astype(f32)
    conv_p = jnp.concatenate([conv_w, conv_b], axis=0)
    gate_g = mine(take(gate_share).reshape(D_INNER), run_ch).astype(f32)

    def head_param():
        x = take(3 * head_share)[:heads].reshape(heads, 3, head_share).astype(f32)
        return mine((x[:, 0] + x[:, 1] + x[:, 2]).reshape(HEADS), run_heads)

    decay_mine, bias_mine, skip_mine = head_param(), head_param(), head_param()
    conv_val = mine(conv_p[:, :D_INNER], run_ch)
    conv_key = lax.dynamic_slice_in_dim(conv_p[:, D_INNER:], h_i * key_ch, key_ch, 1)
    if runs == seqs:
        w_out = lax.all_gather(out_weight, "seq", axis=0, tiled=True)
    else:
        w_out = lax.all_gather(out_weight, BOTH, axis=0, tiled=True)
        w_out = lax.dynamic_slice_in_dim(w_out, h_i * chans, chans, 0)

    inputs = lax.all_gather(hidden_in, "head", axis=1, tiled=True).astype(f32)
    grad_rows = lax.all_gather(out_grad, "head", axis=1, tiled=True)
    inv = lax.rsqrt(jnp.mean(inputs * inputs, axis=-1, keepdims=True) + EPS)
    unit = inputs * inv
    normed_low = (unit * gain).astype(bf16)
    val_in = dot("mtd,dk->mtk", normed_low, w_val).astype(bf16)
    small_in = dot("kd,mtd->mkt", w_small, normed_low).astype(bf16)
    key_in, step_low = small_in[:, :key_ch], small_in[:, key_ch:].astype(f32)
    gate_in = dot("mtd,dk->mtk", normed_low, w_gate)

    positions = s_i * shard - EDGE + jnp.arange(shard + EDGE)
    segs = jnp.sum((seq_starts[:, None, :] <= positions[None, :, None]).astype(jnp.int32), axis=2)
    firsts = jnp.sum(
        (seq_starts[:, None, :] == positions[None, EDGE:, None]).astype(f32), axis=2
    )
    valid = [
        (segs[:, k : k + shard] == segs[:, EDGE:]).astype(f32) for k in range(CONV_K)
    ]
    segs = segs[:, EDGE:]
    rim = jnp.concatenate(
        [val_in[:, shard - EDGE :], jnp.swapaxes(key_in[:, :, shard - EDGE :], 1, 2)], axis=2
    )
    forward = [(i, i + 1) for i in range(seqs - 1)]
    rim = lax.ppermute(rim, "seq", forward)
    val_win = jnp.concatenate([rim[:, :, :chans], val_in], axis=1).astype(f32)
    key_win = jnp.concatenate(
        [jnp.swapaxes(rim[:, :, chans:], 1, 2), key_in], axis=2
    ).astype(f32)
    val_tot = conv_val[CONV_K]
    key_tot = conv_key[CONV_K][:, None]
    for k in range(CONV_K):
        val_tot = val_tot + conv_val[k] * val_win[:, k : k + shard] * valid[k][:, :, None]
        key_tot = key_tot + conv_key[k][:, None] * key_win[:, :, k : k + shard] * valid[k][:, None]
    vals = jax.nn.silu(val_tot).astype(bf16)
    keys = jax.nn.silu(key_tot).astype(bf16)
    keys = lax.all_gather(keys, "head", axis=1, tiled=True)

    blocks = shard // SCAN_BLOCK
    rate = -jnp.exp(decay_mine)
    pre_step = step_low + bias_mine[:, None]
    step = jax.nn.softplus(pre_step)
    logs = jnp.cumsum((step * rate[:, None]).reshape(micro, n_heads, blocks, SCAN_BLOCK), axis=-1)
    step_b = step.reshape(micro, n_heads, blocks, SCAN_BLOCK)
    seg_b = segs.reshape(micro, blocks, SCAN_BLOCK)
    first_b = firsts.reshape(micro, blocks, SCAN_BLOCK)
    vals_b = vals.reshape(micro, blocks, SCAN_BLOCK, n_heads, HEADDIM).astype(f32)
    wkey = keys[:, :STATE].reshape(micro, STATE, blocks, SCAN_BLOCK)
    rkey = keys[:, STATE:].reshape(micro, STATE, blocks, SCAN_BLOCK)
    causal = jnp.arange(SCAN_BLOCK)[:, None] >= jnp.arange(SCAN_BLOCK)[None, :]
    same = (seg_b[..., :, None] == seg_b[..., None, :]) & causal
    open_seq = (jnp.cumsum(first_b, axis=-1) == 0)[:, None]
    carry = jnp.where(open_seq, jnp.exp(logs), 0.0)
    tail = (seg_b == seg_b[..., -1:])[:, None]
    to_end = jnp.where(tail, jnp.exp(jnp.where(tail, logs[..., -1:] - logs, 0.0)), 0.0)
    stepped = jnp.einsum("mjcq,mcqjp->mcqjp", step_b, vals_b)
    ending = jnp.einsum("mjcq,mcqjp->mcqjp", to_end, stepped).astype(bf16)
    stepped = stepped.astype(bf16)
    block_state = dot("mncq,mcqjp->mcjnp", wkey, ending)
    block_decay = carry[..., -1]
    state = jnp.zeros_like(block_state[:, 0])
    reach = jnp.ones_like(block_decay[:, :, 0])
    before, prefix = [], []
    for c in range(blocks):
        before.append(state)
        prefix.append(reach)
        state = block_decay[:, :, c, None, None] * state + block_state[:, c]
        reach = block_decay[:, :, c] * reach
    decay_row = jnp.broadcast_to(reach[:, :, None, None], (micro, n_heads, 8, HEADDIM))
    state_in = linked(jnp.concatenate([state, decay_row], axis=2).astype(bf16), False)
    starts = jnp.stack(
        [before[c] + prefix[c][:, :, None, None] * state_in for c in range(blocks)], axis=1
    )
    starts_low = halves(starts)
    scores = jnp.where(same, dot("mncq,mncs->mcqs", rkey, wkey), 0.0)
    spread_log = logs[..., :, None] - logs[..., None, :]
    within = jnp.exp(jnp.minimum(spread_log, 0.0))
    weights = (scores[:, None] * within).astype(bf16)
    inner = dot("mjcqs,mcsjp->mcqjp", weights, stepped)
    carried = jnp.einsum("mjcq,mcqjp->mcqjp", carry, halved("mncq,mcjnp->mcqjp", rkey, starts_low))
    mixer = inner + carried + skip_mine[:, None] * vals_b
    mixer = mixer.astype(bf16).astype(f32).reshape(micro, shard, chans)

    gate_act, gate_slope = silu_parts(gate_in)
    gated = mixer * gate_act
    d_ynorm = dot("mtd,kd->mtk", grad_rows, w_out)
    pulled = d_ynorm * gate_g
    sums = jnp.stack([jnp.sum(gated * gated, axis=-1), jnp.sum(gated * pulled, axis=-1)])
    sums = lax.psum(sums, "head")
    scale = lax.rsqrt(sums[0] / D_INNER + EPS)[..., None]
    ynorm_low = (gated * scale * gate_g).astype(bf16)
    out_part = dot("mtk,kd->mtd", ynorm_low, w_out).astype(bf16)
    out_sum = lax.psum_scatter(out_part, "head", scatter_dimension=1, tiled=True)
    hidden_out = (hidden_in.astype(f32) + out_sum.astype(f32)).astype(bf16)
    grad_out_part = dot("mtk,mtd->kd", ynorm_low, grad_rows).astype(bf16)
    grad_gate_gain = jnp.sum(d_ynorm * gated * scale, axis=(0, 1))
    d_gated = scale * (pulled - gated * (scale * scale * sums[1][..., None] / D_INNER))
    d_mix = (d_gated * gate_act).astype(bf16)
    d_gate = (d_gated * mixer * gate_slope).astype(bf16)

    d_mix_f = d_mix.astype(f32).reshape(micro, blocks, SCAN_BLOCK, n_heads, HEADDIM)
    d_mix_b = d_mix.reshape(micro, blocks, SCAN_BLOCK, n_heads, HEADDIM)
    carry_d = jnp.einsum("mjcq,mcqjp->mcqjp", carry, d_mix_f).astype(bf16)
    block_adj = dot("mncq,mcqjp->mcjnp", rkey, carry_d)
    adj = jnp.zeros_like(block_adj[:, 0])
    for c in reversed(range(blocks)):
        adj = block_decay[:, :, c, None, None] * adj + block_adj[:, c]
    adj_out = linked(jnp.concatenate([adj, decay_row], axis=2).astype(bf16), True)
    ends = [None] * blocks
    for c in reversed(range(blocks)):
        ends[c] = adj_out
        adj_out = block_decay[:, :, c, None, None] * adj_out + block_adj[:, c]
    ends = jnp.stack(ends, axis=1)
    ends_low = ends.astype(bf16)
    d_weights = dot("mcqjp,mcsjp->mjcqs", d_mix_b, stepped) * within
    d_scores = jnp.where(same, jnp.sum(d_weights, axis=1), 0.0).astype(bf16)
    pairs = d_weights * scores[:, None]
    d_logs = jnp.sum(pairs, axis=-1) - jnp.sum(pairs, axis=-2)
    back_state = dot("mncq,mcjnp->mcqjp", wkey, ends_low)
    d_stepped = dot("mjcqs,mcqjp->mcsjp", weights, d_mix_b)
    d_stepped = d_stepped + jnp.einsum("mjcq,mcqjp->mcqjp", to_end, back_state)
    from_end = jnp.einsum("mcqjp,mcqjp->mjcq", ending.astype(f32), back_state)
    d_logs = d_logs + jnp.einsum("mcqjp,mcqjp->mjcq", d_mix_f, carried) - from_end
    d_last = jnp.sum(from_end, axis=-1)
    d_last = d_last + block_decay * jnp.einsum("mcjnp,mcjnp->mjc", ends, starts)
    d_logs = d_logs.at[..., -1].add(d_last)
    d_decay = jnp.flip(jnp.cumsum(jnp.flip(d_logs, -1), axis=-1), -1)
    d_decay = (d_decay * (1.0 - first_b)[:, None]).reshape(micro, n_heads, shard)
    d_step = jnp.einsum("mcqjp,mcqjp->mjcq", vals_b, d_stepped).reshape(micro, n_heads, shard)
    d_step = d_step + d_decay * rate[:, None]
    grad_decay = jnp.sum(d_decay * step * rate[:, None], axis=(0, 2))
    grad_skip = jnp.einsum("mcqjp,mcqjp->j", d_mix_f, vals_b)
    d_step_raw = d_step * jax.nn.sigmoid(pre_step)
    grad_bias = jnp.sum(d_step_raw, axis=(0, 2))
    d_vals = jnp.einsum("mjcq,mcqjp->mcqjp", step_b, d_stepped) + skip_mine[:, None] * d_mix_f
    d_vals = d_vals.astype(bf16).astype(f32).reshape(micro, shard, chans)
    d_write = dot("mcqs,mncq->mncs", d_scores, rkey) + dot("mcqjp,mcjnp->mncq", ending, ends_low)
    d_read = dot("mcqs,mncs->mncq", d_scores, wkey) + halved("mcqjp,mcjnp->mncq", carry_d, starts_low)
    d_keys = jnp.concatenate([d_write, d_read], axis=1).reshape(micro, 2 * STATE, shard)
    d_keys = lax.psum_scatter(d_keys, "head", scatter_dimension=1, tiled=True)
    d_keys = lax.reduce_precision(d_keys, 8, 7)

    d_val_tot = d_vals * silu_parts(val_tot)[1]
    d_key_tot = d_keys * silu_parts(key_tot)[1]
    d_val_win, d_key_win = 0.0, 0.0
    grad_conv_val, grad_conv_key = [], []
    for k in range(CONV_K):
        held = d_val_tot * valid[k][:, :, None]
        grad_conv_val.append(jnp.sum(held * val_win[:, k : k + shard], axis=(0, 1)))
        d_val_win = d_val_win + jnp.pad(held * conv_val[k], ((0, 0), (k, EDGE - k), (0, 0)))
        held = d_key_tot * valid[k][:, None]
        grad_conv_key.append(jnp.sum(held * key_win[:, :, k : k + shard], axis=(0, 2)))
        d_key_win = d_key_win + jnp.pad(
            held * conv_key[k][:, None], ((0, 0), (0, 0), (k, EDGE - k))
        )
    grad_conv_val.append(jnp.sum(d_val_tot, axis=(0, 1)))
    grad_conv_key.append(jnp.sum(d_key_tot, axis=(0, 2)))
    rim_back = jnp.concatenate(
        [d_val_win[:, :EDGE], jnp.swapaxes(d_key_win[:, :, :EDGE], 1, 2)], axis=2
    )
    rim_back = lax.ppermute(rim_back, "seq", [(i + 1, i) for i in range(seqs - 1)])
    d_val_in = d_val_win[:, EDGE:].at[:, shard - EDGE :].add(rim_back[:, :, :chans])
    d_key_in = d_key_win[:, :, EDGE:].at[:, :, shard - EDGE :].add(
        jnp.swapaxes(rim_back[:, :, chans:], 1, 2)
    )
    d_val_in = d_val_in.astype(bf16)
    d_small = jnp.concatenate([d_key_in, d_step_raw], axis=1).astype(bf16)

    grad_w_gate = dot("mtd,mtk->dk", normed_low, d_gate).astype(bf16)
    grad_w_val = dot("mtd,mtk->dk", normed_low, d_val_in).astype(bf16)
    grad_w_small = dot("mtd,mkt->dk", normed_low, d_small).astype(bf16)
    d_normed = (
        dot("mtk,dk->mtd", d_gate, w_gate)
        + dot("mtk,dk->mtd", d_val_in, w_val)
        + dot("mkt,kd->mtd", d_small, w_small)
    )
    grad_norm_part = jnp.sum(d_normed * unit, axis=(0, 1))
    d_normed = lax.psum_scatter(
        d_normed.astype(bf16), "head", scatter_dimension=1, tiled=True
    ).astype(f32)
    own = hidden_in.astype(f32)
    own_inv = lax.rsqrt(jnp.mean(own * own, axis=-1, keepdims=True) + EPS)
    d_unit = d_normed * gain
    d_inputs = own_inv * (
        d_unit - own * (own_inv * own_inv * jnp.mean(d_unit * own, axis=-1, keepdims=True))
    )
    grad_in = (out_grad.astype(f32) + d_inputs).astype(bf16)

    def collect(part):
        part = lax.psum_scatter(part, "seq", scatter_dimension=0, tiled=True)
        return lax.all_to_all(
            part.reshape(heads, rows, -1), "head", split_axis=0, concat_axis=0, tiled=True
        ).astype(f32)

    def uncolumns(x, size):
        x = x.reshape(heads, rows, runs, size)
        return jnp.transpose(x, (1, 2, 0, 3)).reshape(rows, runs * heads * size)

    g_gate, g_val, g_small = collect(grad_w_gate), collect(grad_w_val), collect(grad_w_small)
    grad_in_weight = jnp.concatenate(
        [
            uncolumns(g_gate, run_ch),
            uncolumns(g_val, run_ch),
            jnp.transpose(g_small[:, :, :key_ch], (1, 0, 2)).reshape(rows, -1),
            uncolumns(g_small[:, :, key_ch:], run_heads),
        ],
        axis=1,
    )
    if runs == seqs:
        grad_out_weight = lax.psum_scatter(
            grad_out_part, "seq", scatter_dimension=0, tiled=True
        ).astype(f32)
    else:
        full = jnp.zeros((D_INNER, width), bf16)
        full = lax.dynamic_update_slice_in_dim(full, grad_out_part, h_i * chans, 0)
        grad_out_weight = lax.psum_scatter(full, BOTH, scatter_dimension=0, tiled=True).astype(f32)

    def placed(x, size):
        lead = x.shape[:-1]
        full = jnp.zeros(lead + (runs, heads, size), f32)
        full = lax.dynamic_update_index_in_dim(
            full, x.reshape(lead + (runs, size)), h_i, len(lead) + 1
        )
        return full.reshape(lead + (runs * heads * size,))

    conv_val_g = placed(jnp.stack(grad_conv_val), run_ch)
    conv_key_g = lax.dynamic_update_slice_in_dim(
        jnp.zeros((CONV_K + 1, 2 * STATE), f32), jnp.stack(grad_conv_key), h_i * key_ch, 1
    )
    conv_g = jnp.concatenate([conv_val_g, conv_key_g], axis=1)
    head_g = placed(jnp.stack([grad_decay, grad_bias, grad_skip]), run_heads)
    gate_g_full = placed(grad_gate_gain, run_ch)
    conv_g, head_g, gate_g_full, norm_g = lax.psum(
        (conv_g, head_g, gate_g_full, grad_norm_part), BOTH
    )
    place = s_i * heads + h_i
    conv_g = lax.dynamic_slice_in_dim(conv_g, place * conv_share, conv_share, 1)
    head_g = lax.dynamic_slice_in_dim(head_g, h_i * head_share, head_share, 1)
    return (
        hidden_out,
        grad_in,
        lax.dynamic_slice_in_dim(norm_g, place * rows, rows, 0),
        grad_in_weight,
        conv_g[:CONV_K],
        conv_g[CONV_K],
        head_g[0],
        head_g[1],
        head_g[2],
        lax.dynamic_slice_in_dim(gate_g_full, place * gate_share, gate_share, 0),
        grad_out_weight,
    )


def solution(mesh):
    tokens = P(None, BOTH, None)
    by_rows = P(BOTH, None)
    return jax.shard_map(
        body,
        mesh=mesh,
        in_specs=(
            tokens,
            P(),
            P(BOTH),
            by_rows,
            P(None, BOTH),
            P(BOTH),
            P("head"),
            P("head"),
            P("head"),
            P(BOTH),
            by_rows,
            tokens,
        ),
        out_specs=(
            tokens,
            tokens,
            P(BOTH),
            by_rows,
            P(None, BOTH),
            P(BOTH),
            P("head"),
            P("head"),
            P("head"),
            P(BOTH),
            by_rows,
        ),
        check_vma=False,
    )
```

```python
import jax
import jax.numpy as jnp
from jax import lax
from jax.experimental import pallas as pl
from jax.experimental.pallas import tpu as pltpu
from jax.sharding import PartitionSpec as P

HEADS = 64
HEADDIM = 64
STATE = 128
CONV_K = 4
SCAN_BLOCK = 256
D_INNER = 4096
CONV_CH = 4352
EDGE = CONV_K - 1
EPS = 1e-05

f32 = jnp.float32
bf16 = jnp.bfloat16
BOTH = ("seq", "head")


def dot(spec, a, b):
    return jnp.einsum(spec, a, b, preferred_element_type=f32)


def three_parts(v):
    parts = []
    for _ in range(3):
        part = lax.reduce_precision(v, 8, 7)
        parts.append(part.astype(bf16))
        v = v - part
    return parts


def linked(payload, back):
    count = lax.axis_size("seq")
    total, reach = 0.0, 1.0
    for k in range(1, count):
        if back:
            pairs = [(i, i - k) for i in range(k, count)]
        else:
            pairs = [(i, i + k) for i in range(count - k)]
        got = lax.ppermute(payload, "seq", pairs).astype(f32)
        total = total + reach * got[:, :STATE]
        reach = reach * got[:, STATE : STATE + 1]
    return total


def after(x, *others):
    return lax.optimization_barrier((x,) + others)[0]


def seq_steps():
    count = lax.axis_size("seq")
    return [(k, [(i, i ^ k) for i in range(count)]) for k in reversed(range(1, count))]


def seq_gather(x):
    place = lax.axis_index("seq")
    got = [(k, lax.ppermute(x, "seq", pairs)) for k, pairs in seq_steps()]
    full = jnp.zeros((lax.axis_size("seq"),) + x.shape, x.dtype)
    for k, part in [(0, x)] + got:
        full = lax.dynamic_update_index_in_dim(full, part, place ^ k, 0)
    return full


def seq_reduce(parts):
    place = lax.axis_index("seq")
    total = lax.dynamic_index_in_dim(parts, place, 0, False).astype(f32)
    got = [
        lax.ppermute(lax.dynamic_index_in_dim(parts, place ^ k, 0, False), "seq", pairs)
        for k, pairs in seq_steps()
    ]
    for part in got:
        total = total + part.astype(f32)
    return total


def head_swap(x):
    return lax.all_to_all(x, "head", split_axis=0, concat_axis=0, tiled=True)


def silu_parts(v):
    sig = jax.nn.sigmoid(v)
    return v * sig, sig * (1.0 + v * (1.0 - sig))


LANES = 128
LOG, STEP, CARRY, TO_END, SEG = 0, 8, 16, 24, 32
SIG = 16
ROWS_SEG = 24


def nt(a, b):
    return lax.dot_general(a, b, (((1,), (1,)), ((), ())), preferred_element_type=f32)


def nn(a, b):
    return lax.dot_general(a, b, (((1,), (0,)), ((), ())), preferred_element_type=f32)


def tn(a, b):
    return lax.dot_general(a, b, (((0,), (0,)), ((), ())), preferred_element_type=f32)


def split(v):
    high = v.astype(bf16)
    return high, (v - high.astype(f32)).astype(bf16)


def left_half(shape):
    return lax.broadcasted_iota(jnp.int32, shape, len(shape) - 1) < HEADDIM


def pair_of(cols, base, p):
    at = base + 2 * p
    shape = (cols.shape[0], LANES)
    return jnp.where(
        left_half(shape),
        jnp.broadcast_to(cols[:, at : at + 1], shape),
        jnp.broadcast_to(cols[:, at + 1 : at + 2], shape),
    )


def running_sum(x, back=False):
    size = x.shape[1]
    lane = lax.broadcasted_iota(jnp.int32, x.shape, 1)
    shift = 1
    while shift < size:
        if back:
            x = x + jnp.where(lane < size - shift, pltpu.roll(x, size - shift, 1), 0.0)
        else:
            x = x + jnp.where(lane >= shift, pltpu.roll(x, shift, 1), 0.0)
        shift *= 2
    return x


def pairs_in(x):
    return x.shape[-1] // LANES


def lanes(p):
    return slice(p * LANES, (p + 1) * LANES)


def prep_kernel(
    step_ref, seg_ref, par_ref, val_ref, key_ref, cols_ref, rows_ref, ktok_ref, start_ref, pre_ref, out_ref, state, reach
):
    @pl.when(pl.program_id(1) == 0)
    def _():
        state[...] = jnp.zeros_like(state)
        reach[...] = jnp.ones_like(reach)

    raw = step_ref[0] + par_ref[:, 0:1]
    small = jnp.exp(-jnp.abs(raw))
    one = 1.0 + small
    step = jnp.maximum(raw, 0.0) + jnp.where(
        one == 1.0, small, jnp.log(one) * (small / jnp.where(one == 1.0, 1.0, one - 1.0))
    )
    sig = jnp.where(raw >= 0.0, 1.0, small) / one
    log = running_sum(step * par_ref[:, 1:2])
    size = log.shape[1]
    segs = seg_ref[0]
    seg, prev = segs[0:1], segs[1:2]
    carry = jnp.where(seg == prev, jnp.exp(log), 0.0)
    to_end = jnp.where(
        seg == seg[:, size - 1 :], jnp.exp(jnp.minimum(log[:, size - 1 :] - log, 0.0)), 0.0
    )
    rows_ref[0] = jnp.concatenate([log, step, sig, segs], axis=0)
    stack = jnp.concatenate(
        [log, step, carry, to_end, segs, jnp.zeros((LANES - 40, size), f32)], axis=0
    )
    cols = stack.T
    cols_ref[0] = cols
    keys = key_ref[0]
    ktok_ref[0] = keys.astype(f32).T.astype(bf16)
    start_ref[0, 0] = state[...]
    pre_ref[0, 0] = reach[...]
    weight = cols[:, TO_END : TO_END + 8] * cols[:, STEP : STEP + 8]
    for p in range(pairs_in(val_ref)):
        ending = (val_ref[0, :, lanes(p)].astype(f32) * pair_of(weight, 0, p)).astype(bf16)
        decay = pair_of(cols[size - 1 :], CARRY, p)
        state[:, lanes(p)] = decay * state[:, lanes(p)] + nn(keys[:STATE], ending)
        reach[:, lanes(p)] = decay * reach[:, lanes(p)]
    out_ref[0] = jnp.concatenate([state[...], reach[...], reach[...]], axis=0).astype(bf16)


def same_mask(cols, rows):
    size = cols.shape[0]
    at = lax.broadcasted_iota(jnp.int32, (size, size), 0)
    of = lax.broadcasted_iota(jnp.int32, (size, size), 1)
    return (cols[:, SEG : SEG + 1] == rows[ROWS_SEG : ROWS_SEG + 1]) & (at >= of)


def within(cols, rows, j):
    return jnp.exp(jnp.minimum(cols[:, j : j + 1] - rows[j : j + 1], 0.0))


def fwd_kernel(
    val_ref, ktok_ref, cols_ref, rows_ref, start_ref, pre_ref, in_ref, gate_ref, dy_ref, chan_ref, mix_ref, sum_ref
):
    cols, rows = cols_ref[0], rows_ref[0]
    rkey = ktok_ref[0, :, STATE:]
    scores = jnp.where(same_mask(cols, rows), nt(rkey, ktok_ref[0, :, :STATE]), 0.0)
    squares, products = 0.0, 0.0
    left = left_half((cols.shape[0], LANES))
    for p in range(pairs_in(val_ref)):
        at = lanes(p)
        vals = val_ref[0, :, at].astype(f32)
        stepped = vals * pair_of(cols, STEP, p)
        high, low = split(start_ref[0, 0, :, at] + pre_ref[0, 0, 0:1, at] * in_ref[0, :, at])
        mixed = pair_of(cols, CARRY, p) * (nn(rkey, high) + nn(rkey, low))
        for half in range(2):
            weights = (scores * within(cols, rows, 2 * p + half)).astype(bf16)
            keep = left if half == 0 else ~left
            mixed = mixed + nn(weights, jnp.where(keep, stepped, 0.0).astype(bf16))
        mixed = (mixed + chan_ref[0:1, at] * vals).astype(bf16)
        mix_ref[0, :, at] = mixed
        gate = gate_ref[0, :, at]
        gated = mixed.astype(f32) * (gate / (1.0 + jnp.exp(-gate)))
        squares = squares + gated * gated
        products = products + gated * (dy_ref[0, :, at] * chan_ref[1:2, at])
    lane = lax.broadcasted_iota(jnp.int32, squares.shape, 1)
    sums = jnp.where(
        lane == 0,
        jnp.sum(squares, axis=1, keepdims=True),
        jnp.where(lane == 1, jnp.sum(products, axis=1, keepdims=True), 0.0),
    )
    sum_ref[0] = sums.T[0:8]


def norm_kernel(
    mix_ref, gate_ref, dy_ref, sum_ref, cols_ref, key_ref, pre_ref, chan_ref, reach_ref,
    yn_ref, dmix_ref, dgate_ref, gain_ref, adj_ref, out_ref, adj
):
    c = pl.program_id(1)

    @pl.when((pl.program_id(0) == 0) & (c == 0))
    def _():
        gain_ref[...] = jnp.zeros_like(gain_ref)

    @pl.when(c == 0)
    def _():
        adj[...] = jnp.zeros_like(adj)

    cols = cols_ref[0]
    size = cols.shape[0]
    rows = sum_ref[0]
    scale_row = lax.rsqrt(rows[0:1] * (1.0 / D_INNER) + EPS)
    pull_row = scale_row * scale_row * rows[1:2] * (1.0 / D_INNER)
    both = jnp.concatenate([scale_row, pull_row, jnp.zeros((LANES - 2, size), f32)], axis=0).T
    scale, pull = both[:, 0:1], both[:, 1:2]
    for p in range(pairs_in(mix_ref)):
        at = lanes(p)
        mixer = mix_ref[0, :, at].astype(f32)
        gate = gate_ref[0, :, at]
        sig = 1.0 / (1.0 + jnp.exp(-gate))
        act = gate * sig
        slope = sig * (1.0 + gate * (1.0 - sig))
        gated = mixer * act
        unit = gated * scale
        gain = chan_ref[1:2, at]
        yn_ref[0, :, at] = (unit * gain).astype(bf16)
        d_y = dy_ref[0, :, at]
        gain_ref[0:1, at] += jnp.sum(d_y * unit, axis=0, keepdims=True)
        d_gated = scale * (d_y * gain - gated * pull)
        d_mix = (d_gated * act).astype(bf16)
        dmix_ref[0, :, at] = d_mix
        dgate_ref[0, :, at] = (d_gated * mixer * slope).astype(bf16)
        carried = (d_mix.astype(f32) * pair_of(cols, CARRY, p)).astype(bf16)
        block = nn(key_ref[0, STATE:], carried)
        adj_ref[0, 0, :, at] = block
        adj[:, at] = pair_of(cols[size - 1 :], CARRY, p) * adj[:, at] + block
    reach = reach_ref[0]
    out_ref[0] = jnp.concatenate([adj[...].astype(bf16), reach], axis=0)


def bwd_kernel(
    val_ref, key_ref, ktok_ref, cols_ref, rows_ref, start_ref, pre_ref, in_ref, dmix_ref, adj_ref, adjin_ref, chan_ref, par_ref,
    dval_ref, dkey_ref, dstep_ref, head_ref, skip_ref, adj
):
    c = pl.program_id(1)

    @pl.when((pl.program_id(0) == 0) & (c == 0))
    def _():
        head_ref[...] = jnp.zeros_like(head_ref)
        skip_ref[...] = jnp.zeros_like(skip_ref)

    @pl.when(c == 0)
    def _():
        adj[...] = adjin_ref[0]

    cols, rows = cols_ref[0], rows_ref[0]
    size = cols.shape[0]
    wkey, rkey = ktok_ref[0, :, :STATE], ktok_ref[0, :, STATE:]
    same = same_mask(cols, rows)
    scores = jnp.where(same, nt(rkey, wkey), 0.0)
    left = left_half((size, LANES))
    lane = lax.broadcasted_iota(jnp.int32, (size, LANES), 1)
    lane_row = lax.broadcasted_iota(jnp.int32, (1, LANES), 1)
    d_scores = jnp.zeros((size, size), f32)
    d_write = jnp.zeros((STATE, size), f32)
    d_read = jnp.zeros((STATE, size), f32)
    by_row = jnp.zeros((size, LANES), f32)
    last = jnp.zeros((1, LANES), f32)
    by_col = []

    def put(total, p, half, values, offset=0):
        where = lane if values.shape[0] == size else lane_row
        return jnp.where(where == offset + 2 * p + half, values, total)

    def halves_of(x):
        first = jnp.sum(jnp.where(left[: x.shape[0]], x, 0.0), axis=1, keepdims=True)
        return first, jnp.sum(x, axis=1, keepdims=True) - first

    for p in range(pairs_in(val_ref)):
        at = lanes(p)
        vals = val_ref[0, :, at].astype(f32)
        d_mix = dmix_ref[0, :, at]
        d_mix_f = d_mix.astype(f32)
        step = pair_of(cols, STEP, p)
        stepped_f = vals * step
        stepped = stepped_f.astype(bf16)
        carry = pair_of(cols, CARRY, p)
        state = start_ref[0, 0, :, at] + pre_ref[0, 0, 0:1, at] * in_ref[0, :, at]
        high, low = split(state)
        end = adj[:, at]
        end_low = end.astype(bf16)
        ending_f = stepped_f * pair_of(cols, TO_END, p)
        ending = ending_f.astype(bf16)
        carried_d = (d_mix_f * carry).astype(bf16)
        back = nn(wkey, end_low)
        d_stepped = pair_of(cols, TO_END, p) * back
        from_end = ending_f * back
        through = d_mix_f * carry * (nn(rkey, high) + nn(rkey, low)) - from_end
        decay = pair_of(cols[size - 1 :], CARRY, p)
        final = jnp.sum(from_end, axis=0, keepdims=True) + decay * jnp.sum(
            end * state, axis=0, keepdims=True
        )
        final = halves_of(final)
        through = halves_of(through)
        for half in range(2):
            keep = left if half == 0 else ~left
            held = jnp.where(keep, d_mix_f, 0.0).astype(bf16)
            j = 2 * p + half
            near = within(cols, rows, j)
            d_near = nt(held, stepped) * near
            d_scores = d_scores + d_near
            pairs = d_near * scores
            by_row = put(by_row, p, half, jnp.sum(pairs, axis=1, keepdims=True) + through[half])
            by_col.append(jnp.sum(pairs, axis=0, keepdims=True))
            last = put(last, p, half, final[half])
            d_stepped = d_stepped + tn((scores * near).astype(bf16), held)
        d_vals = step * d_stepped + chan_ref[0:1, at] * d_mix_f
        dval_ref[0, :, at] = d_vals.astype(bf16)
        skip_ref[0:1, at] += jnp.sum(d_mix_f * vals, axis=0, keepdims=True)
        d_step = halves_of(vals * d_stepped)
        for half in range(2):
            by_row = put(by_row, p, half, d_step[half], 8)
        d_write = d_write + nt(end_low, ending)
        d_read = d_read + nt(high, carried_d) + nt(low, carried_d)
        adj[:, at] = decay * end + adj_ref[0, 0, :, at]
    d_scores = jnp.where(same, d_scores, 0.0).astype(bf16)
    d_write = d_write + nn(key_ref[0, STATE:], d_scores)
    d_read = d_read + nt(key_ref[0, :STATE], d_scores)
    dkey_ref[0] = jnp.concatenate([d_write, d_read], axis=0)
    while len(by_col) < 8:
        by_col.append(jnp.zeros((1, size), f32))
    turned = by_row.T
    last = jnp.broadcast_to(last, (LANES, LANES)).T[0:8, 0:1]
    d_log = turned[0:8] - jnp.concatenate(by_col, axis=0)
    rate = par_ref[:, 1:2]
    first = rows[ROWS_SEG + 2 : ROWS_SEG + 3]
    d_decay = (running_sum(d_log, True) + last) * (1.0 - first)
    d_raw = (turned[8:16] + d_decay * rate) * rows[SIG : SIG + 8]
    dstep_ref[0] = d_raw
    head_lane = lax.broadcasted_iota(jnp.int32, (8, LANES), 1)
    head_ref[...] += jnp.where(
        head_lane == 0,
        jnp.sum(d_decay * rows[STEP : STEP + 8], axis=1, keepdims=True) * rate,
        jnp.where(head_lane == 1, jnp.sum(d_raw, axis=1, keepdims=True), 0.0),
    )


def kernel_call(kernel, grid, ins, outs, scratch, flops):
    return pl.pallas_call(
        kernel,
        grid=grid,
        in_specs=[pl.BlockSpec(block, index) for block, index in ins],
        out_specs=[pl.BlockSpec(block, index) for _, _, block, index in outs],
        out_shape=[jax.ShapeDtypeStruct(shape, dtype) for shape, dtype, _, _ in outs],
        scratch_shapes=scratch,
        compiler_params=pltpu.CompilerParams(
            vmem_limit_bytes=40 * 2**20, dimension_semantics=("arbitrary", "arbitrary")
        ),
        cost_estimate=pl.CostEstimate(flops=flops, bytes_accessed=8 * 2**20, transcendentals=0),
    )


def body(
    hidden_in,
    seq_starts,
    norm_gain,
    in_weight,
    conv_weight,
    conv_bias,
    decay_log,
    dt_bias,
    skip_gain,
    gate_gain,
    out_weight,
    out_grad,
):
    seqs, heads = lax.axis_size("seq"), lax.axis_size("head")
    s_i, h_i = lax.axis_index("seq"), lax.axis_index("head")
    micro, tok, width = hidden_in.shape
    rows = in_weight.shape[0]
    shard = tok * heads
    runs = seqs if HEADS % (seqs * heads) == 0 else 1
    run_ch = D_INNER // (runs * heads)
    run_heads = HEADS // (runs * heads)
    chans, n_heads = runs * run_ch, runs * run_heads
    key_ch = 2 * STATE // heads
    wide = max(chans, LANES)

    def widen(x, axis=-1):
        pads = [(0, 0)] * x.ndim
        pads[axis] = (0, wide - chans)
        return jnp.pad(x, pads) if wide > chans else x

    conv_share, gate_share, head_share = conv_bias.shape[0], gate_gain.shape[0], decay_log.shape[0]

    def mine(x, size):
        lead = x.shape[:-1]
        x = x.reshape(lead + (runs, heads, size))
        x = lax.dynamic_index_in_dim(x, h_i, len(lead) + 1, False)
        return x.reshape(lead + (runs * size,))

    def columns(x, size):
        x = x.reshape(rows, runs, heads, size)
        return jnp.transpose(x, (2, 0, 1, 3)).reshape(heads, rows, runs * size)

    extras = jnp.concatenate(
        [norm_gain, conv_weight.reshape(-1), conv_bias, gate_gain]
        + three_parts(decay_log)
        + three_parts(dt_bias)
        + three_parts(skip_gain)
    )
    extra_cols = -(-extras.shape[0] // rows)
    extras = jnp.pad(extras, (0, extra_cols * rows - extras.shape[0])).reshape(extra_cols, rows)
    key_p = jnp.transpose(
        in_weight[:, 2 * D_INNER : 2 * D_INNER + 2 * STATE].reshape(rows, heads, key_ch), (1, 2, 0)
    )
    step_p = jnp.transpose(
        in_weight[:, 2 * D_INNER + 2 * STATE :].reshape(rows, runs, heads, run_heads), (2, 1, 3, 0)
    ).reshape(heads, n_heads, rows)
    small_p = jnp.concatenate(
        [key_p, step_p, jnp.broadcast_to(extras[None], (heads,) + extras.shape)], axis=1
    )
    small_rows = -(-small_p.shape[1] * rows // chans)
    small_rows += -(rows + small_rows) % 8
    small_f = small_p.reshape(heads, -1)
    small_f = jnp.pad(small_f, ((0, 0), (0, small_rows * chans - small_f.shape[1])))
    small_f = small_f.reshape(heads, small_rows, chans)
    val_p = columns(in_weight[:, D_INNER : 2 * D_INNER], run_ch)
    if runs == seqs:
        w_out = seq_gather(out_weight).reshape(chans, width)
    else:
        w_out = lax.all_gather(out_weight, BOTH, axis=0, tiled=True)
        w_out = widen(lax.dynamic_slice_in_dim(w_out, h_i * chans, chans, 0), 0)
    first = head_swap(jnp.concatenate([val_p, small_f], axis=1))
    second = head_swap(after(columns(in_weight[:, :D_INNER], run_ch), first))
    first = seq_gather(first)
    w_val = widen(first[:, :, :rows].reshape(width, chans))
    small = first[:, :, rows:].reshape(seqs, heads, -1)[:, :, : small_p.shape[1] * rows]
    small = small.reshape(seqs, heads, -1, rows)
    w_gate = widen(seq_gather(second).reshape(width, chans))
    n_small = key_ch + n_heads
    w_small = jnp.transpose(small[:, :, :n_small], (2, 0, 1, 3)).reshape(n_small, width)
    extras = small[:, :, n_small:].reshape(seqs * heads, -1)
    at = 0

    def take(size):
        nonlocal at
        at += size
        return extras[:, at - size : at]

    gain = take(rows).reshape(width).astype(f32)
    conv_w = jnp.transpose(take(CONV_K * conv_share).reshape(-1, CONV_K, conv_share), (1, 0, 2))
    conv_w = conv_w.reshape(CONV_K, CONV_CH).astype(f32)
    conv_b = take(conv_share).reshape(1, CONV_CH).astype(f32)
    conv_p = jnp.concatenate([conv_w, conv_b], axis=0)
    gate_g = mine(take(gate_share).reshape(D_INNER), run_ch).astype(f32)

    def head_param():
        x = take(3 * head_share)[:heads].reshape(heads, 3, head_share).astype(f32)
        return mine((x[:, 0] + x[:, 1] + x[:, 2]).reshape(HEADS), run_heads)

    decay_mine, bias_mine, skip_mine = head_param(), head_param(), head_param()
    conv_val = widen(mine(conv_p[:, :D_INNER], run_ch))
    conv_key = lax.dynamic_slice_in_dim(conv_p[:, D_INNER:], h_i * key_ch, key_ch, 1)
    inputs = lax.all_gather(hidden_in, "head", axis=1, tiled=True)
    grad_rows = lax.all_gather(after(out_grad, inputs), "head", axis=1, tiled=True)
    inputs = inputs.astype(f32)
    inv = lax.rsqrt(jnp.mean(inputs * inputs, axis=-1, keepdims=True) + EPS)
    unit = inputs * inv
    normed_low = (unit * gain).astype(bf16)
    val_in = dot("mtd,dk->mtk", normed_low, w_val).astype(bf16)
    small_in = dot("kd,mtd->mkt", w_small, normed_low).astype(bf16)
    key_in, step_low = small_in[:, :key_ch], small_in[:, key_ch:].astype(f32)
    gate_in = dot("mtd,dk->mtk", normed_low, w_gate)

    positions = s_i * shard - EDGE + jnp.arange(shard + EDGE)
    segs = jnp.sum((seq_starts[:, None, :] <= positions[None, :, None]).astype(jnp.int32), axis=2)
    valid = [
        (segs[:, k : k + shard] == segs[:, EDGE:]).astype(f32) for k in range(CONV_K)
    ]
    segs_w, segs = segs, segs[:, EDGE:]
    rim = jnp.concatenate(
        [val_in[:, shard - EDGE :], jnp.swapaxes(key_in[:, :, shard - EDGE :], 1, 2)], axis=2
    )
    forward = [(i, i + 1) for i in range(seqs - 1)]
    rim = lax.ppermute(rim, "seq", forward)
    val_win = jnp.concatenate([rim[:, :, :wide], val_in], axis=1).astype(f32)
    key_win = jnp.concatenate(
        [jnp.swapaxes(rim[:, :, wide:], 1, 2), key_in], axis=2
    ).astype(f32)
    val_tot = conv_val[CONV_K]
    key_tot = conv_key[CONV_K][:, None]
    for k in range(CONV_K):
        val_tot = val_tot + conv_val[k] * val_win[:, k : k + shard] * valid[k][:, :, None]
        key_tot = key_tot + conv_key[k][:, None] * key_win[:, :, k : k + shard] * valid[k][:, None]
    vals = jax.nn.silu(val_tot).astype(bf16)
    keys = jax.nn.silu(key_tot).astype(bf16)
    keys = lax.all_gather(keys, "head", axis=1, tiled=True)

    blocks = shard // SCAN_BLOCK
    grid = (micro, blocks)
    size = SCAN_BLOCK
    flops = 4 * micro * shard * size * wide
    here = lambda m, c: (m, c, 0)
    along = lambda m, c: (m, 0, c)
    state_at = lambda m, c: (m, c, 0, 0)
    micro_at = lambda m, c: (m, 0, 0)
    fixed = lambda m, c: (0, 0)
    row8 = (1, 8, size)
    tok_c, tok_l = (1, size, wide), (1, size, LANES)
    pad_rows = lambda x: jnp.pad(x, ((0, 0), (0, 8 - x.shape[1]), (0, 0)))
    params = jnp.pad(jnp.stack([bias_mine, -jnp.exp(decay_mine)], axis=1), ((0, 8 - n_heads), (0, LANES - 2)))
    skip_row = jnp.repeat(skip_mine, HEADDIM)
    chan = jnp.pad(jnp.stack([widen(skip_row), widen(gate_g)]), ((0, 6), (0, 0)))
    before = jnp.repeat(segs_w[:, EDGE - 1 : -1].reshape(micro, blocks, size)[:, :, 0], size, axis=1)
    seg_rows = jnp.stack([segs, before, (segs != segs_w[:, EDGE - 1 : -1]).astype(jnp.int32)], axis=1)
    seg_rows = pad_rows(seg_rows.astype(f32))
    n_state = STATE + 16
    f_state = ((1, 1, STATE, wide), state_at)
    f_pre = ((1, 1, 8, wide), state_at)
    cols, rows_t, ktok, starts, prefix, payload = kernel_call(
        prep_kernel,
        grid,
        [(row8, along), (row8, along), ((8, LANES), fixed), (tok_c, here), ((1, 2 * STATE, size), along)],
        [
            ((micro, shard, LANES), f32, tok_l, here),
            ((micro, 32, shard), f32, (1, 32, size), along),
            ((micro, shard, 2 * STATE), bf16, (1, size, 2 * STATE), here),
            ((micro, blocks, STATE, wide), f32) + f_state,
            ((micro, blocks, 8, wide), f32) + f_pre,
            ((micro, n_state, wide), bf16, (1, n_state, wide), micro_at),
        ],
        [pltpu.VMEM((STATE, wide), f32), pltpu.VMEM((8, wide), f32)],
        flops,
    )(pad_rows(step_low), seg_rows, params, vals, keys)
    state_in = linked(payload, False)
    d_ynorm = dot("mtd,kd->mtk", grad_rows, w_out)
    mixer, sums = kernel_call(
        fwd_kernel,
        grid,
        [
            (tok_c, here),
            ((1, size, 2 * STATE), here),
            (tok_l, here),
            ((1, 32, size), along),
            f_state,
            f_pre,
            ((1, STATE, wide), micro_at),
            (tok_c, here),
            (tok_c, here),
            ((8, wide), fixed),
        ],
        [((micro, shard, wide), bf16, tok_c, here), ((micro, 8, shard), f32, row8, along)],
        [],
        2 * flops,
    )(vals, ktok, cols, rows_t, starts, prefix, state_in, gate_in, d_ynorm, chan)

    sums = pad_rows(lax.psum(sums[:, :2], "head"))
    back_here = lambda m, c: (m, blocks - 1 - c, 0)
    back_along = lambda m, c: (m, 0, blocks - 1 - c)
    back_state = lambda m, c: (m, blocks - 1 - c, 0, 0)
    b_state, b_pre = (f_state[0], back_state), (f_pre[0], back_state)
    ynorm_low, d_mix, d_gate, gate_gain_g, block_adj, payload = kernel_call(
        norm_kernel,
        grid,
        [
            (tok_c, back_here),
            (tok_c, back_here),
            (tok_c, back_here),
            (row8, back_along),
            (tok_l, back_here),
            ((1, 2 * STATE, size), back_along),
            b_pre,
            ((8, wide), fixed),
            ((1, 16, wide), micro_at),
        ],
        [
            ((micro, shard, wide), bf16, tok_c, back_here),
            ((micro, shard, wide), bf16, tok_c, back_here),
            ((micro, shard, wide), bf16, tok_c, back_here),
            ((8, wide), f32, (8, wide), fixed),
            ((micro, blocks, STATE, wide), f32) + b_state,
            ((micro, n_state, wide), bf16, (1, n_state, wide), micro_at),
        ],
        [pltpu.VMEM((STATE, wide), f32)],
        flops,
    )(mixer, gate_in, d_ynorm, sums, cols, keys, prefix, chan, payload[:, STATE:])
    adj_in = linked(payload, True)
    out_part = dot("mtk,kd->mtd", ynorm_low, w_out).astype(bf16)
    out_sum = lax.psum_scatter(out_part, "head", scatter_dimension=1, tiled=True)
    hidden_out = (hidden_in.astype(f32) + out_sum.astype(f32)).astype(bf16)
    grad_out_part = dot("mtk,mtd->kd", ynorm_low, grad_rows).astype(bf16)

    d_vals, d_keys, d_step_raw, head_g, skip_g = kernel_call(
        bwd_kernel,
        grid,
        [
            (tok_c, back_here),
            ((1, 2 * STATE, size), back_along),
            ((1, size, 2 * STATE), back_here),
            (tok_l, back_here),
            ((1, 32, size), back_along),
            b_state,
            b_pre,
            ((1, STATE, wide), micro_at),
            (tok_c, back_here),
            b_state,
            ((1, STATE, wide), micro_at),
            ((8, wide), fixed),
            ((8, LANES), fixed),
        ],
        [
            ((micro, shard, wide), bf16, tok_c, back_here),
            ((micro, 2 * STATE, shard), f32, (1, 2 * STATE, size), back_along),
            ((micro, 8, shard), f32, row8, back_along),
            ((8, LANES), f32, (8, LANES), fixed),
            ((8, wide), f32, (8, wide), fixed),
        ],
        [pltpu.VMEM((STATE, wide), f32)],
        4 * flops,
    )(
        vals, keys, ktok, cols, rows_t, starts, prefix, state_in, d_mix, block_adj, adj_in, chan, params
    )
    d_step_raw = d_step_raw[:, :n_heads]
    grad_decay, grad_bias = head_g[:n_heads, 0], head_g[:n_heads, 1]
    grad_skip = jnp.sum(skip_g[0, :chans].reshape(n_heads, HEADDIM), axis=1)
    d_keys = jnp.swapaxes(d_keys.astype(bf16).reshape(micro, heads, key_ch, shard), 0, 1)
    d_keys = jnp.sum(head_swap(d_keys).astype(f32), axis=0)
    d_keys = lax.reduce_precision(d_keys, 8, 7)

    d_val_tot = d_vals.astype(f32) * silu_parts(val_tot)[1]
    d_key_tot = d_keys * silu_parts(key_tot)[1]
    d_val_win, d_key_win = 0.0, 0.0
    grad_conv_val, grad_conv_key = [], []
    for k in range(CONV_K):
        held = d_val_tot * valid[k][:, :, None]
        grad_conv_val.append(jnp.sum(held * val_win[:, k : k + shard], axis=(0, 1)))
        d_val_win = d_val_win + jnp.pad(held * conv_val[k], ((0, 0), (k, EDGE - k), (0, 0)))
        held = d_key_tot * valid[k][:, None]
        grad_conv_key.append(jnp.sum(held * key_win[:, :, k : k + shard], axis=(0, 2)))
        d_key_win = d_key_win + jnp.pad(
            held * conv_key[k][:, None], ((0, 0), (0, 0), (k, EDGE - k))
        )
    grad_conv_val.append(jnp.sum(d_val_tot, axis=(0, 1)))
    grad_conv_key.append(jnp.sum(d_key_tot, axis=(0, 2)))
    rim_back = jnp.concatenate(
        [d_val_win[:, :EDGE], jnp.swapaxes(d_key_win[:, :, :EDGE], 1, 2)], axis=2
    )
    rim_back = lax.ppermute(rim_back, "seq", [(i + 1, i) for i in range(seqs - 1)])
    d_val_in = d_val_win[:, EDGE:].at[:, shard - EDGE :].add(rim_back[:, :, :wide])
    d_key_in = d_key_win[:, :, EDGE:].at[:, :, shard - EDGE :].add(
        jnp.swapaxes(rim_back[:, :, wide:], 1, 2)
    )
    d_val_in = d_val_in.astype(bf16)
    d_small = jnp.concatenate([d_key_in, d_step_raw], axis=1).astype(bf16)

    grad_w_gate = dot("mtd,mtk->dk", normed_low, d_gate)[:, :chans].astype(bf16)
    grad_w_val = dot("mtd,mtk->dk", normed_low, d_val_in)[:, :chans].astype(bf16)
    grad_w_small = dot("mtd,mkt->dk", normed_low, d_small).astype(bf16)
    d_normed = (
        dot("mtk,dk->mtd", d_gate, w_gate)
        + dot("mtk,dk->mtd", d_val_in, w_val)
        + dot("mkt,kd->mtd", d_small, w_small)
    )
    grad_norm_part = jnp.sum(d_normed * unit, axis=(0, 1))
    d_normed = lax.psum_scatter(
        d_normed.astype(bf16), "head", scatter_dimension=1, tiled=True
    ).astype(f32)
    own = hidden_in.astype(f32)
    own_inv = lax.rsqrt(jnp.mean(own * own, axis=-1, keepdims=True) + EPS)
    d_unit = d_normed * gain
    d_inputs = own_inv * (
        d_unit - own * (own_inv * own_inv * jnp.mean(d_unit * own, axis=-1, keepdims=True))
    )
    grad_in = (out_grad.astype(f32) + d_inputs).astype(bf16)

    def collect(part):
        part = seq_reduce(part.reshape(seqs, heads * rows, -1)).astype(bf16)
        return head_swap(part.reshape(heads, rows, -1)).astype(f32)

    def uncolumns(x, size):
        x = x.reshape(heads, rows, runs, size)
        return jnp.transpose(x, (1, 2, 0, 3)).reshape(rows, runs * heads * size)

    g_gate, g_val = collect(grad_w_gate), collect(jnp.concatenate([grad_w_val, grad_w_small], axis=1))
    g_key = g_val[:, :, chans : chans + key_ch]
    grad_in_weight = jnp.concatenate(
        [
            uncolumns(g_gate, run_ch),
            uncolumns(g_val[:, :, :chans], run_ch),
            jnp.transpose(g_key, (1, 0, 2)).reshape(rows, -1),
            uncolumns(g_val[:, :, chans + key_ch :], run_heads),
        ],
        axis=1,
    )
    if runs == seqs:
        grad_out_weight = seq_reduce(grad_out_part.reshape(seqs, run_ch, width))
    else:
        full = jnp.zeros((D_INNER, width), bf16)
        full = lax.dynamic_update_slice_in_dim(full, grad_out_part[:chans], h_i * chans, 0)
        grad_out_weight = lax.psum_scatter(full, BOTH, scatter_dimension=0, tiled=True).astype(f32)

    head_g = jnp.concatenate([grad_decay, grad_bias, grad_skip])
    conv_g = jnp.concatenate(
        [jnp.stack(grad_conv_val)[:, :chans], jnp.stack(grad_conv_key)], axis=1
    ).reshape(-1)
    gate_gg = gate_gain_g[0, :chans]
    norm_g = grad_norm_part.reshape(seqs, heads * rows)
    fixed_part = jnp.concatenate([conv_g, head_g, gate_gg])
    parts = jnp.concatenate(
        [norm_g, jnp.broadcast_to(fixed_part[None], (seqs,) + fixed_part.shape)], axis=1
    )
    fill = -parts.shape[1] % (8 * LANES)
    parts = jnp.pad(parts, ((0, 0), (0, fill))).reshape(seqs, 8, -1)
    sums = lax.all_gather(seq_reduce(parts), "head").reshape(heads, -1)
    at = 0

    def part_of(size):
        nonlocal at
        at += size
        return sums[:, at - size : at]

    norm_g = jnp.sum(part_of(heads * rows), axis=0)
    conv_g = part_of((CONV_K + 1) * (chans + key_ch)).reshape(heads, CONV_K + 1, chans + key_ch)
    head_g = part_of(3 * n_heads).reshape(heads, 3, runs, run_heads)
    gate_gg = part_of(chans).reshape(heads, runs, run_ch)
    conv_gv = jnp.transpose(conv_g[:, :, :chans].reshape(heads, CONV_K + 1, runs, run_ch), (1, 2, 0, 3))
    conv_gk = jnp.transpose(conv_g[:, :, chans:], (1, 0, 2))
    conv_g = jnp.concatenate(
        [conv_gv.reshape(CONV_K + 1, D_INNER), conv_gk.reshape(CONV_K + 1, 2 * STATE)], axis=1
    )
    head_g = jnp.transpose(head_g, (1, 2, 0, 3)).reshape(3, HEADS)
    gate_gg = jnp.transpose(gate_gg, (1, 0, 2)).reshape(D_INNER)
    place = s_i * heads + h_i
    conv_g = lax.dynamic_slice_in_dim(conv_g, place * conv_share, conv_share, 1)
    head_g = lax.dynamic_slice_in_dim(head_g, h_i * head_share, head_share, 1)
    return (
        hidden_out,
        grad_in,
        lax.dynamic_slice_in_dim(norm_g, h_i * rows, rows, 0),
        grad_in_weight,
        conv_g[:CONV_K],
        conv_g[CONV_K],
        head_g[0],
        head_g[1],
        head_g[2],
        lax.dynamic_slice_in_dim(gate_gg, place * gate_share, gate_share, 0),
        grad_out_weight,
    )


def solution(mesh):
    tokens = P(None, BOTH, None)
    by_rows = P(BOTH, None)
    return jax.shard_map(
        body,
        mesh=mesh,
        in_specs=(
            tokens,
            P(),
            P(BOTH),
            by_rows,
            P(None, BOTH),
            P(BOTH),
            P("head"),
            P("head"),
            P("head"),
            P(BOTH),
            by_rows,
            tokens,
        ),
        out_specs=(
            tokens,
            tokens,
            P(BOTH),
            by_rows,
            P(None, BOTH),
            P(BOTH),
            P("head"),
            P("head"),
            P("head"),
            P(BOTH),
            by_rows,
        ),
        check_vma=False,
    )
```

```python
import functools

import jax
import jax.numpy as jnp
from jax import lax
from jax.experimental import pallas as pl
from jax.experimental.pallas import tpu as pltpu
from jax.sharding import PartitionSpec as P

HEADS = 64
HEADDIM = 64
STATE = 128
CONV_K = 4
SCAN_BLOCK = 256
D_INNER = 4096
CONV_CH = 4352
EDGE = CONV_K - 1
EPS = 1e-05

f32 = jnp.float32
bf16 = jnp.bfloat16
BOTH = ("seq", "head")


def dot(spec, a, b):
    return jnp.einsum(spec, a, b, preferred_element_type=f32)


def three_parts(v):
    parts = []
    for _ in range(3):
        part = lax.reduce_precision(v, 8, 7)
        parts.append(part.astype(bf16))
        v = v - part
    return parts


def linked(payload, back, *wait):
    count = lax.axis_size("seq")
    total, reach = 0.0, 1.0
    for k in range(1, count):
        if back:
            pairs = [(i, i - k) for i in range(k, count)]
        else:
            pairs = [(i, i + k) for i in range(count - k)]
        got = after(lax.ppermute(payload, "seq", pairs), *wait).astype(f32)
        total = total + reach * got[:, :STATE]
        reach = reach * got[:, STATE : STATE + 1]
    return total


def after(x, *others):
    return lax.optimization_barrier((x, others))[0]


def seq_steps():
    count = lax.axis_size("seq")
    return [(k, [(i, i ^ k) for i in range(count)]) for k in reversed(range(1, count))]


def seq_gather(x, *wait):
    got = [(k, lax.ppermute(x, "seq", pairs)) for k, pairs in seq_steps()]
    if wait:
        got = [(k, after(part, *wait)) for k, part in got]
    parts = dict(got)
    parts[0] = x
    return [parts[k] for k in sorted(parts)]


def seq_reduce(parts):
    total = parts[0].astype(f32)
    got = [lax.ppermute(parts[k], "seq", pairs) for k, pairs in seq_steps()]
    for part in got:
        total = total + part.astype(f32)
    return total


def from_steps(x, place):
    return jnp.stack([lax.dynamic_index_in_dim(x, place ^ k, 0, False) for k in range(x.shape[0])])


def head_swap(x):
    return lax.all_to_all(x, "head", split_axis=0, concat_axis=0, tiled=True)


def silu_parts(v):
    sig = jax.nn.sigmoid(v)
    return v * sig, sig * (1.0 + v * (1.0 - sig))


LANES = 128
LOG, STEP, CARRY, TO_END, SEG = 0, 8, 16, 24, 32
SIG = 16
ROWS_SEG = 24


def nt(a, b):
    return lax.dot_general(a, b, (((1,), (1,)), ((), ())), preferred_element_type=f32)


def nn(a, b):
    return lax.dot_general(a, b, (((1,), (0,)), ((), ())), preferred_element_type=f32)


def tn(a, b):
    return lax.dot_general(a, b, (((0,), (0,)), ((), ())), preferred_element_type=f32)


def split(v):
    high = v.astype(bf16)
    return high, (v - high.astype(f32)).astype(bf16)


def left_half(shape):
    return lax.broadcasted_iota(jnp.int32, shape, len(shape) - 1) < HEADDIM


def pair_of(cols, base, p):
    at = base + 2 * p
    shape = (cols.shape[0], LANES)
    return jnp.where(
        left_half(shape),
        jnp.broadcast_to(cols[:, at : at + 1], shape),
        jnp.broadcast_to(cols[:, at + 1 : at + 2], shape),
    )


def running_sum(x, back=False):
    size = x.shape[1]
    lane = lax.broadcasted_iota(jnp.int32, x.shape, 1)
    shift = 1
    while shift < size:
        if back:
            x = x + jnp.where(lane < size - shift, pltpu.roll(x, size - shift, 1), 0.0)
        else:
            x = x + jnp.where(lane >= shift, pltpu.roll(x, shift, 1), 0.0)
        shift *= 2
    return x


def pairs_in(x):
    return x.shape[-1] // LANES


def lanes(p):
    return slice(p * LANES, (p + 1) * LANES)


def mask_kernel(place_ref, start_ref, seg_ref, valid_ref, cols_ref):
    m = pl.program_id(0)
    size = seg_ref.shape[2]
    at = place_ref[0] * size + lax.broadcasted_iota(jnp.int32, (1, size), 1)

    def seg_of(position):
        total = jnp.zeros((1, size), f32)
        for i in range(start_ref.shape[1]):
            total = total + jnp.where(position >= start_ref[m, i], 1.0, 0.0)
        return total

    seg = seg_of(at)
    behind = [seg_of(at - by) for by in range(1, CONV_K)]
    block = seg_of(at - at % SCAN_BLOCK - 1)
    first = jnp.where(seg == behind[0], 0.0, 1.0)
    seg_ref[0] = jnp.concatenate([seg, block, first, jnp.zeros((5, size), f32)], axis=0)
    rows = [jnp.where(seg == x, 1.0, 0.0) for x in reversed(behind)] + [jnp.ones((1, size), f32)]
    rows = jnp.concatenate(rows + [jnp.zeros((8 - CONV_K, size), f32)], axis=0)
    valid_ref[0] = rows
    cols_ref[0] = jnp.concatenate([rows, jnp.zeros((LANES - 8, size), f32)], axis=0).T


GAIN_AT, GATE_AT, HEAD_AT, CONV_AT, SENT = 0, 128, 256, 384, 384 + 256 * (CONV_K + 1)


def glue_kernel(place_ref, sent_ref, gain_ref, chan_ref, conv_ref, key_ref, par_ref, turned):
    s, h = place_ref[0], place_ref[1]
    heads = sent_ref.shape[0]
    seqs = gain_ref.shape[0]
    left = left_half((1, LANES))

    def from_head(row):
        chips = heads // 2
        return (h // 2 + chips - row % chips) % chips * 2 + (h % 2 ^ row // chips)

    row = from_head(lax.broadcasted_iota(jnp.int32, (heads, LANES), 0))

    def lanes_from(start):
        return sent_ref[:, start : start + LANES].astype(f32)

    for k in range(seqs):
        gains = lanes_from(k * SENT)
        for p in range(heads // 2):
            of_head = lambda i: jnp.sum(jnp.where(row == i, gains, 0.0), axis=0, keepdims=True)
            second = pltpu.roll(of_head(2 * p + 1), HEADDIM, 1)
            gain_ref[k : k + 1, lanes(p)] = jnp.where(left, of_head(2 * p), second)

    of = from_head(lax.broadcasted_iota(jnp.int32, (8, heads), 1))
    to = lax.broadcasted_iota(jnp.int32, (8, heads), 0)
    head = (to // 2 * heads + h) * 2 + to % 2
    sel = jnp.where(of == head // 8, 1.0, 0.0).astype(bf16)
    found = nn(sel, sent_ref[:, HEAD_AT : HEAD_AT + LANES])
    lane = lax.broadcasted_iota(jnp.int32, (8, LANES), 1)
    local = lax.broadcasted_iota(jnp.int32, (8, LANES), 0)
    place = (h * 2 + local % 2) % 8

    def param(q):
        keep = (lane % 24 == q * 8 + place) & (lane < 72)
        return jnp.sum(jnp.where(keep, found, 0.0), axis=1, keepdims=True)

    decay, bias, skip = param(0), param(1), param(2)
    par_ref[...] = jnp.where(lane == 0, bias, jnp.where(lane == 1, -jnp.exp(decay), 0.0))

    def run_of(r, tap):
        total = jnp.zeros((1, LANES), f32)
        for k in range(seqs):
            source = (s ^ k) * heads + row
            begins = source + source // 16
            base = k * SENT + CONV_AT + tap * 2 * LANES
            part = jnp.where(begins == r, lanes_from(base), 0.0)
            part = part + jnp.where(begins == r - 1, lanes_from(base + LANES), 0.0)
            total = total + jnp.sum(part, axis=0, keepdims=True)
        return total

    chan_ref[...] = jnp.zeros_like(chan_ref)
    conv_ref[...] = jnp.zeros_like(conv_ref)
    for b in range(seqs):
        chan_ref[0:1, lanes(b)] = jnp.where(left, skip[2 * b : 2 * b + 1], skip[2 * b + 1 : 2 * b + 2])
        start = pl.multiple_of((s ^ b) * SENT, LANES) + GATE_AT
        gates = sent_ref[0:1, pl.ds(pl.multiple_of(start, LANES), LANES)]
        chan_ref[1:2, lanes(b)] = gates.astype(f32)
        for tap in range(CONV_K + 1):
            conv_ref[tap : tap + 1, lanes(b)] = run_of(b * heads + h, tap)
    per = key_ref.shape[0]
    each = LANES // per
    taps = [run_of(seqs * heads + h // each, tap) for tap in range(CONV_K + 1)]
    turned[...] = jnp.concatenate(taps + [jnp.zeros((LANES - CONV_K - 1, LANES), f32)], axis=0).T
    key_ref[...] = turned[pl.ds(pl.multiple_of(h % each * per, 8), per), :]


def behind_lanes(x, rim, by):
    return pltpu.roll(jnp.concatenate([rim, x], axis=1), by, 1)[:, LANES:] if by else x


def key_conv_kernel(small_ref, rim_ref, valid_ref, par_ref, out_ref):
    count = par_ref.shape[0]
    x, rim = small_ref[0, 8:].astype(f32)[:count], rim_ref[0, 8:].astype(f32)[:count]
    total = par_ref[:, CONV_K : CONV_K + 1]
    for k in range(CONV_K):
        total = total + par_ref[:, k : k + 1] * behind_lanes(x, rim, EDGE - k) * valid_ref[0, k : k + 1]
    out_ref[0] = (total / (1.0 + jnp.exp(-total))).astype(bf16)


def key_back_kernel(d_ref, small_ref, rim_ref, valid_ref, par_ref, in_ref, back_ref, grad_ref, total_grad):
    @pl.when(pl.program_id(0) == 0)
    def _():
        total_grad[...] = jnp.zeros_like(total_grad)

    count = par_ref.shape[0]
    x, rim = small_ref[0, 8:].astype(f32)[:count], rim_ref[0, 8:].astype(f32)[:count]
    size = x.shape[1]
    total = par_ref[:, CONV_K : CONV_K + 1]
    seen = []
    for k in range(CONV_K):
        seen.append(behind_lanes(x, rim, EDGE - k) * valid_ref[0, k : k + 1])
        total = total + par_ref[:, k : k + 1] * seen[k]
    sig = 1.0 / (1.0 + jnp.exp(-total))
    d_keys = 0.0
    for h in range(d_ref.shape[0]):
        d_keys = d_keys + d_ref[h, 0].astype(f32)
    d_total = d_keys.astype(bf16).astype(f32) * (sig * (1.0 + total * (1.0 - sig)))
    lane = lax.broadcasted_iota(jnp.int32, (count, LANES), 1)
    ahead, d_in = 0.0, 0.0
    grads = jnp.where(lane == CONV_K, jnp.sum(d_total, axis=1, keepdims=True), 0.0)
    empty = jnp.zeros((count, LANES), f32)
    for k in range(CONV_K):
        grads = jnp.where(lane == k, jnp.sum(d_total * seen[k], axis=1, keepdims=True), grads)
        held = d_total * (par_ref[:, k : k + 1] * valid_ref[0, k : k + 1])
        by = EDGE - k
        wide = jnp.concatenate([empty, held], axis=1)
        moved = pltpu.roll(wide, size + LANES - by, 1) if by else wide
        ahead = ahead + moved[:, :LANES]
        if by:
            keep = lax.broadcasted_iota(jnp.int32, (count, size), 1) < size - by
            d_in = d_in + jnp.where(keep, moved[:, LANES:], 0.0)
        else:
            d_in = d_in + held
    in_ref[0] = d_in
    back_ref[0] = jnp.where(lane >= LANES - EDGE, ahead, 0.0)
    total_grad[0:count, :] += grads
    grad_ref[...] = total_grad[...].T[0:8]


def pack_kernel(conv_ref, key_ref, head_ref, skip_ref, out_ref):
    wide = conv_ref.shape[1]
    taps = CONV_K + 1
    out_ref[0:taps, :wide] = conv_ref[0:taps]
    out_ref[0:taps, wide:] = key_ref[0:taps]
    left = left_half((1, LANES))
    lane = lax.broadcasted_iota(jnp.int32, (1, LANES), 1)
    skips = jnp.zeros((1, LANES), f32)
    for p in range(wide // LANES):
        both = skip_ref[0:1, lanes(p)]
        first = jnp.sum(jnp.where(left, both, 0.0), axis=1, keepdims=True)
        second = jnp.sum(both, axis=1, keepdims=True) - first
        skips = jnp.where(lane == 2 * p, first, jnp.where(lane == 2 * p + 1, second, skips))
    heads = jnp.concatenate([head_ref[...], jnp.zeros((LANES - 8, LANES), f32)], axis=0).T
    out_ref[taps : taps + 2, :LANES] = heads[0:2]
    out_ref[taps + 2 : 8, :LANES] = skips
    out_ref[taps:8, LANES:] = jnp.zeros((8 - taps, wide), f32)


def key_join_kernel(in_ref, back_ref, step_ref, key_ref, small_ref):
    x = in_ref[0]
    count, size = x.shape
    key = jnp.concatenate([x[:, : size - LANES], x[:, size - LANES :] + back_ref[0]], axis=1)
    key_ref[0] = key.astype(bf16)
    rows = [jnp.zeros((8, size), f32), key, jnp.zeros((LANES - 8 - count, size), f32)]
    cols = jnp.concatenate(rows, axis=0).T
    small_ref[0] = (cols + step_ref[0].astype(f32)).astype(bf16)


def prep_kernel(
    step_ref, seg_ref, par_ref, val_ref, key_ref, cols_ref, rows_ref, ktok_ref, start_ref, pre_ref, out_ref, state, reach
):
    @pl.when(pl.program_id(1) == 0)
    def _():
        state[...] = jnp.zeros_like(state)
        reach[...] = jnp.ones_like(reach)

    raw = step_ref[0] + par_ref[:, 0:1]
    small = jnp.exp(-jnp.abs(raw))
    one = 1.0 + small
    step = jnp.maximum(raw, 0.0) + jnp.where(
        one == 1.0, small, jnp.log(one) * (small / jnp.where(one == 1.0, 1.0, one - 1.0))
    )
    sig = jnp.where(raw >= 0.0, 1.0, small) / one
    log = running_sum(step * par_ref[:, 1:2])
    size = log.shape[1]
    segs = seg_ref[0]
    seg, prev = segs[0:1], segs[1:2]
    carry = jnp.where(seg == prev, jnp.exp(log), 0.0)
    to_end = jnp.where(
        seg == seg[:, size - 1 :], jnp.exp(jnp.minimum(log[:, size - 1 :] - log, 0.0)), 0.0
    )
    rows_ref[0] = jnp.concatenate([log, step, sig, segs], axis=0)
    stack = jnp.concatenate(
        [log, step, carry, to_end, segs, jnp.zeros((LANES - 40, size), f32)], axis=0
    )
    cols = stack.T
    cols_ref[0] = cols
    keys = key_ref[0]
    ktok_ref[0] = keys.astype(f32).T.astype(bf16)
    start_ref[0, 0] = state[...]
    pre_ref[0, 0] = reach[...]
    weight = cols[:, TO_END : TO_END + 8] * cols[:, STEP : STEP + 8]
    for p in range(pairs_in(val_ref)):
        ending = (val_ref[0, :, lanes(p)].astype(f32) * pair_of(weight, 0, p)).astype(bf16)
        decay = pair_of(cols[size - 1 :], CARRY, p)
        state[:, lanes(p)] = decay * state[:, lanes(p)] + nn(keys[:STATE], ending)
        reach[:, lanes(p)] = decay * reach[:, lanes(p)]
    out_ref[0] = jnp.concatenate([state[...], reach[...], reach[...]], axis=0).astype(bf16)


def same_mask(cols, rows):
    size = cols.shape[0]
    at = lax.broadcasted_iota(jnp.int32, (size, size), 0)
    of = lax.broadcasted_iota(jnp.int32, (size, size), 1)
    return (cols[:, SEG : SEG + 1] == rows[ROWS_SEG : ROWS_SEG + 1]) & (at >= of)


def within(cols, rows, j):
    return jnp.exp(jnp.minimum(cols[:, j : j + 1] - rows[j : j + 1], 0.0))


def step_lanes(place_ref, p, swapped):
    return pl.ds(pl.multiple_of((place_ref[0] ^ p) * LANES, LANES), LANES) if swapped else lanes(p)


def fwd_kernel(
    swapped, place_ref, val_ref, ktok_ref, cols_ref, rows_ref, start_ref, pre_ref, in_ref, gate_ref, dy_ref, chan_ref, mix_ref, sum_ref
):
    cols, rows = cols_ref[0], rows_ref[0]
    rkey = ktok_ref[0, :, STATE:]
    scores = jnp.where(same_mask(cols, rows), nt(rkey, ktok_ref[0, :, :STATE]), 0.0)
    squares, products = 0.0, 0.0
    left = left_half((cols.shape[0], LANES))
    for p in range(pairs_in(val_ref)):
        at = lanes(p)
        vals = val_ref[0, :, at].astype(f32)
        stepped = vals * pair_of(cols, STEP, p)
        high, low = split(start_ref[0, 0, :, at] + pre_ref[0, 0, 0:1, at] * in_ref[0, :, at])
        mixed = pair_of(cols, CARRY, p) * (nn(rkey, high) + nn(rkey, low))
        for half in range(2):
            weights = (scores * within(cols, rows, 2 * p + half)).astype(bf16)
            keep = left if half == 0 else ~left
            mixed = mixed + nn(weights, jnp.where(keep, stepped, 0.0).astype(bf16))
        mixed = (mixed + chan_ref[0:1, at] * vals).astype(bf16)
        mix_ref[0, :, at] = mixed
        gate = gate_ref[0, :, at]
        gated = mixed.astype(f32) * (gate / (1.0 + jnp.exp(-gate)))
        squares = squares + gated * gated
        products = products + gated * (dy_ref[0, :, step_lanes(place_ref, p, swapped)] * chan_ref[1:2, at])
    lane = lax.broadcasted_iota(jnp.int32, squares.shape, 1)
    sums = jnp.where(
        lane == 0,
        jnp.sum(squares, axis=1, keepdims=True),
        jnp.where(lane == 1, jnp.sum(products, axis=1, keepdims=True), 0.0),
    )
    sum_ref[0] = sums.T[0:8]


def norm_kernel(
    swapped, place_ref, mix_ref, gate_ref, dy_ref, sum_ref, cols_ref, key_ref, pre_ref, chan_ref, reach_ref,
    yn_ref, dmix_ref, dgate_ref, adj_ref, out_ref, adj
):
    c = pl.program_id(1)

    @pl.when(c == 0)
    def _():
        adj[...] = jnp.zeros_like(adj)

    cols = cols_ref[0]
    size = cols.shape[0]
    rows = sum_ref[0]
    scale_row = lax.rsqrt(rows[0:1] * (1.0 / D_INNER) + EPS)
    pull_row = scale_row * scale_row * rows[1:2] * (1.0 / D_INNER)
    both = jnp.concatenate([scale_row, pull_row, jnp.zeros((LANES - 2, size), f32)], axis=0).T
    scale, pull = both[:, 0:1], both[:, 1:2]
    for p in range(pairs_in(mix_ref)):
        at = lanes(p)
        mixer = mix_ref[0, :, at].astype(f32)
        gate = gate_ref[0, :, at]
        sig = 1.0 / (1.0 + jnp.exp(-gate))
        act = gate * sig
        slope = sig * (1.0 + gate * (1.0 - sig))
        gated = mixer * act
        unit = gated * scale
        gain = chan_ref[1:2, at]
        step_at = step_lanes(place_ref, p, swapped)
        yn_ref[0, :, step_at] = (unit * gain).astype(bf16)
        d_y = dy_ref[0, :, step_at]
        d_gated = scale * (d_y * gain - gated * pull)
        d_mix = (d_gated * act).astype(bf16)
        dmix_ref[0, :, at] = d_mix
        dgate_ref[0, :, at] = (d_gated * mixer * slope).astype(bf16)
        carried = (d_mix.astype(f32) * pair_of(cols, CARRY, p)).astype(bf16)
        block = nn(key_ref[0, STATE:], carried)
        adj_ref[0, 0, :, at] = block
        adj[:, at] = pair_of(cols[size - 1 :], CARRY, p) * adj[:, at] + block
    reach = reach_ref[0]
    out_ref[0] = jnp.concatenate([adj[...].astype(bf16), reach], axis=0)


def bwd_kernel(
    val_ref, key_ref, ktok_ref, cols_ref, rows_ref, start_ref, pre_ref, in_ref, dmix_ref, adj_ref, adjin_ref, chan_ref, par_ref,
    dval_ref, dkey_ref, dstep_ref, head_ref, skip_ref, adj
):
    c = pl.program_id(1)

    @pl.when((pl.program_id(0) == 0) & (c == 0))
    def _():
        head_ref[...] = jnp.zeros_like(head_ref)
        skip_ref[...] = jnp.zeros_like(skip_ref)

    @pl.when(c == 0)
    def _():
        adj[...] = adjin_ref[0]

    cols, rows = cols_ref[0], rows_ref[0]
    size = cols.shape[0]
    wkey, rkey = ktok_ref[0, :, :STATE], ktok_ref[0, :, STATE:]
    same = same_mask(cols, rows)
    scores = jnp.where(same, nt(rkey, wkey), 0.0)
    left = left_half((size, LANES))
    lane = lax.broadcasted_iota(jnp.int32, (size, LANES), 1)
    lane_row = lax.broadcasted_iota(jnp.int32, (1, LANES), 1)
    d_scores = jnp.zeros((size, size), f32)
    d_write = jnp.zeros((STATE, size), f32)
    d_read = jnp.zeros((STATE, size), f32)
    by_row = jnp.zeros((size, LANES), f32)
    last = jnp.zeros((1, LANES), f32)
    by_col = []

    def put(total, p, half, values, offset=0):
        where = lane if values.shape[0] == size else lane_row
        return jnp.where(where == offset + 2 * p + half, values, total)

    def halves_of(x):
        first = jnp.sum(jnp.where(left[: x.shape[0]], x, 0.0), axis=1, keepdims=True)
        return first, jnp.sum(x, axis=1, keepdims=True) - first

    for p in range(pairs_in(val_ref)):
        at = lanes(p)
        vals = val_ref[0, :, at].astype(f32)
        d_mix = dmix_ref[0, :, at]
        d_mix_f = d_mix.astype(f32)
        step = pair_of(cols, STEP, p)
        stepped_f = vals * step
        stepped = stepped_f.astype(bf16)
        carry = pair_of(cols, CARRY, p)
        state = start_ref[0, 0, :, at] + pre_ref[0, 0, 0:1, at] * in_ref[0, :, at]
        high, low = split(state)
        end = adj[:, at]
        end_low = end.astype(bf16)
        ending_f = stepped_f * pair_of(cols, TO_END, p)
        ending = ending_f.astype(bf16)
        carried_d = (d_mix_f * carry).astype(bf16)
        back = nn(wkey, end_low)
        d_stepped = pair_of(cols, TO_END, p) * back
        from_end = ending_f * back
        through = d_mix_f * carry * (nn(rkey, high) + nn(rkey, low)) - from_end
        decay = pair_of(cols[size - 1 :], CARRY, p)
        final = jnp.sum(from_end, axis=0, keepdims=True) + decay * jnp.sum(
            end * state, axis=0, keepdims=True
        )
        final = halves_of(final)
        through = halves_of(through)
        for half in range(2):
            keep = left if half == 0 else ~left
            held = jnp.where(keep, d_mix_f, 0.0).astype(bf16)
            j = 2 * p + half
            near = within(cols, rows, j)
            d_near = nt(held, stepped) * near
            d_scores = d_scores + d_near
            pairs = d_near * scores
            by_row = put(by_row, p, half, jnp.sum(pairs, axis=1, keepdims=True) + through[half])
            by_col.append(jnp.sum(pairs, axis=0, keepdims=True))
            last = put(last, p, half, final[half])
            d_stepped = d_stepped + tn((scores * near).astype(bf16), held)
        d_vals = step * d_stepped + chan_ref[0:1, at] * d_mix_f
        dval_ref[0, :, at] = d_vals.astype(bf16)
        skip_ref[0:1, at] += jnp.sum(d_mix_f * vals, axis=0, keepdims=True)
        d_step = halves_of(vals * d_stepped)
        for half in range(2):
            by_row = put(by_row, p, half, d_step[half], 8)
        d_write = d_write + nt(end_low, ending)
        d_read = d_read + nt(high, carried_d) + nt(low, carried_d)
        adj[:, at] = decay * end + adj_ref[0, 0, :, at]
    d_scores = jnp.where(same, d_scores, 0.0).astype(bf16)
    d_write = d_write + nn(key_ref[0, STATE:], d_scores)
    d_read = d_read + nt(key_ref[0, :STATE], d_scores)
    dkey_ref[0] = jnp.concatenate([d_write, d_read], axis=0).astype(bf16)
    while len(by_col) < 8:
        by_col.append(jnp.zeros((1, size), f32))
    turned = by_row.T
    last = jnp.broadcast_to(last, (LANES, LANES)).T[0:8, 0:1]
    d_log = turned[0:8] - jnp.concatenate(by_col, axis=0)
    rate = par_ref[:, 1:2]
    first = rows[ROWS_SEG + 2 : ROWS_SEG + 3]
    d_decay = (running_sum(d_log, True) + last) * (1.0 - first)
    d_raw = (turned[8:16] + d_decay * rate) * rows[SIG : SIG + 8]
    dstep_ref[0] = jnp.concatenate([d_raw, jnp.zeros((LANES - 8, size), f32)], axis=0).T.astype(bf16)
    head_lane = lax.broadcasted_iota(jnp.int32, (8, LANES), 1)
    head_ref[...] += jnp.where(
        head_lane == 0,
        jnp.sum(d_decay * rows[STEP : STEP + 8], axis=1, keepdims=True) * rate,
        jnp.where(head_lane == 1, jnp.sum(d_raw, axis=1, keepdims=True), 0.0),
    )


def shifted(x, rim, by):
    if by == 0:
        return x
    head = jnp.concatenate([rim, x[:8]], axis=0)[8 - by : 16 - by]
    return jnp.concatenate([head, pltpu.roll(x, by, 0)[8:]], axis=0)


def conv_kernel(val_ref, rim_ref, valid_ref, par_ref, out_ref):
    for p in range(pairs_in(val_ref)):
        at = lanes(p)
        x = val_ref[0, :, at].astype(f32)
        rim = rim_ref[0, :, at].astype(f32)[8:16]
        total = par_ref[CONV_K : CONV_K + 1, at]
        for k in range(CONV_K):
            total = total + par_ref[k : k + 1, at] * shifted(x, rim, EDGE - k) * valid_ref[0, :, k : k + 1]
        out_ref[0, :, at] = (total / (1.0 + jnp.exp(-total))).astype(bf16)


def conv_back_kernel(d_ref, val_ref, rim_ref, valid_ref, par_ref, in_ref, back_ref, grad_ref):
    @pl.when(pl.program_id(0) == 0)
    def _():
        grad_ref[...] = jnp.zeros_like(grad_ref)

    size = val_ref.shape[1]
    row = lax.broadcasted_iota(jnp.int32, (size, LANES), 0)
    zeros = jnp.zeros((8, LANES), f32)
    for p in range(pairs_in(val_ref)):
        at = lanes(p)
        x = val_ref[0, :, at].astype(f32)
        rim = rim_ref[0, :, at].astype(f32)[8:16]
        total = par_ref[CONV_K : CONV_K + 1, at]
        seen = []
        for k in range(CONV_K):
            seen.append(shifted(x, rim, EDGE - k) * valid_ref[0, :, k : k + 1])
            total = total + par_ref[k : k + 1, at] * seen[k]
        sig = 1.0 / (1.0 + jnp.exp(-total))
        d_total = d_ref[0, :, at].astype(f32) * (sig * (1.0 + total * (1.0 - sig)))
        grad_ref[CONV_K : CONV_K + 1, at] += jnp.sum(d_total, axis=0, keepdims=True)
        d_in, back = 0.0, 0.0
        for k in range(CONV_K):
            grad_ref[k : k + 1, at] += jnp.sum(d_total * seen[k], axis=0, keepdims=True)
            held = d_total * (par_ref[k : k + 1, at] * valid_ref[0, :, k : k + 1])
            by = EDGE - k
            if by:
                d_in = d_in + jnp.where(row < size - by, pltpu.roll(held, size - by, 0), 0.0)
                back = back + jnp.concatenate([zeros, held[:8]], axis=0)[by : by + 8]
            else:
                d_in = d_in + held
        in_ref[0, :, at] = d_in.astype(bf16)
        back_ref[0, :, at] = back


def proj_kernel(place_ref, x_ref, gain_ref, *refs):
    parts, (low_ref, out_ref, small_ref, weight_ref) = refs[:-4], refs[-4:]
    wide = parts[0].shape[1] - LANES
    size = parts[0].shape[0]

    @pl.when((pl.program_id(0) == 0) & (pl.program_id(1) == 0))
    def _():
        for k, part in enumerate(parts):
            turned = part[:, wide:].astype(f32).T
            weight_ref[:, k * size : (k + 1) * size] = turned.astype(bf16)

    x = x_ref[0].astype(f32)
    inv = lax.rsqrt(jnp.mean(x * x, axis=1, keepdims=True) + EPS)
    total = 0.0
    for k, part in enumerate(parts):
        at = pl.ds(pl.multiple_of((place_ref[0] ^ k) * size, LANES), size)
        low = (x_ref[0, :, at].astype(f32) * inv * gain_ref[k : k + 1]).astype(bf16)
        low_ref[0, :, k * size : (k + 1) * size] = low
        total = total + nn(low, part[...])
    out_ref[0] = total.astype(bf16)
    small_ref[0] = total[:, wide:].T.astype(bf16)


def fill_kernel(steps, x_ref, grad_ref, *refs):
    gates, outs, (gate_ref, dy_ref) = refs[:steps], refs[steps:-2], refs[-2:]
    size = gates[0].shape[0]
    total = 0.0
    for k, part in enumerate(gates):
        total = total + nn(x_ref[0, :, k * size : (k + 1) * size], part[...])
    gate_ref[0] = total
    run = outs[0].shape[0]
    for r, part in enumerate(outs):
        dy_ref[0, :, r * run : (r + 1) * run] = nt(grad_ref[0], part[...])


def out_kernel(y_ref, *refs):
    parts, out_ref = refs[:-1], refs[-1]
    run = parts[0].shape[0]
    width = out_ref.shape[2]
    size = min(width, 512)
    for n in range(width // size):
        at = slice(n * size, (n + 1) * size)
        total = 0.0
        for r, part in enumerate(parts):
            total = total + nn(y_ref[0, :, r * run : (r + 1) * run], part[:, at])
        out_ref[0, :, at] = total.astype(bf16)


def weight_kernel(parts, a_ref, *refs):
    outs, b_ref = refs[parts:], refs[0]
    if parts > 1:
        outs, b_ref = refs[parts:-1], refs[-1]

        @pl.when(pl.program_id(0) == 0)
        def _():
            at = 0
            for ref in refs[:parts]:
                b_ref[:, :, at : at + ref.shape[2]] = ref[...]
                at += ref.shape[2]

    total = 0.0
    for m in range(a_ref.shape[0]):
        total = total + tn(a_ref[m], b_ref[m])
    total = total.astype(bf16)
    for k, out in enumerate(outs):

        @pl.when(pl.program_id(0) == k)
        def _():
            out[...] = total


def normed_back_kernel(steps, gate_ref, val_ref, small_ref, *refs):
    gates, firsts, out_ref = refs[:steps], refs[steps:-1], refs[-1]
    gate, val, small = gate_ref[0], val_ref[0], small_ref[0]
    wide = val.shape[1]
    size = gates[0].shape[0]
    for k in range(steps):
        first = firsts[k]
        total = nt(gate, gates[k][...]) + nt(val, first[:, :wide]) + nt(small, first[:, wide:])
        out_ref[0, :, k * size : (k + 1) * size] = total.astype(bf16)


def grad_in_kernel(place_ref, sum_ref, key_ref, row_ref, x_ref, gain_ref, grad_ref, out_ref, d_unit):
    steps = gain_ref.shape[0]
    part = x_ref.shape[2] // steps
    x = x_ref[0].astype(f32)
    inv = lax.rsqrt(jnp.mean(x * x, axis=1, keepdims=True) + EPS)
    keys = jnp.concatenate([key_ref[h, 0] for h in range(key_ref.shape[0])], axis=0)
    total = 0.0
    for k in range(steps):
        at = slice(k * part, (k + 1) * part)
        of = pl.ds(pl.multiple_of((place_ref[0] ^ k) * part, LANES), part)
        d_here = sum_ref[0, :, at].astype(f32) + tn(keys, row_ref[:, at])
        d_here = d_here * gain_ref[k : k + 1]
        d_unit[:, of] = d_here
        total = total + jnp.sum(d_here * x_ref[0, :, of].astype(f32), axis=1, keepdims=True)
    shared = inv * inv * total * (1.0 / x.shape[1])
    out_ref[0] = (grad_ref[0].astype(f32) + inv * (d_unit[...] - x * shared)).astype(bf16)


def weight_grad_kernel(gate_ref, first_ref, w_ref, out_ref, sum_ref):
    heads, rows, wide = gate_ref.shape
    runs = wide // LANES
    total = jnp.zeros((rows, LANES), f32)

    def place(value, at):
        out_ref[:, at : at + value.shape[1]] = value
        return jnp.sum(value * w_ref[:, at : at + value.shape[1]].astype(f32), axis=1, keepdims=True)

    for ref, base in ((gate_ref, 0), (first_ref, D_INNER)):
        for h in range(heads):
            for b in range(runs):
                value = ref[h, :rows, lanes(b)].astype(f32)
                at = base + (b * heads + h) * LANES
                out_ref[:, at : at + LANES] = value
                total = total + value * w_ref[:, at : at + LANES].astype(f32)
    small = [first_ref[h, :rows, wide:].astype(f32) for h in range(heads)]
    per = 2 * STATE // heads
    keys = jnp.concatenate([x[:, 8 : 8 + per] for x in small], axis=1)
    sums = jnp.sum(total, axis=1, keepdims=True) + place(keys, 2 * D_INNER)
    steps = jnp.concatenate([x[:, :8] for x in small], axis=1).astype(bf16)
    per = 8 // runs
    of = lax.broadcasted_iota(jnp.int32, (HEADS, HEADS), 0)
    to = lax.broadcasted_iota(jnp.int32, (HEADS, HEADS), 1)
    source = (to // per % heads) * 8 + (to // (per * heads)) * per + to % per
    steps = nn(steps, (of == source).astype(f32).astype(bf16))
    sums = sums + place(steps, 2 * D_INNER + 2 * STATE)
    sum_ref[...] = jnp.broadcast_to(sums, (rows, LANES))


ABOUT_US = {
    "proj_kernel": 0,
    "fill_kernel": 9,
    "out_kernel": 5,
    "weight_kernel": 4,
    "normed_back_kernel": 7,
    "bwd_kernel": 20,
    "fwd_kernel": 6,
    "norm_kernel": 5,
    "prep_kernel": 6,
    "conv_back_kernel": 7,
    "conv_kernel": 3,
    "grad_in_kernel": 2,
    "weight_grad_kernel": 2,
    "mask_kernel": 0,
    "pack_kernel": 1,
    "glue_kernel": 0,
    "key_conv_kernel": 1,
    "key_back_kernel": 2,
    "key_join_kernel": 1,
}


def kernel_call(kernel, grid, ins, outs, scratch=(), wait=()):
    us = ABOUT_US[getattr(kernel, "func", kernel).__name__]
    specs = [
        pl.BlockSpec(memory_space=pltpu.SMEM) if block is None else pl.BlockSpec(block, index)
        for block, index in ins
    ]
    wait = jax.tree.leaves(wait)
    count = len(specs)
    specs = specs + [pl.BlockSpec(memory_space=pl.ANY)] * len(wait)

    def run(*refs):
        kernel(*refs[:count], *refs[count + len(wait) :])

    call = pl.pallas_call(
        run,
        grid=grid,
        in_specs=specs,
        out_specs=[pl.BlockSpec(block, index) for _, _, block, index in outs],
        out_shape=[jax.ShapeDtypeStruct(shape, dtype) for shape, dtype, _, _ in outs],
        scratch_shapes=list(scratch),
        compiler_params=pltpu.CompilerParams(
            vmem_limit_bytes=58 * 2**20, dimension_semantics=("arbitrary",) * len(grid)
        ),
        name=getattr(kernel, "func", kernel).__name__,
        cost_estimate=pl.CostEstimate(flops=us * 2**30, bytes_accessed=us * 3 * 2**20, transcendentals=0),
    )
    return lambda *args: call(*args, *wait)


def body(
    hidden_in,
    seq_starts,
    norm_gain,
    in_weight,
    conv_weight,
    conv_bias,
    decay_log,
    dt_bias,
    skip_gain,
    gate_gain,
    out_weight,
    out_grad,
):
    seqs, heads = lax.axis_size("seq"), lax.axis_size("head")
    s_i, h_i = lax.axis_index("seq"), lax.axis_index("head")
    micro, tok, width = hidden_in.shape
    rows = in_weight.shape[0]
    shard = tok * heads
    runs = seqs if HEADS % (seqs * heads) == 0 else 1
    run_ch = D_INNER // (runs * heads)
    run_heads = HEADS // (runs * heads)
    chans, n_heads = runs * run_ch, runs * run_heads
    key_ch = 2 * STATE // heads
    wide = max(chans, LANES)

    def widen(x, axis=-1):
        pads = [(0, 0)] * x.ndim
        pads[axis] = (0, wide - chans)
        return jnp.pad(x, pads) if wide > chans else x

    conv_share, gate_share, head_share = conv_bias.shape[0], gate_gain.shape[0], decay_log.shape[0]

    def mine(x, size):
        lead = x.shape[:-1]
        x = x.reshape(lead + (runs, heads, size))
        x = lax.dynamic_index_in_dim(x, h_i, len(lead) + 1, False)
        return x.reshape(lead + (runs * size,))

    place = s_i[None].astype(jnp.int32)
    scalar = (None, None)
    forward = [(i, i + 1) for i in range(seqs - 1)]
    backward = [(i + 1, i) for i in range(seqs - 1)]
    swapped = runs == seqs
    if swapped and run_ch != LANES:
        raise ValueError("run width")

    def columns(x, size):
        x = x.reshape(rows, runs, heads, size)
        return jnp.transpose(x, (2, 0, 1, 3)).reshape(heads, rows, runs * size)

    def fill(x, axis, size):
        return jnp.pad(x, [(0, size - x.shape[axis] if i == axis else 0) for i in range(x.ndim)])

    val_p = fill(columns(in_weight[:, D_INNER : 2 * D_INNER], run_ch), 2, wide)
    step_p = fill(columns(in_weight[:, 2 * D_INNER + 2 * STATE :], run_heads), 2, 8)
    key_p = in_weight[:, 2 * D_INNER : 2 * D_INNER + 2 * STATE].reshape(rows, heads, key_ch)
    key_p = fill(jnp.swapaxes(key_p, 0, 1), 2, LANES - 8)
    gate_p = fill(columns(in_weight[:, :D_INNER], run_ch), 2, wide)
    first = head_swap(jnp.concatenate([val_p, step_p, key_p], axis=2)).reshape(heads * rows, -1)
    inputs = lax.all_gather(hidden_in, "head", axis=1, tiled=True)

    blocks = shard // SCAN_BLOCK
    by_micro = lambda *shape: ((1,) + shape, lambda m: (m,) + (0,) * len(shape))
    seg_rows, valid, valid_cols = kernel_call(
        mask_kernel,
        (micro,),
        [scalar, scalar],
        [
            ((micro, 8, shard), f32) + by_micro(8, shard),
            ((micro, 8, shard), f32) + by_micro(8, shard),
            ((micro, shard, LANES), f32) + by_micro(shard, LANES),
        ],
    )(place, seq_starts)


    every = seqs * heads
    linear = s_i * heads + h_i
    halo = lax.ppermute(hidden_in[:, tok - EDGE :], BOTH, [(i, i + 1) for i in range(every - 1)])
    taps = jnp.concatenate([conv_weight, conv_bias[None]], axis=0)
    heads_par = jnp.concatenate(three_parts(jnp.concatenate([decay_log, dt_bias, skip_gain])))
    key_rows_n = -(-key_ch // 8) * 8
    if swapped:
        window = jnp.zeros((CONV_K + 1, 2 * LANES), bf16)
        window = lax.dynamic_update_slice_in_dim(window, taps, (linear & 15) * 8, 1)
        sent = [fill(norm_gain, 0, LANES), gate_gain, fill(heads_par, 0, LANES), window.reshape(-1)]
    else:
        sent = [norm_gain, taps.reshape(-1), gate_gain, heads_par]
        sent.append(jnp.zeros((-sum(x.shape[0] for x in sent) % LANES,), bf16))
    sent = jnp.concatenate(sent)
    size = sent.shape[0]
    if swapped:
        w_out = seq_gather(out_weight)
        sent = after(jnp.concatenate(seq_gather(sent) + [halo.reshape(-1)])[None], first, w_out)
        chips = heads // 2
        turns = [[(i, (i + 2 * k) % heads) for i in range(heads)] for k in range(1, chips)]
        sent = jnp.concatenate([sent] + [lax.ppermute(sent, "head", pairs) for pairs in turns], axis=0)
        other = lax.ppermute(sent, "head", [(i, i ^ 1) for i in range(heads)])
        sent = jnp.concatenate([sent, other], axis=0)
        first_row = (h_i >> 1) + (h_i & 1) * chips
    else:
        sent = lax.all_gather(sent, "seq").reshape(-1)
        sent = lax.all_gather(jnp.concatenate([sent, halo.reshape(-1)]), "head")
        first_row = 0
    halo = lax.dynamic_index_in_dim(sent, first_row, 0, False)[seqs * size :].reshape(halo.shape)
    halo = jnp.pad(halo, ((0, 0), (LANES - EDGE, 0), (0, 0)))
    first = seq_gather(first)
    if swapped:
        all_of = lambda shape: (shape, lambda m: (0,) * len(shape))
        outs = [(seqs, width // seqs), (8, wide), (8, wide), (key_ch, LANES), (8, LANES)]
        gain_steps, chan, conv_par, key_par, params = kernel_call(
            glue_kernel,
            (1,),
            [scalar, all_of((heads, seqs * size))],
            [(shape, f32) + all_of(shape) for shape in outs],
            [pltpu.VMEM((LANES, LANES), f32)],
            (first, seg_rows, gate_p, halo),
        )(jnp.stack([s_i, h_i]), sent)
    else:
        sent = jnp.swapaxes(sent[:, : seqs * size].reshape(heads, seqs, -1), 0, 1).reshape(every, -1)
        at = 0

        def take(count):
            nonlocal at
            at += count
            return sent[:, at - count : at]

        gain_steps = from_steps(take(rows).reshape(seqs, heads * rows), s_i).astype(f32)
        conv_p = take((CONV_K + 1) * conv_share).reshape(every, CONV_K + 1, conv_share)
        conv_p = jnp.transpose(conv_p, (1, 0, 2)).reshape(CONV_K + 1, CONV_CH).astype(f32)
        gate_g = mine(take(gate_share).reshape(D_INNER), run_ch).astype(f32)
        par = jnp.sum(take(9 * head_share)[:heads].astype(f32).reshape(heads, 3, 3, head_share), axis=1)
        par = mine(jnp.swapaxes(par, 0, 1).reshape(3, HEADS), run_heads)
        params = fill(fill(jnp.stack([par[1], -jnp.exp(par[0])], axis=1), 0, 8), 1, LANES)
        chan = fill(jnp.stack([widen(jnp.repeat(par[2], HEADDIM)), widen(gate_g)]), 0, 8)
        conv_par = fill(widen(mine(conv_p[:, :D_INNER], run_ch)), 0, 8)
        key_par = lax.dynamic_slice_in_dim(conv_p[:, D_INNER:], h_i * key_ch, key_ch, 1).T
        key_par = fill(fill(key_par, 0, key_rows_n), 1, LANES)

    tile = lambda m, c: (m, c, 0)
    fixed = lambda m, c: (0, 0)
    def project(x, size):
        many = x.shape[1]
        return kernel_call(
            proj_kernel,
            (micro, many // size),
            [scalar, ((1, size, width), tile), (gain_steps.shape, fixed)] + [(first[0].shape, fixed)] * seqs,
            [
                ((micro, many, width), bf16, (1, size, width), tile),
                ((micro, many, wide + LANES), bf16, (1, size, wide + LANES), tile),
                ((micro, LANES, many), bf16, (1, LANES, size), lambda m, c: (m, 0, c)),
                ((LANES, width), bf16, (LANES, width), fixed),
            ],
        )(place, x, gain_steps, *first)

    normed_low, proj, small_in, key_rows = project(inputs, min(shard, 256))
    _, proj_rim, small_rim, _ = project(halo, LANES)
    second = head_swap(after(gate_p, proj))
    grad_rows = lax.all_gather(after(out_grad, proj), "head", axis=1, tiled=True)
    step_low = small_in[:, :8].astype(f32)

    w_gate = seq_gather(second.reshape(heads * rows, wide))
    if not swapped:
        w_out = lax.all_gather(out_weight, BOTH, axis=0, tiled=True)
        w_out = [widen(lax.dynamic_slice_in_dim(w_out, h_i * chans, chans, 0), 0)]
    gate_specs = [(w_gate[0].shape, fixed)] * seqs
    out_specs = [(part.shape, fixed) for part in w_out]


    whole = ((1, shard, wide), lambda m: (m, 0, 0))
    conv_ins = [
        whole,
        ((1, 16, wide), lambda m: (m, LANES // 16 - 1, 0)),
        by_micro(shard, LANES),
        ((8, wide), lambda m: (0, 0)),
    ]
    key_ins = [
        by_micro(LANES, shard),
        by_micro(LANES, LANES),
        by_micro(8, shard),
        ((key_rows_n, LANES), lambda m: (0, 0)),
    ]
    vals = kernel_call(conv_kernel, (micro,), conv_ins, [((micro, shard, wide), bf16) + whole])(
        proj, proj_rim, valid_cols, conv_par
    )[0]
    keys = kernel_call(
        key_conv_kernel, (micro,), key_ins, [((micro, key_rows_n, shard), bf16) + by_micro(key_rows_n, shard)]
    )(small_in, small_rim, valid, key_par)[0]
    keys = after(keys[:, :key_ch], second)
    keys = lax.all_gather(keys, "head", axis=1, tiled=True)

    grid = (micro, blocks)
    size = SCAN_BLOCK
    here = lambda m, c: (m, c, 0)
    along = lambda m, c: (m, 0, c)
    state_at = lambda m, c: (m, c, 0, 0)
    micro_at = lambda m, c: (m, 0, 0)
    fixed = lambda m, c: (0, 0)
    row8 = (1, 8, size)
    tok_c, tok_l = (1, size, wide), (1, size, LANES)
    n_state = STATE + 16
    f_state = ((1, 1, STATE, wide), state_at)
    f_pre = ((1, 1, 8, wide), state_at)
    cols, rows_t, ktok, starts, prefix, payload = kernel_call(
        prep_kernel,
        grid,
        [(row8, along), (row8, along), ((8, LANES), fixed), (tok_c, here), ((1, 2 * STATE, size), along)],
        [
            ((micro, shard, LANES), f32, tok_l, here),
            ((micro, 32, shard), f32, (1, 32, size), along),
            ((micro, shard, 2 * STATE), bf16, (1, size, 2 * STATE), here),
            ((micro, blocks, STATE, wide), f32) + f_state,
            ((micro, blocks, 8, wide), f32) + f_pre,
            ((micro, n_state, wide), bf16, (1, n_state, wide), micro_at),
        ],
        [pltpu.VMEM((STATE, wide), f32), pltpu.VMEM((8, wide), f32)],
    )(step_low, seg_rows, params, vals, keys)
    key_rows = lax.all_gather(after(key_rows[8 : 8 + key_ch], payload), "head")
    size = min(shard, 256)
    gate_in, d_ynorm = kernel_call(
        functools.partial(fill_kernel, seqs),
        (micro, shard // size),
        [((1, size, width), tile)] * 2 + gate_specs + out_specs,
        [((micro, shard, wide), f32, (1, size, wide), tile)] * 2,
        (),
        (payload,),
    )(normed_low, grad_rows, *w_gate, *w_out)
    size = SCAN_BLOCK
    state_in = linked(payload, False, gate_in)
    mixer, sums = kernel_call(
        functools.partial(fwd_kernel, swapped),
        grid,
        [
            scalar,
            (tok_c, here),
            ((1, size, 2 * STATE), here),
            (tok_l, here),
            ((1, 32, size), along),
            f_state,
            f_pre,
            ((1, STATE, wide), micro_at),
            (tok_c, here),
            (tok_c, here),
            ((8, wide), fixed),
        ],
        [((micro, shard, wide), bf16, tok_c, here), ((micro, 8, shard), f32, row8, along)],
        (),
        (key_rows,),
    )(place, vals, ktok, cols, rows_t, starts, prefix, state_in, gate_in, d_ynorm, chan)

    sums = fill(lax.psum(sums[:, :2], "head"), 1, 8)
    back_here = lambda m, c: (m, blocks - 1 - c, 0)
    back_along = lambda m, c: (m, 0, blocks - 1 - c)
    back_state = lambda m, c: (m, blocks - 1 - c, 0, 0)
    b_state, b_pre = (f_state[0], back_state), (f_pre[0], back_state)
    ynorm_low, d_mix, d_gate, block_adj, payload = kernel_call(
        functools.partial(norm_kernel, swapped),
        grid,
        [
            scalar,
            (tok_c, back_here),
            (tok_c, back_here),
            (tok_c, back_here),
            (row8, back_along),
            (tok_l, back_here),
            ((1, 2 * STATE, size), back_along),
            b_pre,
            ((8, wide), fixed),
            ((1, 16, wide), micro_at),
        ],
        [
            ((micro, shard, wide), bf16, tok_c, back_here),
            ((micro, shard, wide), bf16, tok_c, back_here),
            ((micro, shard, wide), bf16, tok_c, back_here),
            ((micro, blocks, STATE, wide), f32) + b_state,
            ((micro, n_state, wide), bf16, (1, n_state, wide), micro_at),
        ],
        [pltpu.VMEM((STATE, wide), f32)],
    )(place, mixer, gate_in, d_ynorm, sums, cols, keys, prefix, chan, payload[:, STATE:])
    out_part = kernel_call(
        out_kernel,
        grid,
        [(tok_c, here)] + out_specs,
        [((micro, shard, width), bf16, (1, size, width), here)],
    )(ynorm_low, *w_out)[0]
    out_sum = lax.psum_scatter(out_part, "head", scatter_dimension=1, tiled=True)

    def weight_parts(a, count, *b, wait=()):
        run = a.shape[2] // count
        out = (run, sum(x.shape[2] for x in b))
        return kernel_call(
            functools.partial(weight_kernel, len(b)),
            (count,),
            [((micro, shard, run), lambda k: (0, 0, k))] + [(x.shape, lambda k: (0, 0, 0)) for x in b],
            [(out, bf16, out, lambda k: (0, 0))] * count,
            [pltpu.VMEM(b[0].shape[:2] + out[1:], bf16)] * (len(b) > 1),
            wait,
        )(a, *b)

    if swapped:
        grad_out_part = weight_parts(ynorm_low, runs, grad_rows)
    else:
        grad_out_part = dot("mtk,mtd->kd", ynorm_low, grad_rows).astype(bf16)
    grad_w_gate = weight_parts(normed_low, seqs, d_gate)
    adj_in = linked(payload, True, out_part, grad_out_part, grad_w_gate)

    d_vals, d_keys, d_step, head_g, skip_g = kernel_call(
        bwd_kernel,
        grid,
        [
            (tok_c, back_here),
            ((1, 2 * STATE, size), back_along),
            ((1, size, 2 * STATE), back_here),
            (tok_l, back_here),
            ((1, 32, size), back_along),
            b_state,
            b_pre,
            ((1, STATE, wide), micro_at),
            (tok_c, back_here),
            b_state,
            ((1, STATE, wide), micro_at),
            ((8, wide), fixed),
            ((8, LANES), fixed),
        ],
        [
            ((micro, shard, wide), bf16, tok_c, back_here),
            ((micro, 2 * STATE, shard), bf16, (1, 2 * STATE, size), back_along),
            ((micro, shard, LANES), bf16, tok_l, back_here),
            ((8, LANES), f32, (8, LANES), fixed),
            ((8, wide), f32, (8, wide), fixed),
        ],
        [pltpu.VMEM((STATE, wide), f32)],
    )(
        vals, keys, ktok, cols, rows_t, starts, prefix, state_in, d_mix, block_adj, adj_in, chan, params
    )
    by_head = lambda x: x.astype(bf16).reshape(heads, rows, -1)
    g_gate = by_head(seq_reduce([after(part, adj_in) for part in grad_w_gate]))
    if swapped:
        grad_out_weight = None
    else:
        full = jnp.zeros((D_INNER, width), bf16)
        full = lax.dynamic_update_slice_in_dim(full, grad_out_part[:chans], h_i * chans, 0)
        grad_out_weight = lax.psum_scatter(full, BOTH, scatter_dimension=0, tiled=True).astype(f32)

    d_val_in, val_back, conv_val_g = kernel_call(
        conv_back_kernel,
        (micro,),
        [whole] + conv_ins,
        [
            ((micro, shard, wide), bf16) + whole,
            ((micro, 8, wide), f32, (1, 8, wide), lambda m: (m, 0, 0)),
            ((8, wide), f32, (8, wide), lambda m: (0, 0)),
        ],
        (),
        (g_gate,),
    )(d_vals, proj, proj_rim, valid_cols, conv_par)
    d_keys = jnp.swapaxes(d_keys.reshape(micro, heads, key_ch, shard), 0, 1)
    d_keys = head_swap(d_keys)
    val_back = lax.ppermute(val_back, "seq", backward)
    rim_sum = d_val_in[:, shard - 16 :].astype(f32) + jnp.pad(val_back, ((0, 0), (8, 0), (0, 0)))
    d_val_in = lax.dynamic_update_slice_in_dim(d_val_in, rim_sum.astype(bf16), shard - 16, 1)

    size = min(shard, 256)
    tile = lambda m, c: (m, c, 0)
    tile_c, tile_l, tile_w = ((1, size, n) for n in (wide, LANES, width))
    d_normed = kernel_call(
        functools.partial(normed_back_kernel, seqs),
        (micro, shard // size),
        [(tile_c, tile), (tile_c, tile), (tile_l, tile)] + gate_specs + [(first[0].shape, fixed)] * seqs,
        [((micro, shard, width), bf16, tile_w, tile)],
        (),
        (out_sum, d_keys),
    )(d_gate, d_val_in, d_step, *w_gate, *first)[0]
    d_normed_sum = lax.psum_scatter(d_normed, "head", scatter_dimension=1, tiled=True)

    d_keys = jnp.pad(d_keys, ((0, 0), (0, 0), (0, key_rows_n - key_ch), (0, 0)))
    d_key_in, key_back, conv_key_g = kernel_call(
        key_back_kernel,
        (micro,),
        [((heads, 1, key_rows_n, shard), lambda m: (0, m, 0, 0))] + key_ins,
        [
            ((micro, key_rows_n, shard), f32) + by_micro(key_rows_n, shard),
            ((micro, key_rows_n, LANES), f32) + by_micro(key_rows_n, LANES),
            ((8, LANES), f32, (8, LANES), lambda m: (0, 0)),
        ],
        [pltpu.VMEM((LANES, LANES), f32)],
        (d_normed,),
    )(d_keys, small_in, small_rim, valid, key_par)
    key_back = lax.ppermute(key_back, "seq", backward)

    fixed1 = lambda m: (0, 0)
    blocks8 = [(8, wide), (8, LANES), (8, LANES), (8, wide)]
    packed = (8, wide + LANES)
    parts = kernel_call(
        pack_kernel,
        (1,),
        [(block, fixed1) for block in blocks8],
        [(packed, f32, packed, fixed1)],
    )(conv_val_g, conv_key_g, head_g, skip_g)[0]
    parts = seq_reduce([parts] * seqs)

    d_key_in, d_small = kernel_call(
        key_join_kernel,
        (micro,),
        [by_micro(key_rows_n, shard), by_micro(key_rows_n, LANES), by_micro(shard, LANES)],
        [
            ((micro, key_rows_n, shard), bf16) + by_micro(key_rows_n, shard),
            ((micro, shard, LANES), bf16) + by_micro(shard, LANES),
        ],
        (),
        (parts,),
    )(d_key_in, key_back, d_step)
    d_key_in = d_key_in[:, :key_ch]
    g_first = weight_parts(normed_low, seqs, d_val_in, d_small)
    if swapped:
        grad_out_weight = seq_reduce([after(part, g_first) for part in grad_out_part])
    key_own = jnp.transpose(d_key_in.reshape(micro, key_ch, heads, tok), (2, 0, 1, 3))
    key_own = head_swap(after(key_own, g_first))
    g_first = by_head(seq_reduce(g_first))
    hidden_out = (hidden_in.astype(f32) + after(out_sum, g_first).astype(f32)).astype(bf16)
    g_gate = head_swap(after(g_gate, key_own))
    parts = three_parts(parts)[:2]
    parts = [jnp.broadcast_to(part[None], (heads,) + part.shape) for part in parts]
    g_first = head_swap(jnp.concatenate([after(g_first, g_gate, key_own)] + parts, axis=1))
    sums = g_first[:, rows : rows + 8].astype(f32) + g_first[:, rows + 8 : rows + 16].astype(f32)
    if swapped:
        own_at = lambda m: (m, 0, 0)
        own = (1, tok, width)
        flat = lambda m: (0, 0)
        steps = (seqs, width // seqs)
        grad_in = kernel_call(
            grad_in_kernel,
            (micro,),
            [
                scalar,
                (own, own_at),
                ((heads, 1, key_ch, tok), lambda m: (0, m, 0, 0)),
                ((2 * STATE, width), flat),
                (own, own_at),
                (steps, flat),
                (own, own_at),
            ],
            [((micro, tok, width), bf16, own, own_at)],
            [pltpu.VMEM((tok, width), f32)],
        )(place, d_normed_sum, key_own, key_rows.reshape(2 * STATE, width), hidden_in, gain_steps, out_grad)[0]
        whole3 = lambda shape: (shape, lambda m: (0,) * len(shape))
        grad_in_weight, norm_sum = kernel_call(
            weight_grad_kernel,
            (1,),
            [whole3(g_gate.shape), whole3(g_first.shape), whole3(in_weight.shape)],
            [
                (in_weight.shape, f32) + whole3(in_weight.shape),
                ((rows, LANES), f32) + whole3((rows, LANES)),
            ],
        )(g_gate, g_first, in_weight)
        norm_sum = norm_sum[:, 0]
    else:
        key_part = dot("hmct,hcd->mtd", key_own, key_rows)
        d_normed = (d_normed_sum.astype(f32) + key_part).reshape(micro, tok, seqs, -1)
        d_normed = from_steps(jnp.moveaxis(d_normed, 2, 0), s_i)
        d_normed = jnp.moveaxis(d_normed, 0, 2).reshape(micro, tok, width)
        own = hidden_in.astype(f32)
        own_inv = lax.rsqrt(jnp.mean(own * own, axis=-1, keepdims=True) + EPS)
        d_unit = d_normed * from_steps(gain_steps, s_i).reshape(-1)
        shared = own_inv * own_inv * jnp.mean(d_unit * own, axis=-1, keepdims=True)
        grad_in = (out_grad.astype(f32) + own_inv * (d_unit - own * shared)).astype(bf16)

        def uncolumns(x, size):
            x = x.astype(f32).reshape(heads, rows, runs, size)
            return jnp.transpose(x, (1, 2, 0, 3)).reshape(rows, runs * heads * size)

        g_key = jnp.transpose(g_first[:, :rows, wide + 8 : wide + 8 + key_ch], (1, 0, 2))
        grad_in_weight = jnp.concatenate(
            [
                uncolumns(g_gate[:, :, :chans], run_ch),
                uncolumns(g_first[:, :rows, :chans], run_ch),
                g_key.astype(f32).reshape(rows, -1),
                uncolumns(g_first[:, :rows, wide : wide + n_heads], run_heads),
            ],
            axis=1,
        )
        norm_sum = jnp.sum(grad_in_weight * in_weight.astype(f32), axis=1)
    norm_g = norm_sum / norm_gain.astype(f32)
    gate_gg = jnp.sum(after(grad_out_weight, g_first) * out_weight.astype(f32), axis=1) / gate_gain.astype(f32)

    conv_g = jnp.concatenate(
        [sums[:, : CONV_K + 1, :chans], sums[:, : CONV_K + 1, wide : wide + key_ch]], axis=2
    )
    head_g = sums[:, CONV_K + 1 : CONV_K + 4, :n_heads].reshape(heads, 3, runs, run_heads)
    conv_gv = jnp.transpose(conv_g[:, :, :chans].reshape(heads, CONV_K + 1, runs, run_ch), (1, 2, 0, 3))
    conv_gk = jnp.transpose(conv_g[:, :, chans:], (1, 0, 2))
    conv_g = jnp.concatenate(
        [conv_gv.reshape(CONV_K + 1, D_INNER), conv_gk.reshape(CONV_K + 1, 2 * STATE)], axis=1
    )
    head_g = jnp.transpose(head_g, (1, 2, 0, 3)).reshape(3, HEADS)
    conv_g = lax.dynamic_slice_in_dim(conv_g, linear * conv_share, conv_share, 1)
    head_g = lax.dynamic_slice_in_dim(head_g, h_i * head_share, head_share, 1)
    return (
        hidden_out,
        grad_in,
        norm_g,
        grad_in_weight,
        conv_g[:CONV_K],
        conv_g[CONV_K],
        head_g[0],
        head_g[1],
        head_g[2],
        gate_gg,
        grad_out_weight,
    )


def solution(mesh):
    tokens = P(None, BOTH, None)
    by_rows = P(BOTH, None)
    return jax.shard_map(
        body,
        mesh=mesh,
        in_specs=(
            tokens,
            P(),
            P(BOTH),
            by_rows,
            P(None, BOTH),
            P(BOTH),
            P("head"),
            P("head"),
            P("head"),
            P(BOTH),
            by_rows,
            tokens,
        ),
        out_specs=(
            tokens,
            tokens,
            P(BOTH),
            by_rows,
            P(None, BOTH),
            P(BOTH),
            P("head"),
            P("head"),
            P("head"),
            P(BOTH),
            by_rows,
        ),
        check_vma=False,
    )
```

```python
import functools

import jax
import jax.numpy as jnp
from jax import lax
from jax.experimental import pallas as pl
from jax.experimental.pallas import tpu as pltpu
from jax.sharding import PartitionSpec as P

HEADS = 64
HEADDIM = 64
STATE = 128
CONV_K = 4
SCAN_BLOCK = 256
D_INNER = 4096
CONV_CH = 4352
EDGE = CONV_K - 1
EPS = 1e-05

f32 = jnp.float32
bf16 = jnp.bfloat16
BOTH = ("seq", "head")


def dot(spec, a, b):
    return jnp.einsum(spec, a, b, preferred_element_type=f32)


def three_parts(v):
    parts = []
    for _ in range(3):
        part = lax.reduce_precision(v, 8, 7)
        parts.append(part.astype(bf16))
        v = v - part
    return parts


def linked(payload, back, *wait):
    count = lax.axis_size("seq")
    total, reach = 0.0, 1.0
    for k in range(1, count):
        if back:
            pairs = [(i, i - k) for i in range(k, count)]
        else:
            pairs = [(i, i + k) for i in range(count - k)]
        got = after(lax.ppermute(payload, "seq", pairs), *wait).astype(f32)
        total = total + reach * got[:, :STATE]
        reach = reach * got[:, STATE : STATE + 1]
    return total


def after(x, *others):
    return lax.optimization_barrier((x, others))[0]


def seq_steps():
    count = lax.axis_size("seq")
    return [(k, [(i, i ^ k) for i in range(count)]) for k in reversed(range(1, count))]


def seq_gather(x, *wait):
    got = [(k, lax.ppermute(x, "seq", pairs)) for k, pairs in seq_steps()]
    if wait:
        got = [(k, after(part, *wait)) for k, part in got]
    parts = dict(got)
    parts[0] = x
    return [parts[k] for k in sorted(parts)]


def seq_reduce(parts):
    total = parts[0].astype(f32)
    got = [lax.ppermute(parts[k], "seq", pairs) for k, pairs in seq_steps()]
    for part in got:
        total = total + part.astype(f32)
    return total


def from_steps(x, place):
    return jnp.stack([lax.dynamic_index_in_dim(x, place ^ k, 0, False) for k in range(x.shape[0])])


def head_swap(x):
    return lax.all_to_all(x, "head", split_axis=0, concat_axis=0, tiled=True)


def silu_parts(v):
    sig = jax.nn.sigmoid(v)
    return v * sig, sig * (1.0 + v * (1.0 - sig))


LANES = 128
LOG, STEP, CARRY, TO_END, SEG = 0, 8, 16, 24, 32
SIG = 16
ROWS_SEG = 24


def nt(a, b):
    return lax.dot_general(a, b, (((1,), (1,)), ((), ())), preferred_element_type=f32)


def nn(a, b):
    return lax.dot_general(a, b, (((1,), (0,)), ((), ())), preferred_element_type=f32)


def tn(a, b):
    return lax.dot_general(a, b, (((0,), (0,)), ((), ())), preferred_element_type=f32)


def split(v):
    high = v.astype(bf16)
    return high, (v - high.astype(f32)).astype(bf16)


def left_half(shape):
    return lax.broadcasted_iota(jnp.int32, shape, len(shape) - 1) < HEADDIM


def pair_of(cols, base, p):
    at = base + 2 * p
    shape = (cols.shape[0], LANES)
    return jnp.where(
        left_half(shape),
        jnp.broadcast_to(cols[:, at : at + 1], shape),
        jnp.broadcast_to(cols[:, at + 1 : at + 2], shape),
    )


def running_sum(x, back=False):
    size = x.shape[1]
    lane = lax.broadcasted_iota(jnp.int32, x.shape, 1)
    shift = 1
    while shift < size:
        if back:
            x = x + jnp.where(lane < size - shift, pltpu.roll(x, size - shift, 1), 0.0)
        else:
            x = x + jnp.where(lane >= shift, pltpu.roll(x, shift, 1), 0.0)
        shift *= 2
    return x


def pairs_in(x):
    return x.shape[-1] // LANES


def lanes(p):
    return slice(p * LANES, (p + 1) * LANES)


def mask_kernel(place_ref, start_ref, seg_ref, valid_ref, cols_ref):
    m = pl.program_id(0)
    size = seg_ref.shape[2]
    at = place_ref[0] * size + lax.broadcasted_iota(jnp.int32, (1, size), 1)

    def seg_of(position):
        total = jnp.zeros((1, size), f32)
        for i in range(start_ref.shape[1]):
            total = total + jnp.where(position >= start_ref[m, i], 1.0, 0.0)
        return total

    seg = seg_of(at)
    behind = [seg_of(at - by) for by in range(1, CONV_K)]
    block = seg_of(at - at % SCAN_BLOCK - 1)
    first = jnp.where(seg == behind[0], 0.0, 1.0)
    seg_ref[0] = jnp.concatenate([seg, block, first, jnp.zeros((5, size), f32)], axis=0)
    rows = [jnp.where(seg == x, 1.0, 0.0) for x in reversed(behind)] + [jnp.ones((1, size), f32)]
    rows = jnp.concatenate(rows + [jnp.zeros((8 - CONV_K, size), f32)], axis=0)
    valid_ref[0] = rows
    cols_ref[0] = jnp.concatenate([rows, jnp.zeros((LANES - 8, size), f32)], axis=0).T


GAIN_AT, GATE_AT, HEAD_AT, CONV_AT, SENT = 0, 128, 256, 384, 384 + 256 * (CONV_K + 1)


def glue_kernel(place_ref, sent_ref, gain_ref, chan_ref, conv_ref, key_ref, par_ref, turned):
    s, h = place_ref[0], place_ref[1]
    heads = sent_ref.shape[0]
    seqs = gain_ref.shape[0]
    left = left_half((1, LANES))

    def from_head(row):
        chips = heads // 2
        return (h // 2 + chips - row % chips) % chips * 2 + (h % 2 ^ row // chips)

    row = from_head(lax.broadcasted_iota(jnp.int32, (heads, LANES), 0))

    def lanes_from(start):
        return sent_ref[:, start : start + LANES].astype(f32)

    for k in range(seqs):
        gains = lanes_from(k * SENT)
        for p in range(heads // 2):
            of_head = lambda i: jnp.sum(jnp.where(row == i, gains, 0.0), axis=0, keepdims=True)
            second = pltpu.roll(of_head(2 * p + 1), HEADDIM, 1)
            gain_ref[k : k + 1, lanes(p)] = jnp.where(left, of_head(2 * p), second)

    of = from_head(lax.broadcasted_iota(jnp.int32, (8, heads), 1))
    to = lax.broadcasted_iota(jnp.int32, (8, heads), 0)
    head = (to // 2 * heads + h) * 2 + to % 2
    sel = jnp.where(of == head // 8, 1.0, 0.0).astype(bf16)
    found = nn(sel, sent_ref[:, HEAD_AT : HEAD_AT + LANES])
    lane = lax.broadcasted_iota(jnp.int32, (8, LANES), 1)
    local = lax.broadcasted_iota(jnp.int32, (8, LANES), 0)
    place = (h * 2 + local % 2) % 8

    def param(q):
        keep = (lane % 24 == q * 8 + place) & (lane < 72)
        return jnp.sum(jnp.where(keep, found, 0.0), axis=1, keepdims=True)

    decay, bias, skip = param(0), param(1), param(2)
    par_ref[...] = jnp.where(lane == 0, bias, jnp.where(lane == 1, -jnp.exp(decay), 0.0))

    def run_of(r, tap):
        total = jnp.zeros((1, LANES), f32)
        for k in range(seqs):
            source = (s ^ k) * heads + row
            begins = source + source // 16
            base = k * SENT + CONV_AT + tap * 2 * LANES
            part = jnp.where(begins == r, lanes_from(base), 0.0)
            part = part + jnp.where(begins == r - 1, lanes_from(base + LANES), 0.0)
            total = total + jnp.sum(part, axis=0, keepdims=True)
        return total

    chan_ref[...] = jnp.zeros_like(chan_ref)
    conv_ref[...] = jnp.zeros_like(conv_ref)
    for b in range(seqs):
        chan_ref[0:1, lanes(b)] = jnp.where(left, skip[2 * b : 2 * b + 1], skip[2 * b + 1 : 2 * b + 2])
        start = pl.multiple_of((s ^ b) * SENT, LANES) + GATE_AT
        gates = sent_ref[0:1, pl.ds(pl.multiple_of(start, LANES), LANES)]
        chan_ref[1:2, lanes(b)] = gates.astype(f32)
        for tap in range(CONV_K + 1):
            conv_ref[tap : tap + 1, lanes(b)] = run_of(b * heads + h, tap)
    per = key_ref.shape[0]
    each = LANES // per
    taps = [run_of(seqs * heads + h // each, tap) for tap in range(CONV_K + 1)]
    turned[...] = jnp.concatenate(taps + [jnp.zeros((LANES - CONV_K - 1, LANES), f32)], axis=0).T
    key_ref[...] = turned[pl.ds(pl.multiple_of(h % each * per, 8), per), :]


def behind_lanes(x, rim, by):
    return pltpu.roll(jnp.concatenate([rim, x], axis=1), by, 1)[:, LANES:] if by else x


def key_conv_kernel(small_ref, rim_ref, valid_ref, par_ref, out_ref):
    count = par_ref.shape[0]
    x, rim = small_ref[0, 8:].astype(f32)[:count], rim_ref[0, 8:].astype(f32)[:count]
    total = par_ref[:, CONV_K : CONV_K + 1]
    for k in range(CONV_K):
        total = total + par_ref[:, k : k + 1] * behind_lanes(x, rim, EDGE - k) * valid_ref[0, k : k + 1]
    out_ref[0] = (total / (1.0 + jnp.exp(-total))).astype(bf16)


def key_back_kernel(d_ref, small_ref, rim_ref, valid_ref, par_ref, in_ref, back_ref, grad_ref, total_grad):
    @pl.when(pl.program_id(0) == 0)
    def _():
        total_grad[...] = jnp.zeros_like(total_grad)

    count = par_ref.shape[0]
    x, rim = small_ref[0, 8:].astype(f32)[:count], rim_ref[0, 8:].astype(f32)[:count]
    size = x.shape[1]
    total = par_ref[:, CONV_K : CONV_K + 1]
    seen = []
    for k in range(CONV_K):
        seen.append(behind_lanes(x, rim, EDGE - k) * valid_ref[0, k : k + 1])
        total = total + par_ref[:, k : k + 1] * seen[k]
    sig = 1.0 / (1.0 + jnp.exp(-total))
    d_keys = 0.0
    for h in range(d_ref.shape[0]):
        d_keys = d_keys + d_ref[h, 0].astype(f32)
    d_total = d_keys.astype(bf16).astype(f32) * (sig * (1.0 + total * (1.0 - sig)))
    lane = lax.broadcasted_iota(jnp.int32, (count, LANES), 1)
    ahead, d_in = 0.0, 0.0
    grads = jnp.where(lane == CONV_K, jnp.sum(d_total, axis=1, keepdims=True), 0.0)
    empty = jnp.zeros((count, LANES), f32)
    for k in range(CONV_K):
        grads = jnp.where(lane == k, jnp.sum(d_total * seen[k], axis=1, keepdims=True), grads)
        held = d_total * (par_ref[:, k : k + 1] * valid_ref[0, k : k + 1])
        by = EDGE - k
        wide = jnp.concatenate([empty, held], axis=1)
        moved = pltpu.roll(wide, size + LANES - by, 1) if by else wide
        ahead = ahead + moved[:, :LANES]
        if by:
            keep = lax.broadcasted_iota(jnp.int32, (count, size), 1) < size - by
            d_in = d_in + jnp.where(keep, moved[:, LANES:], 0.0)
        else:
            d_in = d_in + held
    in_ref[0] = d_in
    back_ref[0] = jnp.where(lane >= LANES - EDGE, ahead, 0.0)
    total_grad[0:count, :] += grads
    grad_ref[...] = total_grad[...].T[0:8]


def pack_kernel(conv_ref, key_ref, head_ref, skip_ref, out_ref):
    wide = conv_ref.shape[1]
    taps = CONV_K + 1
    out_ref[0:taps, :wide] = conv_ref[0:taps]
    out_ref[0:taps, wide:] = key_ref[0:taps]
    left = left_half((1, LANES))
    lane = lax.broadcasted_iota(jnp.int32, (1, LANES), 1)
    skips = jnp.zeros((1, LANES), f32)
    for p in range(wide // LANES):
        both = skip_ref[0:1, lanes(p)]
        first = jnp.sum(jnp.where(left, both, 0.0), axis=1, keepdims=True)
        second = jnp.sum(both, axis=1, keepdims=True) - first
        skips = jnp.where(lane == 2 * p, first, jnp.where(lane == 2 * p + 1, second, skips))
    heads = jnp.concatenate([head_ref[...], jnp.zeros((LANES - 8, LANES), f32)], axis=0).T
    out_ref[taps : taps + 2, :LANES] = heads[0:2]
    out_ref[taps + 2 : 8, :LANES] = skips
    out_ref[taps:8, LANES:] = jnp.zeros((8 - taps, wide), f32)


def unpack_kernel(place_ref, sums_ref, conv_ref, head_ref, total):
    s, h = place_ref[0], place_ref[1]
    heads = sums_ref.shape[0]
    wide = sums_ref.shape[2] - LANES
    for i in range(heads):
        total[i] = sums_ref[i, 0:8].astype(f32) + sums_ref[i, 8:16].astype(f32)
    linear = s * heads + h
    lane = lax.broadcasted_iota(jnp.int32, (8, LANES), 1)
    runs = wide // LANES
    per = 2 * STATE // heads

    def run(r):
        at = pl.multiple_of(((r // heads) & (runs - 1)) * LANES, LANES)
        vals = total[r & (heads - 1), :, pl.ds(at, LANES)]
        keys = jnp.zeros((8, LANES), f32)
        first = jnp.clip(r - runs * heads, 0, 2 * STATE // LANES - 1) * (LANES // per)
        for q in range(LANES // per):
            piece = jnp.where(lane < per, total[first + q, :, wide:], 0.0)
            keys = keys + (pltpu.roll(piece, per * q, 1) if q else piece)
        return jnp.where(r < runs * heads, vals, keys)

    begins = linear + linear // 16
    both = jnp.concatenate([run(begins), run(begins + 1)], axis=1)
    shift = (2 * LANES - (linear & 15) * 8) & (2 * LANES - 1)
    conv_ref[...] = pltpu.roll(both, shift, 1)
    out = jnp.zeros((8, LANES), f32)
    for j in range(heads // 2):
        mine = total[(h & 1) * (heads // 2) + j, :, 0:LANES]
        moved = pltpu.roll(mine, (2 * j + LANES - 2 * (h // 2)) & (LANES - 1), 1)
        out = jnp.where(lane // 2 == j, moved, out)
    head_ref[...] = out


def key_join_kernel(in_ref, back_ref, step_ref, key_ref, small_ref):
    x = in_ref[0]
    count, size = x.shape
    key = jnp.concatenate([x[:, : size - LANES], x[:, size - LANES :] + back_ref[0]], axis=1)
    key_ref[0] = key.astype(bf16)
    rows = [jnp.zeros((8, size), f32), key, jnp.zeros((LANES - 8 - count, size), f32)]
    cols = jnp.concatenate(rows, axis=0).T
    small_ref[0] = (cols + step_ref[0].astype(f32)).astype(bf16)


def prep_kernel(
    m, step_ref, seg_ref, par_ref, val_ref, key_ref, cols_ref, rows_ref, ktok_ref, start_ref, pre_ref, out_ref, state, reach
):
    @pl.when(pl.program_id(0) == 0)
    def _():
        state[...] = jnp.zeros(state.shape, f32)
        reach[...] = jnp.ones(reach.shape, f32)

    raw = step_ref[0] + par_ref[:, 0:1]
    small = jnp.exp(-jnp.abs(raw))
    one = 1.0 + small
    step = jnp.maximum(raw, 0.0) + jnp.where(
        one == 1.0, small, jnp.log(one) * (small / jnp.where(one == 1.0, 1.0, one - 1.0))
    )
    sig = jnp.where(raw >= 0.0, 1.0, small) / one
    log = running_sum(step * par_ref[:, 1:2])
    size = log.shape[1]
    segs = seg_ref[0]
    seg, prev = segs[0:1], segs[1:2]
    carry = jnp.where(seg == prev, jnp.exp(log), 0.0)
    to_end = jnp.where(
        seg == seg[:, size - 1 :], jnp.exp(jnp.minimum(log[:, size - 1 :] - log, 0.0)), 0.0
    )
    rows_ref[0] = jnp.concatenate([log, step, sig, segs], axis=0)
    stack = jnp.concatenate(
        [log, step, carry, to_end, segs, jnp.zeros((LANES - 40, size), f32)], axis=0
    )
    cols = stack.T
    cols_ref[0] = cols
    keys = key_ref[0]
    ktok_ref[0] = keys.astype(f32).T.astype(bf16)
    start_ref[0, 0] = state[...]
    pre_ref[0, 0] = reach[...]
    weight = cols[:, TO_END : TO_END + 8] * cols[:, STEP : STEP + 8]
    for p in range(pairs_in(val_ref)):
        ending = (val_ref[0, :, lanes(p)].astype(f32) * pair_of(weight, 0, p)).astype(bf16)
        decay = pair_of(cols[size - 1 :], CARRY, p)
        state[:, lanes(p)] = decay * state[:, lanes(p)] + nn(keys[:STATE], ending)
        reach[:, lanes(p)] = decay * reach[:, lanes(p)]
    out_ref[0] = jnp.concatenate([state[...], reach[...], reach[...]], axis=0).astype(bf16)


def same_mask(cols, rows):
    size = cols.shape[0]
    at = lax.broadcasted_iota(jnp.int32, (size, size), 0)
    of = lax.broadcasted_iota(jnp.int32, (size, size), 1)
    return (cols[:, SEG : SEG + 1] == rows[ROWS_SEG : ROWS_SEG + 1]) & (at >= of)


def within(cols, rows, j):
    return jnp.exp(jnp.minimum(cols[:, j : j + 1] - rows[j : j + 1], 0.0))


def step_lanes(place_ref, p, swapped):
    return pl.ds(pl.multiple_of((place_ref[0] ^ p) * LANES, LANES), LANES) if swapped else lanes(p)


def fwd_kernel(
    swapped, m, place_ref, val_ref, ktok_ref, cols_ref, rows_ref, start_ref, pre_ref, in_ref, gate_ref, dy_ref, chan_ref, mix_ref, sum_ref
):
    cols, rows = cols_ref[0], rows_ref[0]
    rkey = ktok_ref[0, :, STATE:]
    scores = jnp.where(same_mask(cols, rows), nt(rkey, ktok_ref[0, :, :STATE]), 0.0)
    squares, products = 0.0, 0.0
    left = left_half((cols.shape[0], LANES))
    for p in range(pairs_in(val_ref)):
        at = lanes(p)
        vals = val_ref[0, :, at].astype(f32)
        stepped = vals * pair_of(cols, STEP, p)
        high, low = split(start_ref[0, 0, :, at] + pre_ref[0, 0, 0:1, at] * in_ref[0, :, at])
        mixed = pair_of(cols, CARRY, p) * (nn(rkey, high) + nn(rkey, low))
        weights = [(scores * within(cols, rows, 2 * p + half)).astype(bf16) for half in range(2)]
        held = [jnp.where(keep, stepped, 0.0).astype(bf16) for keep in (left, ~left)]
        mixed = mixed + nn(jnp.concatenate(weights, axis=1), jnp.concatenate(held, axis=0))
        mixed = (mixed + chan_ref[0:1, at] * vals).astype(bf16)
        mix_ref[0, :, at] = mixed
        gate = gate_ref[0, :, at]
        gated = mixed.astype(f32) * (gate / (1.0 + jnp.exp(-gate)))
        squares = squares + gated * gated
        products = products + gated * (dy_ref[0, :, step_lanes(place_ref, p, swapped)] * chan_ref[1:2, at])
    lane = lax.broadcasted_iota(jnp.int32, squares.shape, 1)
    sums = jnp.where(
        lane == 0,
        jnp.sum(squares, axis=1, keepdims=True),
        jnp.where(lane == 1, jnp.sum(products, axis=1, keepdims=True), 0.0),
    )
    sum_ref[0] = sums.T[0:8]


def norm_kernel(
    swapped, m, place_ref, mix_ref, gate_ref, dy_ref, sum_ref, cols_ref, key_ref, pre_ref, chan_ref, reach_ref,
    yn_ref, dmix_ref, dgate_ref, adj_ref, out_ref, adj
):
    @pl.when(pl.program_id(0) == 0)
    def _():
        adj[...] = jnp.zeros(adj.shape, f32)

    cols = cols_ref[0]
    size = cols.shape[0]
    rows = sum_ref[0]
    scale_row = lax.rsqrt(rows[0:1] * (1.0 / D_INNER) + EPS)
    pull_row = scale_row * scale_row * rows[1:2] * (1.0 / D_INNER)
    both = jnp.concatenate([scale_row, pull_row, jnp.zeros((LANES - 2, size), f32)], axis=0).T
    scale, pull = both[:, 0:1], both[:, 1:2]
    for p in range(pairs_in(mix_ref)):
        at = lanes(p)
        mixer = mix_ref[0, :, at].astype(f32)
        gate = gate_ref[0, :, at]
        sig = 1.0 / (1.0 + jnp.exp(-gate))
        act = gate * sig
        slope = sig * (1.0 + gate * (1.0 - sig))
        gated = mixer * act
        unit = gated * scale
        gain = chan_ref[1:2, at]
        step_at = step_lanes(place_ref, p, swapped)
        yn_ref[0, :, step_at] = (unit * gain).astype(bf16)
        d_y = dy_ref[0, :, step_at]
        d_gated = scale * (d_y * gain - gated * pull)
        d_mix = (d_gated * act).astype(bf16)
        dmix_ref[0, :, at] = d_mix
        dgate_ref[0, :, at] = (d_gated * mixer * slope).astype(bf16)
        carried = (d_mix.astype(f32) * pair_of(cols, CARRY, p)).astype(bf16)
        block = nn(key_ref[0, STATE:], carried)
        adj_ref[0, 0, :, at] = block
        adj[:, at] = pair_of(cols[size - 1 :], CARRY, p) * adj[:, at] + block
    reach = reach_ref[0]
    out_ref[0] = jnp.concatenate([adj[...].astype(bf16), reach], axis=0)


def bwd_kernel(
    m, val_ref, key_ref, ktok_ref, cols_ref, rows_ref, start_ref, pre_ref, in_ref, dmix_ref, adj_ref, adjin_ref, chan_ref, par_ref,
    dval_ref, dkey_ref, dstep_ref, head_ref, skip_ref, adj
):
    @pl.when(pl.program_id(0) == 0)
    def _():
        if m == 0:
            head_ref[...] = jnp.zeros_like(head_ref)
            skip_ref[...] = jnp.zeros_like(skip_ref)
        adj[...] = adjin_ref[0]

    cols, rows = cols_ref[0], rows_ref[0]
    size = cols.shape[0]
    wkey, rkey = ktok_ref[0, :, :STATE], ktok_ref[0, :, STATE:]
    same = same_mask(cols, rows)
    scores = jnp.where(same, nt(rkey, wkey), 0.0)
    both_scores = jnp.concatenate([scores, scores], axis=0)
    left = left_half((size, LANES))
    lane = lax.broadcasted_iota(jnp.int32, (size, LANES), 1)
    lane_row = lax.broadcasted_iota(jnp.int32, (1, LANES), 1)
    d_scores = jnp.zeros((size, size), f32)
    d_write = jnp.zeros((STATE, size), f32)
    d_read = jnp.zeros((STATE, size), f32)
    by_row = jnp.zeros((size, LANES), f32)
    last = jnp.zeros((1, LANES), f32)
    by_col = []

    def put(total, p, half, values, offset=0):
        where = lane if values.shape[0] == size else lane_row
        return jnp.where(where == offset + 2 * p + half, values, total)

    def halves_of(x):
        first = jnp.sum(jnp.where(left[: x.shape[0]], x, 0.0), axis=1, keepdims=True)
        return first, jnp.sum(x, axis=1, keepdims=True) - first

    for p in range(pairs_in(val_ref)):
        at = lanes(p)
        vals = val_ref[0, :, at].astype(f32)
        d_mix = dmix_ref[0, :, at]
        d_mix_f = d_mix.astype(f32)
        step = pair_of(cols, STEP, p)
        stepped_f = vals * step
        stepped = stepped_f.astype(bf16)
        carry = pair_of(cols, CARRY, p)
        state = start_ref[0, 0, :, at] + pre_ref[0, 0, 0:1, at] * in_ref[0, :, at]
        high, low = split(state)
        end = adj[:, at]
        end_low = end.astype(bf16)
        ending_f = stepped_f * pair_of(cols, TO_END, p)
        ending = ending_f.astype(bf16)
        carried_d = (d_mix_f * carry).astype(bf16)
        back = nn(wkey, end_low)
        d_stepped = pair_of(cols, TO_END, p) * back
        from_end = ending_f * back
        through = d_mix_f * carry * (nn(rkey, high) + nn(rkey, low)) - from_end
        decay = pair_of(cols[size - 1 :], CARRY, p)
        final = jnp.sum(from_end, axis=0, keepdims=True) + decay * jnp.sum(
            end * state, axis=0, keepdims=True
        )
        final = halves_of(final)
        through = halves_of(through)
        held = [jnp.where(keep, d_mix_f, 0.0).astype(bf16) for keep in (left, ~left)]
        held = jnp.concatenate(held, axis=0)
        near = jnp.concatenate([within(cols, rows, 2 * p), within(cols, rows, 2 * p + 1)], axis=0)
        d_near = nt(held, stepped) * near
        d_scores = d_scores + (d_near[:size] + d_near[size:])
        pairs = d_near * both_scores
        row_sums = jnp.sum(pairs, axis=1, keepdims=True)
        for half in range(2):
            mine = slice(half * size, (half + 1) * size)
            by_row = put(by_row, p, half, row_sums[mine] + through[half])
            by_col.append(jnp.sum(pairs[mine], axis=0, keepdims=True))
            last = put(last, p, half, final[half])
        d_stepped = d_stepped + tn((both_scores * near).astype(bf16), held)
        d_vals = step * d_stepped + chan_ref[0:1, at] * d_mix_f
        dval_ref[0, :, at] = d_vals.astype(bf16)
        skip_ref[0:1, at] += jnp.sum(d_mix_f * vals, axis=0, keepdims=True)
        d_step = halves_of(vals * d_stepped)
        for half in range(2):
            by_row = put(by_row, p, half, d_step[half], 8)
        d_write = d_write + nt(end_low, ending)
        d_read = d_read + nt(high, carried_d) + nt(low, carried_d)
        adj[:, at] = decay * end + adj_ref[0, 0, :, at]
    d_scores = jnp.where(same, d_scores, 0.0).astype(bf16)
    d_write = d_write + nn(key_ref[0, STATE:], d_scores)
    d_read = d_read + nt(key_ref[0, :STATE], d_scores)
    d_keys = jnp.concatenate([d_write, d_read], axis=0).astype(bf16)
    each = dkey_ref.shape[2]
    for h in range(dkey_ref.shape[0]):
        dkey_ref[h, m] = d_keys[h * each : (h + 1) * each]
    while len(by_col) < 8:
        by_col.append(jnp.zeros((1, size), f32))
    turned = by_row.T
    last = jnp.broadcast_to(last, (LANES, LANES)).T[0:8, 0:1]
    d_log = turned[0:8] - jnp.concatenate(by_col, axis=0)
    rate = par_ref[:, 1:2]
    first = rows[ROWS_SEG + 2 : ROWS_SEG + 3]
    d_decay = (running_sum(d_log, True) + last) * (1.0 - first)
    d_raw = (turned[8:16] + d_decay * rate) * rows[SIG : SIG + 8]
    dstep_ref[0] = jnp.concatenate([d_raw, jnp.zeros((LANES - 8, size), f32)], axis=0).T.astype(bf16)
    head_lane = lax.broadcasted_iota(jnp.int32, (8, LANES), 1)
    head_ref[...] += jnp.where(
        head_lane == 0,
        jnp.sum(d_decay * rows[STEP : STEP + 8], axis=1, keepdims=True) * rate,
        jnp.where(head_lane == 1, jnp.sum(d_raw, axis=1, keepdims=True), 0.0),
    )


def shifted(x, rim, by):
    if by == 0:
        return x
    head = jnp.concatenate([rim, x[:8]], axis=0)[8 - by : 16 - by]
    return jnp.concatenate([head, pltpu.roll(x, by, 0)[8:]], axis=0)


def conv_kernel(val_ref, rim_ref, valid_ref, par_ref, out_ref):
    for p in range(pairs_in(val_ref)):
        at = lanes(p)
        x = val_ref[0, :, at].astype(f32)
        rim = rim_ref[0, :, at].astype(f32)[8:16]
        total = par_ref[CONV_K : CONV_K + 1, at]
        for k in range(CONV_K):
            total = total + par_ref[k : k + 1, at] * shifted(x, rim, EDGE - k) * valid_ref[0, :, k : k + 1]
        out_ref[0, :, at] = (total / (1.0 + jnp.exp(-total))).astype(bf16)


def conv_back_kernel(d_ref, val_ref, rim_ref, valid_ref, par_ref, in_ref, back_ref, grad_ref):
    @pl.when(pl.program_id(0) == 0)
    def _():
        grad_ref[...] = jnp.zeros_like(grad_ref)

    size = val_ref.shape[1]
    row = lax.broadcasted_iota(jnp.int32, (size, LANES), 0)
    zeros = jnp.zeros((8, LANES), f32)
    for p in range(pairs_in(val_ref)):
        at = lanes(p)
        x = val_ref[0, :, at].astype(f32)
        rim = rim_ref[0, :, at].astype(f32)[8:16]
        total = par_ref[CONV_K : CONV_K + 1, at]
        seen = []
        for k in range(CONV_K):
            seen.append(shifted(x, rim, EDGE - k) * valid_ref[0, :, k : k + 1])
            total = total + par_ref[k : k + 1, at] * seen[k]
        sig = 1.0 / (1.0 + jnp.exp(-total))
        d_total = d_ref[0, :, at].astype(f32) * (sig * (1.0 + total * (1.0 - sig)))
        grad_ref[CONV_K : CONV_K + 1, at] += jnp.sum(d_total, axis=0, keepdims=True)
        d_in, back = 0.0, 0.0
        for k in range(CONV_K):
            grad_ref[k : k + 1, at] += jnp.sum(d_total * seen[k], axis=0, keepdims=True)
            held = d_total * (par_ref[k : k + 1, at] * valid_ref[0, :, k : k + 1])
            by = EDGE - k
            if by:
                d_in = d_in + jnp.where(row < size - by, pltpu.roll(held, size - by, 0), 0.0)
                back = back + jnp.concatenate([zeros, held[:8]], axis=0)[by : by + 8]
            else:
                d_in = d_in + held
        in_ref[0, :, at] = d_in.astype(bf16)
        back_ref[0, :, at] = back


def proj_kernel(place_ref, x_ref, gain_ref, *refs):
    parts, (low_ref, out_ref, small_ref, weight_ref) = refs[:-4], refs[-4:]
    wide = parts[0].shape[1] - LANES
    size = parts[0].shape[0]

    @pl.when((pl.program_id(0) == 0) & (pl.program_id(1) == 0))
    def _():
        for k, part in enumerate(parts):
            turned = part[:, wide:].astype(f32).T
            weight_ref[:, k * size : (k + 1) * size] = turned.astype(bf16)

    x = x_ref[0].astype(f32)
    inv = lax.rsqrt(jnp.mean(x * x, axis=1, keepdims=True) + EPS)
    total = 0.0
    for k, part in enumerate(parts):
        at = pl.ds(pl.multiple_of((place_ref[0] ^ k) * size, LANES), size)
        low = (x_ref[0, :, at].astype(f32) * inv * gain_ref[k : k + 1]).astype(bf16)
        low_ref[0, :, k * size : (k + 1) * size] = low
        total = total + nn(low, part[...])
    out_ref[0] = total.astype(bf16)
    small_ref[0] = total[:, wide:].T.astype(bf16)


def gather_runs(parts, whole):
    run = parts[0].shape[0]

    @pl.when((pl.program_id(0) == 0) & (pl.program_id(1) == 0))
    def _():
        for r, part in enumerate(parts):
            whole[r * run : (r + 1) * run] = part[...]


def fill_kernel(steps, x_ref, grad_ref, *refs):
    gates, outs, (gate_ref, dy_ref, whole) = refs[:steps], refs[steps:-3], refs[-3:]
    gather_runs(outs, whole)
    size = gates[0].shape[0]
    total = 0.0
    for k, part in enumerate(gates):
        total = total + nn(x_ref[0, :, k * size : (k + 1) * size], part[...])
    gate_ref[0] = total
    dy_ref[0] = nt(grad_ref[0], whole[...])


def out_kernel(y_ref, *refs):
    parts, (out_ref, whole) = refs[:-2], refs[-2:]
    gather_runs(parts, whole)
    width = out_ref.shape[2]
    size = min(width, 512)
    for n in range(width // size):
        at = slice(n * size, (n + 1) * size)
        out_ref[0, :, at] = nn(y_ref[0], whole[:, at]).astype(bf16)


def rows_kernel(place_ref, a_ref, b_ref, out_ref):
    total = 0.0
    for m in range(a_ref.shape[0]):
        total = total + tn(a_ref[m], b_ref[m])
    run = a_ref.shape[2]
    at = pl.multiple_of((place_ref[0] ^ pl.program_id(0)) * run, run)
    out_ref[pl.ds(at, run), :] = total.astype(bf16)


def weight_kernel(parts, has_below, a_ref, *refs):
    below = None
    if has_below:
        below, refs = refs[parts], refs[:parts] + refs[parts + 1 :]
    outs, b_ref = refs[parts:], refs[0]
    if parts > 1:
        outs, b_ref = refs[parts:-1], refs[-1]

        @pl.when(pl.program_id(0) == 0)
        def _():
            at = 0
            for ref in refs[:parts]:
                b_ref[:, :, at : at + ref.shape[2]] = ref[...]
                at += ref.shape[2]

    total = 0.0
    for m in range(a_ref.shape[0]):
        total = total + tn(a_ref[m], b_ref[m])
    total = total.astype(bf16)
    run = total.shape[0]
    for k, out in enumerate(outs):

        @pl.when(pl.program_id(0) == k)
        def _():
            out[0:run] = total
            if below is not None:
                out[run:] = below[...]


def normed_back_kernel(steps, gate_ref, val_ref, small_ref, *refs):
    gates, firsts, out_ref = refs[:steps], refs[steps:-1], refs[-1]
    gate, val, small = gate_ref[0], val_ref[0], small_ref[0]
    wide = val.shape[1]
    size = gates[0].shape[0]
    for k in range(steps):
        first = firsts[k]
        total = nt(gate, gates[k][...]) + nt(val, first[:, :wide]) + nt(small, first[:, wide:])
        out_ref[0, :, k * size : (k + 1) * size] = total.astype(bf16)


def grad_in_kernel(place_ref, sum_ref, key_ref, row_ref, x_ref, gain_ref, grad_ref, out_ref, d_unit):
    steps = gain_ref.shape[0]
    part = x_ref.shape[2] // steps
    x = x_ref[0].astype(f32)
    inv = lax.rsqrt(jnp.mean(x * x, axis=1, keepdims=True) + EPS)
    keys = jnp.concatenate([key_ref[h, 0] for h in range(key_ref.shape[0])], axis=0)
    total = 0.0
    for k in range(steps):
        at = slice(k * part, (k + 1) * part)
        of = pl.ds(pl.multiple_of((place_ref[0] ^ k) * part, LANES), part)
        d_here = sum_ref[0, :, at].astype(f32) + tn(keys, row_ref[:, at])
        d_here = d_here * gain_ref[k : k + 1]
        d_unit[:, of] = d_here
        total = total + jnp.sum(d_here * x_ref[0, :, of].astype(f32), axis=1, keepdims=True)
    shared = inv * inv * total * (1.0 / x.shape[1])
    out_ref[0] = (grad_ref[0].astype(f32) + inv * (d_unit[...] - x * shared)).astype(bf16)


def weight_grad_kernel(gate_ref, first_ref, w_ref, out_ref, sum_ref):
    heads, _, wide = gate_ref.shape
    rows = w_ref.shape[0]
    runs = wide // LANES
    total = jnp.zeros((rows, LANES), f32)

    def place(value, at):
        out_ref[:, at : at + value.shape[1]] = value
        return jnp.sum(value * w_ref[:, at : at + value.shape[1]].astype(f32), axis=1, keepdims=True)

    for ref, base in ((gate_ref, 0), (first_ref, D_INNER)):
        for h in range(heads):
            for b in range(runs):
                value = ref[h, :rows, lanes(b)].astype(f32)
                at = base + (b * heads + h) * LANES
                out_ref[:, at : at + LANES] = value
                total = total + value * w_ref[:, at : at + LANES].astype(f32)
    small = [first_ref[h, :rows, wide:].astype(f32) for h in range(heads)]
    per = 2 * STATE // heads
    keys = jnp.concatenate([x[:, 8 : 8 + per] for x in small], axis=1)
    sums = jnp.sum(total, axis=1, keepdims=True) + place(keys, 2 * D_INNER)
    steps = jnp.concatenate([x[:, :8] for x in small], axis=1).astype(bf16)
    per = 8 // runs
    of = lax.broadcasted_iota(jnp.int32, (HEADS, HEADS), 0)
    to = lax.broadcasted_iota(jnp.int32, (HEADS, HEADS), 1)
    source = (to // per % heads) * 8 + (to // (per * heads)) * per + to % per
    steps = nn(steps, (of == source).astype(f32).astype(bf16))
    sums = sums + place(steps, 2 * D_INNER + 2 * STATE)
    sum_ref[...] = jnp.broadcast_to(sums, (rows, LANES))


ABOUT_US = {
    "proj_kernel": 0,
    "fill_kernel": 9,
    "out_kernel": 0,
    "weight_kernel": 40,
    "rows_kernel": 0,
    "normed_back_kernel": 10,
    "bwd_kernel": 80,
    "fwd_kernel": 6,
    "norm_kernel": 5,
    "prep_kernel": 6,
    "conv_back_kernel": 10,
    "conv_kernel": 3,
    "grad_in_kernel": 30,
    "weight_grad_kernel": 10,
    "mask_kernel": 0,
    "pack_kernel": 0,
    "unpack_kernel": 0,
    "glue_kernel": 0,
    "key_conv_kernel": 1,
    "key_back_kernel": 5,
    "key_join_kernel": 60,
}


def kernel_call(kernel, grid, ins, outs, scratch=(), wait=(), us=None):
    us = ABOUT_US[getattr(kernel, "func", kernel).__name__] if us is None else us
    specs = [
        pl.BlockSpec(memory_space=pltpu.SMEM) if block is None else pl.BlockSpec(block, index)
        for block, index in ins
    ]
    wait = jax.tree.leaves(wait)
    count = len(specs)
    specs = specs + [pl.BlockSpec(memory_space=pl.ANY)] * len(wait)

    def run(*refs):
        kernel(*refs[:count], *refs[count + len(wait) :])

    call = pl.pallas_call(
        run,
        grid=grid,
        in_specs=specs,
        out_specs=[pl.BlockSpec(block, index) for _, _, block, index in outs],
        out_shape=[jax.ShapeDtypeStruct(shape, dtype) for shape, dtype, _, _ in outs],
        scratch_shapes=list(scratch),
        compiler_params=pltpu.CompilerParams(
            vmem_limit_bytes=58 * 2**20, dimension_semantics=("arbitrary",) * len(grid)
        ),
        name=getattr(kernel, "func", kernel).__name__,
        cost_estimate=pl.CostEstimate(flops=us * 2**30, bytes_accessed=us * 3 * 2**20, transcendentals=0),
    )
    return lambda *args: call(*args, *wait)


def fixed(m, c):
    return (0, 0)


def micro_call(kernel, micro, blocks, ins, outs, scratch=(), wait=()):
    shared = [block is None or index is fixed for block, index in ins]
    shared += [index is fixed or block[0] != 1 for _, _, block, index in outs]

    def whole(block, index):
        if block is None:
            return None, None
        if index is fixed:
            return block, lambda c: (0, 0)
        if block[0] != 1:
            return (block[0], micro) + block[2:], lambda c: index(0, c)
        return (micro,) + block[1:], lambda c: index(0, c)

    def run(*refs):
        for m in range(micro):
            views = [ref if one else ref.at[m : m + 1] for ref, one in zip(refs, shared)]
            kernel(m, *views, *[ref.at[m] for ref in refs[len(shared) :]])

    run.__name__ = getattr(kernel, "func", kernel).__name__
    return kernel_call(
        run,
        (blocks,),
        [whole(*spec) for spec in ins],
        [(shape, dtype) + whole(block, index) for shape, dtype, block, index in outs],
        [pltpu.VMEM((micro,) + shape, f32) for shape in scratch],
        wait,
    )


def body(
    hidden_in,
    seq_starts,
    norm_gain,
    in_weight,
    conv_weight,
    conv_bias,
    decay_log,
    dt_bias,
    skip_gain,
    gate_gain,
    out_weight,
    out_grad,
):
    seqs, heads = lax.axis_size("seq"), lax.axis_size("head")
    s_i, h_i = lax.axis_index("seq"), lax.axis_index("head")
    micro, tok, width = hidden_in.shape
    rows = in_weight.shape[0]
    shard = tok * heads
    runs = seqs if HEADS % (seqs * heads) == 0 else 1
    run_ch = D_INNER // (runs * heads)
    run_heads = HEADS // (runs * heads)
    chans, n_heads = runs * run_ch, runs * run_heads
    key_ch = 2 * STATE // heads
    wide = max(chans, LANES)

    def widen(x, axis=-1):
        pads = [(0, 0)] * x.ndim
        pads[axis] = (0, wide - chans)
        return jnp.pad(x, pads) if wide > chans else x

    conv_share, gate_share, head_share = conv_bias.shape[0], gate_gain.shape[0], decay_log.shape[0]

    def mine(x, size):
        lead = x.shape[:-1]
        x = x.reshape(lead + (runs, heads, size))
        x = lax.dynamic_index_in_dim(x, h_i, len(lead) + 1, False)
        return x.reshape(lead + (runs * size,))

    place = s_i[None].astype(jnp.int32)
    scalar = (None, None)
    forward = [(i, i + 1) for i in range(seqs - 1)]
    backward = [(i + 1, i) for i in range(seqs - 1)]
    swapped = runs == seqs
    if swapped and run_ch != LANES:
        raise ValueError("run width")

    def columns(x, size):
        x = x.reshape(rows, runs, heads, size)
        return jnp.transpose(x, (2, 0, 1, 3)).reshape(heads, rows, runs * size)

    def fill(x, axis, size):
        return jnp.pad(x, [(0, size - x.shape[axis] if i == axis else 0) for i in range(x.ndim)])

    val_p = fill(columns(in_weight[:, D_INNER : 2 * D_INNER], run_ch), 2, wide)
    step_p = fill(columns(in_weight[:, 2 * D_INNER + 2 * STATE :], run_heads), 2, 8)
    key_p = in_weight[:, 2 * D_INNER : 2 * D_INNER + 2 * STATE].reshape(rows, heads, key_ch)
    key_p = fill(jnp.swapaxes(key_p, 0, 1), 2, LANES - 8)
    gate_p = fill(columns(in_weight[:, :D_INNER], run_ch), 2, wide)
    first = head_swap(jnp.concatenate([val_p, step_p, key_p], axis=2)).reshape(heads * rows, -1)
    inputs = lax.all_gather(hidden_in, "head", axis=1, tiled=True)

    blocks = shard // SCAN_BLOCK
    by_micro = lambda *shape: ((1,) + shape, lambda m: (m,) + (0,) * len(shape))
    seg_rows, valid, valid_cols = kernel_call(
        mask_kernel,
        (micro,),
        [scalar, scalar],
        [
            ((micro, 8, shard), f32) + by_micro(8, shard),
            ((micro, 8, shard), f32) + by_micro(8, shard),
            ((micro, shard, LANES), f32) + by_micro(shard, LANES),
        ],
    )(place, seq_starts)


    every = seqs * heads
    linear = s_i * heads + h_i
    halo = lax.ppermute(hidden_in[:, tok - EDGE :], BOTH, [(i, i + 1) for i in range(every - 1)])
    taps = jnp.concatenate([conv_weight, conv_bias[None]], axis=0)
    heads_par = jnp.concatenate(three_parts(jnp.concatenate([decay_log, dt_bias, skip_gain])))
    key_rows_n = -(-key_ch // 8) * 8
    if swapped:
        window = jnp.zeros((CONV_K + 1, 2 * LANES), bf16)
        window = lax.dynamic_update_slice_in_dim(window, taps, (linear & 15) * 8, 1)
        sent = [fill(norm_gain, 0, LANES), gate_gain, fill(heads_par, 0, LANES), window.reshape(-1)]
    else:
        sent = [norm_gain, taps.reshape(-1), gate_gain, heads_par]
        sent.append(jnp.zeros((-sum(x.shape[0] for x in sent) % LANES,), bf16))
    sent = jnp.concatenate(sent)
    size = sent.shape[0]
    if swapped:
        w_out = seq_gather(out_weight)
        sent = after(jnp.concatenate(seq_gather(sent) + [halo.reshape(-1)])[None], first, w_out)
        chips = heads // 2
        turns = [[(i, (i + 2 * k) % heads) for i in range(heads)] for k in range(1, chips)]
        sent = jnp.concatenate([sent] + [lax.ppermute(sent, "head", pairs) for pairs in turns], axis=0)
        other = lax.ppermute(sent, "head", [(i, i ^ 1) for i in range(heads)])
        sent = jnp.concatenate([sent, other], axis=0)
        first_row = (h_i >> 1) + (h_i & 1) * chips
    else:
        sent = lax.all_gather(sent, "seq").reshape(-1)
        sent = lax.all_gather(jnp.concatenate([sent, halo.reshape(-1)]), "head")
        first_row = 0
    halo = lax.dynamic_index_in_dim(sent, first_row, 0, False)[seqs * size :].reshape(halo.shape)
    halo = jnp.pad(halo, ((0, 0), (LANES - EDGE, 0), (0, 0)))
    first = seq_gather(first)
    if swapped:
        all_of = lambda shape: (shape, lambda m: (0,) * len(shape))
        outs = [(seqs, width // seqs), (8, wide), (8, wide), (key_ch, LANES), (8, LANES)]
        gain_steps, chan, conv_par, key_par, params = kernel_call(
            glue_kernel,
            (1,),
            [scalar, all_of((heads, seqs * size))],
            [(shape, f32) + all_of(shape) for shape in outs],
            [pltpu.VMEM((LANES, LANES), f32)],
            (first, seg_rows, gate_p, halo),
        )(jnp.stack([s_i, h_i]), sent)
    else:
        sent = jnp.swapaxes(sent[:, : seqs * size].reshape(heads, seqs, -1), 0, 1).reshape(every, -1)
        at = 0

        def take(count):
            nonlocal at
            at += count
            return sent[:, at - count : at]

        gain_steps = from_steps(take(rows).reshape(seqs, heads * rows), s_i).astype(f32)
        conv_p = take((CONV_K + 1) * conv_share).reshape(every, CONV_K + 1, conv_share)
        conv_p = jnp.transpose(conv_p, (1, 0, 2)).reshape(CONV_K + 1, CONV_CH).astype(f32)
        gate_g = mine(take(gate_share).reshape(D_INNER), run_ch).astype(f32)
        par = jnp.sum(take(9 * head_share)[:heads].astype(f32).reshape(heads, 3, 3, head_share), axis=1)
        par = mine(jnp.swapaxes(par, 0, 1).reshape(3, HEADS), run_heads)
        params = fill(fill(jnp.stack([par[1], -jnp.exp(par[0])], axis=1), 0, 8), 1, LANES)
        chan = fill(jnp.stack([widen(jnp.repeat(par[2], HEADDIM)), widen(gate_g)]), 0, 8)
        conv_par = fill(widen(mine(conv_p[:, :D_INNER], run_ch)), 0, 8)
        key_par = lax.dynamic_slice_in_dim(conv_p[:, D_INNER:], h_i * key_ch, key_ch, 1).T
        key_par = fill(fill(key_par, 0, key_rows_n), 1, LANES)

    tile = lambda m, c: (m, c, 0)
    second = head_swap(after(gate_p, first[0]))

    def project(x, size, wait=()):
        many = x.shape[1]
        return kernel_call(
            proj_kernel,
            (micro, many // size),
            [scalar, ((1, size, width), tile), (gain_steps.shape, fixed)] + [(first[0].shape, fixed)] * seqs,
            [
                ((micro, many, width), bf16, (1, size, width), tile),
                ((micro, many, wide + LANES), bf16, (1, size, wide + LANES), tile),
                ((micro, LANES, many), bf16, (1, LANES, size), lambda m, c: (m, 0, c)),
                ((LANES, width), bf16, (LANES, width), fixed),
            ],
            (),
            wait,
        )(place, x, gain_steps, *first)

    normed_low, proj, small_in, key_rows = project(inputs, min(shard, 512), (second,))
    _, proj_rim, small_rim, _ = project(halo, LANES)
    grad_rows = lax.all_gather(after(out_grad, proj), "head", axis=1, tiled=True)
    step_low = small_in[:, :8].astype(f32)

    w_gate = seq_gather(second.reshape(heads * rows, wide))
    if not swapped:
        w_out = lax.all_gather(out_weight, BOTH, axis=0, tiled=True)
        w_out = [widen(lax.dynamic_slice_in_dim(w_out, h_i * chans, chans, 0), 0)]
    gate_specs = [(w_gate[0].shape, fixed)] * seqs
    out_specs = [(part.shape, fixed) for part in w_out]


    whole = ((1, shard, wide), lambda m: (m, 0, 0))
    conv_ins = [
        whole,
        ((1, 16, wide), lambda m: (m, LANES // 16 - 1, 0)),
        by_micro(shard, LANES),
        ((8, wide), lambda m: (0, 0)),
    ]
    key_ins = [
        by_micro(LANES, shard),
        by_micro(LANES, LANES),
        by_micro(8, shard),
        ((key_rows_n, LANES), lambda m: (0, 0)),
    ]
    vals = kernel_call(conv_kernel, (micro,), conv_ins, [((micro, shard, wide), bf16) + whole])(
        proj, proj_rim, valid_cols, conv_par
    )[0]
    keys = kernel_call(
        key_conv_kernel, (micro,), key_ins, [((micro, key_rows_n, shard), bf16) + by_micro(key_rows_n, shard)]
    )(small_in, small_rim, valid, key_par)[0]
    keys = keys[:, :key_ch]
    keys = lax.all_gather(keys, "head", axis=1, tiled=True)

    grid = (micro, blocks)
    size = SCAN_BLOCK
    here = lambda m, c: (m, c, 0)
    along = lambda m, c: (m, 0, c)
    state_at = lambda m, c: (m, c, 0, 0)
    micro_at = lambda m, c: (m, 0, 0)
    row8 = (1, 8, size)
    tok_c, tok_l = (1, size, wide), (1, size, LANES)
    n_state = STATE + 16
    f_state = ((1, 1, STATE, wide), state_at)
    f_pre = ((1, 1, 8, wide), state_at)
    cols, rows_t, ktok, starts, prefix, payload = micro_call(
        prep_kernel,
        micro,
        blocks,
        [(row8, along), (row8, along), ((8, LANES), fixed), (tok_c, here), ((1, 2 * STATE, size), along)],
        [
            ((micro, shard, LANES), f32, tok_l, here),
            ((micro, 32, shard), f32, (1, 32, size), along),
            ((micro, shard, 2 * STATE), bf16, (1, size, 2 * STATE), here),
            ((micro, blocks, STATE, wide), f32) + f_state,
            ((micro, blocks, 8, wide), f32) + f_pre,
            ((micro, n_state, wide), bf16, (1, n_state, wide), micro_at),
        ],
        [(STATE, wide), (8, wide)],
        w_gate,
    )(step_low, seg_rows, params, vals, keys)
    key_rows = lax.all_gather(after(key_rows[8 : 8 + key_ch], payload), "head")
    size = min(shard, 512)
    gate_in, d_ynorm = kernel_call(
        functools.partial(fill_kernel, seqs),
        (micro, shard // size),
        [((1, size, width), tile)] * 2 + gate_specs + out_specs,
        [((micro, shard, wide), f32, (1, size, wide), tile)] * 2,
        [pltpu.VMEM((wide, width), bf16)],
        (payload,),
    )(normed_low, grad_rows, *w_gate, *w_out)
    size = SCAN_BLOCK
    state_in = linked(payload, False, gate_in)
    mixer, sums = micro_call(
        functools.partial(fwd_kernel, swapped),
        micro,
        blocks,
        [
            scalar,
            (tok_c, here),
            ((1, size, 2 * STATE), here),
            (tok_l, here),
            ((1, 32, size), along),
            f_state,
            f_pre,
            ((1, STATE, wide), micro_at),
            (tok_c, here),
            (tok_c, here),
            ((8, wide), fixed),
        ],
        [((micro, shard, wide), bf16, tok_c, here), ((micro, 8, shard), f32, row8, along)],
    )(place, vals, ktok, cols, rows_t, starts, prefix, state_in, gate_in, d_ynorm, chan)

    sums = fill(lax.psum(sums[:, :2], "head"), 1, 8)
    back_here = lambda m, c: (m, blocks - 1 - c, 0)
    back_along = lambda m, c: (m, 0, blocks - 1 - c)
    back_state = lambda m, c: (m, blocks - 1 - c, 0, 0)
    b_state, b_pre = (f_state[0], back_state), (f_pre[0], back_state)
    ynorm_low, d_mix, d_gate, block_adj, payload = micro_call(
        functools.partial(norm_kernel, swapped),
        micro,
        blocks,
        [
            scalar,
            (tok_c, back_here),
            (tok_c, back_here),
            (tok_c, back_here),
            (row8, back_along),
            (tok_l, back_here),
            ((1, 2 * STATE, size), back_along),
            b_pre,
            ((8, wide), fixed),
            ((1, 16, wide), micro_at),
        ],
        [
            ((micro, shard, wide), bf16, tok_c, back_here),
            ((micro, shard, wide), bf16, tok_c, back_here),
            ((micro, shard, wide), bf16, tok_c, back_here),
            ((micro, blocks, STATE, wide), f32) + b_state,
            ((micro, n_state, wide), bf16, (1, n_state, wide), micro_at),
        ],
        [(STATE, wide)],
        (key_rows,),
    )(place, mixer, gate_in, d_ynorm, sums, cols, keys, prefix, chan, payload[:, STATE:])
    wide_tile = min(shard, 512)
    out_part = kernel_call(
        out_kernel,
        (micro, shard // wide_tile),
        [((1, wide_tile, wide), here)] + out_specs,
        [((micro, shard, width), bf16, (1, wide_tile, width), here)],
        [pltpu.VMEM((wide, width), bf16)],
    )(ynorm_low, *w_out)[0]
    out_sum = lax.psum_scatter(out_part, "head", scatter_dimension=1, tiled=True)

    def weight_parts(a, count, *b, below=None, wait=(), us=None):
        run = a.shape[2] // count
        wide_b = sum(x.shape[2] for x in b)
        extra = [] if below is None else [below]
        out = (run + sum(x.shape[0] for x in extra), wide_b)
        return kernel_call(
            functools.partial(weight_kernel, len(b), below is not None),
            (count,),
            [((micro, shard, run), lambda k: (0, 0, k))]
            + [(x.shape, lambda k: (0, 0, 0)) for x in b]
            + [(x.shape, lambda k: (0, 0)) for x in extra],
            [(out, bf16, out, lambda k: (0, 0))] * count,
            [pltpu.VMEM(b[0].shape[:2] + (wide_b,), bf16)] * (len(b) > 1),
            wait,
            us,
        )(a, *b, *extra)

    if swapped:
        out = (wide, width)
        grad_out_part = kernel_call(
            rows_kernel,
            (runs,),
            [
                scalar,
                ((micro, shard, run_ch), lambda k: (0, 0, k)),
                (grad_rows.shape, lambda k: (0, 0, 0)),
            ],
            [(out, bf16, out, lambda k: (0, 0))],
        )(place, ynorm_low, grad_rows)[0]
    else:
        grad_out_part = ()
    grad_w_gate = weight_parts(normed_low, seqs, d_gate, us=0)
    adj_in = linked(payload, True, out_part, grad_w_gate, grad_out_part)

    by_heads = key_ch % 16 == 0
    key_shape = (heads, micro, key_ch, shard) if by_heads else (1, micro, 2 * STATE, shard)
    d_vals, d_keys, d_step, head_g, skip_g = micro_call(
        bwd_kernel,
        micro,
        blocks,
        [
            (tok_c, back_here),
            ((1, 2 * STATE, size), back_along),
            ((1, size, 2 * STATE), back_here),
            (tok_l, back_here),
            ((1, 32, size), back_along),
            b_state,
            b_pre,
            ((1, STATE, wide), micro_at),
            (tok_c, back_here),
            b_state,
            ((1, STATE, wide), micro_at),
            ((8, wide), fixed),
            ((8, LANES), fixed),
        ],
        [
            ((micro, shard, wide), bf16, tok_c, back_here),
            (key_shape, bf16, (key_shape[0], 1, key_shape[2], size), lambda m, c: (0, 0, 0, blocks - 1 - c)),
            ((micro, shard, LANES), bf16, tok_l, back_here),
            ((8, LANES), f32, (8, LANES), fixed),
            ((8, wide), f32, (8, wide), fixed),
        ],
        [(STATE, wide)],
    )(
        vals, keys, ktok, cols, rows_t, starts, prefix, state_in, d_mix, block_adj, adj_in, chan, params
    )
    by_head = lambda x: x.astype(bf16).reshape(heads, rows, -1)
    g_gate = by_head(seq_reduce([after(part, adj_in) for part in grad_w_gate]))
    d_val_in, val_back, conv_val_g = kernel_call(
        conv_back_kernel,
        (micro,),
        [whole] + conv_ins,
        [
            ((micro, shard, wide), bf16) + whole,
            ((micro, 8, wide), f32, (1, 8, wide), lambda m: (m, 0, 0)),
            ((8, wide), f32, (8, wide), lambda m: (0, 0)),
        ],
        (),
        (g_gate,),
    )(d_vals, proj, proj_rim, valid_cols, conv_par)
    if not by_heads:
        d_keys = jnp.swapaxes(d_keys.reshape(micro, heads, key_ch, shard), 0, 1)
    d_keys = head_swap(d_keys)
    g_gate_own = head_swap(after(g_gate, d_keys))
    val_back = lax.ppermute(val_back, "seq", backward)
    rim_sum = d_val_in[:, shard - 16 :].astype(f32) + jnp.pad(val_back, ((0, 0), (8, 0), (0, 0)))
    d_val_in = lax.dynamic_update_slice_in_dim(d_val_in, rim_sum.astype(bf16), shard - 16, 1)

    d_keys = jnp.pad(d_keys, ((0, 0), (0, 0), (0, key_rows_n - key_ch), (0, 0)))
    d_key_in, key_back, conv_key_g = kernel_call(
        key_back_kernel,
        (micro,),
        [((heads, 1, key_rows_n, shard), lambda m: (0, m, 0, 0))] + key_ins,
        [
            ((micro, key_rows_n, shard), f32) + by_micro(key_rows_n, shard),
            ((micro, key_rows_n, LANES), f32) + by_micro(key_rows_n, LANES),
            ((8, LANES), f32, (8, LANES), lambda m: (0, 0)),
        ],
        [pltpu.VMEM((LANES, LANES), f32)],
    )(d_keys, small_in, small_rim, valid, key_par)
    key_back = lax.ppermute(key_back, "seq", backward)

    size = min(shard, 512)
    tile = lambda m, c: (m, c, 0)
    tile_c, tile_l, tile_w = ((1, size, n) for n in (wide, LANES, width))
    d_normed = kernel_call(
        functools.partial(normed_back_kernel, seqs),
        (micro, shard // size),
        [(tile_c, tile), (tile_c, tile), (tile_l, tile)] + gate_specs + [(first[0].shape, fixed)] * seqs,
        [((micro, shard, width), bf16, tile_w, tile)],
        (),
        (out_sum, d_key_in),
    )(d_gate, d_val_in, d_step, *w_gate, *first)[0]
    d_normed_sum = lax.psum_scatter(d_normed, "head", scatter_dimension=1, tiled=True)

    fixed1 = lambda m: (0, 0)
    blocks8 = [(8, wide), (8, LANES), (8, LANES), (8, wide)]
    packed = (8, wide + LANES)
    small = kernel_call(
        pack_kernel,
        (1,),
        [(block, fixed1) for block in blocks8],
        [(packed, f32, packed, fixed1)],
    )(conv_val_g, conv_key_g, head_g, skip_g)[0]
    small = seq_reduce([small] * seqs)

    d_key_in, d_small = kernel_call(
        key_join_kernel,
        (micro,),
        [by_micro(key_rows_n, shard), by_micro(key_rows_n, LANES), by_micro(shard, LANES)],
        [
            ((micro, key_rows_n, shard), bf16) + by_micro(key_rows_n, shard),
            ((micro, shard, LANES), bf16) + by_micro(shard, LANES),
        ],
        (),
        (g_gate_own,),
    )(d_key_in, key_back, d_step)
    d_key_in = d_key_in[:, :key_ch]
    g_first = weight_parts(normed_low, seqs, d_val_in, d_small)
    if swapped:
        grad_out_weight = lax.psum_scatter(
            grad_out_part, "seq", scatter_dimension=0, tiled=True
        ).astype(f32)
    else:
        full = dot("mtk,mtd->kd", ynorm_low, grad_rows).astype(bf16)[:chans]
        full = lax.dynamic_update_slice_in_dim(jnp.zeros((D_INNER, width), bf16), full, h_i * chans, 0)
        grad_out_weight = lax.psum_scatter(full, BOTH, scatter_dimension=0, tiled=True).astype(f32)
    d_key_in, small = after((d_key_in, small), g_first)
    key_own = jnp.transpose(d_key_in.reshape(micro, key_ch, heads, tok), (2, 0, 1, 3))
    count = key_own.size // heads
    key_n = -(-count // (8 * (wide + LANES))) * 8
    key_own = fill(key_own.reshape(heads, count), 1, key_n * (wide + LANES)).reshape(heads, key_n, -1)
    small = [jnp.broadcast_to(part[None], (heads,) + part.shape) for part in three_parts(small)[:2]]
    small = head_swap(after(jnp.concatenate(small + [key_own], axis=1), g_first))
    key_own = small[:, 16:].reshape(heads, -1)[:, :count].reshape(heads, micro, key_ch, tok)

    if swapped:
        conv_g, head_g = kernel_call(
            unpack_kernel,
            (1,),
            [scalar, ((heads, 16, wide + LANES), lambda m: (0, 0, 0))],
            [
                ((8, 2 * LANES), f32, (8, 2 * LANES), lambda m: (0, 0)),
                ((8, LANES), f32, (8, LANES), lambda m: (0, 0)),
            ],
            [pltpu.VMEM((heads, 8, wide + LANES), f32)],
        )(jnp.stack([s_i, h_i]), small)
        conv_g = conv_g[: CONV_K + 1, :conv_share]
        head_g = head_g[CONV_K + 1 :, :head_share]
    else:
        sums = small[:, :8].astype(f32) + small[:, 8:16].astype(f32)
        conv_g = jnp.concatenate(
            [sums[:, : CONV_K + 1, :chans], sums[:, : CONV_K + 1, wide : wide + key_ch]], axis=2
        )
        head_g = sums[:, CONV_K + 1 : CONV_K + 4, :n_heads].reshape(heads, 3, runs, run_heads)
        conv_gv = jnp.transpose(conv_g[:, :, :chans].reshape(heads, CONV_K + 1, runs, run_ch), (1, 2, 0, 3))
        conv_gk = jnp.transpose(conv_g[:, :, chans:], (1, 0, 2))
        conv_g = jnp.concatenate(
            [conv_gv.reshape(CONV_K + 1, D_INNER), conv_gk.reshape(CONV_K + 1, 2 * STATE)], axis=1
        )
        head_g = jnp.transpose(head_g, (1, 2, 0, 3)).reshape(3, HEADS)
        conv_g = lax.dynamic_slice_in_dim(conv_g, linear * conv_share, conv_share, 1)
        head_g = lax.dynamic_slice_in_dim(head_g, h_i * head_share, head_share, 1)
    hidden_out = (hidden_in.astype(f32) + after(out_sum, g_first).astype(f32)).astype(bf16)
    gate_gg = jnp.sum(after(grad_out_weight, g_first) * out_weight.astype(f32), axis=1) / gate_gain.astype(f32)
    g_first = by_head(seq_reduce(g_first))
    g_first = head_swap(after(g_first, conv_g, head_g, hidden_out, gate_gg, key_own))
    if swapped:
        own_at = lambda m: (m, 0, 0)
        own = (1, tok, width)
        flat = lambda m: (0, 0)
        steps = (seqs, width // seqs)
        grad_in = kernel_call(
            grad_in_kernel,
            (micro,),
            [
                scalar,
                (own, own_at),
                ((heads, 1, key_ch, tok), lambda m: (0, m, 0, 0)),
                ((2 * STATE, width), flat),
                (own, own_at),
                (steps, flat),
                (own, own_at),
            ],
            [((micro, tok, width), bf16, own, own_at)],
            [pltpu.VMEM((tok, width), f32)],
        )(place, d_normed_sum, key_own, key_rows.reshape(2 * STATE, width), hidden_in, gain_steps, out_grad)[0]
        whole3 = lambda shape: (shape, lambda m: (0,) * len(shape))
        grad_in_weight, norm_sum = kernel_call(
            weight_grad_kernel,
            (1,),
            [whole3(g_gate_own.shape), whole3(g_first.shape), whole3(in_weight.shape)],
            [
                (in_weight.shape, f32) + whole3(in_weight.shape),
                ((rows, LANES), f32) + whole3((rows, LANES)),
            ],
            (),
            (grad_in,),
        )(g_gate_own, g_first, in_weight)
        norm_sum = norm_sum[:, 0]
    else:
        key_part = dot("hmct,hcd->mtd", key_own, key_rows)
        d_normed = (d_normed_sum.astype(f32) + key_part).reshape(micro, tok, seqs, -1)
        d_normed = from_steps(jnp.moveaxis(d_normed, 2, 0), s_i)
        d_normed = jnp.moveaxis(d_normed, 0, 2).reshape(micro, tok, width)
        own = hidden_in.astype(f32)
        own_inv = lax.rsqrt(jnp.mean(own * own, axis=-1, keepdims=True) + EPS)
        d_unit = d_normed * from_steps(gain_steps, s_i).reshape(-1)
        shared = own_inv * own_inv * jnp.mean(d_unit * own, axis=-1, keepdims=True)
        grad_in = (out_grad.astype(f32) + own_inv * (d_unit - own * shared)).astype(bf16)

        def uncolumns(x, size):
            x = x.astype(f32).reshape(heads, rows, runs, size)
            return jnp.transpose(x, (1, 2, 0, 3)).reshape(rows, runs * heads * size)

        g_key = jnp.transpose(g_first[:, :rows, wide + 8 : wide + 8 + key_ch], (1, 0, 2))
        grad_in_weight = jnp.concatenate(
            [
                uncolumns(g_gate_own[:, :rows, :chans], run_ch),
                uncolumns(g_first[:, :rows, :chans], run_ch),
                g_key.astype(f32).reshape(rows, -1),
                uncolumns(g_first[:, :rows, wide : wide + n_heads], run_heads),
            ],
            axis=1,
        )
        norm_sum = jnp.sum(grad_in_weight * in_weight.astype(f32), axis=1)
    norm_g = norm_sum / norm_gain.astype(f32)

    return (
        hidden_out,
        grad_in,
        norm_g,
        grad_in_weight,
        conv_g[:CONV_K],
        conv_g[CONV_K],
        head_g[0],
        head_g[1],
        head_g[2],
        gate_gg,
        grad_out_weight,
    )


def solution(mesh):
    tokens = P(None, BOTH, None)
    by_rows = P(BOTH, None)
    return jax.shard_map(
        body,
        mesh=mesh,
        in_specs=(
            tokens,
            P(),
            P(BOTH),
            by_rows,
            P(None, BOTH),
            P(BOTH),
            P("head"),
            P("head"),
            P("head"),
            P(BOTH),
            by_rows,
            tokens,
        ),
        out_specs=(
            tokens,
            tokens,
            P(BOTH),
            by_rows,
            P(None, BOTH),
            P(BOTH),
            P("head"),
            P("head"),
            P("head"),
            P(BOTH),
            by_rows,
        ),
        check_vma=False,
    )
```

```python
import functools

import jax
import jax.numpy as jnp
from jax import lax
from jax.experimental import pallas as pl
from jax.experimental.pallas import tpu as pltpu
from jax.sharding import PartitionSpec as P

HEADS = 64
HEADDIM = 64
STATE = 128
CONV_K = 4
SCAN_BLOCK = 256
D_INNER = 4096
CONV_CH = 4352
EDGE = CONV_K - 1
EPS = 1e-05

f32 = jnp.float32
bf16 = jnp.bfloat16
BOTH = ("seq", "head")


def dot(spec, a, b):
    return jnp.einsum(spec, a, b, preferred_element_type=f32)


def three_parts(v):
    parts = []
    for _ in range(3):
        part = lax.reduce_precision(v, 8, 7)
        parts.append(part.astype(bf16))
        v = v - part
    return parts


def linked(payload, back, *wait):
    count = lax.axis_size("seq")
    got = []
    for k in range(1, count):
        if back:
            pairs = [(i, i - k) for i in range(k, count)]
        else:
            pairs = [(i, i + k) for i in range(count - k)]
        got.append(after(lax.ppermute(payload, "seq", pairs), *wait))
    return got


def after(x, *others):
    return lax.optimization_barrier((x, others))[0]


def seq_steps():
    count = lax.axis_size("seq")
    return [(k, [(i, i ^ k) for i in range(count)]) for k in reversed(range(1, count))]


def seq_gather(x, *wait):
    got = [(k, lax.ppermute(x, "seq", pairs)) for k, pairs in seq_steps()]
    if wait:
        got = [(k, after(part, *wait)) for k, part in got]
    parts = dict(got)
    parts[0] = x
    return [parts[k] for k in sorted(parts)]


def seq_exchange(parts):
    return [parts[0]] + [lax.ppermute(parts[k], "seq", pairs) for k, pairs in seq_steps()]


def total_of(parts):
    return functools.reduce(lambda a, b: a + b, [part.astype(f32) for part in parts])


def seq_reduce(parts):
    return total_of(seq_exchange(parts))


def from_steps(x, place):
    return jnp.stack([lax.dynamic_index_in_dim(x, place ^ k, 0, False) for k in range(x.shape[0])])


def head_swap(x):
    return lax.all_to_all(x, "head", split_axis=0, concat_axis=0, tiled=True)


def silu_parts(v):
    sig = jax.nn.sigmoid(v)
    return v * sig, sig * (1.0 + v * (1.0 - sig))


LANES = 128
LOG, STEP, CARRY, TO_END, SEG = 0, 8, 16, 24, 32
SIG = 16
ROWS_SEG = 24


def nt(a, b):
    return lax.dot_general(a, b, (((1,), (1,)), ((), ())), preferred_element_type=f32)


def nn(a, b):
    return lax.dot_general(a, b, (((1,), (0,)), ((), ())), preferred_element_type=f32)


def tn(a, b):
    return lax.dot_general(a, b, (((0,), (0,)), ((), ())), preferred_element_type=f32)


def split(v):
    high = v.astype(bf16)
    return high, (v - high.astype(f32)).astype(bf16)


def left_half(shape):
    return lax.broadcasted_iota(jnp.int32, shape, len(shape) - 1) < HEADDIM


def pair_of(cols, base, p):
    at = base + 2 * p
    shape = (cols.shape[0], LANES)
    return jnp.where(
        left_half(shape),
        jnp.broadcast_to(cols[:, at : at + 1], shape),
        jnp.broadcast_to(cols[:, at + 1 : at + 2], shape),
    )


def running_sum(x, back=False):
    size = x.shape[1]
    lane = lax.broadcasted_iota(jnp.int32, x.shape, 1)
    shift = 1
    while shift < size:
        if back:
            x = x + jnp.where(lane < size - shift, pltpu.roll(x, size - shift, 1), 0.0)
        else:
            x = x + jnp.where(lane >= shift, pltpu.roll(x, shift, 1), 0.0)
        shift *= 2
    return x


def pairs_in(x):
    return x.shape[-1] // LANES


def lanes(p):
    return slice(p * LANES, (p + 1) * LANES)


def mask_kernel(place_ref, start_ref, seg_ref, valid_ref, cols_ref):
    m = pl.program_id(0)
    size = seg_ref.shape[2]
    at = place_ref[0] * size + lax.broadcasted_iota(jnp.int32, (1, size), 1)

    def seg_of(position):
        total = jnp.zeros((1, size), f32)
        for i in range(start_ref.shape[1]):
            total = total + jnp.where(position >= start_ref[m, i], 1.0, 0.0)
        return total

    seg = seg_of(at)
    behind = [seg_of(at - by) for by in range(1, CONV_K)]
    block = seg_of(at - at % SCAN_BLOCK - 1)
    first = jnp.where(seg == behind[0], 0.0, 1.0)
    seg_ref[0] = jnp.concatenate([seg, block, first, jnp.zeros((5, size), f32)], axis=0)
    rows = [jnp.where(seg == x, 1.0, 0.0) for x in reversed(behind)] + [jnp.ones((1, size), f32)]
    rows = jnp.concatenate(rows + [jnp.zeros((8 - CONV_K, size), f32)], axis=0)
    valid_ref[0] = rows
    cols_ref[0] = jnp.concatenate([rows, jnp.zeros((LANES - 8, size), f32)], axis=0).T


GAIN_AT, GATE_AT, HEAD_AT, CONV_AT, SENT = 0, 128, 256, 384, 384 + 256 * (CONV_K + 1)


def glue_kernel(place_ref, sent_ref, gain_ref, chan_ref, conv_ref, key_ref, par_ref, turned):
    s, h = place_ref[0], place_ref[1]
    heads = sent_ref.shape[0]
    seqs = gain_ref.shape[0]
    left = left_half((1, LANES))

    def from_head(row):
        chips = heads // 2
        return (h // 2 + chips - row % chips) % chips * 2 + (h % 2 ^ row // chips)

    row = from_head(lax.broadcasted_iota(jnp.int32, (heads, LANES), 0))

    def lanes_from(start):
        return sent_ref[:, start : start + LANES].astype(f32)

    for k in range(seqs):
        gains = lanes_from(k * SENT)
        for p in range(heads // 2):
            of_head = lambda i: jnp.sum(jnp.where(row == i, gains, 0.0), axis=0, keepdims=True)
            second = pltpu.roll(of_head(2 * p + 1), HEADDIM, 1)
            gain_ref[k : k + 1, lanes(p)] = jnp.where(left, of_head(2 * p), second)

    of = from_head(lax.broadcasted_iota(jnp.int32, (8, heads), 1))
    to = lax.broadcasted_iota(jnp.int32, (8, heads), 0)
    head = (to // 2 * heads + h) * 2 + to % 2
    sel = jnp.where(of == head // 8, 1.0, 0.0).astype(bf16)
    found = nn(sel, sent_ref[:, HEAD_AT : HEAD_AT + LANES])
    lane = lax.broadcasted_iota(jnp.int32, (8, LANES), 1)
    local = lax.broadcasted_iota(jnp.int32, (8, LANES), 0)
    place = (h * 2 + local % 2) % 8

    def param(q):
        keep = (lane % 24 == q * 8 + place) & (lane < 72)
        return jnp.sum(jnp.where(keep, found, 0.0), axis=1, keepdims=True)

    decay, bias, skip = param(0), param(1), param(2)
    par_ref[...] = jnp.where(lane == 0, bias, jnp.where(lane == 1, -jnp.exp(decay), 0.0))

    def run_of(r, tap):
        total = jnp.zeros((1, LANES), f32)
        for k in range(seqs):
            source = (s ^ k) * heads + row
            begins = source + source // 16
            base = k * SENT + CONV_AT + tap * 2 * LANES
            part = jnp.where(begins == r, lanes_from(base), 0.0)
            part = part + jnp.where(begins == r - 1, lanes_from(base + LANES), 0.0)
            total = total + jnp.sum(part, axis=0, keepdims=True)
        return total

    chan_ref[...] = jnp.zeros_like(chan_ref)
    conv_ref[...] = jnp.zeros_like(conv_ref)
    for b in range(seqs):
        chan_ref[0:1, lanes(b)] = jnp.where(left, skip[2 * b : 2 * b + 1], skip[2 * b + 1 : 2 * b + 2])
        start = pl.multiple_of((s ^ b) * SENT, LANES) + GATE_AT
        gates = sent_ref[0:1, pl.ds(pl.multiple_of(start, LANES), LANES)]
        chan_ref[1:2, lanes(b)] = gates.astype(f32)
        for tap in range(CONV_K + 1):
            conv_ref[tap : tap + 1, lanes(b)] = run_of(b * heads + h, tap)
    per = key_ref.shape[0]
    each = LANES // per
    taps = [run_of(seqs * heads + h // each, tap) for tap in range(CONV_K + 1)]
    turned[...] = jnp.concatenate(taps + [jnp.zeros((LANES - CONV_K - 1, LANES), f32)], axis=0).T
    key_ref[...] = turned[pl.ds(pl.multiple_of(h % each * per, 8), per), :]


def behind_lanes(x, rim, by):
    return pltpu.roll(jnp.concatenate([rim, x], axis=1), by, 1)[:, LANES:] if by else x


def key_conv_kernel(small_ref, rim_ref, valid_ref, par_ref, out_ref):
    count = par_ref.shape[0]
    x, rim = small_ref[0, 8:].astype(f32)[:count], rim_ref[0, 8:].astype(f32)[:count]
    total = par_ref[:, CONV_K : CONV_K + 1]
    for k in range(CONV_K):
        total = total + par_ref[:, k : k + 1] * behind_lanes(x, rim, EDGE - k) * valid_ref[0, k : k + 1]
    out_ref[0] = (total / (1.0 + jnp.exp(-total))).astype(bf16)


def key_back_kernel(d_ref, small_ref, rim_ref, valid_ref, par_ref, in_ref, back_ref, grad_ref, total_grad):
    @pl.when(pl.program_id(0) == 0)
    def _():
        total_grad[...] = jnp.zeros_like(total_grad)

    count = par_ref.shape[0]
    x, rim = small_ref[0, 8:].astype(f32)[:count], rim_ref[0, 8:].astype(f32)[:count]
    size = x.shape[1]
    total = par_ref[:, CONV_K : CONV_K + 1]
    seen = []
    for k in range(CONV_K):
        seen.append(behind_lanes(x, rim, EDGE - k) * valid_ref[0, k : k + 1])
        total = total + par_ref[:, k : k + 1] * seen[k]
    sig = 1.0 / (1.0 + jnp.exp(-total))
    d_keys = 0.0
    for h in range(d_ref.shape[0]):
        d_keys = d_keys + d_ref[h, 0].astype(f32)
    d_total = d_keys.astype(bf16).astype(f32) * (sig * (1.0 + total * (1.0 - sig)))
    lane = lax.broadcasted_iota(jnp.int32, (count, LANES), 1)
    ahead, d_in = 0.0, 0.0
    grads = jnp.where(lane == CONV_K, jnp.sum(d_total, axis=1, keepdims=True), 0.0)
    empty = jnp.zeros((count, LANES), f32)
    for k in range(CONV_K):
        grads = jnp.where(lane == k, jnp.sum(d_total * seen[k], axis=1, keepdims=True), grads)
        held = d_total * (par_ref[:, k : k + 1] * valid_ref[0, k : k + 1])
        by = EDGE - k
        wide = jnp.concatenate([empty, held], axis=1)
        moved = pltpu.roll(wide, size + LANES - by, 1) if by else wide
        ahead = ahead + moved[:, :LANES]
        if by:
            keep = lax.broadcasted_iota(jnp.int32, (count, size), 1) < size - by
            d_in = d_in + jnp.where(keep, moved[:, LANES:], 0.0)
        else:
            d_in = d_in + held
    in_ref[0] = d_in
    back_ref[0] = jnp.where(lane >= LANES - EDGE, ahead, 0.0)
    total_grad[0:count, :] += grads
    grad_ref[...] = total_grad[...].T[0:8]


def pack_kernel(conv_ref, key_ref, head_ref, skip_ref, out_ref):
    wide = conv_ref.shape[1]
    taps = CONV_K + 1
    out_ref[0:taps, :wide] = conv_ref[0:taps]
    out_ref[0:taps, wide:] = key_ref[0:taps]
    left = left_half((1, LANES))
    lane = lax.broadcasted_iota(jnp.int32, (1, LANES), 1)
    skips = jnp.zeros((1, LANES), f32)
    for p in range(wide // LANES):
        both = skip_ref[0:1, lanes(p)]
        first = jnp.sum(jnp.where(left, both, 0.0), axis=1, keepdims=True)
        second = jnp.sum(both, axis=1, keepdims=True) - first
        skips = jnp.where(lane == 2 * p, first, jnp.where(lane == 2 * p + 1, second, skips))
    heads = jnp.concatenate([head_ref[...], jnp.zeros((LANES - 8, LANES), f32)], axis=0).T
    out_ref[taps : taps + 2, :LANES] = heads[0:2]
    out_ref[taps + 2 : 8, :LANES] = skips
    out_ref[taps:8, LANES:] = jnp.zeros((8 - taps, wide), f32)


def unpack_kernel(place_ref, sums_ref, conv_ref, head_ref, total):
    s, h = place_ref[0], place_ref[1]
    heads = sums_ref.shape[0]
    wide = sums_ref.shape[2] - LANES
    for i in range(heads):
        total[i] = sums_ref[i, 0:8].astype(f32) + sums_ref[i, 8:16].astype(f32)
    linear = s * heads + h
    lane = lax.broadcasted_iota(jnp.int32, (8, LANES), 1)
    runs = wide // LANES
    per = 2 * STATE // heads

    def run(r):
        at = pl.multiple_of(((r // heads) & (runs - 1)) * LANES, LANES)
        vals = total[r & (heads - 1), :, pl.ds(at, LANES)]
        keys = jnp.zeros((8, LANES), f32)
        first = jnp.clip(r - runs * heads, 0, 2 * STATE // LANES - 1) * (LANES // per)
        for q in range(LANES // per):
            piece = jnp.where(lane < per, total[first + q, :, wide:], 0.0)
            keys = keys + (pltpu.roll(piece, per * q, 1) if q else piece)
        return jnp.where(r < runs * heads, vals, keys)

    begins = linear + linear // 16
    both = jnp.concatenate([run(begins), run(begins + 1)], axis=1)
    shift = (2 * LANES - (linear & 15) * 8) & (2 * LANES - 1)
    conv_ref[...] = pltpu.roll(both, shift, 1)
    out = jnp.zeros((8, LANES), f32)
    for j in range(heads // 2):
        mine = total[(h & 1) * (heads // 2) + j, :, 0:LANES]
        moved = pltpu.roll(mine, (2 * j + LANES - 2 * (h // 2)) & (LANES - 1), 1)
        out = jnp.where(lane // 2 == j, moved, out)
    head_ref[...] = out


def key_join_kernel(in_ref, back_ref, step_ref, key_ref, small_ref):
    x = in_ref[0]
    count, size = x.shape
    key = jnp.concatenate([x[:, : size - LANES], x[:, size - LANES :] + back_ref[0]], axis=1)
    key_ref[0] = key.astype(bf16)
    rows = [jnp.zeros((8, size), f32), key, jnp.zeros((LANES - 8 - count, size), f32)]
    cols = jnp.concatenate(rows, axis=0).T
    small_ref[0] = (cols + step_ref[0].astype(f32)).astype(bf16)


def chained(refs, at):
    total, reach = 0.0, 1.0
    for ref in refs:
        total = total + reach * ref[0, :STATE, at].astype(f32)
        reach = reach * ref[0, STATE : STATE + 1, at].astype(f32)
    return total


def prep_kernel(
    m, step_ref, seg_ref, par_ref, val_ref, key_ref, cols_ref, rows_ref, ktok_ref, start_ref, pre_ref, out_ref, state, reach
):
    @pl.when(pl.program_id(0) == 0)
    def _():
        state[...] = jnp.zeros(state.shape, f32)
        reach[...] = jnp.ones(reach.shape, f32)

    raw = step_ref[0].astype(f32)[0:8] + par_ref[:, 0:1]
    small = jnp.exp(-jnp.abs(raw))
    one = 1.0 + small
    step = jnp.maximum(raw, 0.0) + jnp.where(
        one == 1.0, small, jnp.log(one) * (small / jnp.where(one == 1.0, 1.0, one - 1.0))
    )
    sig = jnp.where(raw >= 0.0, 1.0, small) / one
    log = running_sum(step * par_ref[:, 1:2])
    size = log.shape[1]
    segs = seg_ref[0]
    seg, prev = segs[0:1], segs[1:2]
    carry = jnp.where(seg == prev, jnp.exp(log), 0.0)
    to_end = jnp.where(
        seg == seg[:, size - 1 :], jnp.exp(jnp.minimum(log[:, size - 1 :] - log, 0.0)), 0.0
    )
    rows_ref[0] = jnp.concatenate([log, step, sig, segs], axis=0)
    stack = jnp.concatenate(
        [log, step, carry, to_end, segs, jnp.zeros((LANES - 40, size), f32)], axis=0
    )
    cols = stack.T
    cols_ref[0] = cols
    keys = key_ref[0]
    ktok_ref[0] = keys.astype(f32).T.astype(bf16)
    start_ref[0, 0] = state[...]
    pre_ref[0, 0] = reach[...]
    weight = cols[:, TO_END : TO_END + 8] * cols[:, STEP : STEP + 8]
    for p in range(pairs_in(val_ref)):
        ending = (val_ref[0, :, lanes(p)].astype(f32) * pair_of(weight, 0, p)).astype(bf16)
        decay = pair_of(cols[size - 1 :], CARRY, p)
        state[:, lanes(p)] = decay * state[:, lanes(p)] + nn(keys[:STATE], ending)
        reach[:, lanes(p)] = decay * reach[:, lanes(p)]
    out_ref[0] = jnp.concatenate([state[...], reach[...], reach[...]], axis=0).astype(bf16)


def same_mask(cols, rows):
    size = cols.shape[0]
    at = lax.broadcasted_iota(jnp.int32, (size, size), 0)
    of = lax.broadcasted_iota(jnp.int32, (size, size), 1)
    return (cols[:, SEG : SEG + 1] == rows[ROWS_SEG : ROWS_SEG + 1]) & (at >= of)


def within(cols, rows, j):
    return jnp.exp(jnp.minimum(cols[:, j : j + 1] - rows[j : j + 1], 0.0))


def step_lanes(place_ref, p, swapped):
    return pl.ds(pl.multiple_of((place_ref[0] ^ p) * LANES, LANES), LANES) if swapped else lanes(p)


def fwd_kernel(
    swapped, near, m, place_ref, val_ref, ktok_ref, cols_ref, rows_ref, start_ref, pre_ref, gate_ref, dy_ref, chan_ref, *refs
):
    in_refs, (mix_ref, sum_ref, in_ref) = refs[:near], refs[near:]

    @pl.when(pl.program_id(0) == 0)
    def _():
        for p in range(pairs_in(val_ref)):
            in_ref[:, lanes(p)] = chained(in_refs, lanes(p))

    cols, rows = cols_ref[0], rows_ref[0]
    rkey = ktok_ref[0, :, STATE:]
    scores = jnp.where(same_mask(cols, rows), nt(rkey, ktok_ref[0, :, :STATE]), 0.0)
    squares, products = 0.0, 0.0
    left = left_half((cols.shape[0], LANES))
    for p in range(pairs_in(val_ref)):
        at = lanes(p)
        vals = val_ref[0, :, at].astype(f32)
        stepped = vals * pair_of(cols, STEP, p)
        high, low = split(start_ref[0, 0, :, at] + pre_ref[0, 0, 0:1, at] * in_ref[:, at])
        mixed = pair_of(cols, CARRY, p) * (nn(rkey, high) + nn(rkey, low))
        weights = [(scores * within(cols, rows, 2 * p + half)).astype(bf16) for half in range(2)]
        held = [jnp.where(keep, stepped, 0.0).astype(bf16) for keep in (left, ~left)]
        mixed = mixed + nn(jnp.concatenate(weights, axis=1), jnp.concatenate(held, axis=0))
        mixed = (mixed + chan_ref[0:1, at] * vals).astype(bf16)
        mix_ref[0, :, at] = mixed
        gate = gate_ref[0, :, at]
        gated = mixed.astype(f32) * (gate / (1.0 + jnp.exp(-gate)))
        squares = squares + gated * gated
        products = products + gated * (dy_ref[0, :, step_lanes(place_ref, p, swapped)] * chan_ref[1:2, at])
    lane = lax.broadcasted_iota(jnp.int32, squares.shape, 1)
    sums = jnp.where(
        lane == 0,
        jnp.sum(squares, axis=1, keepdims=True),
        jnp.where(lane == 1, jnp.sum(products, axis=1, keepdims=True), 0.0),
    )
    sum_ref[0] = sums.T[0:8]


def norm_kernel(
    swapped, m, place_ref, mix_ref, gate_ref, dy_ref, sum_ref, cols_ref, key_ref, pre_ref, chan_ref, reach_ref,
    yn_ref, dmix_ref, dgate_ref, adj_ref, out_ref, adj
):
    @pl.when(pl.program_id(0) == 0)
    def _():
        adj[...] = jnp.zeros(adj.shape, f32)

    cols = cols_ref[0]
    size = cols.shape[0]
    rows = sum_ref[0]
    scale_row = lax.rsqrt(rows[0:1] * (1.0 / D_INNER) + EPS)
    pull_row = scale_row * scale_row * rows[1:2] * (1.0 / D_INNER)
    both = jnp.concatenate([scale_row, pull_row, jnp.zeros((LANES - 2, size), f32)], axis=0).T
    scale, pull = both[:, 0:1], both[:, 1:2]
    for p in range(pairs_in(mix_ref)):
        at = lanes(p)
        mixer = mix_ref[0, :, at].astype(f32)
        gate = gate_ref[0, :, at]
        sig = 1.0 / (1.0 + jnp.exp(-gate))
        act = gate * sig
        slope = sig * (1.0 + gate * (1.0 - sig))
        gated = mixer * act
        unit = gated * scale
        gain = chan_ref[1:2, at]
        step_at = step_lanes(place_ref, p, swapped)
        yn_ref[0, :, step_at] = (unit * gain).astype(bf16)
        d_y = dy_ref[0, :, step_at]
        d_gated = scale * (d_y * gain - gated * pull)
        d_mix = (d_gated * act).astype(bf16)
        dmix_ref[0, :, at] = d_mix
        dgate_ref[0, :, at] = (d_gated * mixer * slope).astype(bf16)
        carried = (d_mix.astype(f32) * pair_of(cols, CARRY, p)).astype(bf16)
        block = nn(key_ref[0, STATE:], carried)
        adj_ref[0, 0, :, at] = block
        adj[:, at] = pair_of(cols[size - 1 :], CARRY, p) * adj[:, at] + block
    reach = reach_ref[0]
    out_ref[0] = jnp.concatenate([adj[...].astype(bf16), reach], axis=0)


def bwd_kernel(
    near, m, val_ref, key_ref, ktok_ref, cols_ref, rows_ref, start_ref, pre_ref, dmix_ref, adj_ref, chan_ref, par_ref, *refs
):
    in_refs, adjin_refs, refs = refs[:near], refs[near : 2 * near], refs[2 * near :]
    dval_ref, dkey_ref, dstep_ref, head_ref, skip_ref, adj, in_ref = refs

    @pl.when(pl.program_id(0) == 0)
    def _():
        if m == 0:
            head_ref[...] = jnp.zeros_like(head_ref)
            skip_ref[...] = jnp.zeros_like(skip_ref)
        for p in range(pairs_in(val_ref)):
            in_ref[:, lanes(p)] = chained(in_refs, lanes(p))
            adj[:, lanes(p)] = chained(adjin_refs, lanes(p))

    cols, rows = cols_ref[0], rows_ref[0]
    size = cols.shape[0]
    wkey, rkey = ktok_ref[0, :, :STATE], ktok_ref[0, :, STATE:]
    same = same_mask(cols, rows)
    scores = jnp.where(same, nt(rkey, wkey), 0.0)
    both_scores = jnp.concatenate([scores, scores], axis=0)
    left = left_half((size, LANES))
    lane = lax.broadcasted_iota(jnp.int32, (size, LANES), 1)
    lane_row = lax.broadcasted_iota(jnp.int32, (1, LANES), 1)
    d_scores = jnp.zeros((size, size), f32)
    d_write = jnp.zeros((STATE, size), f32)
    d_read = jnp.zeros((STATE, size), f32)
    by_row = jnp.zeros((size, LANES), f32)
    last = jnp.zeros((1, LANES), f32)
    by_col = []

    def put(total, p, half, values, offset=0):
        where = lane if values.shape[0] == size else lane_row
        return jnp.where(where == offset + 2 * p + half, values, total)

    def halves_of(x):
        first = jnp.sum(jnp.where(left[: x.shape[0]], x, 0.0), axis=1, keepdims=True)
        return first, jnp.sum(x, axis=1, keepdims=True) - first

    for p in range(pairs_in(val_ref)):
        at = lanes(p)
        vals = val_ref[0, :, at].astype(f32)
        d_mix = dmix_ref[0, :, at]
        d_mix_f = d_mix.astype(f32)
        step = pair_of(cols, STEP, p)
        stepped_f = vals * step
        stepped = stepped_f.astype(bf16)
        carry = pair_of(cols, CARRY, p)
        state = start_ref[0, 0, :, at] + pre_ref[0, 0, 0:1, at] * in_ref[:, at]
        high, low = split(state)
        end = adj[:, at]
        end_low = end.astype(bf16)
        ending_f = stepped_f * pair_of(cols, TO_END, p)
        ending = ending_f.astype(bf16)
        carried_d = (d_mix_f * carry).astype(bf16)
        back = nn(wkey, end_low)
        d_stepped = pair_of(cols, TO_END, p) * back
        from_end = ending_f * back
        through = d_mix_f * carry * (nn(rkey, high) + nn(rkey, low)) - from_end
        decay = pair_of(cols[size - 1 :], CARRY, p)
        final = jnp.sum(from_end, axis=0, keepdims=True) + decay * jnp.sum(
            end * state, axis=0, keepdims=True
        )
        final = halves_of(final)
        through = halves_of(through)
        held = [jnp.where(keep, d_mix_f, 0.0).astype(bf16) for keep in (left, ~left)]
        held = jnp.concatenate(held, axis=0)
        near = jnp.concatenate([within(cols, rows, 2 * p), within(cols, rows, 2 * p + 1)], axis=0)
        d_near = nt(held, stepped) * near
        d_scores = d_scores + (d_near[:size] + d_near[size:])
        pairs = d_near * both_scores
        row_sums = jnp.sum(pairs, axis=1, keepdims=True)
        for half in range(2):
            mine = slice(half * size, (half + 1) * size)
            by_row = put(by_row, p, half, row_sums[mine] + through[half])
            by_col.append(jnp.sum(pairs[mine], axis=0, keepdims=True))
            last = put(last, p, half, final[half])
        d_stepped = d_stepped + tn((both_scores * near).astype(bf16), held)
        d_vals = step * d_stepped + chan_ref[0:1, at] * d_mix_f
        dval_ref[0, :, at] = d_vals.astype(bf16)
        skip_ref[0:1, at] += jnp.sum(d_mix_f * vals, axis=0, keepdims=True)
        d_step = halves_of(vals * d_stepped)
        for half in range(2):
            by_row = put(by_row, p, half, d_step[half], 8)
        d_write = d_write + nt(end_low, ending)
        d_read = d_read + nt(high, carried_d) + nt(low, carried_d)
        adj[:, at] = decay * end + adj_ref[0, 0, :, at]
    d_scores = jnp.where(same, d_scores, 0.0).astype(bf16)
    d_write = d_write + nn(key_ref[0, STATE:], d_scores)
    d_read = d_read + nt(key_ref[0, :STATE], d_scores)
    d_keys = jnp.concatenate([d_write, d_read], axis=0).astype(bf16)
    each = dkey_ref.shape[2]
    for h in range(dkey_ref.shape[0]):
        dkey_ref[h, m] = d_keys[h * each : (h + 1) * each]
    while len(by_col) < 8:
        by_col.append(jnp.zeros((1, size), f32))
    turned = by_row.T
    last = jnp.broadcast_to(last, (LANES, LANES)).T[0:8, 0:1]
    d_log = turned[0:8] - jnp.concatenate(by_col, axis=0)
    rate = par_ref[:, 1:2]
    first = rows[ROWS_SEG + 2 : ROWS_SEG + 3]
    d_decay = (running_sum(d_log, True) + last) * (1.0 - first)
    d_raw = (turned[8:16] + d_decay * rate) * rows[SIG : SIG + 8]
    dstep_ref[0] = jnp.concatenate([d_raw, jnp.zeros((LANES - 8, size), f32)], axis=0).T.astype(bf16)
    head_lane = lax.broadcasted_iota(jnp.int32, (8, LANES), 1)
    head_ref[...] += jnp.where(
        head_lane == 0,
        jnp.sum(d_decay * rows[STEP : STEP + 8], axis=1, keepdims=True) * rate,
        jnp.where(head_lane == 1, jnp.sum(d_raw, axis=1, keepdims=True), 0.0),
    )


def shifted(x, rim, by):
    if by == 0:
        return x
    head = jnp.concatenate([rim, x[:8]], axis=0)[8 - by : 16 - by]
    return jnp.concatenate([head, pltpu.roll(x, by, 0)[8:]], axis=0)


def conv_kernel(val_ref, rim_ref, valid_ref, par_ref, out_ref):
    shape = (val_ref.shape[1], LANES)
    valid = [jnp.broadcast_to(valid_ref[0, :, k : k + 1], shape) for k in range(CONV_K)]
    for p in range(pairs_in(out_ref)):
        at = lanes(p)
        x = val_ref[0, :, at].astype(f32)
        rim = rim_ref[0, :, at].astype(f32)[8:16]
        total = par_ref[CONV_K : CONV_K + 1, at]
        for k in range(CONV_K):
            total = total + par_ref[k : k + 1, at] * shifted(x, rim, EDGE - k) * valid[k]
        out_ref[0, :, at] = (total / (1.0 + jnp.exp(-total))).astype(bf16)


def conv_back_kernel(d_ref, val_ref, rim_ref, valid_ref, par_ref, in_ref, back_ref, grad_ref):
    @pl.when(pl.program_id(0) == 0)
    def _():
        grad_ref[...] = jnp.zeros_like(grad_ref)

    size = val_ref.shape[1]
    row = lax.broadcasted_iota(jnp.int32, (size, LANES), 0)
    zeros = jnp.zeros((8, LANES), f32)
    valid = [jnp.broadcast_to(valid_ref[0, :, k : k + 1], (size, LANES)) for k in range(CONV_K)]
    for p in range(pairs_in(d_ref)):
        at = lanes(p)
        x = val_ref[0, :, at].astype(f32)
        rim = rim_ref[0, :, at].astype(f32)[8:16]
        total = par_ref[CONV_K : CONV_K + 1, at]
        seen = []
        for k in range(CONV_K):
            seen.append(shifted(x, rim, EDGE - k) * valid[k])
            total = total + par_ref[k : k + 1, at] * seen[k]
        sig = 1.0 / (1.0 + jnp.exp(-total))
        d_total = d_ref[0, :, at].astype(f32) * (sig * (1.0 + total * (1.0 - sig)))
        grad_ref[CONV_K : CONV_K + 1, at] += jnp.sum(d_total, axis=0, keepdims=True)
        d_in, back = 0.0, 0.0
        for k in range(CONV_K):
            grad_ref[k : k + 1, at] += jnp.sum(d_total * seen[k], axis=0, keepdims=True)
            held = d_total * (par_ref[k : k + 1, at] * valid[k])
            by = EDGE - k
            if by:
                d_in = d_in + jnp.where(row < size - by, pltpu.roll(held, size - by, 0), 0.0)
                back = back + jnp.concatenate([zeros, held[:8]], axis=0)[by : by + 8]
            else:
                d_in = d_in + held
        in_ref[0, :, at] = d_in.astype(bf16)
        back_ref[0, :, at] = back


def proj_kernel(place_ref, x_ref, gain_ref, *refs):
    parts, (low_ref, out_ref, small_ref, weight_ref) = refs[:-4], refs[-4:]
    wide = parts[0].shape[1] - LANES
    size = parts[0].shape[0]

    @pl.when((pl.program_id(0) == 0) & (pl.program_id(1) == 0))
    def _():
        for k, part in enumerate(parts):
            turned = part[:, wide:].astype(f32).T
            at = slice(8, 8 + weight_ref.shape[0])
            weight_ref[:, k * size : (k + 1) * size] = turned[at].astype(bf16)

    x = x_ref[0].astype(f32)
    inv = lax.rsqrt(jnp.mean(x * x, axis=1, keepdims=True) + EPS)
    total = 0.0
    for k, part in enumerate(parts):
        at = pl.ds(pl.multiple_of((place_ref[0] ^ k) * size, LANES), size)
        low = (x_ref[0, :, at].astype(f32) * inv * gain_ref[k : k + 1]).astype(bf16)
        low_ref[0, :, k * size : (k + 1) * size] = low
        total = total + nn(low, part[...])
    out_ref[0] = total.astype(bf16)
    small_ref[0] = total[:, wide:].T.astype(bf16)


def gather_runs(parts, whole):
    run = parts[0].shape[0]

    @pl.when((pl.program_id(0) == 0) & (pl.program_id(1) == 0))
    def _():
        for r, part in enumerate(parts):
            whole[r * run : (r + 1) * run] = part[...]


def fill_kernel(steps, x_ref, grad_ref, *refs):
    gates, outs, (gate_ref, dy_ref, whole) = refs[:steps], refs[steps:-3], refs[-3:]
    gather_runs(outs, whole)
    size = gates[0].shape[0]
    total = 0.0
    for k, part in enumerate(gates):
        total = total + nn(x_ref[0, :, k * size : (k + 1) * size], part[...])
    gate_ref[0] = total
    dy_ref[0] = nt(grad_ref[0], whole[...])


def out_kernel(y_ref, *refs):
    parts, (out_ref, whole) = refs[:-2], refs[-2:]
    gather_runs(parts, whole)
    width = out_ref.shape[2]
    size = min(width, 512)
    for n in range(width // size):
        at = slice(n * size, (n + 1) * size)
        out_ref[0, :, at] = nn(y_ref[0], whole[:, at]).astype(bf16)


def rows_kernel(place_ref, a_ref, b_ref, out_ref):
    total = 0.0
    for m in range(a_ref.shape[0]):
        total = total + tn(a_ref[m], b_ref[m])
    run = a_ref.shape[2]
    at = pl.multiple_of((place_ref[0] ^ pl.program_id(0)) * run, run)
    out_ref[pl.ds(at, run), :] = total.astype(bf16)


def weight_kernel(parts, has_below, a_ref, *refs):
    below = None
    if has_below:
        below, refs = refs[parts], refs[:parts] + refs[parts + 1 :]
    outs, b_ref = refs[parts:], refs[0]
    if parts > 1:
        outs, b_ref = refs[parts:-1], refs[-1]

        @pl.when(pl.program_id(0) == 0)
        def _():
            at = 0
            for ref in refs[:parts]:
                b_ref[:, :, at : at + ref.shape[2]] = ref[...]
                at += ref.shape[2]

    total = 0.0
    for m in range(a_ref.shape[0]):
        total = total + tn(a_ref[m], b_ref[m])
    total = total.astype(bf16)
    run = total.shape[0]
    for k, out in enumerate(outs):

        @pl.when(pl.program_id(0) == k)
        def _():
            out[0:run] = total
            if below is not None:
                out[run:] = below[...]


def normed_back_kernel(steps, gate_ref, val_ref, small_ref, *refs):
    gates, firsts, out_ref = refs[:steps], refs[steps:-1], refs[-1]
    gate, val, small = gate_ref[0], val_ref[0], small_ref[0]
    wide = val.shape[1]
    size = gates[0].shape[0]
    for k in range(steps):
        first = firsts[k]
        total = nt(gate, gates[k][...]) + nt(val, first[:, :wide]) + nt(small, first[:, wide:])
        out_ref[0, :, k * size : (k + 1) * size] = total.astype(bf16)


def grad_in_kernel(place_ref, sum_ref, key_ref, row_ref, x_ref, gain_ref, grad_ref, out_ref, d_unit):
    steps = gain_ref.shape[0]
    part = x_ref.shape[2] // steps
    x = x_ref[0].astype(f32)
    inv = lax.rsqrt(jnp.mean(x * x, axis=1, keepdims=True) + EPS)
    keys = jnp.concatenate([key_ref[h, 0] for h in range(key_ref.shape[0])], axis=0)
    total = 0.0
    for k in range(steps):
        at = slice(k * part, (k + 1) * part)
        of = pl.ds(pl.multiple_of((place_ref[0] ^ k) * part, LANES), part)
        d_here = sum_ref[0, :, at].astype(f32) + tn(keys, row_ref[:, at])
        d_here = d_here * gain_ref[k : k + 1]
        d_unit[:, of] = d_here
        total = total + jnp.sum(d_here * x_ref[0, :, of].astype(f32), axis=1, keepdims=True)
    shared = inv * inv * total * (1.0 / x.shape[1])
    out_ref[0] = (grad_ref[0].astype(f32) + inv * (d_unit[...] - x * shared)).astype(bf16)


def weight_grad_kernel(gate_ref, first_ref, w_ref, out_ref, sum_ref):
    heads, _, wide = gate_ref.shape
    rows = w_ref.shape[0]
    runs = wide // LANES
    total = jnp.zeros((rows, LANES), f32)

    def place(value, at):
        out_ref[:, at : at + value.shape[1]] = value
        return jnp.sum(value * w_ref[:, at : at + value.shape[1]].astype(f32), axis=1, keepdims=True)

    for ref, base in ((gate_ref, 0), (first_ref, D_INNER)):
        for h in range(heads):
            for b in range(runs):
                value = ref[h, :rows, lanes(b)].astype(f32)
                at = base + (b * heads + h) * LANES
                out_ref[:, at : at + LANES] = value
                total = total + value * w_ref[:, at : at + LANES].astype(f32)
    small = [first_ref[h, :rows, wide:].astype(f32) for h in range(heads)]
    per = 2 * STATE // heads
    keys = jnp.concatenate([x[:, 8 : 8 + per] for x in small], axis=1)
    sums = jnp.sum(total, axis=1, keepdims=True) + place(keys, 2 * D_INNER)
    steps = jnp.concatenate([x[:, :8] for x in small], axis=1).astype(bf16)
    per = 8 // runs
    of = lax.broadcasted_iota(jnp.int32, (HEADS, HEADS), 0)
    to = lax.broadcasted_iota(jnp.int32, (HEADS, HEADS), 1)
    source = (to // per % heads) * 8 + (to // (per * heads)) * per + to % per
    steps = nn(steps, (of == source).astype(f32).astype(bf16))
    sums = sums + place(steps, 2 * D_INNER + 2 * STATE)
    sum_ref[...] = jnp.broadcast_to(sums, (rows, LANES))


SMALL = (
    "conv_kernel",
    "conv_back_kernel",
    "key_conv_kernel",
    "key_back_kernel",
    "key_join_kernel",
    "glue_kernel",
    "mask_kernel",
    "pack_kernel",
    "unpack_kernel",
    "out_kernel",
    "weight_kernel",
    "rows_kernel",
    "grad_in_kernel",
    "weight_grad_kernel",
)
ABOUT_US = {
    "proj_kernel": 0,
    "fill_kernel": 9,
    "out_kernel": 0,
    "weight_kernel": 40,
    "rows_kernel": 0,
    "normed_back_kernel": 10,
    "bwd_kernel": 80,
    "fwd_kernel": 6,
    "norm_kernel": 5,
    "prep_kernel": 6,
    "conv_back_kernel": 10,
    "conv_kernel": 3,
    "grad_in_kernel": 30,
    "weight_grad_kernel": 10,
    "mask_kernel": 0,
    "pack_kernel": 0,
    "unpack_kernel": 0,
    "glue_kernel": 0,
    "key_conv_kernel": 1,
    "key_back_kernel": 5,
    "key_join_kernel": 60,
}


def kernel_call(kernel, grid, ins, outs, scratch=(), wait=(), us=None):
    name = getattr(kernel, "func", kernel).__name__
    us = ABOUT_US[name] if us is None else us
    specs = [
        pl.BlockSpec(memory_space=pltpu.SMEM) if block is None else pl.BlockSpec(block, index)
        for block, index in ins
    ]
    wait = jax.tree.leaves(wait)
    count = len(specs)
    specs = specs + [pl.BlockSpec(memory_space=pl.ANY)] * len(wait)

    def run(*refs):
        kernel(*refs[:count], *refs[count + len(wait) :])

    call = pl.pallas_call(
        run,
        grid=grid,
        in_specs=specs,
        out_specs=[pl.BlockSpec(block, index) for _, _, block, index in outs],
        out_shape=[jax.ShapeDtypeStruct(shape, dtype) for shape, dtype, _, _ in outs],
        scratch_shapes=list(scratch),
        compiler_params=pltpu.CompilerParams(
            vmem_limit_bytes=(32 if name in SMALL else 58) * 2**20, dimension_semantics=("arbitrary",) * len(grid)
        ),
        name=name,
        cost_estimate=pl.CostEstimate(flops=us * 2**30, bytes_accessed=us * 3 * 2**20, transcendentals=0),
    )
    return lambda *args: call(*args, *wait)


def fixed(m, c):
    return (0, 0)


def micro_call(kernel, micro, blocks, ins, outs, scratch=(), wait=()):
    shared = [block is None or index is fixed for block, index in ins]
    shared += [index is fixed or block[0] != 1 for _, _, block, index in outs]

    def whole(block, index):
        if block is None:
            return None, None
        if index is fixed:
            return block, lambda c: (0, 0)
        if block[0] != 1:
            return (block[0], micro) + block[2:], lambda c: index(0, c)
        return (micro,) + block[1:], lambda c: index(0, c)

    def run(*refs):
        for m in range(micro):
            views = [ref if one else ref.at[m : m + 1] for ref, one in zip(refs, shared)]
            kernel(m, *views, *[ref.at[m] for ref in refs[len(shared) :]])

    run.__name__ = getattr(kernel, "func", kernel).__name__
    return kernel_call(
        run,
        (blocks,),
        [whole(*spec) for spec in ins],
        [(shape, dtype) + whole(block, index) for shape, dtype, block, index in outs],
        [pltpu.VMEM((micro,) + shape, f32) for shape in scratch],
        wait,
    )


def body(
    hidden_in,
    seq_starts,
    norm_gain,
    in_weight,
    conv_weight,
    conv_bias,
    decay_log,
    dt_bias,
    skip_gain,
    gate_gain,
    out_weight,
    out_grad,
):
    seqs, heads = lax.axis_size("seq"), lax.axis_size("head")
    s_i, h_i = lax.axis_index("seq"), lax.axis_index("head")
    micro, tok, width = hidden_in.shape
    rows = in_weight.shape[0]
    shard = tok * heads
    runs = seqs if HEADS % (seqs * heads) == 0 else 1
    run_ch = D_INNER // (runs * heads)
    run_heads = HEADS // (runs * heads)
    chans, n_heads = runs * run_ch, runs * run_heads
    key_ch = 2 * STATE // heads
    wide = max(chans, LANES)

    def widen(x, axis=-1):
        pads = [(0, 0)] * x.ndim
        pads[axis] = (0, wide - chans)
        return jnp.pad(x, pads) if wide > chans else x

    conv_share, gate_share, head_share = conv_bias.shape[0], gate_gain.shape[0], decay_log.shape[0]

    def mine(x, size):
        lead = x.shape[:-1]
        x = x.reshape(lead + (runs, heads, size))
        x = lax.dynamic_index_in_dim(x, h_i, len(lead) + 1, False)
        return x.reshape(lead + (runs * size,))

    place = s_i[None].astype(jnp.int32)
    scalar = (None, None)
    forward = [(i, i + 1) for i in range(seqs - 1)]
    backward = [(i + 1, i) for i in range(seqs - 1)]
    swapped = runs == seqs
    if swapped and run_ch != LANES:
        raise ValueError("run width")

    def columns(x, size):
        x = x.reshape(rows, runs, heads, size)
        return jnp.transpose(x, (2, 0, 1, 3)).reshape(heads, rows, runs * size)

    def fill(x, axis, size):
        return jnp.pad(x, [(0, size - x.shape[axis] if i == axis else 0) for i in range(x.ndim)])

    val_p = fill(columns(in_weight[:, D_INNER : 2 * D_INNER], run_ch), 2, wide)
    step_p = fill(columns(in_weight[:, 2 * D_INNER + 2 * STATE :], run_heads), 2, 8)
    key_p = in_weight[:, 2 * D_INNER : 2 * D_INNER + 2 * STATE].reshape(rows, heads, key_ch)
    key_p = fill(jnp.swapaxes(key_p, 0, 1), 2, LANES - 8)
    gate_p = fill(columns(in_weight[:, :D_INNER], run_ch), 2, wide)
    first = head_swap(jnp.concatenate([val_p, step_p, key_p], axis=2)).reshape(heads * rows, -1)
    inputs = lax.all_gather(hidden_in, "head", axis=1, tiled=True)

    blocks = shard // SCAN_BLOCK
    by_micro = lambda *shape: ((1,) + shape, lambda m: (m,) + (0,) * len(shape))
    seg_rows, valid, valid_cols = kernel_call(
        mask_kernel,
        (micro,),
        [scalar, scalar],
        [
            ((micro, 8, shard), f32) + by_micro(8, shard),
            ((micro, 8, shard), f32) + by_micro(8, shard),
            ((micro, shard, LANES), f32) + by_micro(shard, LANES),
        ],
    )(place, seq_starts)


    every = seqs * heads
    linear = s_i * heads + h_i
    halo = lax.ppermute(hidden_in[:, tok - EDGE :], BOTH, [(i, i + 1) for i in range(every - 1)])
    taps = jnp.concatenate([conv_weight, conv_bias[None]], axis=0)
    heads_par = jnp.concatenate(three_parts(jnp.concatenate([decay_log, dt_bias, skip_gain])))
    key_rows_n = -(-key_ch // 8) * 8
    if swapped:
        window = jnp.zeros((CONV_K + 1, 2 * LANES), bf16)
        window = lax.dynamic_update_slice_in_dim(window, taps, (linear & 15) * 8, 1)
        sent = [fill(norm_gain, 0, LANES), gate_gain, fill(heads_par, 0, LANES), window.reshape(-1)]
    else:
        sent = [norm_gain, taps.reshape(-1), gate_gain, heads_par]
        sent.append(jnp.zeros((-sum(x.shape[0] for x in sent) % LANES,), bf16))
    sent = jnp.concatenate(sent)
    size = sent.shape[0]
    if swapped:
        sent = seq_gather(sent)
        w_out = seq_gather(after(out_weight, *sent))
        sent = after(jnp.concatenate(sent + [halo.reshape(-1)])[None], first, w_out)
        chips = heads // 2
        turns = [[(i, (i + 2 * k) % heads) for i in range(heads)] for k in range(1, chips)]
        sent = jnp.concatenate([sent] + [lax.ppermute(sent, "head", pairs) for pairs in turns], axis=0)
        other = lax.ppermute(sent, "head", [(i, i ^ 1) for i in range(heads)])
        sent = jnp.concatenate([sent, other], axis=0)
        first_row = (h_i >> 1) + (h_i & 1) * chips
    else:
        sent = lax.all_gather(sent, "seq").reshape(-1)
        sent = lax.all_gather(jnp.concatenate([sent, halo.reshape(-1)]), "head")
        first_row = 0
    halo = lax.dynamic_index_in_dim(sent, first_row, 0, False)[seqs * size :].reshape(halo.shape)
    halo = jnp.pad(halo, ((0, 0), (LANES - EDGE, 0), (0, 0)))
    first = seq_gather(first)
    if swapped:
        all_of = lambda shape: (shape, lambda m: (0,) * len(shape))
        outs = [(seqs, width // seqs), (8, wide), (8, wide), (key_ch, LANES), (8, LANES)]
        gain_steps, chan, conv_par, key_par, params = kernel_call(
            glue_kernel,
            (1,),
            [scalar, all_of((heads, seqs * size))],
            [(shape, f32) + all_of(shape) for shape in outs],
            [pltpu.VMEM((LANES, LANES), f32)],
            (first, seg_rows, gate_p, halo),
        )(jnp.stack([s_i, h_i]), sent)
    else:
        sent = jnp.swapaxes(sent[:, : seqs * size].reshape(heads, seqs, -1), 0, 1).reshape(every, -1)
        at = 0

        def take(count):
            nonlocal at
            at += count
            return sent[:, at - count : at]

        gain_steps = from_steps(take(rows).reshape(seqs, heads * rows), s_i).astype(f32)
        conv_p = take((CONV_K + 1) * conv_share).reshape(every, CONV_K + 1, conv_share)
        conv_p = jnp.transpose(conv_p, (1, 0, 2)).reshape(CONV_K + 1, CONV_CH).astype(f32)
        gate_g = mine(take(gate_share).reshape(D_INNER), run_ch).astype(f32)
        par = jnp.sum(take(9 * head_share)[:heads].astype(f32).reshape(heads, 3, 3, head_share), axis=1)
        par = mine(jnp.swapaxes(par, 0, 1).reshape(3, HEADS), run_heads)
        params = fill(fill(jnp.stack([par[1], -jnp.exp(par[0])], axis=1), 0, 8), 1, LANES)
        chan = fill(jnp.stack([widen(jnp.repeat(par[2], HEADDIM)), widen(gate_g)]), 0, 8)
        conv_par = fill(widen(mine(conv_p[:, :D_INNER], run_ch)), 0, 8)
        key_par = lax.dynamic_slice_in_dim(conv_p[:, D_INNER:], h_i * key_ch, key_ch, 1).T
        key_par = fill(fill(key_par, 0, key_rows_n), 1, LANES)

    tile = lambda m, c: (m, c, 0)
    second = head_swap(after(gate_p, first[0]))

    def project(x, size, wait=()):
        many = x.shape[1]
        return kernel_call(
            proj_kernel,
            (micro, many // size),
            [scalar, ((1, size, width), tile), (gain_steps.shape, fixed)] + [(first[0].shape, fixed)] * seqs,
            [
                ((micro, many, width), bf16, (1, size, width), tile),
                ((micro, many, wide + LANES), bf16, (1, size, wide + LANES), tile),
                ((micro, LANES, many), bf16, (1, LANES, size), lambda m, c: (m, 0, c)),
                ((key_ch, width), bf16, (key_ch, width), fixed),
            ],
            (),
            wait,
        )(place, x, gain_steps, *first)

    normed_low, proj, small_in, key_rows = project(inputs, min(shard, 512), (second,))
    _, proj_rim, small_rim, _ = project(halo, LANES)
    grad_rows = lax.all_gather(after(out_grad, proj), "head", axis=1, tiled=True)

    w_gate = seq_gather(second.reshape(heads * rows, wide))
    if not swapped:
        w_out = lax.all_gather(out_weight, BOTH, axis=0, tiled=True)
        w_out = [widen(lax.dynamic_slice_in_dim(w_out, h_i * chans, chans, 0), 0)]
    gate_specs = [(w_gate[0].shape, fixed)] * seqs
    out_specs = [(part.shape, fixed) for part in w_out]


    whole = ((1, shard, wide), lambda m: (m, 0, 0))
    conv_ins = [
        whole,
        ((1, 16, wide), lambda m: (m, LANES // 16 - 1, 0)),
        by_micro(shard, LANES),
        ((8, wide), lambda m: (0, 0)),
    ]
    key_ins = [
        by_micro(LANES, shard),
        by_micro(LANES, LANES),
        by_micro(8, shard),
        ((key_rows_n, LANES), lambda m: (0, 0)),
    ]
    vals = kernel_call(conv_kernel, (micro,), conv_ins, [((micro, shard, wide), bf16) + whole])(
        proj, proj_rim, valid_cols, conv_par
    )[0]
    keys = kernel_call(
        key_conv_kernel, (micro,), key_ins, [((micro, key_rows_n, shard), bf16) + by_micro(key_rows_n, shard)]
    )(small_in, small_rim, valid, key_par)[0]
    keys = keys[:, :key_ch]
    keys = lax.all_gather(keys, "head", axis=1, tiled=True)

    grid = (micro, blocks)
    size = SCAN_BLOCK
    here = lambda m, c: (m, c, 0)
    along = lambda m, c: (m, 0, c)
    state_at = lambda m, c: (m, c, 0, 0)
    micro_at = lambda m, c: (m, 0, 0)
    row8 = (1, 8, size)
    tok_c, tok_l = (1, size, wide), (1, size, LANES)
    n_state = STATE + 16
    f_state = ((1, 1, STATE, wide), state_at)
    f_pre = ((1, 1, 8, wide), state_at)
    cols, rows_t, ktok, starts, prefix, payload = micro_call(
        prep_kernel,
        micro,
        blocks,
        [((1, 16, size), along), (row8, along), ((8, LANES), fixed), (tok_c, here), ((1, 2 * STATE, size), along)],
        [
            ((micro, shard, LANES), f32, tok_l, here),
            ((micro, 32, shard), f32, (1, 32, size), along),
            ((micro, shard, 2 * STATE), bf16, (1, size, 2 * STATE), here),
            ((micro, blocks, STATE, wide), f32) + f_state,
            ((micro, blocks, 8, wide), f32) + f_pre,
            ((micro, n_state, wide), bf16, (1, n_state, wide), micro_at),
        ],
        [(STATE, wide), (8, wide)],
        w_gate,
    )(small_in, seg_rows, params, vals, keys)
    key_rows = lax.all_gather(after(key_rows, payload), "head")
    size = min(shard, 512)
    gate_in, d_ynorm = kernel_call(
        functools.partial(fill_kernel, seqs),
        (micro, shard // size),
        [((1, size, width), tile)] * 2 + gate_specs + out_specs,
        [((micro, shard, wide), f32, (1, size, wide), tile)] * 2,
        [pltpu.VMEM((wide, width), bf16)],
        (payload,),
    )(normed_low, grad_rows, *w_gate, *w_out)
    size = SCAN_BLOCK
    state_in = linked(payload, False, gate_in)
    mixer, sums = micro_call(
        functools.partial(fwd_kernel, swapped, seqs - 1),
        micro,
        blocks,
        [
            scalar,
            (tok_c, here),
            ((1, size, 2 * STATE), here),
            (tok_l, here),
            ((1, 32, size), along),
            f_state,
            f_pre,
            (tok_c, here),
            (tok_c, here),
            ((8, wide), fixed),
        ]
        + [((1, n_state, wide), micro_at)] * (seqs - 1),
        [((micro, shard, wide), bf16, tok_c, here), ((micro, 8, shard), f32, row8, along)],
        [(STATE, wide)],
    )(place, vals, ktok, cols, rows_t, starts, prefix, gate_in, d_ynorm, chan, *state_in)

    sums = fill(lax.psum(sums[:, :2], "head"), 1, 8)
    back_here = lambda m, c: (m, blocks - 1 - c, 0)
    back_along = lambda m, c: (m, 0, blocks - 1 - c)
    back_state = lambda m, c: (m, blocks - 1 - c, 0, 0)
    b_state, b_pre = (f_state[0], back_state), (f_pre[0], back_state)
    ynorm_low, d_mix, d_gate, block_adj, payload = micro_call(
        functools.partial(norm_kernel, swapped),
        micro,
        blocks,
        [
            scalar,
            (tok_c, back_here),
            (tok_c, back_here),
            (tok_c, back_here),
            (row8, back_along),
            (tok_l, back_here),
            ((1, 2 * STATE, size), back_along),
            b_pre,
            ((8, wide), fixed),
            ((1, 16, wide), lambda m, c: (m, STATE // 16, 0)),
        ],
        [
            ((micro, shard, wide), bf16, tok_c, back_here),
            ((micro, shard, wide), bf16, tok_c, back_here),
            ((micro, shard, wide), bf16, tok_c, back_here),
            ((micro, blocks, STATE, wide), f32) + b_state,
            ((micro, n_state, wide), bf16, (1, n_state, wide), micro_at),
        ],
        [(STATE, wide)],
        (key_rows,),
    )(place, mixer, gate_in, d_ynorm, sums, cols, keys, prefix, chan, payload)
    wide_tile = min(shard, 512)
    out_part = kernel_call(
        out_kernel,
        (micro, shard // wide_tile),
        [((1, wide_tile, wide), here)] + out_specs,
        [((micro, shard, width), bf16, (1, wide_tile, width), here)],
        [pltpu.VMEM((wide, width), bf16)],
    )(ynorm_low, *w_out)[0]
    out_sum = lax.psum_scatter(out_part, "head", scatter_dimension=1, tiled=True)

    def weight_parts(a, count, *b, below=None, wait=(), us=None):
        run = a.shape[2] // count
        wide_b = sum(x.shape[2] for x in b)
        extra = [] if below is None else [below]
        out = (run + sum(x.shape[0] for x in extra), wide_b)
        return kernel_call(
            functools.partial(weight_kernel, len(b), below is not None),
            (count,),
            [((micro, shard, run), lambda k: (0, 0, k))]
            + [(x.shape, lambda k: (0, 0, 0)) for x in b]
            + [(x.shape, lambda k: (0, 0)) for x in extra],
            [(out, bf16, out, lambda k: (0, 0))] * count,
            [pltpu.VMEM(b[0].shape[:2] + (wide_b,), bf16)] * (len(b) > 1),
            wait,
            us,
        )(a, *b, *extra)

    if swapped:
        out = (wide, width)
        grad_out_part = kernel_call(
            rows_kernel,
            (runs,),
            [
                scalar,
                ((micro, shard, run_ch), lambda k: (0, 0, k)),
                (grad_rows.shape, lambda k: (0, 0, 0)),
            ],
            [(out, bf16, out, lambda k: (0, 0))],
        )(place, ynorm_low, grad_rows)[0]
    else:
        grad_out_part = ()
    grad_w_gate = weight_parts(normed_low, seqs, d_gate, us=0)
    adj_in = linked(payload, True, out_part, grad_w_gate, grad_out_part)

    by_heads = key_ch % 16 == 0
    key_shape = (heads, micro, key_ch, shard) if by_heads else (1, micro, 2 * STATE, shard)
    d_vals, d_keys, d_step, head_g, skip_g = micro_call(
        functools.partial(bwd_kernel, seqs - 1),
        micro,
        blocks,
        [
            (tok_c, back_here),
            ((1, 2 * STATE, size), back_along),
            ((1, size, 2 * STATE), back_here),
            (tok_l, back_here),
            ((1, 32, size), back_along),
            b_state,
            b_pre,
            (tok_c, back_here),
            b_state,
            ((8, wide), fixed),
            ((8, LANES), fixed),
        ]
        + [((1, n_state, wide), micro_at)] * (2 * seqs - 2),
        [
            ((micro, shard, wide), bf16, tok_c, back_here),
            (key_shape, bf16, (key_shape[0], 1, key_shape[2], size), lambda m, c: (0, 0, 0, blocks - 1 - c)),
            ((micro, shard, LANES), bf16, tok_l, back_here),
            ((8, LANES), f32, (8, LANES), fixed),
            ((8, wide), f32, (8, wide), fixed),
        ],
        [(STATE, wide)] * 2,
    )(
        vals, keys, ktok, cols, rows_t, starts, prefix, d_mix, block_adj, chan, params, *state_in, *adj_in
    )
    by_head = lambda x: x.astype(bf16).reshape(heads, rows, -1)
    gate_parts = seq_exchange([after(part, adj_in) for part in grad_w_gate])
    g_gate = by_head(total_of(gate_parts))
    d_val_in, val_back, conv_val_g = kernel_call(
        conv_back_kernel,
        (micro,),
        [whole] + conv_ins,
        [
            ((micro, shard, wide), bf16) + whole,
            ((micro, 8, wide), f32, (1, 8, wide), lambda m: (m, 0, 0)),
            ((8, wide), f32, (8, wide), lambda m: (0, 0)),
        ],
        (),
        gate_parts[1:],
    )(d_vals, proj, proj_rim, valid_cols, conv_par)
    if not by_heads:
        d_keys = jnp.swapaxes(d_keys.reshape(micro, heads, key_ch, shard), 0, 1)
    d_keys = head_swap(d_keys)
    g_gate_own = head_swap(after(g_gate, d_keys))
    val_back = lax.ppermute(val_back, "seq", backward)
    rim_sum = d_val_in[:, shard - 16 :].astype(f32) + jnp.pad(val_back, ((0, 0), (8, 0), (0, 0)))
    d_val_in = lax.dynamic_update_slice_in_dim(d_val_in, rim_sum.astype(bf16), shard - 16, 1)

    d_keys = jnp.pad(d_keys, ((0, 0), (0, 0), (0, key_rows_n - key_ch), (0, 0)))
    d_key_in, key_back, conv_key_g = kernel_call(
        key_back_kernel,
        (micro,),
        [((heads, 1, key_rows_n, shard), lambda m: (0, m, 0, 0))] + key_ins,
        [
            ((micro, key_rows_n, shard), f32) + by_micro(key_rows_n, shard),
            ((micro, key_rows_n, LANES), f32) + by_micro(key_rows_n, LANES),
            ((8, LANES), f32, (8, LANES), lambda m: (0, 0)),
        ],
        [pltpu.VMEM((LANES, LANES), f32)],
    )(d_keys, small_in, small_rim, valid, key_par)
    key_back = lax.ppermute(key_back, "seq", backward)

    size = min(shard, 512)
    tile = lambda m, c: (m, c, 0)
    tile_c, tile_l, tile_w = ((1, size, n) for n in (wide, LANES, width))
    d_normed = kernel_call(
        functools.partial(normed_back_kernel, seqs),
        (micro, shard // size),
        [(tile_c, tile), (tile_c, tile), (tile_l, tile)] + gate_specs + [(first[0].shape, fixed)] * seqs,
        [((micro, shard, width), bf16, tile_w, tile)],
        (),
        (out_sum, d_key_in),
    )(d_gate, d_val_in, d_step, *w_gate, *first)[0]
    d_normed_sum = lax.psum_scatter(d_normed, "head", scatter_dimension=1, tiled=True)

    fixed1 = lambda m: (0, 0)
    blocks8 = [(8, wide), (8, LANES), (8, LANES), (8, wide)]
    packed = (8, wide + LANES)
    small = kernel_call(
        pack_kernel,
        (1,),
        [(block, fixed1) for block in blocks8],
        [(packed, f32, packed, fixed1)],
    )(conv_val_g, conv_key_g, head_g, skip_g)[0]
    small = seq_reduce([small] * seqs)

    d_key_in, d_small = kernel_call(
        key_join_kernel,
        (micro,),
        [by_micro(key_rows_n, shard), by_micro(key_rows_n, LANES), by_micro(shard, LANES)],
        [
            ((micro, key_rows_n, shard), bf16) + by_micro(key_rows_n, shard),
            ((micro, shard, LANES), bf16) + by_micro(shard, LANES),
        ],
        (),
        (g_gate_own,),
    )(d_key_in, key_back, d_step)
    d_key_in = d_key_in[:, :key_ch]
    g_first = weight_parts(normed_low, seqs, d_val_in, d_small)
    if swapped:
        grad_out_weight = lax.psum_scatter(
            grad_out_part, "seq", scatter_dimension=0, tiled=True
        ).astype(f32)
    else:
        full = dot("mtk,mtd->kd", ynorm_low, grad_rows).astype(bf16)[:chans]
        full = lax.dynamic_update_slice_in_dim(jnp.zeros((D_INNER, width), bf16), full, h_i * chans, 0)
        grad_out_weight = lax.psum_scatter(full, BOTH, scatter_dimension=0, tiled=True).astype(f32)
    d_key_in, small = after((d_key_in, small), g_first)
    key_own = jnp.transpose(d_key_in.reshape(micro, key_ch, heads, tok), (2, 0, 1, 3))
    count = key_own.size // heads
    key_n = -(-count // (8 * (wide + LANES))) * 8
    key_own = fill(key_own.reshape(heads, count), 1, key_n * (wide + LANES)).reshape(heads, key_n, -1)
    small = [jnp.broadcast_to(part[None], (heads,) + part.shape) for part in three_parts(small)[:2]]
    small = head_swap(after(jnp.concatenate(small + [key_own], axis=1), g_first))
    key_own = small[:, 16:].reshape(heads, -1)[:, :count].reshape(heads, micro, key_ch, tok)

    if swapped:
        conv_g, head_g = kernel_call(
            unpack_kernel,
            (1,),
            [scalar, ((heads, 16, wide + LANES), lambda m: (0, 0, 0))],
            [
                ((8, 2 * LANES), f32, (8, 2 * LANES), lambda m: (0, 0)),
                ((8, LANES), f32, (8, LANES), lambda m: (0, 0)),
            ],
            [pltpu.VMEM((heads, 8, wide + LANES), f32)],
        )(jnp.stack([s_i, h_i]), small)
        conv_g = conv_g[: CONV_K + 1, :conv_share]
        head_g = head_g[CONV_K + 1 :, :head_share]
    else:
        sums = small[:, :8].astype(f32) + small[:, 8:16].astype(f32)
        conv_g = jnp.concatenate(
            [sums[:, : CONV_K + 1, :chans], sums[:, : CONV_K + 1, wide : wide + key_ch]], axis=2
        )
        head_g = sums[:, CONV_K + 1 : CONV_K + 4, :n_heads].reshape(heads, 3, runs, run_heads)
        conv_gv = jnp.transpose(conv_g[:, :, :chans].reshape(heads, CONV_K + 1, runs, run_ch), (1, 2, 0, 3))
        conv_gk = jnp.transpose(conv_g[:, :, chans:], (1, 0, 2))
        conv_g = jnp.concatenate(
            [conv_gv.reshape(CONV_K + 1, D_INNER), conv_gk.reshape(CONV_K + 1, 2 * STATE)], axis=1
        )
        head_g = jnp.transpose(head_g, (1, 2, 0, 3)).reshape(3, HEADS)
        conv_g = lax.dynamic_slice_in_dim(conv_g, linear * conv_share, conv_share, 1)
        head_g = lax.dynamic_slice_in_dim(head_g, h_i * head_share, head_share, 1)
    hidden_out = (hidden_in.astype(f32) + after(out_sum, g_first).astype(f32)).astype(bf16)
    gate_gg = jnp.sum(after(grad_out_weight, g_first) * out_weight.astype(f32), axis=1) / gate_gain.astype(f32)
    g_first = by_head(seq_reduce(g_first))
    g_first = head_swap(after(g_first, conv_g, head_g, hidden_out, gate_gg, key_own))
    if swapped:
        own_at = lambda m: (m, 0, 0)
        own = (1, tok, width)
        flat = lambda m: (0, 0)
        steps = (seqs, width // seqs)
        grad_in = kernel_call(
            grad_in_kernel,
            (micro,),
            [
                scalar,
                (own, own_at),
                ((heads, 1, key_ch, tok), lambda m: (0, m, 0, 0)),
                ((2 * STATE, width), flat),
                (own, own_at),
                (steps, flat),
                (own, own_at),
            ],
            [((micro, tok, width), bf16, own, own_at)],
            [pltpu.VMEM((tok, width), f32)],
        )(place, d_normed_sum, key_own, key_rows.reshape(2 * STATE, width), hidden_in, gain_steps, out_grad)[0]
        whole3 = lambda shape: (shape, lambda m: (0,) * len(shape))
        grad_in_weight, norm_sum = kernel_call(
            weight_grad_kernel,
            (1,),
            [whole3(g_gate_own.shape), whole3(g_first.shape), whole3(in_weight.shape)],
            [
                (in_weight.shape, f32) + whole3(in_weight.shape),
                ((rows, LANES), f32) + whole3((rows, LANES)),
            ],
            (),
            (grad_in,),
        )(g_gate_own, g_first, in_weight)
        norm_sum = norm_sum[:, 0]
    else:
        key_part = dot("hmct,hcd->mtd", key_own, key_rows)
        d_normed = (d_normed_sum.astype(f32) + key_part).reshape(micro, tok, seqs, -1)
        d_normed = from_steps(jnp.moveaxis(d_normed, 2, 0), s_i)
        d_normed = jnp.moveaxis(d_normed, 0, 2).reshape(micro, tok, width)
        own = hidden_in.astype(f32)
        own_inv = lax.rsqrt(jnp.mean(own * own, axis=-1, keepdims=True) + EPS)
        d_unit = d_normed * from_steps(gain_steps, s_i).reshape(-1)
        shared = own_inv * own_inv * jnp.mean(d_unit * own, axis=-1, keepdims=True)
        grad_in = (out_grad.astype(f32) + own_inv * (d_unit - own * shared)).astype(bf16)

        def uncolumns(x, size):
            x = x.astype(f32).reshape(heads, rows, runs, size)
            return jnp.transpose(x, (1, 2, 0, 3)).reshape(rows, runs * heads * size)

        g_key = jnp.transpose(g_first[:, :rows, wide + 8 : wide + 8 + key_ch], (1, 0, 2))
        grad_in_weight = jnp.concatenate(
            [
                uncolumns(g_gate_own[:, :rows, :chans], run_ch),
                uncolumns(g_first[:, :rows, :chans], run_ch),
                g_key.astype(f32).reshape(rows, -1),
                uncolumns(g_first[:, :rows, wide : wide + n_heads], run_heads),
            ],
            axis=1,
        )
        norm_sum = jnp.sum(grad_in_weight * in_weight.astype(f32), axis=1)
    norm_g = norm_sum / norm_gain.astype(f32)

    return (
        hidden_out,
        grad_in,
        norm_g,
        grad_in_weight,
        conv_g[:CONV_K],
        conv_g[CONV_K],
        head_g[0],
        head_g[1],
        head_g[2],
        gate_gg,
        grad_out_weight,
    )


def solution(mesh):
    tokens = P(None, BOTH, None)
    by_rows = P(BOTH, None)
    return jax.shard_map(
        body,
        mesh=mesh,
        in_specs=(
            tokens,
            P(),
            P(BOTH),
            by_rows,
            P(None, BOTH),
            P(BOTH),
            P("head"),
            P("head"),
            P("head"),
            P(BOTH),
            by_rows,
            tokens,
        ),
        out_specs=(
            tokens,
            tokens,
            P(BOTH),
            by_rows,
            P(None, BOTH),
            P(BOTH),
            P("head"),
            P("head"),
            P("head"),
            P(BOTH),
            by_rows,
        ),
        check_vma=False,
    )
```

```python
import functools

import jax
import jax.numpy as jnp
from jax import lax
from jax.experimental import pallas as pl
from jax.experimental.pallas import tpu as pltpu
from jax.sharding import PartitionSpec as P

HEADS = 64
HEADDIM = 64
STATE = 128
CONV_K = 4
SCAN_BLOCK = 256
D_INNER = 4096
CONV_CH = 4352
EDGE = CONV_K - 1
EPS = 1e-05

f32 = jnp.float32
bf16 = jnp.bfloat16
BOTH = ("seq", "head")


def dot(spec, a, b):
    return jnp.einsum(spec, a, b, preferred_element_type=f32)


def three_parts(v):
    parts = []
    for _ in range(3):
        part = lax.reduce_precision(v, 8, 7)
        parts.append(part.astype(bf16))
        v = v - part
    return parts


def linked(payload, back, *wait):
    count = lax.axis_size("seq")
    got = []
    for k in range(1, count):
        if back:
            pairs = [(i, i - k) for i in range(k, count)]
        else:
            pairs = [(i, i + k) for i in range(count - k)]
        got.append(after(lax.ppermute(payload, "seq", pairs), *wait))
    return got


def after(x, *others):
    return lax.optimization_barrier((x, others))[0]


def seq_steps():
    count = lax.axis_size("seq")
    return [(k, [(i, i ^ k) for i in range(count)]) for k in reversed(range(1, count))]


def seq_gather(x, *wait):
    got = [(k, lax.ppermute(x, "seq", pairs)) for k, pairs in seq_steps()]
    if wait:
        got = [(k, after(part, *wait)) for k, part in got]
    parts = dict(got)
    parts[0] = x
    return [parts[k] for k in sorted(parts)]


def seq_exchange(parts):
    return [parts[0]] + [lax.ppermute(parts[k], "seq", pairs) for k, pairs in seq_steps()]


def total_of(parts):
    return functools.reduce(lambda a, b: a + b, [part.astype(f32) for part in parts])


def seq_reduce(parts):
    return total_of(seq_exchange(parts))


def from_steps(x, place):
    return jnp.stack([lax.dynamic_index_in_dim(x, place ^ k, 0, False) for k in range(x.shape[0])])


def head_swap(x):
    return lax.all_to_all(x, "head", split_axis=0, concat_axis=0, tiled=True)


def silu_parts(v):
    sig = jax.nn.sigmoid(v)
    return v * sig, sig * (1.0 + v * (1.0 - sig))


LANES = 128
LOG, STEP, CARRY, TO_END, SEG = 0, 8, 16, 24, 32
SIG = 16
ROWS_SEG = 24


def nt(a, b):
    return lax.dot_general(a, b, (((1,), (1,)), ((), ())), preferred_element_type=f32)


def nn(a, b):
    return lax.dot_general(a, b, (((1,), (0,)), ((), ())), preferred_element_type=f32)


def tn(a, b):
    return lax.dot_general(a, b, (((0,), (0,)), ((), ())), preferred_element_type=f32)


def split(v):
    high = v.astype(bf16)
    return high, (v - high.astype(f32)).astype(bf16)


def left_half(shape):
    return lax.broadcasted_iota(jnp.int32, shape, len(shape) - 1) < HEADDIM


def pair_of(cols, base, p):
    at = base + 2 * p
    shape = (cols.shape[0], LANES)
    return jnp.where(
        left_half(shape),
        jnp.broadcast_to(cols[:, at : at + 1], shape),
        jnp.broadcast_to(cols[:, at + 1 : at + 2], shape),
    )


def running_sum(x, back=False):
    size = x.shape[1]
    lane = lax.broadcasted_iota(jnp.int32, x.shape, 1)
    shift = 1
    while shift < size:
        if back:
            x = x + jnp.where(lane < size - shift, pltpu.roll(x, size - shift, 1), 0.0)
        else:
            x = x + jnp.where(lane >= shift, pltpu.roll(x, shift, 1), 0.0)
        shift *= 2
    return x


def pairs_in(x):
    return x.shape[-1] // LANES


def lanes(p):
    return slice(p * LANES, (p + 1) * LANES)


def mask_kernel(place_ref, start_ref, seg_ref, valid_ref, cols_ref):
    m = pl.program_id(0)
    size = seg_ref.shape[2]
    at = place_ref[0] * size + lax.broadcasted_iota(jnp.int32, (1, size), 1)

    def seg_of(position):
        total = jnp.zeros((1, size), f32)
        for i in range(start_ref.shape[1]):
            total = total + jnp.where(position >= start_ref[m, i], 1.0, 0.0)
        return total

    seg = seg_of(at)
    behind = [seg_of(at - by) for by in range(1, CONV_K)]
    block = seg_of(at - at % SCAN_BLOCK - 1)
    first = jnp.where(seg == behind[0], 0.0, 1.0)
    seg_ref[0] = jnp.concatenate([seg, block, first, jnp.zeros((5, size), f32)], axis=0)
    rows = [jnp.where(seg == x, 1.0, 0.0) for x in reversed(behind)] + [jnp.ones((1, size), f32)]
    rows = jnp.concatenate(rows + [jnp.zeros((8 - CONV_K, size), f32)], axis=0)
    valid_ref[0] = rows
    cols_ref[0] = jnp.concatenate([rows, jnp.zeros((LANES - 8, size), f32)], axis=0).T


GAIN_AT, GATE_AT, HEAD_AT, CONV_AT, SENT = 0, 128, 256, 384, 384 + 256 * (CONV_K + 1)


def glue_kernel(place_ref, sent_ref, gain_ref, chan_ref, conv_ref, key_ref, par_ref, turned):
    s, h = place_ref[0], place_ref[1]
    heads = sent_ref.shape[0]
    seqs = gain_ref.shape[0]
    left = left_half((1, LANES))

    def from_head(row):
        chips = heads // 2
        return (h // 2 + chips - row % chips) % chips * 2 + (h % 2 ^ row // chips)

    row = from_head(lax.broadcasted_iota(jnp.int32, (heads, LANES), 0))

    def lanes_from(start):
        return sent_ref[:, start : start + LANES].astype(f32)

    for k in range(seqs):
        gains = lanes_from(k * SENT)
        for p in range(heads // 2):
            of_head = lambda i: jnp.sum(jnp.where(row == i, gains, 0.0), axis=0, keepdims=True)
            second = pltpu.roll(of_head(2 * p + 1), HEADDIM, 1)
            gain_ref[k : k + 1, lanes(p)] = jnp.where(left, of_head(2 * p), second)

    of = from_head(lax.broadcasted_iota(jnp.int32, (8, heads), 1))
    to = lax.broadcasted_iota(jnp.int32, (8, heads), 0)
    head = (to // 2 * heads + h) * 2 + to % 2
    sel = jnp.where(of == head // 8, 1.0, 0.0).astype(bf16)
    found = nn(sel, sent_ref[:, HEAD_AT : HEAD_AT + LANES])
    lane = lax.broadcasted_iota(jnp.int32, (8, LANES), 1)
    local = lax.broadcasted_iota(jnp.int32, (8, LANES), 0)
    place = (h * 2 + local % 2) % 8

    def param(q):
        keep = (lane % 24 == q * 8 + place) & (lane < 72)
        return jnp.sum(jnp.where(keep, found, 0.0), axis=1, keepdims=True)

    decay, bias, skip = param(0), param(1), param(2)
    par_ref[...] = jnp.where(lane == 0, bias, jnp.where(lane == 1, -jnp.exp(decay), 0.0))

    def run_of(r, tap):
        total = jnp.zeros((1, LANES), f32)
        for k in range(seqs):
            source = (s ^ k) * heads + row
            begins = source + source // 16
            base = k * SENT + CONV_AT + tap * 2 * LANES
            part = jnp.where(begins == r, lanes_from(base), 0.0)
            part = part + jnp.where(begins == r - 1, lanes_from(base + LANES), 0.0)
            total = total + jnp.sum(part, axis=0, keepdims=True)
        return total

    chan_ref[...] = jnp.zeros_like(chan_ref)
    conv_ref[...] = jnp.zeros_like(conv_ref)
    for b in range(seqs):
        chan_ref[0:1, lanes(b)] = jnp.where(left, skip[2 * b : 2 * b + 1], skip[2 * b + 1 : 2 * b + 2])
        start = pl.multiple_of((s ^ b) * SENT, LANES) + GATE_AT
        gates = sent_ref[0:1, pl.ds(pl.multiple_of(start, LANES), LANES)]
        chan_ref[1:2, lanes(b)] = gates.astype(f32)
        for tap in range(CONV_K + 1):
            conv_ref[tap : tap + 1, lanes(b)] = run_of(b * heads + h, tap)
    per = key_ref.shape[0]
    each = LANES // per
    taps = [run_of(seqs * heads + h // each, tap) for tap in range(CONV_K + 1)]
    turned[...] = jnp.concatenate(taps + [jnp.zeros((LANES - CONV_K - 1, LANES), f32)], axis=0).T
    key_ref[...] = turned[pl.ds(pl.multiple_of(h % each * per, 8), per), :]


def behind_lanes(x, rim, by):
    return pltpu.roll(jnp.concatenate([rim, x], axis=1), by, 1)[:, LANES:] if by else x


def key_conv_kernel(small_ref, rim_ref, valid_ref, par_ref, out_ref):
    count = par_ref.shape[0]
    x, rim = small_ref[0, 8:].astype(f32)[:count], rim_ref[0, 8:].astype(f32)[:count]
    total = par_ref[:, CONV_K : CONV_K + 1]
    for k in range(CONV_K):
        total = total + par_ref[:, k : k + 1] * behind_lanes(x, rim, EDGE - k) * valid_ref[0, k : k + 1]
    out_ref[0] = (total / (1.0 + jnp.exp(-total))).astype(bf16)


def key_back_kernel(d_ref, small_ref, rim_ref, valid_ref, par_ref, in_ref, back_ref, grad_ref, total_grad):
    @pl.when(pl.program_id(0) == 0)
    def _():
        total_grad[...] = jnp.zeros_like(total_grad)

    count = par_ref.shape[0]
    x, rim = small_ref[0, 8:].astype(f32)[:count], rim_ref[0, 8:].astype(f32)[:count]
    size = x.shape[1]
    total = par_ref[:, CONV_K : CONV_K + 1]
    seen = []
    for k in range(CONV_K):
        seen.append(behind_lanes(x, rim, EDGE - k) * valid_ref[0, k : k + 1])
        total = total + par_ref[:, k : k + 1] * seen[k]
    sig = 1.0 / (1.0 + jnp.exp(-total))
    d_keys = 0.0
    for h in range(d_ref.shape[0]):
        d_keys = d_keys + d_ref[h, 0].astype(f32)
    d_total = d_keys.astype(bf16).astype(f32) * (sig * (1.0 + total * (1.0 - sig)))
    lane = lax.broadcasted_iota(jnp.int32, (count, LANES), 1)
    ahead, d_in = 0.0, 0.0
    grads = jnp.where(lane == CONV_K, jnp.sum(d_total, axis=1, keepdims=True), 0.0)
    empty = jnp.zeros((count, LANES), f32)
    for k in range(CONV_K):
        grads = jnp.where(lane == k, jnp.sum(d_total * seen[k], axis=1, keepdims=True), grads)
        held = d_total * (par_ref[:, k : k + 1] * valid_ref[0, k : k + 1])
        by = EDGE - k
        wide = jnp.concatenate([empty, held], axis=1)
        moved = pltpu.roll(wide, size + LANES - by, 1) if by else wide
        ahead = ahead + moved[:, :LANES]
        if by:
            keep = lax.broadcasted_iota(jnp.int32, (count, size), 1) < size - by
            d_in = d_in + jnp.where(keep, moved[:, LANES:], 0.0)
        else:
            d_in = d_in + held
    in_ref[0] = d_in
    back_ref[0] = jnp.where(lane >= LANES - EDGE, ahead, 0.0)
    total_grad[0:count, :] += grads
    grad_ref[...] = total_grad[...].T[0:8]


def pack_kernel(conv_ref, key_ref, head_ref, skip_ref, out_ref):
    wide = conv_ref.shape[1]
    taps = CONV_K + 1
    out_ref[0:taps, :wide] = conv_ref[0:taps]
    out_ref[0:taps, wide:] = key_ref[0:taps]
    left = left_half((1, LANES))
    lane = lax.broadcasted_iota(jnp.int32, (1, LANES), 1)
    skips = jnp.zeros((1, LANES), f32)
    for p in range(wide // LANES):
        both = skip_ref[0:1, lanes(p)]
        first = jnp.sum(jnp.where(left, both, 0.0), axis=1, keepdims=True)
        second = jnp.sum(both, axis=1, keepdims=True) - first
        skips = jnp.where(lane == 2 * p, first, jnp.where(lane == 2 * p + 1, second, skips))
    heads = jnp.concatenate([head_ref[...], jnp.zeros((LANES - 8, LANES), f32)], axis=0).T
    out_ref[taps : taps + 2, :LANES] = heads[0:2]
    out_ref[taps + 2 : 8, :LANES] = skips
    out_ref[taps:8, LANES:] = jnp.zeros((8 - taps, wide), f32)


def unpack_kernel(place_ref, sums_ref, conv_ref, head_ref, total):
    s, h = place_ref[0], place_ref[1]
    heads = sums_ref.shape[0]
    wide = sums_ref.shape[2] - LANES
    for i in range(heads):
        total[i] = sums_ref[i, 0:8].astype(f32) + sums_ref[i, 8:16].astype(f32)
    linear = s * heads + h
    lane = lax.broadcasted_iota(jnp.int32, (8, LANES), 1)
    runs = wide // LANES
    per = 2 * STATE // heads

    def run(r):
        at = pl.multiple_of(((r // heads) & (runs - 1)) * LANES, LANES)
        vals = total[r & (heads - 1), :, pl.ds(at, LANES)]
        keys = jnp.zeros((8, LANES), f32)
        first = jnp.clip(r - runs * heads, 0, 2 * STATE // LANES - 1) * (LANES // per)
        for q in range(LANES // per):
            piece = jnp.where(lane < per, total[first + q, :, wide:], 0.0)
            keys = keys + (pltpu.roll(piece, per * q, 1) if q else piece)
        return jnp.where(r < runs * heads, vals, keys)

    begins = linear + linear // 16
    both = jnp.concatenate([run(begins), run(begins + 1)], axis=1)
    shift = (2 * LANES - (linear & 15) * 8) & (2 * LANES - 1)
    conv_ref[...] = pltpu.roll(both, shift, 1)
    out = jnp.zeros((8, LANES), f32)
    for j in range(heads // 2):
        mine = total[(h & 1) * (heads // 2) + j, :, 0:LANES]
        moved = pltpu.roll(mine, (2 * j + LANES - 2 * (h // 2)) & (LANES - 1), 1)
        out = jnp.where(lane // 2 == j, moved, out)
    head_ref[...] = out


def key_join_kernel(in_ref, back_ref, step_ref, key_ref, small_ref):
    x = in_ref[0]
    count, size = x.shape
    key = jnp.concatenate([x[:, : size - LANES], x[:, size - LANES :] + back_ref[0]], axis=1)
    key_ref[0] = key.astype(bf16)
    rows = [jnp.zeros((8, size), f32), key, jnp.zeros((LANES - 8 - count, size), f32)]
    cols = jnp.concatenate(rows, axis=0).T
    small_ref[0] = (cols + step_ref[0].astype(f32)).astype(bf16)


def chained(refs, at):
    total, reach = 0.0, 1.0
    for ref in refs:
        total = total + reach * ref[0, :STATE, at].astype(f32)
        reach = reach * ref[0, STATE : STATE + 1, at].astype(f32)
    return total


def prep_kernel(
    m, step_ref, seg_ref, par_ref, val_ref, key_ref, cols_ref, rows_ref, ktok_ref, start_ref, pre_ref, out_ref, state, reach
):
    @pl.when(pl.program_id(0) == 0)
    def _():
        state[...] = jnp.zeros(state.shape, f32)
        reach[...] = jnp.ones(reach.shape, f32)

    raw = step_ref[0].astype(f32)[0:8] + par_ref[:, 0:1]
    small = jnp.exp(-jnp.abs(raw))
    one = 1.0 + small
    step = jnp.maximum(raw, 0.0) + jnp.where(
        one == 1.0, small, jnp.log(one) * (small / jnp.where(one == 1.0, 1.0, one - 1.0))
    )
    sig = jnp.where(raw >= 0.0, 1.0, small) / one
    log = running_sum(step * par_ref[:, 1:2])
    size = log.shape[1]
    segs = seg_ref[0]
    seg, prev = segs[0:1], segs[1:2]
    carry = jnp.where(seg == prev, jnp.exp(log), 0.0)
    to_end = jnp.where(
        seg == seg[:, size - 1 :], jnp.exp(jnp.minimum(log[:, size - 1 :] - log, 0.0)), 0.0
    )
    rows_ref[0] = jnp.concatenate([log, step, sig, segs], axis=0)
    stack = jnp.concatenate(
        [log, step, carry, to_end, segs, jnp.zeros((LANES - 40, size), f32)], axis=0
    )
    cols = stack.T
    cols_ref[0] = cols
    keys = key_ref[0]
    ktok_ref[0] = keys.astype(f32).T.astype(bf16)
    start_ref[0, 0] = state[...]
    pre_ref[0, 0] = reach[...]
    weight = cols[:, TO_END : TO_END + 8] * cols[:, STEP : STEP + 8]
    for p in range(pairs_in(val_ref)):
        ending = (val_ref[0, :, lanes(p)].astype(f32) * pair_of(weight, 0, p)).astype(bf16)
        decay = pair_of(cols[size - 1 :], CARRY, p)
        state[:, lanes(p)] = decay * state[:, lanes(p)] + nn(keys[:STATE], ending)
        reach[:, lanes(p)] = decay * reach[:, lanes(p)]
    out_ref[0] = jnp.concatenate([state[...], reach[...], reach[...]], axis=0).astype(bf16)


def same_mask(cols, rows):
    size = cols.shape[0]
    at = lax.broadcasted_iota(jnp.int32, (size, size), 0)
    of = lax.broadcasted_iota(jnp.int32, (size, size), 1)
    return (cols[:, SEG : SEG + 1] == rows[ROWS_SEG : ROWS_SEG + 1]) & (at >= of)


def within(cols, rows, j):
    return jnp.exp(jnp.minimum(cols[:, j : j + 1] - rows[j : j + 1], 0.0))


def step_lanes(place_ref, p, swapped):
    return pl.ds(pl.multiple_of((place_ref[0] ^ p) * LANES, LANES), LANES) if swapped else lanes(p)


def fwd_kernel(
    swapped, near, m, place_ref, val_ref, ktok_ref, cols_ref, rows_ref, start_ref, pre_ref, gate_ref, dy_ref, chan_ref, *refs
):
    in_refs, (mix_ref, sum_ref, in_ref) = refs[:near], refs[near:]

    @pl.when(pl.program_id(0) == 0)
    def _():
        for p in range(pairs_in(val_ref)):
            in_ref[:, lanes(p)] = chained(in_refs, lanes(p))

    cols, rows = cols_ref[0], rows_ref[0]
    rkey = ktok_ref[0, :, STATE:]
    scores = jnp.where(same_mask(cols, rows), nt(rkey, ktok_ref[0, :, :STATE]), 0.0)
    squares, products = 0.0, 0.0
    left = left_half((cols.shape[0], LANES))
    for p in range(pairs_in(val_ref)):
        at = lanes(p)
        vals = val_ref[0, :, at].astype(f32)
        stepped = vals * pair_of(cols, STEP, p)
        high, low = split(start_ref[0, 0, :, at] + pre_ref[0, 0, 0:1, at] * in_ref[:, at])
        mixed = pair_of(cols, CARRY, p) * (nn(rkey, high) + nn(rkey, low))
        weights = [(scores * within(cols, rows, 2 * p + half)).astype(bf16) for half in range(2)]
        held = [jnp.where(keep, stepped, 0.0).astype(bf16) for keep in (left, ~left)]
        mixed = mixed + nn(jnp.concatenate(weights, axis=1), jnp.concatenate(held, axis=0))
        mixed = (mixed + chan_ref[0:1, at] * vals).astype(bf16)
        mix_ref[0, :, at] = mixed
        gate = gate_ref[0, :, at]
        gated = mixed.astype(f32) * (gate / (1.0 + jnp.exp(-gate)))
        squares = squares + gated * gated
        products = products + gated * (dy_ref[0, :, step_lanes(place_ref, p, swapped)] * chan_ref[1:2, at])
    lane = lax.broadcasted_iota(jnp.int32, squares.shape, 1)
    sums = jnp.where(
        lane == 0,
        jnp.sum(squares, axis=1, keepdims=True),
        jnp.where(lane == 1, jnp.sum(products, axis=1, keepdims=True), 0.0),
    )
    sum_ref[0] = sums.T[0:8]


def norm_kernel(
    swapped, m, place_ref, mix_ref, gate_ref, dy_ref, sum_ref, cols_ref, key_ref, pre_ref, chan_ref, reach_ref,
    yn_ref, dmix_ref, dgate_ref, adj_ref, out_ref, adj
):
    @pl.when(pl.program_id(0) == 0)
    def _():
        adj[...] = jnp.zeros(adj.shape, f32)

    cols = cols_ref[0]
    size = cols.shape[0]
    rows = sum_ref[0]
    scale_row = lax.rsqrt(rows[0:1] * (1.0 / D_INNER) + EPS)
    pull_row = scale_row * scale_row * rows[1:2] * (1.0 / D_INNER)
    both = jnp.concatenate([scale_row, pull_row, jnp.zeros((LANES - 2, size), f32)], axis=0).T
    scale, pull = both[:, 0:1], both[:, 1:2]
    for p in range(pairs_in(mix_ref)):
        at = lanes(p)
        mixer = mix_ref[0, :, at].astype(f32)
        gate = gate_ref[0, :, at]
        sig = 1.0 / (1.0 + jnp.exp(-gate))
        act = gate * sig
        slope = sig * (1.0 + gate * (1.0 - sig))
        gated = mixer * act
        unit = gated * scale
        gain = chan_ref[1:2, at]
        step_at = step_lanes(place_ref, p, swapped)
        yn_ref[0, :, step_at] = (unit * gain).astype(bf16)
        d_y = dy_ref[0, :, step_at]
        d_gated = scale * (d_y * gain - gated * pull)
        d_mix = (d_gated * act).astype(bf16)
        dmix_ref[0, :, at] = d_mix
        dgate_ref[0, :, at] = (d_gated * mixer * slope).astype(bf16)
        carried = (d_mix.astype(f32) * pair_of(cols, CARRY, p)).astype(bf16)
        block = nn(key_ref[0, STATE:], carried)
        adj_ref[0, 0, :, at] = block
        adj[:, at] = pair_of(cols[size - 1 :], CARRY, p) * adj[:, at] + block
    reach = reach_ref[0]
    out_ref[0] = jnp.concatenate([adj[...].astype(bf16), reach], axis=0)


def bwd_kernel(
    near, m, val_ref, key_ref, ktok_ref, cols_ref, rows_ref, start_ref, pre_ref, dmix_ref, adj_ref, chan_ref, par_ref, *refs
):
    in_refs, adjin_refs, refs = refs[:near], refs[near : 2 * near], refs[2 * near :]
    dval_ref, dkey_ref, dstep_ref, head_ref, skip_ref, adj, in_ref = refs

    @pl.when(pl.program_id(0) == 0)
    def _():
        if m == 0:
            head_ref[...] = jnp.zeros_like(head_ref)
            skip_ref[...] = jnp.zeros_like(skip_ref)
        for p in range(pairs_in(val_ref)):
            in_ref[:, lanes(p)] = chained(in_refs, lanes(p))
            adj[:, lanes(p)] = chained(adjin_refs, lanes(p))

    cols, rows = cols_ref[0], rows_ref[0]
    size = cols.shape[0]
    wkey, rkey = ktok_ref[0, :, :STATE], ktok_ref[0, :, STATE:]
    same = same_mask(cols, rows)
    scores = jnp.where(same, nt(rkey, wkey), 0.0)
    both_scores = jnp.concatenate([scores, scores], axis=0)
    left = left_half((size, LANES))
    lane = lax.broadcasted_iota(jnp.int32, (size, LANES), 1)
    lane_row = lax.broadcasted_iota(jnp.int32, (1, LANES), 1)
    d_scores = jnp.zeros((size, size), f32)
    d_write = jnp.zeros((STATE, size), f32)
    d_read = jnp.zeros((STATE, size), f32)
    by_row = jnp.zeros((size, LANES), f32)
    last = jnp.zeros((1, LANES), f32)
    by_col = []

    def put(total, p, half, values, offset=0):
        where = lane if values.shape[0] == size else lane_row
        return jnp.where(where == offset + 2 * p + half, values, total)

    def halves_of(x):
        first = jnp.sum(jnp.where(left[: x.shape[0]], x, 0.0), axis=1, keepdims=True)
        return first, jnp.sum(x, axis=1, keepdims=True) - first

    for p in range(pairs_in(val_ref)):
        at = lanes(p)
        vals = val_ref[0, :, at].astype(f32)
        d_mix = dmix_ref[0, :, at]
        d_mix_f = d_mix.astype(f32)
        step = pair_of(cols, STEP, p)
        stepped_f = vals * step
        stepped = stepped_f.astype(bf16)
        carry = pair_of(cols, CARRY, p)
        state = start_ref[0, 0, :, at] + pre_ref[0, 0, 0:1, at] * in_ref[:, at]
        high, low = split(state)
        end = adj[:, at]
        end_low = end.astype(bf16)
        ending_f = stepped_f * pair_of(cols, TO_END, p)
        ending = ending_f.astype(bf16)
        carried_d = (d_mix_f * carry).astype(bf16)
        back = nn(wkey, end_low)
        d_stepped = pair_of(cols, TO_END, p) * back
        from_end = ending_f * back
        through = d_mix_f * carry * (nn(rkey, high) + nn(rkey, low)) - from_end
        decay = pair_of(cols[size - 1 :], CARRY, p)
        final = jnp.sum(from_end, axis=0, keepdims=True) + decay * jnp.sum(
            end * state, axis=0, keepdims=True
        )
        final = halves_of(final)
        through = halves_of(through)
        held = [jnp.where(keep, d_mix_f, 0.0).astype(bf16) for keep in (left, ~left)]
        held = jnp.concatenate(held, axis=0)
        near = jnp.concatenate([within(cols, rows, 2 * p), within(cols, rows, 2 * p + 1)], axis=0)
        d_near = nt(held, stepped) * near
        d_scores = d_scores + (d_near[:size] + d_near[size:])
        pairs = d_near * both_scores
        row_sums = jnp.sum(pairs, axis=1, keepdims=True)
        for half in range(2):
            mine = slice(half * size, (half + 1) * size)
            by_row = put(by_row, p, half, row_sums[mine] + through[half])
            by_col.append(jnp.sum(pairs[mine], axis=0, keepdims=True))
            last = put(last, p, half, final[half])
        d_stepped = d_stepped + tn((both_scores * near).astype(bf16), held)
        d_vals = step * d_stepped + chan_ref[0:1, at] * d_mix_f
        dval_ref[0, :, at] = d_vals.astype(bf16)
        skip_ref[0:1, at] += jnp.sum(d_mix_f * vals, axis=0, keepdims=True)
        d_step = halves_of(vals * d_stepped)
        for half in range(2):
            by_row = put(by_row, p, half, d_step[half], 8)
        d_write = d_write + nt(end_low, ending)
        d_read = d_read + nt(high, carried_d) + nt(low, carried_d)
        adj[:, at] = decay * end + adj_ref[0, 0, :, at]
    d_scores = jnp.where(same, d_scores, 0.0).astype(bf16)
    d_write = d_write + nn(key_ref[0, STATE:], d_scores)
    d_read = d_read + nt(key_ref[0, :STATE], d_scores)
    d_keys = jnp.concatenate([d_write, d_read], axis=0).astype(bf16)
    each = dkey_ref.shape[2]
    for h in range(dkey_ref.shape[0]):
        dkey_ref[h, m] = d_keys[h * each : (h + 1) * each]
    while len(by_col) < 8:
        by_col.append(jnp.zeros((1, size), f32))
    turned = by_row.T
    last = jnp.broadcast_to(last, (LANES, LANES)).T[0:8, 0:1]
    d_log = turned[0:8] - jnp.concatenate(by_col, axis=0)
    rate = par_ref[:, 1:2]
    first = rows[ROWS_SEG + 2 : ROWS_SEG + 3]
    d_decay = (running_sum(d_log, True) + last) * (1.0 - first)
    d_raw = (turned[8:16] + d_decay * rate) * rows[SIG : SIG + 8]
    dstep_ref[0] = jnp.concatenate([d_raw, jnp.zeros((LANES - 8, size), f32)], axis=0).T.astype(bf16)
    head_lane = lax.broadcasted_iota(jnp.int32, (8, LANES), 1)
    head_ref[...] += jnp.where(
        head_lane == 0,
        jnp.sum(d_decay * rows[STEP : STEP + 8], axis=1, keepdims=True) * rate,
        jnp.where(head_lane == 1, jnp.sum(d_raw, axis=1, keepdims=True), 0.0),
    )


def shifted(x, rim, by):
    if by == 0:
        return x
    head = jnp.concatenate([rim, x[:8]], axis=0)[8 - by : 16 - by]
    return jnp.concatenate([head, pltpu.roll(x, by, 0)[8:]], axis=0)


def conv_kernel(val_ref, rim_ref, valid_ref, par_ref, out_ref):
    shape = (val_ref.shape[1], LANES)
    valid = [jnp.broadcast_to(valid_ref[0, :, k : k + 1], shape) for k in range(CONV_K)]
    for p in range(pairs_in(out_ref)):
        at = lanes(p)
        x = val_ref[0, :, at].astype(f32)
        rim = rim_ref[0, :, at].astype(f32)[8:16]
        total = par_ref[CONV_K : CONV_K + 1, at]
        for k in range(CONV_K):
            total = total + par_ref[k : k + 1, at] * shifted(x, rim, EDGE - k) * valid[k]
        out_ref[0, :, at] = (total / (1.0 + jnp.exp(-total))).astype(bf16)


def conv_back_kernel(d_ref, val_ref, rim_ref, valid_ref, par_ref, in_ref, back_ref, grad_ref):
    @pl.when(pl.program_id(0) == 0)
    def _():
        grad_ref[...] = jnp.zeros_like(grad_ref)

    size = val_ref.shape[1]
    row = lax.broadcasted_iota(jnp.int32, (size, LANES), 0)
    zeros = jnp.zeros((8, LANES), f32)
    valid = [jnp.broadcast_to(valid_ref[0, :, k : k + 1], (size, LANES)) for k in range(CONV_K)]
    for p in range(pairs_in(d_ref)):
        at = lanes(p)
        x = val_ref[0, :, at].astype(f32)
        rim = rim_ref[0, :, at].astype(f32)[8:16]
        total = par_ref[CONV_K : CONV_K + 1, at]
        seen = []
        for k in range(CONV_K):
            seen.append(shifted(x, rim, EDGE - k) * valid[k])
            total = total + par_ref[k : k + 1, at] * seen[k]
        sig = 1.0 / (1.0 + jnp.exp(-total))
        d_total = d_ref[0, :, at].astype(f32) * (sig * (1.0 + total * (1.0 - sig)))
        grad_ref[CONV_K : CONV_K + 1, at] += jnp.sum(d_total, axis=0, keepdims=True)
        d_in, back = 0.0, 0.0
        for k in range(CONV_K):
            grad_ref[k : k + 1, at] += jnp.sum(d_total * seen[k], axis=0, keepdims=True)
            held = d_total * (par_ref[k : k + 1, at] * valid[k])
            by = EDGE - k
            if by:
                d_in = d_in + jnp.where(row < size - by, pltpu.roll(held, size - by, 0), 0.0)
                back = back + jnp.concatenate([zeros, held[:8]], axis=0)[by : by + 8]
            else:
                d_in = d_in + held
        in_ref[0, :, at] = d_in.astype(bf16)
        back_ref[0, :, at] = back


def proj_kernel(place_ref, x_ref, gain_ref, *refs):
    parts, (low_ref, out_ref, small_ref, weight_ref) = refs[:-4], refs[-4:]
    wide = parts[0].shape[1] - LANES
    size = parts[0].shape[0]

    @pl.when((pl.program_id(0) == 0) & (pl.program_id(1) == 0))
    def _():
        for k, part in enumerate(parts):
            turned = part[:, wide:].astype(f32).T
            at = slice(8, 8 + weight_ref.shape[0])
            weight_ref[:, k * size : (k + 1) * size] = turned[at].astype(bf16)

    x = x_ref[0].astype(f32)
    inv = lax.rsqrt(jnp.mean(x * x, axis=1, keepdims=True) + EPS)
    total = 0.0
    for k, part in enumerate(parts):
        at = pl.ds(pl.multiple_of((place_ref[0] ^ k) * size, LANES), size)
        low = (x_ref[0, :, at].astype(f32) * inv * gain_ref[k : k + 1]).astype(bf16)
        low_ref[0, :, k * size : (k + 1) * size] = low
        total = total + nn(low, part[...])
    out_ref[0] = total.astype(bf16)
    small_ref[0] = total[:, wide:].T.astype(bf16)


def gather_runs(parts, whole):
    run = parts[0].shape[0]

    @pl.when((pl.program_id(0) == 0) & (pl.program_id(1) == 0))
    def _():
        for r, part in enumerate(parts):
            whole[r * run : (r + 1) * run] = part[...]


def fill_kernel(steps, x_ref, grad_ref, *refs):
    gates, outs, (gate_ref, dy_ref, whole) = refs[:steps], refs[steps:-3], refs[-3:]
    gather_runs(outs, whole)
    size = gates[0].shape[0]
    total = 0.0
    for k, part in enumerate(gates):
        total = total + nn(x_ref[0, :, k * size : (k + 1) * size], part[...])
    gate_ref[0] = total
    dy_ref[0] = nt(grad_ref[0], whole[...])


def out_kernel(y_ref, *refs):
    parts, (out_ref, whole) = refs[:-2], refs[-2:]
    gather_runs(parts, whole)
    width = out_ref.shape[2]
    size = min(width, 512)
    for n in range(width // size):
        at = slice(n * size, (n + 1) * size)
        out_ref[0, :, at] = nn(y_ref[0], whole[:, at]).astype(bf16)


def rows_kernel(place_ref, a_ref, b_ref, out_ref):
    total = 0.0
    for m in range(a_ref.shape[0]):
        total = total + tn(a_ref[m], b_ref[m])
    run = a_ref.shape[2]
    at = pl.multiple_of((place_ref[0] ^ pl.program_id(0)) * run, run)
    out_ref[pl.ds(at, run), :] = total.astype(bf16)


def weight_kernel(parts, has_below, a_ref, *refs):
    below = None
    if has_below:
        below, refs = refs[parts], refs[:parts] + refs[parts + 1 :]
    outs, b_ref = refs[parts:], refs[0]
    if parts > 1:
        outs, b_ref = refs[parts:-1], refs[-1]

        @pl.when(pl.program_id(0) == 0)
        def _():
            at = 0
            for ref in refs[:parts]:
                b_ref[:, :, at : at + ref.shape[2]] = ref[...]
                at += ref.shape[2]

    total = 0.0
    for m in range(a_ref.shape[0]):
        total = total + tn(a_ref[m], b_ref[m])
    total = total.astype(bf16)
    run = total.shape[0]
    for k, out in enumerate(outs):

        @pl.when(pl.program_id(0) == k)
        def _():
            out[0:run] = total
            if below is not None:
                out[run:] = below[...]


def normed_back_kernel(steps, gate_ref, val_ref, small_ref, *refs):
    gates, firsts, out_ref = refs[:steps], refs[steps:-1], refs[-1]
    gate, val, small = gate_ref[0], val_ref[0], small_ref[0]
    wide = val.shape[1]
    size = gates[0].shape[0]
    for k in range(steps):
        first = firsts[k]
        total = nt(gate, gates[k][...]) + nt(val, first[:, :wide]) + nt(small, first[:, wide:])
        out_ref[0, :, k * size : (k + 1) * size] = total.astype(bf16)


def grad_in_kernel(place_ref, sum_ref, key_ref, row_ref, x_ref, gain_ref, grad_ref, out_ref, d_unit):
    steps = gain_ref.shape[0]
    part = x_ref.shape[2] // steps
    x = x_ref[0].astype(f32)
    inv = lax.rsqrt(jnp.mean(x * x, axis=1, keepdims=True) + EPS)
    keys = jnp.concatenate([key_ref[h, 0] for h in range(key_ref.shape[0])], axis=0)
    total = 0.0
    for k in range(steps):
        at = slice(k * part, (k + 1) * part)
        of = pl.ds(pl.multiple_of((place_ref[0] ^ k) * part, LANES), part)
        d_here = sum_ref[0, :, at].astype(f32) + tn(keys, row_ref[:, at])
        d_here = d_here * gain_ref[k : k + 1]
        d_unit[:, of] = d_here
        total = total + jnp.sum(d_here * x_ref[0, :, of].astype(f32), axis=1, keepdims=True)
    shared = inv * inv * total * (1.0 / x.shape[1])
    out_ref[0] = (grad_ref[0].astype(f32) + inv * (d_unit[...] - x * shared)).astype(bf16)


def weight_grad_kernel(gate_ref, first_ref, w_ref, out_ref, sum_ref):
    heads, _, wide = gate_ref.shape
    rows = w_ref.shape[0]
    runs = wide // LANES
    total = jnp.zeros((rows, LANES), f32)

    def place(value, at):
        out_ref[:, at : at + value.shape[1]] = value
        return jnp.sum(value * w_ref[:, at : at + value.shape[1]].astype(f32), axis=1, keepdims=True)

    for ref, base in ((gate_ref, 0), (first_ref, D_INNER)):
        for h in range(heads):
            for b in range(runs):
                value = ref[h, :rows, lanes(b)].astype(f32)
                at = base + (b * heads + h) * LANES
                out_ref[:, at : at + LANES] = value
                total = total + value * w_ref[:, at : at + LANES].astype(f32)
    small = [first_ref[h, :rows, wide:].astype(f32) for h in range(heads)]
    per = 2 * STATE // heads
    keys = jnp.concatenate([x[:, 8 : 8 + per] for x in small], axis=1)
    sums = jnp.sum(total, axis=1, keepdims=True) + place(keys, 2 * D_INNER)
    steps = jnp.concatenate([x[:, :8] for x in small], axis=1).astype(bf16)
    per = 8 // runs
    of = lax.broadcasted_iota(jnp.int32, (HEADS, HEADS), 0)
    to = lax.broadcasted_iota(jnp.int32, (HEADS, HEADS), 1)
    source = (to // per % heads) * 8 + (to // (per * heads)) * per + to % per
    steps = nn(steps, (of == source).astype(f32).astype(bf16))
    sums = sums + place(steps, 2 * D_INNER + 2 * STATE)
    sum_ref[...] = jnp.broadcast_to(sums, (rows, LANES))


SMALL = (
    "conv_kernel",
    "conv_back_kernel",
    "key_conv_kernel",
    "key_back_kernel",
    "key_join_kernel",
    "glue_kernel",
    "mask_kernel",
    "pack_kernel",
    "unpack_kernel",
    "out_kernel",
    "weight_kernel",
    "rows_kernel",
    "grad_in_kernel",
    "weight_grad_kernel",
)
ABOUT_US = {
    "proj_kernel": 0,
    "fill_kernel": 9,
    "out_kernel": 0,
    "weight_kernel": 40,
    "rows_kernel": 0,
    "normed_back_kernel": 10,
    "bwd_kernel": 80,
    "fwd_kernel": 6,
    "norm_kernel": 5,
    "prep_kernel": 6,
    "conv_back_kernel": 10,
    "conv_kernel": 3,
    "grad_in_kernel": 30,
    "weight_grad_kernel": 10,
    "mask_kernel": 0,
    "pack_kernel": 0,
    "unpack_kernel": 0,
    "glue_kernel": 0,
    "key_conv_kernel": 1,
    "key_back_kernel": 5,
    "key_join_kernel": 60,
}


def kernel_call(kernel, grid, ins, outs, scratch=(), wait=(), us=None):
    name = getattr(kernel, "func", kernel).__name__
    us = ABOUT_US[name] if us is None else us
    specs = [
        pl.BlockSpec(memory_space=pltpu.SMEM) if block is None else pl.BlockSpec(block, index)
        for block, index in ins
    ]
    wait = jax.tree.leaves(wait)
    count = len(specs)
    specs = specs + [pl.BlockSpec(memory_space=pl.ANY)] * len(wait)

    def run(*refs):
        kernel(*refs[:count], *refs[count + len(wait) :])

    call = pl.pallas_call(
        run,
        grid=grid,
        in_specs=specs,
        out_specs=[pl.BlockSpec(block, index) for _, _, block, index in outs],
        out_shape=[jax.ShapeDtypeStruct(shape, dtype) for shape, dtype, _, _ in outs],
        scratch_shapes=list(scratch),
        compiler_params=pltpu.CompilerParams(
            vmem_limit_bytes=(32 if name in SMALL else 58) * 2**20, dimension_semantics=("arbitrary",) * len(grid)
        ),
        name=name,
        cost_estimate=pl.CostEstimate(flops=us * 2**30, bytes_accessed=us * 3 * 2**20, transcendentals=0),
    )
    return lambda *args: call(*args, *wait)


def fixed(m, c):
    return (0, 0)


def micro_call(kernel, micro, blocks, ins, outs, scratch=(), wait=()):
    shared = [block is None or index is fixed for block, index in ins]
    shared += [index is fixed or block[0] != 1 for _, _, block, index in outs]

    def whole(block, index):
        if block is None:
            return None, None
        if index is fixed:
            return block, lambda c: (0, 0)
        if block[0] != 1:
            return (block[0], micro) + block[2:], lambda c: index(0, c)
        return (micro,) + block[1:], lambda c: index(0, c)

    def run(*refs):
        for m in range(micro):
            views = [ref if one else ref.at[m : m + 1] for ref, one in zip(refs, shared)]
            kernel(m, *views, *[ref.at[m] for ref in refs[len(shared) :]])

    run.__name__ = getattr(kernel, "func", kernel).__name__
    return kernel_call(
        run,
        (blocks,),
        [whole(*spec) for spec in ins],
        [(shape, dtype) + whole(block, index) for shape, dtype, block, index in outs],
        [pltpu.VMEM((micro,) + shape, f32) for shape in scratch],
        wait,
    )


def body(
    hidden_in,
    seq_starts,
    norm_gain,
    in_weight,
    conv_weight,
    conv_bias,
    decay_log,
    dt_bias,
    skip_gain,
    gate_gain,
    out_weight,
    out_grad,
):
    seqs, heads = lax.axis_size("seq"), lax.axis_size("head")
    s_i, h_i = lax.axis_index("seq"), lax.axis_index("head")
    micro, tok, width = hidden_in.shape
    rows = in_weight.shape[0]
    shard = tok * heads
    runs = seqs if HEADS % (seqs * heads) == 0 else 1
    run_ch = D_INNER // (runs * heads)
    run_heads = HEADS // (runs * heads)
    chans, n_heads = runs * run_ch, runs * run_heads
    key_ch = 2 * STATE // heads
    wide = max(chans, LANES)

    def widen(x, axis=-1):
        pads = [(0, 0)] * x.ndim
        pads[axis] = (0, wide - chans)
        return jnp.pad(x, pads) if wide > chans else x

    conv_share, gate_share, head_share = conv_bias.shape[0], gate_gain.shape[0], decay_log.shape[0]

    def mine(x, size):
        lead = x.shape[:-1]
        x = x.reshape(lead + (runs, heads, size))
        x = lax.dynamic_index_in_dim(x, h_i, len(lead) + 1, False)
        return x.reshape(lead + (runs * size,))

    place = s_i[None].astype(jnp.int32)
    scalar = (None, None)
    forward = [(i, i + 1) for i in range(seqs - 1)]
    backward = [(i + 1, i) for i in range(seqs - 1)]
    swapped = runs == seqs
    if swapped and run_ch != LANES:
        raise ValueError("run width")

    def columns(x, size):
        x = x.reshape(rows, runs, heads, size)
        return jnp.transpose(x, (2, 0, 1, 3)).reshape(heads, rows, runs * size)

    def fill(x, axis, size):
        return jnp.pad(x, [(0, size - x.shape[axis] if i == axis else 0) for i in range(x.ndim)])

    val_p = fill(columns(in_weight[:, D_INNER : 2 * D_INNER], run_ch), 2, wide)
    step_p = fill(columns(in_weight[:, 2 * D_INNER + 2 * STATE :], run_heads), 2, 8)
    key_p = in_weight[:, 2 * D_INNER : 2 * D_INNER + 2 * STATE].reshape(rows, heads, key_ch)
    key_p = fill(jnp.swapaxes(key_p, 0, 1), 2, LANES - 8)
    gate_p = fill(columns(in_weight[:, :D_INNER], run_ch), 2, wide)
    first = head_swap(jnp.concatenate([val_p, step_p, key_p], axis=2)).reshape(heads * rows, -1)
    inputs = lax.all_gather(hidden_in, "head", axis=1, tiled=True)

    blocks = shard // SCAN_BLOCK
    by_micro = lambda *shape: ((1,) + shape, lambda m: (m,) + (0,) * len(shape))
    seg_rows, valid, valid_cols = kernel_call(
        mask_kernel,
        (micro,),
        [scalar, scalar],
        [
            ((micro, 8, shard), f32) + by_micro(8, shard),
            ((micro, 8, shard), f32) + by_micro(8, shard),
            ((micro, shard, LANES), f32) + by_micro(shard, LANES),
        ],
    )(place, seq_starts)


    every = seqs * heads
    linear = s_i * heads + h_i
    halo = lax.ppermute(hidden_in[:, tok - EDGE :], BOTH, [(i, i + 1) for i in range(every - 1)])
    taps = jnp.concatenate([conv_weight, conv_bias[None]], axis=0)
    heads_par = jnp.concatenate(three_parts(jnp.concatenate([decay_log, dt_bias, skip_gain])))
    key_rows_n = -(-key_ch // 8) * 8
    if swapped:
        window = jnp.zeros((CONV_K + 1, 2 * LANES), bf16)
        window = lax.dynamic_update_slice_in_dim(window, taps, (linear & 15) * 8, 1)
        sent = [fill(norm_gain, 0, LANES), gate_gain, fill(heads_par, 0, LANES), window.reshape(-1)]
    else:
        sent = [norm_gain, taps.reshape(-1), gate_gain, heads_par]
        sent.append(jnp.zeros((-sum(x.shape[0] for x in sent) % LANES,), bf16))
    sent = jnp.concatenate(sent)
    size = sent.shape[0]
    if swapped:
        sent = seq_gather(sent)
        w_out = seq_gather(after(out_weight, *sent))
        sent = after(jnp.concatenate(sent + [halo.reshape(-1)])[None], first, w_out)
        chips = heads // 2
        turns = [[(i, (i + 2 * k) % heads) for i in range(heads)] for k in range(1, chips)]
        sent = jnp.concatenate([sent] + [lax.ppermute(sent, "head", pairs) for pairs in turns], axis=0)
        other = lax.ppermute(sent, "head", [(i, i ^ 1) for i in range(heads)])
        sent = jnp.concatenate([sent, other], axis=0)
        first_row = (h_i >> 1) + (h_i & 1) * chips
    else:
        sent = lax.all_gather(sent, "seq").reshape(-1)
        sent = lax.all_gather(jnp.concatenate([sent, halo.reshape(-1)]), "head")
        first_row = 0
    halo = lax.dynamic_index_in_dim(sent, first_row, 0, False)[seqs * size :].reshape(halo.shape)
    halo = jnp.pad(halo, ((0, 0), (LANES - EDGE, 0), (0, 0)))
    first = seq_gather(first)
    if swapped:
        all_of = lambda shape: (shape, lambda m: (0,) * len(shape))
        outs = [(seqs, width // seqs), (8, wide), (8, wide), (key_ch, LANES), (8, LANES)]
        gain_steps, chan, conv_par, key_par, params = kernel_call(
            glue_kernel,
            (1,),
            [scalar, all_of((heads, seqs * size))],
            [(shape, f32) + all_of(shape) for shape in outs],
            [pltpu.VMEM((LANES, LANES), f32)],
            (first, seg_rows, gate_p, halo),
        )(jnp.stack([s_i, h_i]), sent)
    else:
        sent = jnp.swapaxes(sent[:, : seqs * size].reshape(heads, seqs, -1), 0, 1).reshape(every, -1)
        at = 0

        def take(count):
            nonlocal at
            at += count
            return sent[:, at - count : at]

        gain_steps = from_steps(take(rows).reshape(seqs, heads * rows), s_i).astype(f32)
        conv_p = take((CONV_K + 1) * conv_share).reshape(every, CONV_K + 1, conv_share)
        conv_p = jnp.transpose(conv_p, (1, 0, 2)).reshape(CONV_K + 1, CONV_CH).astype(f32)
        gate_g = mine(take(gate_share).reshape(D_INNER), run_ch).astype(f32)
        par = jnp.sum(take(9 * head_share)[:heads].astype(f32).reshape(heads, 3, 3, head_share), axis=1)
        par = mine(jnp.swapaxes(par, 0, 1).reshape(3, HEADS), run_heads)
        params = fill(fill(jnp.stack([par[1], -jnp.exp(par[0])], axis=1), 0, 8), 1, LANES)
        chan = fill(jnp.stack([widen(jnp.repeat(par[2], HEADDIM)), widen(gate_g)]), 0, 8)
        conv_par = fill(widen(mine(conv_p[:, :D_INNER], run_ch)), 0, 8)
        key_par = lax.dynamic_slice_in_dim(conv_p[:, D_INNER:], h_i * key_ch, key_ch, 1).T
        key_par = fill(fill(key_par, 0, key_rows_n), 1, LANES)

    tile = lambda m, c: (m, c, 0)
    second = head_swap(after(gate_p, first[0]))

    def project(x, size, wait=()):
        many = x.shape[1]
        return kernel_call(
            proj_kernel,
            (micro, many // size),
            [scalar, ((1, size, width), tile), (gain_steps.shape, fixed)] + [(first[0].shape, fixed)] * seqs,
            [
                ((micro, many, width), bf16, (1, size, width), tile),
                ((micro, many, wide + LANES), bf16, (1, size, wide + LANES), tile),
                ((micro, LANES, many), bf16, (1, LANES, size), lambda m, c: (m, 0, c)),
                ((key_ch, width), bf16, (key_ch, width), fixed),
            ],
            (),
            wait,
        )(place, x, gain_steps, *first)

    normed_low, proj, small_in, key_rows = project(inputs, min(shard, 512), (second,))
    _, proj_rim, small_rim, _ = project(halo, LANES)
    grad_rows = lax.all_gather(after(out_grad, proj), "head", axis=1, tiled=True)

    w_gate = seq_gather(second.reshape(heads * rows, wide))
    if not swapped:
        w_out = lax.all_gather(out_weight, BOTH, axis=0, tiled=True)
        w_out = [widen(lax.dynamic_slice_in_dim(w_out, h_i * chans, chans, 0), 0)]
    gate_specs = [(w_gate[0].shape, fixed)] * seqs
    out_specs = [(part.shape, fixed) for part in w_out]


    whole = ((1, shard, wide), lambda m: (m, 0, 0))
    conv_ins = [
        whole,
        ((1, 16, wide), lambda m: (m, LANES // 16 - 1, 0)),
        by_micro(shard, LANES),
        ((8, wide), lambda m: (0, 0)),
    ]
    key_ins = [
        by_micro(LANES, shard),
        by_micro(LANES, LANES),
        by_micro(8, shard),
        ((key_rows_n, LANES), lambda m: (0, 0)),
    ]
    vals = kernel_call(conv_kernel, (micro,), conv_ins, [((micro, shard, wide), bf16) + whole])(
        proj, proj_rim, valid_cols, conv_par
    )[0]
    keys = kernel_call(
        key_conv_kernel, (micro,), key_ins, [((micro, key_rows_n, shard), bf16) + by_micro(key_rows_n, shard)]
    )(small_in, small_rim, valid, key_par)[0]
    keys = keys[:, :key_ch]
    keys = lax.all_gather(keys, "head", axis=1, tiled=True)

    grid = (micro, blocks)
    size = SCAN_BLOCK
    here = lambda m, c: (m, c, 0)
    along = lambda m, c: (m, 0, c)
    state_at = lambda m, c: (m, c, 0, 0)
    micro_at = lambda m, c: (m, 0, 0)
    row8 = (1, 8, size)
    tok_c, tok_l = (1, size, wide), (1, size, LANES)
    n_state = STATE + 16
    f_state = ((1, 1, STATE, wide), state_at)
    f_pre = ((1, 1, 8, wide), state_at)
    cols, rows_t, ktok, starts, prefix, payload = micro_call(
        prep_kernel,
        micro,
        blocks,
        [((1, 16, size), along), (row8, along), ((8, LANES), fixed), (tok_c, here), ((1, 2 * STATE, size), along)],
        [
            ((micro, shard, LANES), f32, tok_l, here),
            ((micro, 32, shard), f32, (1, 32, size), along),
            ((micro, shard, 2 * STATE), bf16, (1, size, 2 * STATE), here),
            ((micro, blocks, STATE, wide), f32) + f_state,
            ((micro, blocks, 8, wide), f32) + f_pre,
            ((micro, n_state, wide), bf16, (1, n_state, wide), micro_at),
        ],
        [(STATE, wide), (8, wide)],
        w_gate,
    )(small_in, seg_rows, params, vals, keys)
    key_rows = lax.all_gather(after(key_rows, payload), "head")
    size = min(shard, 512)
    gate_in, d_ynorm = kernel_call(
        functools.partial(fill_kernel, seqs),
        (micro, shard // size),
        [((1, size, width), tile)] * 2 + gate_specs + out_specs,
        [((micro, shard, wide), f32, (1, size, wide), tile)] * 2,
        [pltpu.VMEM((wide, width), bf16)],
        (payload,),
    )(normed_low, grad_rows, *w_gate, *w_out)
    size = SCAN_BLOCK
    state_in = linked(payload, False, gate_in)
    mixer, sums = micro_call(
        functools.partial(fwd_kernel, swapped, seqs - 1),
        micro,
        blocks,
        [
            scalar,
            (tok_c, here),
            ((1, size, 2 * STATE), here),
            (tok_l, here),
            ((1, 32, size), along),
            f_state,
            f_pre,
            (tok_c, here),
            (tok_c, here),
            ((8, wide), fixed),
        ]
        + [((1, n_state, wide), micro_at)] * (seqs - 1),
        [((micro, shard, wide), bf16, tok_c, here), ((micro, 8, shard), f32, row8, along)],
        [(STATE, wide)],
    )(place, vals, ktok, cols, rows_t, starts, prefix, gate_in, d_ynorm, chan, *state_in)

    sums = fill(lax.psum(sums[:, :2], "head"), 1, 8)
    back_here = lambda m, c: (m, blocks - 1 - c, 0)
    back_along = lambda m, c: (m, 0, blocks - 1 - c)
    back_state = lambda m, c: (m, blocks - 1 - c, 0, 0)
    b_state, b_pre = (f_state[0], back_state), (f_pre[0], back_state)
    ynorm_low, d_mix, d_gate, block_adj, payload = micro_call(
        functools.partial(norm_kernel, swapped),
        micro,
        blocks,
        [
            scalar,
            (tok_c, back_here),
            (tok_c, back_here),
            (tok_c, back_here),
            (row8, back_along),
            (tok_l, back_here),
            ((1, 2 * STATE, size), back_along),
            b_pre,
            ((8, wide), fixed),
            ((1, 16, wide), lambda m, c: (m, STATE // 16, 0)),
        ],
        [
            ((micro, shard, wide), bf16, tok_c, back_here),
            ((micro, shard, wide), bf16, tok_c, back_here),
            ((micro, shard, wide), bf16, tok_c, back_here),
            ((micro, blocks, STATE, wide), f32) + b_state,
            ((micro, n_state, wide), bf16, (1, n_state, wide), micro_at),
        ],
        [(STATE, wide)],
        (key_rows,),
    )(place, mixer, gate_in, d_ynorm, sums, cols, keys, prefix, chan, payload)
    wide_tile = min(shard, 512)
    out_part = kernel_call(
        out_kernel,
        (micro, shard // wide_tile),
        [((1, wide_tile, wide), here)] + out_specs,
        [((micro, shard, width), bf16, (1, wide_tile, width), here)],
        [pltpu.VMEM((wide, width), bf16)],
    )(ynorm_low, *w_out)[0]
    out_sum = lax.psum_scatter(out_part, "head", scatter_dimension=1, tiled=True)

    def weight_parts(a, count, *b, below=None, wait=(), us=None):
        run = a.shape[2] // count
        wide_b = sum(x.shape[2] for x in b)
        extra = [] if below is None else [below]
        out = (run + sum(x.shape[0] for x in extra), wide_b)
        return kernel_call(
            functools.partial(weight_kernel, len(b), below is not None),
            (count,),
            [((micro, shard, run), lambda k: (0, 0, k))]
            + [(x.shape, lambda k: (0, 0, 0)) for x in b]
            + [(x.shape, lambda k: (0, 0)) for x in extra],
            [(out, bf16, out, lambda k: (0, 0))] * count,
            [pltpu.VMEM(b[0].shape[:2] + (wide_b,), bf16)] * (len(b) > 1),
            wait,
            us,
        )(a, *b, *extra)

    if swapped:
        out = (wide, width)
        grad_out_part = kernel_call(
            rows_kernel,
            (runs,),
            [
                scalar,
                ((micro, shard, run_ch), lambda k: (0, 0, k)),
                (grad_rows.shape, lambda k: (0, 0, 0)),
            ],
            [(out, bf16, out, lambda k: (0, 0))],
        )(place, ynorm_low, grad_rows)[0]
    else:
        grad_out_part = ()
    grad_w_gate = weight_parts(normed_low, seqs, d_gate, us=0)
    adj_in = linked(payload, True, out_part, grad_w_gate, grad_out_part)

    by_heads = key_ch % 16 == 0
    key_shape = (heads, micro, key_ch, shard) if by_heads else (1, micro, 2 * STATE, shard)
    d_vals, d_keys, d_step, head_g, skip_g = micro_call(
        functools.partial(bwd_kernel, seqs - 1),
        micro,
        blocks,
        [
            (tok_c, back_here),
            ((1, 2 * STATE, size), back_along),
            ((1, size, 2 * STATE), back_here),
            (tok_l, back_here),
            ((1, 32, size), back_along),
            b_state,
            b_pre,
            (tok_c, back_here),
            b_state,
            ((8, wide), fixed),
            ((8, LANES), fixed),
        ]
        + [((1, n_state, wide), micro_at)] * (2 * seqs - 2),
        [
            ((micro, shard, wide), bf16, tok_c, back_here),
            (key_shape, bf16, (key_shape[0], 1, key_shape[2], size), lambda m, c: (0, 0, 0, blocks - 1 - c)),
            ((micro, shard, LANES), bf16, tok_l, back_here),
            ((8, LANES), f32, (8, LANES), fixed),
            ((8, wide), f32, (8, wide), fixed),
        ],
        [(STATE, wide)] * 2,
    )(
        vals, keys, ktok, cols, rows_t, starts, prefix, d_mix, block_adj, chan, params, *state_in, *adj_in
    )
    by_head = lambda x: x.astype(bf16).reshape(heads, rows, -1)
    gate_parts = seq_exchange([after(part, adj_in) for part in grad_w_gate])
    g_gate = by_head(total_of(gate_parts))
    d_val_in, val_back, conv_val_g = kernel_call(
        conv_back_kernel,
        (micro,),
        [whole] + conv_ins,
        [
            ((micro, shard, wide), bf16) + whole,
            ((micro, 8, wide), f32, (1, 8, wide), lambda m: (m, 0, 0)),
            ((8, wide), f32, (8, wide), lambda m: (0, 0)),
        ],
        (),
        gate_parts[1:],
    )(d_vals, proj, proj_rim, valid_cols, conv_par)
    if not by_heads:
        d_keys = jnp.swapaxes(d_keys.reshape(micro, heads, key_ch, shard), 0, 1)
    d_keys = head_swap(d_keys)
    g_gate_own = head_swap(after(g_gate, d_keys))
    val_back = lax.ppermute(val_back, "seq", backward)
    rim_sum = d_val_in[:, shard - 16 :].astype(f32) + jnp.pad(val_back, ((0, 0), (8, 0), (0, 0)))
    d_val_in = lax.dynamic_update_slice_in_dim(d_val_in, rim_sum.astype(bf16), shard - 16, 1)

    d_keys = jnp.pad(d_keys, ((0, 0), (0, 0), (0, key_rows_n - key_ch), (0, 0)))
    d_key_in, key_back, conv_key_g = kernel_call(
        key_back_kernel,
        (micro,),
        [((heads, 1, key_rows_n, shard), lambda m: (0, m, 0, 0))] + key_ins,
        [
            ((micro, key_rows_n, shard), f32) + by_micro(key_rows_n, shard),
            ((micro, key_rows_n, LANES), f32) + by_micro(key_rows_n, LANES),
            ((8, LANES), f32, (8, LANES), lambda m: (0, 0)),
        ],
        [pltpu.VMEM((LANES, LANES), f32)],
    )(d_keys, small_in, small_rim, valid, key_par)
    key_back = lax.ppermute(key_back, "seq", backward)

    size = min(shard, 512)
    tile = lambda m, c: (m, c, 0)
    tile_c, tile_l, tile_w = ((1, size, n) for n in (wide, LANES, width))
    d_normed = kernel_call(
        functools.partial(normed_back_kernel, seqs),
        (micro, shard // size),
        [(tile_c, tile), (tile_c, tile), (tile_l, tile)] + gate_specs + [(first[0].shape, fixed)] * seqs,
        [((micro, shard, width), bf16, tile_w, tile)],
        (),
        (out_sum, d_key_in),
    )(d_gate, d_val_in, d_step, *w_gate, *first)[0]
    d_normed_sum = lax.psum_scatter(d_normed, "head", scatter_dimension=1, tiled=True)

    fixed1 = lambda m: (0, 0)
    blocks8 = [(8, wide), (8, LANES), (8, LANES), (8, wide)]
    packed = (8, wide + LANES)
    small = kernel_call(
        pack_kernel,
        (1,),
        [(block, fixed1) for block in blocks8],
        [(packed, f32, packed, fixed1)],
    )(conv_val_g, conv_key_g, head_g, skip_g)[0]
    small = seq_reduce([small] * seqs)

    d_key_in, d_small = kernel_call(
        key_join_kernel,
        (micro,),
        [by_micro(key_rows_n, shard), by_micro(key_rows_n, LANES), by_micro(shard, LANES)],
        [
            ((micro, key_rows_n, shard), bf16) + by_micro(key_rows_n, shard),
            ((micro, shard, LANES), bf16) + by_micro(shard, LANES),
        ],
        (),
        (g_gate_own,),
    )(d_key_in, key_back, d_step)
    d_key_in = d_key_in[:, :key_ch]
    g_first = weight_parts(normed_low, seqs, d_val_in, d_small)
    if swapped:
        grad_out_weight = lax.psum_scatter(
            grad_out_part, "seq", scatter_dimension=0, tiled=True
        ).astype(f32)
    else:
        full = dot("mtk,mtd->kd", ynorm_low, grad_rows).astype(bf16)[:chans]
        full = lax.dynamic_update_slice_in_dim(jnp.zeros((D_INNER, width), bf16), full, h_i * chans, 0)
        grad_out_weight = lax.psum_scatter(full, BOTH, scatter_dimension=0, tiled=True).astype(f32)
    d_key_in, small = after((d_key_in, small), g_first)
    key_own = jnp.transpose(d_key_in.reshape(micro, key_ch, heads, tok), (2, 0, 1, 3))
    count = key_own.size // heads
    key_n = -(-count // (8 * (wide + LANES))) * 8
    key_own = fill(key_own.reshape(heads, count), 1, key_n * (wide + LANES)).reshape(heads, key_n, -1)
    small = [jnp.broadcast_to(part[None], (heads,) + part.shape) for part in three_parts(small)[:2]]
    small = head_swap(after(jnp.concatenate(small + [key_own], axis=1), g_first))
    key_own = small[:, 16:].reshape(heads, -1)[:, :count].reshape(heads, micro, key_ch, tok)

    hidden_out = (hidden_in.astype(f32) + after(out_sum, g_first).astype(f32)).astype(bf16)
    gate_gg = jnp.sum(after(grad_out_weight, g_first) * out_weight.astype(f32), axis=1) / gate_gain.astype(f32)

    if swapped:
        conv_g, head_g = kernel_call(
            unpack_kernel,
            (1,),
            [scalar, ((heads, 16, wide + LANES), lambda m: (0, 0, 0))],
            [
                ((8, 2 * LANES), f32, (8, 2 * LANES), lambda m: (0, 0)),
                ((8, LANES), f32, (8, LANES), lambda m: (0, 0)),
            ],
            [pltpu.VMEM((heads, 8, wide + LANES), f32)],
        )(jnp.stack([s_i, h_i]), small)
        conv_g = conv_g[: CONV_K + 1, :conv_share]
        head_g = head_g[CONV_K + 1 :, :head_share]
    else:
        sums = small[:, :8].astype(f32) + small[:, 8:16].astype(f32)
        conv_g = jnp.concatenate(
            [sums[:, : CONV_K + 1, :chans], sums[:, : CONV_K + 1, wide : wide + key_ch]], axis=2
        )
        head_g = sums[:, CONV_K + 1 : CONV_K + 4, :n_heads].reshape(heads, 3, runs, run_heads)
        conv_gv = jnp.transpose(conv_g[:, :, :chans].reshape(heads, CONV_K + 1, runs, run_ch), (1, 2, 0, 3))
        conv_gk = jnp.transpose(conv_g[:, :, chans:], (1, 0, 2))
        conv_g = jnp.concatenate(
            [conv_gv.reshape(CONV_K + 1, D_INNER), conv_gk.reshape(CONV_K + 1, 2 * STATE)], axis=1
        )
        head_g = jnp.transpose(head_g, (1, 2, 0, 3)).reshape(3, HEADS)
        conv_g = lax.dynamic_slice_in_dim(conv_g, linear * conv_share, conv_share, 1)
        head_g = lax.dynamic_slice_in_dim(head_g, h_i * head_share, head_share, 1)
    g_first = by_head(seq_reduce(g_first))
    g_first = head_swap(after(g_first, conv_g, head_g, key_own))
    if swapped:
        own_at = lambda m: (m, 0, 0)
        own = (1, tok, width)
        flat = lambda m: (0, 0)
        steps = (seqs, width // seqs)
        grad_in = kernel_call(
            grad_in_kernel,
            (micro,),
            [
                scalar,
                (own, own_at),
                ((heads, 1, key_ch, tok), lambda m: (0, m, 0, 0)),
                ((2 * STATE, width), flat),
                (own, own_at),
                (steps, flat),
                (own, own_at),
            ],
            [((micro, tok, width), bf16, own, own_at)],
            [pltpu.VMEM((tok, width), f32)],
            (hidden_out, gate_gg),
        )(place, d_normed_sum, key_own, key_rows.reshape(2 * STATE, width), hidden_in, gain_steps, out_grad)[0]
        whole3 = lambda shape: (shape, lambda m: (0,) * len(shape))
        grad_in_weight, norm_sum = kernel_call(
            weight_grad_kernel,
            (1,),
            [whole3(g_gate_own.shape), whole3(g_first.shape), whole3(in_weight.shape)],
            [
                (in_weight.shape, f32) + whole3(in_weight.shape),
                ((rows, LANES), f32) + whole3((rows, LANES)),
            ],
            (),
            (grad_in,),
        )(g_gate_own, g_first, in_weight)
        norm_sum = norm_sum[:, 0]
    else:
        key_part = dot("hmct,hcd->mtd", key_own, key_rows)
        d_normed = (d_normed_sum.astype(f32) + key_part).reshape(micro, tok, seqs, -1)
        d_normed = from_steps(jnp.moveaxis(d_normed, 2, 0), s_i)
        d_normed = jnp.moveaxis(d_normed, 0, 2).reshape(micro, tok, width)
        own = hidden_in.astype(f32)
        own_inv = lax.rsqrt(jnp.mean(own * own, axis=-1, keepdims=True) + EPS)
        d_unit = d_normed * from_steps(gain_steps, s_i).reshape(-1)
        shared = own_inv * own_inv * jnp.mean(d_unit * own, axis=-1, keepdims=True)
        grad_in = (out_grad.astype(f32) + own_inv * (d_unit - own * shared)).astype(bf16)

        def uncolumns(x, size):
            x = x.astype(f32).reshape(heads, rows, runs, size)
            return jnp.transpose(x, (1, 2, 0, 3)).reshape(rows, runs * heads * size)

        g_key = jnp.transpose(g_first[:, :rows, wide + 8 : wide + 8 + key_ch], (1, 0, 2))
        grad_in_weight = jnp.concatenate(
            [
                uncolumns(g_gate_own[:, :rows, :chans], run_ch),
                uncolumns(g_first[:, :rows, :chans], run_ch),
                g_key.astype(f32).reshape(rows, -1),
                uncolumns(g_first[:, :rows, wide : wide + n_heads], run_heads),
            ],
            axis=1,
        )
        norm_sum = jnp.sum(grad_in_weight * in_weight.astype(f32), axis=1)
    norm_g = norm_sum / norm_gain.astype(f32)

    return (
        hidden_out,
        grad_in,
        norm_g,
        grad_in_weight,
        conv_g[:CONV_K],
        conv_g[CONV_K],
        head_g[0],
        head_g[1],
        head_g[2],
        gate_gg,
        grad_out_weight,
    )


def solution(mesh):
    tokens = P(None, BOTH, None)
    by_rows = P(BOTH, None)
    return jax.shard_map(
        body,
        mesh=mesh,
        in_specs=(
            tokens,
            P(),
            P(BOTH),
            by_rows,
            P(None, BOTH),
            P(BOTH),
            P("head"),
            P("head"),
            P("head"),
            P(BOTH),
            by_rows,
            tokens,
        ),
        out_specs=(
            tokens,
            tokens,
            P(BOTH),
            by_rows,
            P(None, BOTH),
            P(BOTH),
            P("head"),
            P("head"),
            P("head"),
            P(BOTH),
            by_rows,
        ),
        check_vma=False,
    )
```

```python
import functools

import jax
import jax.numpy as jnp
from jax import lax
from jax.experimental import pallas as pl
from jax.experimental.pallas import tpu as pltpu
from jax.sharding import PartitionSpec as P

HEADS = 64
HEADDIM = 64
STATE = 128
CONV_K = 4
SCAN_BLOCK = 256
D_INNER = 4096
CONV_CH = 4352
EDGE = CONV_K - 1
EPS = 1e-05

f32 = jnp.float32
bf16 = jnp.bfloat16
BOTH = ("seq", "head")


def dot(spec, a, b):
    return jnp.einsum(spec, a, b, preferred_element_type=f32)


def three_parts(v):
    parts = []
    for _ in range(3):
        part = lax.reduce_precision(v, 8, 7)
        parts.append(part.astype(bf16))
        v = v - part
    return parts


def linked(payload, back, *wait):
    count = lax.axis_size("seq")
    got = []
    for k in range(1, count):
        if back:
            pairs = [(i, i - k) for i in range(k, count)]
        else:
            pairs = [(i, i + k) for i in range(count - k)]
        got.append(after(lax.ppermute(payload, "seq", pairs), *wait))
    return got


def after(x, *others):
    return lax.optimization_barrier((x, others))[0]


def seq_steps():
    count = lax.axis_size("seq")
    return [(k, [(i, i ^ k) for i in range(count)]) for k in reversed(range(1, count))]


def seq_gather(x, *wait):
    got = [(k, lax.ppermute(x, "seq", pairs)) for k, pairs in seq_steps()]
    if wait:
        got = [(k, after(part, *wait)) for k, part in got]
    parts = dict(got)
    parts[0] = x
    return [parts[k] for k in sorted(parts)]


def seq_exchange(parts):
    return [parts[0]] + [lax.ppermute(parts[k], "seq", pairs) for k, pairs in seq_steps()]


def total_of(parts):
    return functools.reduce(lambda a, b: a + b, [part.astype(f32) for part in parts])


def seq_reduce(parts):
    return total_of(seq_exchange(parts))


def from_steps(x, place):
    return jnp.stack([lax.dynamic_index_in_dim(x, place ^ k, 0, False) for k in range(x.shape[0])])


def head_swap(x):
    return lax.all_to_all(x, "head", split_axis=0, concat_axis=0, tiled=True)


def silu_parts(v):
    sig = jax.nn.sigmoid(v)
    return v * sig, sig * (1.0 + v * (1.0 - sig))


LANES = 128
LOG, STEP, CARRY, TO_END, SEG = 0, 8, 16, 24, 32
SIG = 16
ROWS_SEG = 24


def nt(a, b):
    return lax.dot_general(a, b, (((1,), (1,)), ((), ())), preferred_element_type=f32)


def nn(a, b):
    return lax.dot_general(a, b, (((1,), (0,)), ((), ())), preferred_element_type=f32)


def tn(a, b):
    return lax.dot_general(a, b, (((0,), (0,)), ((), ())), preferred_element_type=f32)


def split(v):
    high = v.astype(bf16)
    return high, (v - high.astype(f32)).astype(bf16)


def left_half(shape):
    return lax.broadcasted_iota(jnp.int32, shape, len(shape) - 1) < HEADDIM


def pair_of(cols, base, p):
    at = base + 2 * p
    shape = (cols.shape[0], LANES)
    return jnp.where(
        left_half(shape),
        jnp.broadcast_to(cols[:, at : at + 1], shape),
        jnp.broadcast_to(cols[:, at + 1 : at + 2], shape),
    )


def running_sum(x, back=False):
    size = x.shape[1]
    lane = lax.broadcasted_iota(jnp.int32, x.shape, 1)
    shift = 1
    while shift < size:
        if back:
            x = x + jnp.where(lane < size - shift, pltpu.roll(x, size - shift, 1), 0.0)
        else:
            x = x + jnp.where(lane >= shift, pltpu.roll(x, shift, 1), 0.0)
        shift *= 2
    return x


def pairs_in(x):
    return x.shape[-1] // LANES


def lanes(p):
    return slice(p * LANES, (p + 1) * LANES)


def mask_kernel(place_ref, start_ref, seg_ref, valid_ref, cols_ref):
    m = pl.program_id(0)
    size = seg_ref.shape[2]
    at = place_ref[0] * size + lax.broadcasted_iota(jnp.int32, (1, size), 1)

    def seg_of(position):
        total = jnp.zeros((1, size), f32)
        for i in range(start_ref.shape[1]):
            total = total + jnp.where(position >= start_ref[m, i], 1.0, 0.0)
        return total

    seg = seg_of(at)
    behind = [seg_of(at - by) for by in range(1, CONV_K)]
    block = seg_of(at - at % SCAN_BLOCK - 1)
    first = jnp.where(seg == behind[0], 0.0, 1.0)
    seg_ref[0] = jnp.concatenate([seg, block, first, jnp.zeros((5, size), f32)], axis=0)
    rows = [jnp.where(seg == x, 1.0, 0.0) for x in reversed(behind)] + [jnp.ones((1, size), f32)]
    rows = jnp.concatenate(rows + [jnp.zeros((8 - CONV_K, size), f32)], axis=0)
    valid_ref[0] = rows
    cols_ref[0] = jnp.concatenate([rows, jnp.zeros((LANES - 8, size), f32)], axis=0).T


GAIN_AT, GATE_AT, HEAD_AT, CONV_AT, SENT = 0, 128, 256, 384, 384 + 256 * (CONV_K + 1)


def glue_kernel(place_ref, sent_ref, gain_ref, chan_ref, conv_ref, key_ref, par_ref, turned):
    s, h = place_ref[0], place_ref[1]
    heads = sent_ref.shape[0]
    seqs = gain_ref.shape[0]
    left = left_half((1, LANES))

    def from_head(row):
        chips = heads // 2
        return (h // 2 + chips - row % chips) % chips * 2 + (h % 2 ^ row // chips)

    row = from_head(lax.broadcasted_iota(jnp.int32, (heads, LANES), 0))

    def lanes_from(start):
        return sent_ref[:, start : start + LANES].astype(f32)

    for k in range(seqs):
        gains = lanes_from(k * SENT)
        for p in range(heads // 2):
            of_head = lambda i: jnp.sum(jnp.where(row == i, gains, 0.0), axis=0, keepdims=True)
            second = pltpu.roll(of_head(2 * p + 1), HEADDIM, 1)
            gain_ref[k : k + 1, lanes(p)] = jnp.where(left, of_head(2 * p), second)

    of = from_head(lax.broadcasted_iota(jnp.int32, (8, heads), 1))
    to = lax.broadcasted_iota(jnp.int32, (8, heads), 0)
    head = (to // 2 * heads + h) * 2 + to % 2
    sel = jnp.where(of == head // 8, 1.0, 0.0).astype(bf16)
    found = nn(sel, sent_ref[:, HEAD_AT : HEAD_AT + LANES])
    lane = lax.broadcasted_iota(jnp.int32, (8, LANES), 1)
    local = lax.broadcasted_iota(jnp.int32, (8, LANES), 0)
    place = (h * 2 + local % 2) % 8

    def param(q):
        keep = (lane % 24 == q * 8 + place) & (lane < 72)
        return jnp.sum(jnp.where(keep, found, 0.0), axis=1, keepdims=True)

    decay, bias, skip = param(0), param(1), param(2)
    par_ref[...] = jnp.where(lane == 0, bias, jnp.where(lane == 1, -jnp.exp(decay), 0.0))

    def run_of(r, tap):
        total = jnp.zeros((1, LANES), f32)
        for k in range(seqs):
            source = (s ^ k) * heads + row
            begins = source + source // 16
            base = k * SENT + CONV_AT + tap * 2 * LANES
            part = jnp.where(begins == r, lanes_from(base), 0.0)
            part = part + jnp.where(begins == r - 1, lanes_from(base + LANES), 0.0)
            total = total + jnp.sum(part, axis=0, keepdims=True)
        return total

    chan_ref[...] = jnp.zeros_like(chan_ref)
    conv_ref[...] = jnp.zeros_like(conv_ref)
    for b in range(seqs):
        chan_ref[0:1, lanes(b)] = jnp.where(left, skip[2 * b : 2 * b + 1], skip[2 * b + 1 : 2 * b + 2])
        start = pl.multiple_of((s ^ b) * SENT, LANES) + GATE_AT
        gates = sent_ref[:, pl.ds(pl.multiple_of(start, LANES), LANES)].astype(f32)
        chan_ref[1:2, lanes(b)] = gates[0:1]
        for tap in range(CONV_K + 1):
            conv_ref[tap : tap + 1, lanes(b)] = run_of(b * heads + h, tap)
    per = key_ref.shape[0]
    each = LANES // per
    taps = [run_of(seqs * heads + h // each, tap) for tap in range(CONV_K + 1)]
    turned[...] = jnp.concatenate(taps + [jnp.zeros((LANES - CONV_K - 1, LANES), f32)], axis=0).T
    key_ref[...] = turned[pl.ds(pl.multiple_of(h % each * per, 8), per), :]


def behind_lanes(x, rim, by):
    return pltpu.roll(jnp.concatenate([rim, x], axis=1), by, 1)[:, LANES:] if by else x


def key_conv_kernel(small_ref, rim_ref, valid_ref, par_ref, out_ref):
    count = par_ref.shape[0]
    x, rim = (ref[0].astype(f32)[8 : 8 + count] for ref in (small_ref, rim_ref))
    total = par_ref[:, CONV_K : CONV_K + 1]
    for k in range(CONV_K):
        total = total + par_ref[:, k : k + 1] * behind_lanes(x, rim, EDGE - k) * valid_ref[0, k : k + 1]
    out_ref[0] = (total / (1.0 + jnp.exp(-total))).astype(bf16)


def key_back_kernel(d_ref, small_ref, rim_ref, valid_ref, par_ref, in_ref, back_ref, grad_ref, total_grad):
    @pl.when(pl.program_id(0) == 0)
    def _():
        total_grad[...] = jnp.zeros_like(total_grad)

    count = par_ref.shape[0]
    x, rim = (ref[0].astype(f32)[8 : 8 + count] for ref in (small_ref, rim_ref))
    size = x.shape[1]
    total = par_ref[:, CONV_K : CONV_K + 1]
    seen = []
    for k in range(CONV_K):
        seen.append(behind_lanes(x, rim, EDGE - k) * valid_ref[0, k : k + 1])
        total = total + par_ref[:, k : k + 1] * seen[k]
    sig = 1.0 / (1.0 + jnp.exp(-total))
    d_keys = 0.0
    for h in range(d_ref.shape[0]):
        d_keys = d_keys + d_ref[h, 0].astype(f32)
    d_total = d_keys.astype(bf16).astype(f32) * (sig * (1.0 + total * (1.0 - sig)))
    lane = lax.broadcasted_iota(jnp.int32, (count, LANES), 1)
    ahead, d_in = 0.0, 0.0
    grads = jnp.where(lane == CONV_K, jnp.sum(d_total, axis=1, keepdims=True), 0.0)
    empty = jnp.zeros((count, LANES), f32)
    for k in range(CONV_K):
        grads = jnp.where(lane == k, jnp.sum(d_total * seen[k], axis=1, keepdims=True), grads)
        held = d_total * (par_ref[:, k : k + 1] * valid_ref[0, k : k + 1])
        by = EDGE - k
        wide = jnp.concatenate([empty, held], axis=1)
        moved = pltpu.roll(wide, size + LANES - by, 1) if by else wide
        ahead = ahead + moved[:, :LANES]
        if by:
            keep = lax.broadcasted_iota(jnp.int32, (count, size), 1) < size - by
            d_in = d_in + jnp.where(keep, moved[:, LANES:], 0.0)
        else:
            d_in = d_in + held
    in_ref[0] = d_in
    back_ref[0] = jnp.where(lane >= LANES - EDGE, ahead, 0.0)
    total_grad[0:count, :] += grads
    grad_ref[...] = total_grad[...].T[0:8]


def pack_kernel(conv_ref, key_ref, head_ref, skip_ref, out_ref):
    wide = conv_ref.shape[1]
    taps = CONV_K + 1
    out_ref[0:taps, :wide] = conv_ref[0:taps]
    out_ref[0:taps, wide:] = key_ref[0:taps]
    left = left_half((1, LANES))
    lane = lax.broadcasted_iota(jnp.int32, (1, LANES), 1)
    skips = jnp.zeros((1, LANES), f32)
    for p in range(wide // LANES):
        both = skip_ref[0:1, lanes(p)]
        first = jnp.sum(jnp.where(left, both, 0.0), axis=1, keepdims=True)
        second = jnp.sum(both, axis=1, keepdims=True) - first
        skips = jnp.where(lane == 2 * p, first, jnp.where(lane == 2 * p + 1, second, skips))
    heads = jnp.concatenate([head_ref[...], jnp.zeros((LANES - 8, LANES), f32)], axis=0).T
    out_ref[taps : taps + 2, :LANES] = heads[0:2]
    out_ref[taps + 2 : 8, :LANES] = skips
    out_ref[taps:8, LANES:] = jnp.zeros((8 - taps, wide), f32)


def unpack_kernel(place_ref, sums_ref, conv_ref, head_ref, total):
    s, h = place_ref[0], place_ref[1]
    heads = sums_ref.shape[0]
    wide = sums_ref.shape[2] - LANES
    for i in range(heads):
        both = sums_ref[i].astype(f32)
        total[i] = both[0:8] + both[8:16]
    linear = s * heads + h
    lane = lax.broadcasted_iota(jnp.int32, (8, LANES), 1)
    runs = wide // LANES
    per = 2 * STATE // heads

    def run(r):
        at = pl.multiple_of(((r // heads) & (runs - 1)) * LANES, LANES)
        vals = total[r & (heads - 1), :, pl.ds(at, LANES)]
        keys = jnp.zeros((8, LANES), f32)
        first = jnp.clip(r - runs * heads, 0, 2 * STATE // LANES - 1) * (LANES // per)
        for q in range(LANES // per):
            piece = jnp.where(lane < per, total[first + q, :, wide:], 0.0)
            keys = keys + (pltpu.roll(piece, per * q, 1) if q else piece)
        return jnp.where(r < runs * heads, vals, keys)

    begins = linear + linear // 16
    both = jnp.concatenate([run(begins), run(begins + 1)], axis=1)
    shift = (2 * LANES - (linear & 15) * 8) & (2 * LANES - 1)
    conv_ref[...] = pltpu.roll(both, shift, 1)
    out = jnp.zeros((8, LANES), f32)
    for j in range(heads // 2):
        mine = total[(h & 1) * (heads // 2) + j, :, 0:LANES]
        moved = pltpu.roll(mine, (2 * j + LANES - 2 * (h // 2)) & (LANES - 1), 1)
        out = jnp.where(lane // 2 == j, moved, out)
    head_ref[...] = out


def key_join_kernel(in_ref, back_ref, step_ref, key_ref, small_ref):
    x = in_ref[0]
    count, size = x.shape
    key = jnp.concatenate([x[:, : size - LANES], x[:, size - LANES :] + back_ref[0]], axis=1)
    key_ref[0] = key.astype(bf16)
    rows = [jnp.zeros((8, size), f32), key, jnp.zeros((LANES - 8 - count, size), f32)]
    cols = jnp.concatenate(rows, axis=0).T
    small_ref[0] = (cols + step_ref[0].astype(f32)).astype(bf16)


def chained(refs, at):
    total, reach = 0.0, 1.0
    for ref in refs:
        total = total + reach * ref[0, :STATE, at].astype(f32)
        reach = reach * ref[0, STATE : STATE + 16, at].astype(f32)[0:1]
    return total


def prep_kernel(
    m, step_ref, seg_ref, par_ref, val_ref, key_ref, cols_ref, rows_ref, ktok_ref, start_ref, pre_ref, out_ref, state, reach
):
    @pl.when(pl.program_id(0) == 0)
    def _():
        state[...] = jnp.zeros(state.shape, f32)
        reach[...] = jnp.ones(reach.shape, f32)

    raw = step_ref[0].astype(f32)[0:8] + par_ref[:, 0:1]
    small = jnp.exp(-jnp.abs(raw))
    one = 1.0 + small
    step = jnp.maximum(raw, 0.0) + jnp.where(
        one == 1.0, small, jnp.log(one) * (small / jnp.where(one == 1.0, 1.0, one - 1.0))
    )
    sig = jnp.where(raw >= 0.0, 1.0, small) / one
    log = running_sum(step * par_ref[:, 1:2])
    size = log.shape[1]
    segs = seg_ref[0]
    seg, prev = segs[0:1], segs[1:2]
    carry = jnp.where(seg == prev, jnp.exp(log), 0.0)
    to_end = jnp.where(
        seg == seg[:, size - 1 :], jnp.exp(jnp.minimum(log[:, size - 1 :] - log, 0.0)), 0.0
    )
    rows_ref[0] = jnp.concatenate([log, step, sig, segs], axis=0)
    stack = jnp.concatenate(
        [log, step, carry, to_end, segs, jnp.zeros((LANES - 40, size), f32)], axis=0
    )
    cols = stack.T
    cols_ref[0] = cols
    keys = key_ref[0]
    ktok_ref[0] = keys.astype(f32).T.astype(bf16)
    start_ref[0, 0] = state[...]
    pre_ref[0, 0] = reach[...]
    weight = cols[:, TO_END : TO_END + 8] * cols[:, STEP : STEP + 8]
    for p in range(pairs_in(val_ref)):
        ending = (val_ref[0, :, lanes(p)].astype(f32) * pair_of(weight, 0, p)).astype(bf16)
        decay = pair_of(cols[size - 1 :], CARRY, p)
        state[:, lanes(p)] = decay * state[:, lanes(p)] + nn(keys[:STATE], ending)
        reach[:, lanes(p)] = decay * reach[:, lanes(p)]
    out_ref[0] = jnp.concatenate([state[...], reach[...], reach[...]], axis=0).astype(bf16)


def same_mask(cols, rows):
    size = cols.shape[0]
    at = lax.broadcasted_iota(jnp.int32, (size, size), 0)
    of = lax.broadcasted_iota(jnp.int32, (size, size), 1)
    return (cols[:, SEG : SEG + 1] == rows[ROWS_SEG : ROWS_SEG + 1]) & (at >= of)


def within(cols, rows, j):
    return jnp.exp(jnp.minimum(cols[:, j : j + 1] - rows[j : j + 1], 0.0))


def step_lanes(place_ref, p, swapped):
    return pl.ds(pl.multiple_of((place_ref[0] ^ p) * LANES, LANES), LANES) if swapped else lanes(p)


def fwd_kernel(
    swapped, near, m, place_ref, val_ref, ktok_ref, cols_ref, rows_ref, start_ref, pre_ref, gate_ref, dy_ref, chan_ref, *refs
):
    in_refs, (mix_ref, sum_ref, in_ref) = refs[:near], refs[near:]

    @pl.when(pl.program_id(0) == 0)
    def _():
        for p in range(pairs_in(val_ref)):
            in_ref[:, lanes(p)] = chained(in_refs, lanes(p))

    cols, rows = cols_ref[0], rows_ref[0]
    rkey = ktok_ref[0, :, STATE:]
    scores = jnp.where(same_mask(cols, rows), nt(rkey, ktok_ref[0, :, :STATE]), 0.0)
    squares, products = 0.0, 0.0
    left = left_half((cols.shape[0], LANES))
    for p in range(pairs_in(val_ref)):
        at = lanes(p)
        vals = val_ref[0, :, at].astype(f32)
        stepped = vals * pair_of(cols, STEP, p)
        high, low = split(start_ref[0, 0, :, at] + pre_ref[0, 0, 0:1, at] * in_ref[:, at])
        mixed = pair_of(cols, CARRY, p) * (nn(rkey, high) + nn(rkey, low))
        weights = [(scores * within(cols, rows, 2 * p + half)).astype(bf16) for half in range(2)]
        held = [jnp.where(keep, stepped, 0.0).astype(bf16) for keep in (left, ~left)]
        mixed = mixed + nn(jnp.concatenate(weights, axis=1), jnp.concatenate(held, axis=0))
        mixed = (mixed + chan_ref[0:1, at] * vals).astype(bf16)
        mix_ref[0, :, at] = mixed
        gate = gate_ref[0, :, at]
        gated = mixed.astype(f32) * (gate / (1.0 + jnp.exp(-gate)))
        squares = squares + gated * gated
        products = products + gated * (dy_ref[0, :, step_lanes(place_ref, p, swapped)] * chan_ref[1:2, at])
    lane = lax.broadcasted_iota(jnp.int32, squares.shape, 1)
    sums = jnp.where(
        lane == 0,
        jnp.sum(squares, axis=1, keepdims=True),
        jnp.where(lane == 1, jnp.sum(products, axis=1, keepdims=True), 0.0),
    )
    sum_ref[0] = sums.T[0:8]


def norm_kernel(
    swapped, m, place_ref, mix_ref, gate_ref, dy_ref, sum_ref, cols_ref, key_ref, pre_ref, chan_ref, reach_ref,
    yn_ref, dmix_ref, dgate_ref, adj_ref, out_ref, adj
):
    @pl.when(pl.program_id(0) == 0)
    def _():
        adj[...] = jnp.zeros(adj.shape, f32)

    cols = cols_ref[0]
    size = cols.shape[0]
    rows = sum_ref[0]
    scale_row = lax.rsqrt(rows[0:1] * (1.0 / D_INNER) + EPS)
    pull_row = scale_row * scale_row * rows[1:2] * (1.0 / D_INNER)
    both = jnp.concatenate([scale_row, pull_row, jnp.zeros((LANES - 2, size), f32)], axis=0).T
    scale, pull = both[:, 0:1], both[:, 1:2]
    for p in range(pairs_in(mix_ref)):
        at = lanes(p)
        mixer = mix_ref[0, :, at].astype(f32)
        gate = gate_ref[0, :, at]
        sig = 1.0 / (1.0 + jnp.exp(-gate))
        act = gate * sig
        slope = sig * (1.0 + gate * (1.0 - sig))
        gated = mixer * act
        unit = gated * scale
        gain = chan_ref[1:2, at]
        step_at = step_lanes(place_ref, p, swapped)
        yn_ref[0, :, step_at] = (unit * gain).astype(bf16)
        d_y = dy_ref[0, :, step_at]
        d_gated = scale * (d_y * gain - gated * pull)
        d_mix = (d_gated * act).astype(bf16)
        dmix_ref[0, :, at] = d_mix
        dgate_ref[0, :, at] = (d_gated * mixer * slope).astype(bf16)
        carried = (d_mix.astype(f32) * pair_of(cols, CARRY, p)).astype(bf16)
        block = nn(key_ref[0, STATE:], carried)
        adj_ref[0, 0, :, at] = block
        adj[:, at] = pair_of(cols[size - 1 :], CARRY, p) * adj[:, at] + block
    reach = reach_ref[0]
    out_ref[0] = jnp.concatenate([adj[...].astype(bf16), reach], axis=0)


def bwd_kernel(
    near, m, val_ref, key_ref, ktok_ref, cols_ref, rows_ref, start_ref, pre_ref, dmix_ref, adj_ref, chan_ref, par_ref, *refs
):
    in_refs, adjin_refs, refs = refs[:near], refs[near : 2 * near], refs[2 * near :]
    dval_ref, dkey_ref, dstep_ref, head_ref, skip_ref, adj, in_ref = refs

    @pl.when(pl.program_id(0) == 0)
    def _():
        if m == 0:
            head_ref[...] = jnp.zeros_like(head_ref)
            skip_ref[...] = jnp.zeros_like(skip_ref)
        for p in range(pairs_in(val_ref)):
            in_ref[:, lanes(p)] = chained(in_refs, lanes(p))
            adj[:, lanes(p)] = chained(adjin_refs, lanes(p))

    cols, rows = cols_ref[0], rows_ref[0]
    size = cols.shape[0]
    wkey, rkey = ktok_ref[0, :, :STATE], ktok_ref[0, :, STATE:]
    same = same_mask(cols, rows)
    scores = jnp.where(same, nt(rkey, wkey), 0.0)
    both_scores = jnp.concatenate([scores, scores], axis=0)
    left = left_half((size, LANES))
    lane = lax.broadcasted_iota(jnp.int32, (size, LANES), 1)
    lane_row = lax.broadcasted_iota(jnp.int32, (1, LANES), 1)
    d_scores = jnp.zeros((size, size), f32)
    d_write = jnp.zeros((STATE, size), f32)
    d_read = jnp.zeros((STATE, size), f32)
    by_row = jnp.zeros((size, LANES), f32)
    last = jnp.zeros((1, LANES), f32)
    by_col = []

    def put(total, p, half, values, offset=0):
        where = lane if values.shape[0] == size else lane_row
        return jnp.where(where == offset + 2 * p + half, values, total)

    def halves_of(x):
        first = jnp.sum(jnp.where(left[: x.shape[0]], x, 0.0), axis=1, keepdims=True)
        return first, jnp.sum(x, axis=1, keepdims=True) - first

    for p in range(pairs_in(val_ref)):
        at = lanes(p)
        vals = val_ref[0, :, at].astype(f32)
        d_mix = dmix_ref[0, :, at]
        d_mix_f = d_mix.astype(f32)
        step = pair_of(cols, STEP, p)
        stepped_f = vals * step
        stepped = stepped_f.astype(bf16)
        carry = pair_of(cols, CARRY, p)
        state = start_ref[0, 0, :, at] + pre_ref[0, 0, 0:1, at] * in_ref[:, at]
        high, low = split(state)
        end = adj[:, at]
        end_low = end.astype(bf16)
        ending_f = stepped_f * pair_of(cols, TO_END, p)
        ending = ending_f.astype(bf16)
        carried_d = (d_mix_f * carry).astype(bf16)
        back = nn(wkey, end_low)
        d_stepped = pair_of(cols, TO_END, p) * back
        from_end = ending_f * back
        through = d_mix_f * carry * (nn(rkey, high) + nn(rkey, low)) - from_end
        decay = pair_of(cols[size - 1 :], CARRY, p)
        final = jnp.sum(from_end, axis=0, keepdims=True) + decay * jnp.sum(
            end * state, axis=0, keepdims=True
        )
        final = halves_of(final)
        through = halves_of(through)
        held = [jnp.where(keep, d_mix_f, 0.0).astype(bf16) for keep in (left, ~left)]
        held = jnp.concatenate(held, axis=0)
        near = jnp.concatenate([within(cols, rows, 2 * p), within(cols, rows, 2 * p + 1)], axis=0)
        d_near = nt(held, stepped) * near
        d_scores = d_scores + (d_near[:size] + d_near[size:])
        pairs = d_near * both_scores
        row_sums = jnp.sum(pairs, axis=1, keepdims=True)
        for half in range(2):
            mine = slice(half * size, (half + 1) * size)
            by_row = put(by_row, p, half, row_sums[mine] + through[half])
            by_col.append(jnp.sum(pairs[mine], axis=0, keepdims=True))
            last = put(last, p, half, final[half])
        d_stepped = d_stepped + tn((both_scores * near).astype(bf16), held)
        d_vals = step * d_stepped + chan_ref[0:1, at] * d_mix_f
        dval_ref[0, :, at] = d_vals.astype(bf16)
        skip_ref[0:1, at] += jnp.sum(d_mix_f * vals, axis=0, keepdims=True)
        d_step = halves_of(vals * d_stepped)
        for half in range(2):
            by_row = put(by_row, p, half, d_step[half], 8)
        d_write = d_write + nt(end_low, ending)
        d_read = d_read + nt(high, carried_d) + nt(low, carried_d)
        adj[:, at] = decay * end + adj_ref[0, 0, :, at]
    d_scores = jnp.where(same, d_scores, 0.0).astype(bf16)
    d_write = d_write + nn(key_ref[0, STATE:], d_scores)
    d_read = d_read + nt(key_ref[0, :STATE], d_scores)
    d_keys = jnp.concatenate([d_write, d_read], axis=0).astype(bf16)
    each = dkey_ref.shape[2]
    for h in range(dkey_ref.shape[0]):
        dkey_ref[h, m] = d_keys[h * each : (h + 1) * each]
    while len(by_col) < 8:
        by_col.append(jnp.zeros((1, size), f32))
    turned = by_row.T
    last = jnp.broadcast_to(last, (LANES, LANES)).T[0:8, 0:1]
    d_log = turned[0:8] - jnp.concatenate(by_col, axis=0)
    rate = par_ref[:, 1:2]
    first = rows[ROWS_SEG + 2 : ROWS_SEG + 3]
    d_decay = (running_sum(d_log, True) + last) * (1.0 - first)
    d_raw = (turned[8:16] + d_decay * rate) * rows[SIG : SIG + 8]
    dstep_ref[0] = jnp.concatenate([d_raw, jnp.zeros((LANES - 8, size), f32)], axis=0).T.astype(bf16)
    head_lane = lax.broadcasted_iota(jnp.int32, (8, LANES), 1)
    head_ref[...] += jnp.where(
        head_lane == 0,
        jnp.sum(d_decay * rows[STEP : STEP + 8], axis=1, keepdims=True) * rate,
        jnp.where(head_lane == 1, jnp.sum(d_raw, axis=1, keepdims=True), 0.0),
    )


def shifted(x, rim, by):
    if by == 0:
        return x
    head = jnp.concatenate([rim, x[:8]], axis=0)[8 - by : 16 - by]
    return jnp.concatenate([head, pltpu.roll(x, by, 0)[8:]], axis=0)


def conv_kernel(val_ref, rim_ref, valid_ref, par_ref, out_ref):
    shape = (val_ref.shape[1], LANES)
    valid = [jnp.broadcast_to(valid_ref[0, :, k : k + 1], shape) for k in range(CONV_K)]
    for p in range(pairs_in(out_ref)):
        at = lanes(p)
        x = val_ref[0, :, at].astype(f32)
        rim = rim_ref[0, :, at].astype(f32)[8:16]
        total = par_ref[CONV_K : CONV_K + 1, at]
        for k in range(CONV_K):
            total = total + par_ref[k : k + 1, at] * shifted(x, rim, EDGE - k) * valid[k]
        out_ref[0, :, at] = (total / (1.0 + jnp.exp(-total))).astype(bf16)


def conv_back_kernel(d_ref, val_ref, rim_ref, valid_ref, par_ref, in_ref, back_ref, grad_ref):
    @pl.when(pl.program_id(0) == 0)
    def _():
        grad_ref[...] = jnp.zeros_like(grad_ref)

    size = val_ref.shape[1]
    row = lax.broadcasted_iota(jnp.int32, (size, LANES), 0)
    zeros = jnp.zeros((8, LANES), f32)
    valid = [jnp.broadcast_to(valid_ref[0, :, k : k + 1], (size, LANES)) for k in range(CONV_K)]
    for p in range(pairs_in(d_ref)):
        at = lanes(p)
        x = val_ref[0, :, at].astype(f32)
        rim = rim_ref[0, :, at].astype(f32)[8:16]
        total = par_ref[CONV_K : CONV_K + 1, at]
        seen = []
        for k in range(CONV_K):
            seen.append(shifted(x, rim, EDGE - k) * valid[k])
            total = total + par_ref[k : k + 1, at] * seen[k]
        sig = 1.0 / (1.0 + jnp.exp(-total))
        d_total = d_ref[0, :, at].astype(f32) * (sig * (1.0 + total * (1.0 - sig)))
        grad_ref[CONV_K : CONV_K + 1, at] += jnp.sum(d_total, axis=0, keepdims=True)
        d_in, back = 0.0, 0.0
        for k in range(CONV_K):
            grad_ref[k : k + 1, at] += jnp.sum(d_total * seen[k], axis=0, keepdims=True)
            held = d_total * (par_ref[k : k + 1, at] * valid[k])
            by = EDGE - k
            if by:
                d_in = d_in + jnp.where(row < size - by, pltpu.roll(held, size - by, 0), 0.0)
                back = back + jnp.concatenate([zeros, held[:8]], axis=0)[by : by + 8]
            else:
                d_in = d_in + held
        in_ref[0, :, at] = d_in.astype(bf16)
        back_ref[0, :, at] = back


def proj_kernel(place_ref, x_ref, gain_ref, *refs):
    parts, (low_ref, out_ref, small_ref, weight_ref) = refs[:-4], refs[-4:]
    wide = parts[0].shape[1] - LANES
    size = parts[0].shape[0]

    @pl.when((pl.program_id(0) == 0) & (pl.program_id(1) == 0))
    def _():
        for k, part in enumerate(parts):
            turned = part[:, wide:].astype(f32).T
            at = slice(8, 8 + weight_ref.shape[0])
            weight_ref[:, k * size : (k + 1) * size] = turned[at].astype(bf16)

    x = x_ref[0].astype(f32)
    inv = lax.rsqrt(jnp.mean(x * x, axis=1, keepdims=True) + EPS)
    total = 0.0
    for k, part in enumerate(parts):
        at = pl.ds(pl.multiple_of((place_ref[0] ^ k) * size, LANES), size)
        low = (x_ref[0, :, at].astype(f32) * inv * gain_ref[k : k + 1]).astype(bf16)
        low_ref[0, :, k * size : (k + 1) * size] = low
        total = total + nn(low, part[...])
    out_ref[0] = total.astype(bf16)
    small_ref[0] = total[:, wide:].T.astype(bf16)


def gather_runs(parts, whole):
    run = parts[0].shape[0]

    @pl.when((pl.program_id(0) == 0) & (pl.program_id(1) == 0))
    def _():
        for r, part in enumerate(parts):
            whole[r * run : (r + 1) * run] = part[...]


def fill_kernel(steps, x_ref, grad_ref, *refs):
    gates, outs, (gate_ref, dy_ref, whole) = refs[:steps], refs[steps:-3], refs[-3:]
    gather_runs(outs, whole)
    size = gates[0].shape[0]
    total = 0.0
    for k, part in enumerate(gates):
        total = total + nn(x_ref[0, :, k * size : (k + 1) * size], part[...])
    gate_ref[0] = total
    dy_ref[0] = nt(grad_ref[0], whole[...])


def out_kernel(y_ref, *refs):
    parts, (out_ref, whole) = refs[:-2], refs[-2:]
    gather_runs(parts, whole)
    width = out_ref.shape[2]
    size = min(width, 512)
    for n in range(width // size):
        at = slice(n * size, (n + 1) * size)
        out_ref[0, :, at] = nn(y_ref[0], whole[:, at]).astype(bf16)


def rows_kernel(place_ref, a_ref, b_ref, out_ref):
    total = 0.0
    for m in range(a_ref.shape[0]):
        total = total + tn(a_ref[m], b_ref[m])
    run = a_ref.shape[2]
    at = pl.multiple_of((place_ref[0] ^ pl.program_id(0)) * run, run)
    out_ref[pl.ds(at, run), :] = total.astype(bf16)


def weight_kernel(parts, has_below, a_ref, *refs):
    below = None
    if has_below:
        below, refs = refs[parts], refs[:parts] + refs[parts + 1 :]
    outs, b_ref = refs[parts:], refs[0]
    if parts > 1:
        outs, b_ref = refs[parts:-1], refs[-1]

        @pl.when(pl.program_id(0) == 0)
        def _():
            at = 0
            for ref in refs[:parts]:
                b_ref[:, :, at : at + ref.shape[2]] = ref[...]
                at += ref.shape[2]

    total = 0.0
    for m in range(a_ref.shape[0]):
        total = total + tn(a_ref[m], b_ref[m])
    total = total.astype(bf16)
    run = total.shape[0]
    for k, out in enumerate(outs):

        @pl.when(pl.program_id(0) == k)
        def _():
            out[0:run] = total
            if below is not None:
                out[run:] = below[...]


def normed_back_kernel(steps, gate_ref, val_ref, small_ref, *refs):
    gates, firsts, out_ref = refs[:steps], refs[steps:-1], refs[-1]
    gate, val, small = gate_ref[0], val_ref[0], small_ref[0]
    wide = val.shape[1]
    size = gates[0].shape[0]
    for k in range(steps):
        first = firsts[k]
        total = nt(gate, gates[k][...]) + nt(val, first[:, :wide]) + nt(small, first[:, wide:])
        out_ref[0, :, k * size : (k + 1) * size] = total.astype(bf16)


def grad_in_kernel(place_ref, sum_ref, key_ref, row_ref, x_ref, gain_ref, grad_ref, out_ref, d_unit):
    steps = gain_ref.shape[0]
    part = x_ref.shape[2] // steps
    x = x_ref[0].astype(f32)
    inv = lax.rsqrt(jnp.mean(x * x, axis=1, keepdims=True) + EPS)
    keys = jnp.concatenate([key_ref[h, 0] for h in range(key_ref.shape[0])], axis=0)
    total = 0.0
    for k in range(steps):
        at = slice(k * part, (k + 1) * part)
        of = pl.ds(pl.multiple_of((place_ref[0] ^ k) * part, LANES), part)
        d_here = sum_ref[0, :, at].astype(f32) + tn(keys, row_ref[:, at])
        d_here = d_here * gain_ref[k : k + 1]
        d_unit[:, of] = d_here
        total = total + jnp.sum(d_here * x_ref[0, :, of].astype(f32), axis=1, keepdims=True)
    shared = inv * inv * total * (1.0 / x.shape[1])
    out_ref[0] = (grad_ref[0].astype(f32) + inv * (d_unit[...] - x * shared)).astype(bf16)


def weight_grad_kernel(gate_ref, first_ref, w_ref, out_ref, sum_ref):
    heads, _, wide = gate_ref.shape
    rows = w_ref.shape[0]
    runs = wide // LANES
    total = jnp.zeros((rows, LANES), f32)

    def place(value, at):
        out_ref[:, at : at + value.shape[1]] = value
        return jnp.sum(value * w_ref[:, at : at + value.shape[1]].astype(f32), axis=1, keepdims=True)

    for ref, base in ((gate_ref, 0), (first_ref, D_INNER)):
        for h in range(heads):
            for b in range(runs):
                value = ref[h, :rows, lanes(b)].astype(f32)
                at = base + (b * heads + h) * LANES
                out_ref[:, at : at + LANES] = value
                total = total + value * w_ref[:, at : at + LANES].astype(f32)
    small = [first_ref[h, :rows, wide:].astype(f32) for h in range(heads)]
    per = 2 * STATE // heads
    keys = jnp.concatenate([x[:, 8 : 8 + per] for x in small], axis=1)
    sums = jnp.sum(total, axis=1, keepdims=True) + place(keys, 2 * D_INNER)
    steps = jnp.concatenate([x[:, :8] for x in small], axis=1).astype(bf16)
    per = 8 // runs
    of = lax.broadcasted_iota(jnp.int32, (HEADS, HEADS), 0)
    to = lax.broadcasted_iota(jnp.int32, (HEADS, HEADS), 1)
    source = (to // per % heads) * 8 + (to // (per * heads)) * per + to % per
    steps = nn(steps, (of == source).astype(f32).astype(bf16))
    sums = sums + place(steps, 2 * D_INNER + 2 * STATE)
    sum_ref[...] = jnp.broadcast_to(sums, (rows, LANES))


SMALL = (
    "conv_kernel",
    "conv_back_kernel",
    "key_conv_kernel",
    "key_back_kernel",
    "key_join_kernel",
    "glue_kernel",
    "mask_kernel",
    "pack_kernel",
    "unpack_kernel",
    "out_kernel",
    "weight_kernel",
    "rows_kernel",
    "grad_in_kernel",
    "weight_grad_kernel",
)
ABOUT_US = {
    "proj_kernel": 0,
    "fill_kernel": 9,
    "out_kernel": 0,
    "weight_kernel": 40,
    "rows_kernel": 0,
    "normed_back_kernel": 10,
    "bwd_kernel": 80,
    "fwd_kernel": 6,
    "norm_kernel": 5,
    "prep_kernel": 6,
    "conv_back_kernel": 10,
    "conv_kernel": 3,
    "grad_in_kernel": 30,
    "weight_grad_kernel": 10,
    "mask_kernel": 0,
    "pack_kernel": 0,
    "unpack_kernel": 0,
    "glue_kernel": 0,
    "key_conv_kernel": 1,
    "key_back_kernel": 5,
    "key_join_kernel": 60,
}


def kernel_call(kernel, grid, ins, outs, scratch=(), wait=(), us=None):
    name = getattr(kernel, "func", kernel).__name__
    us = ABOUT_US[name] if us is None else us
    specs = [
        pl.BlockSpec(memory_space=pltpu.SMEM) if block is None else pl.BlockSpec(block, index)
        for block, index in ins
    ]
    wait = jax.tree.leaves(wait)
    count = len(specs)
    specs = specs + [pl.BlockSpec(memory_space=pl.ANY)] * len(wait)

    def run(*refs):
        kernel(*refs[:count], *refs[count + len(wait) :])

    call = pl.pallas_call(
        run,
        grid=grid,
        in_specs=specs,
        out_specs=[pl.BlockSpec(block, index) for _, _, block, index in outs],
        out_shape=[jax.ShapeDtypeStruct(shape, dtype) for shape, dtype, _, _ in outs],
        scratch_shapes=list(scratch),
        compiler_params=pltpu.CompilerParams(
            vmem_limit_bytes=(32 if name in SMALL else 58) * 2**20, dimension_semantics=("arbitrary",) * len(grid)
        ),
        name=name,
        cost_estimate=pl.CostEstimate(flops=us * 2**30, bytes_accessed=us * 3 * 2**20, transcendentals=0),
    )
    return lambda *args: call(*args, *wait)


def fixed(m, c):
    return (0, 0)


def micro_call(kernel, micro, blocks, ins, outs, scratch=(), wait=()):
    shared = [block is None or index is fixed for block, index in ins]
    shared += [index is fixed or block[0] != 1 for _, _, block, index in outs]

    def whole(block, index):
        if block is None:
            return None, None
        if index is fixed:
            return block, lambda c: (0, 0)
        if block[0] != 1:
            return (block[0], micro) + block[2:], lambda c: index(0, c)
        return (micro,) + block[1:], lambda c: index(0, c)

    def run(*refs):
        for m in range(micro):
            views = [ref if one else ref.at[m : m + 1] for ref, one in zip(refs, shared)]
            kernel(m, *views, *[ref.at[m] for ref in refs[len(shared) :]])

    run.__name__ = getattr(kernel, "func", kernel).__name__
    return kernel_call(
        run,
        (blocks,),
        [whole(*spec) for spec in ins],
        [(shape, dtype) + whole(block, index) for shape, dtype, block, index in outs],
        [pltpu.VMEM((micro,) + shape, f32) for shape in scratch],
        wait,
    )


def body(
    hidden_in,
    seq_starts,
    norm_gain,
    in_weight,
    conv_weight,
    conv_bias,
    decay_log,
    dt_bias,
    skip_gain,
    gate_gain,
    out_weight,
    out_grad,
):
    seqs, heads = lax.axis_size("seq"), lax.axis_size("head")
    s_i, h_i = lax.axis_index("seq"), lax.axis_index("head")
    micro, tok, width = hidden_in.shape
    rows = in_weight.shape[0]
    shard = tok * heads
    runs = seqs if HEADS % (seqs * heads) == 0 else 1
    run_ch = D_INNER // (runs * heads)
    run_heads = HEADS // (runs * heads)
    chans, n_heads = runs * run_ch, runs * run_heads
    key_ch = 2 * STATE // heads
    wide = max(chans, LANES)

    def widen(x, axis=-1):
        pads = [(0, 0)] * x.ndim
        pads[axis] = (0, wide - chans)
        return jnp.pad(x, pads) if wide > chans else x

    conv_share, gate_share, head_share = conv_bias.shape[0], gate_gain.shape[0], decay_log.shape[0]

    def mine(x, size):
        lead = x.shape[:-1]
        x = x.reshape(lead + (runs, heads, size))
        x = lax.dynamic_index_in_dim(x, h_i, len(lead) + 1, False)
        return x.reshape(lead + (runs * size,))

    place = s_i[None].astype(jnp.int32)
    scalar = (None, None)
    forward = [(i, i + 1) for i in range(seqs - 1)]
    backward = [(i + 1, i) for i in range(seqs - 1)]
    swapped = runs == seqs
    if swapped and run_ch != LANES:
        raise ValueError("run width")

    def columns(x, size):
        x = x.reshape(rows, runs, heads, size)
        return jnp.transpose(x, (2, 0, 1, 3)).reshape(heads, rows, runs * size)

    def fill(x, axis, size):
        return jnp.pad(x, [(0, size - x.shape[axis] if i == axis else 0) for i in range(x.ndim)])

    val_p = fill(columns(in_weight[:, D_INNER : 2 * D_INNER], run_ch), 2, wide)
    step_p = fill(columns(in_weight[:, 2 * D_INNER + 2 * STATE :], run_heads), 2, 8)
    key_p = in_weight[:, 2 * D_INNER : 2 * D_INNER + 2 * STATE].reshape(rows, heads, key_ch)
    key_p = fill(jnp.swapaxes(key_p, 0, 1), 2, LANES - 8)
    gate_p = fill(columns(in_weight[:, :D_INNER], run_ch), 2, wide)
    first = head_swap(jnp.concatenate([val_p, step_p, key_p], axis=2)).reshape(heads * rows, -1)
    inputs = lax.all_gather(hidden_in, "head", axis=1, tiled=True)

    blocks = shard // SCAN_BLOCK
    by_micro = lambda *shape: ((1,) + shape, lambda m: (m,) + (0,) * len(shape))
    seg_rows, valid, valid_cols = kernel_call(
        mask_kernel,
        (micro,),
        [scalar, scalar],
        [
            ((micro, 8, shard), f32) + by_micro(8, shard),
            ((micro, 8, shard), f32) + by_micro(8, shard),
            ((micro, shard, LANES), f32) + by_micro(shard, LANES),
        ],
    )(place, seq_starts)


    every = seqs * heads
    linear = s_i * heads + h_i
    halo = lax.ppermute(hidden_in[:, tok - EDGE :], BOTH, [(i, i + 1) for i in range(every - 1)])
    taps = jnp.concatenate([conv_weight, conv_bias[None]], axis=0)
    heads_par = jnp.concatenate(three_parts(jnp.concatenate([decay_log, dt_bias, skip_gain])))
    key_rows_n = -(-key_ch // 8) * 8
    if swapped:
        window = jnp.zeros((CONV_K + 1, 2 * LANES), bf16)
        window = lax.dynamic_update_slice_in_dim(window, taps, (linear & 15) * 8, 1)
        sent = [fill(norm_gain, 0, LANES), gate_gain, fill(heads_par, 0, LANES), window.reshape(-1)]
    else:
        sent = [norm_gain, taps.reshape(-1), gate_gain, heads_par]
        sent.append(jnp.zeros((-sum(x.shape[0] for x in sent) % LANES,), bf16))
    sent = jnp.concatenate(sent)
    size = sent.shape[0]
    if swapped:
        sent = seq_gather(sent)
        w_out = seq_gather(after(out_weight, *sent))
        sent = after(jnp.concatenate(sent + [halo.reshape(-1)])[None], first, w_out)
        chips = heads // 2
        turns = [[(i, (i + 2 * k) % heads) for i in range(heads)] for k in range(1, chips)]
        sent = jnp.concatenate([sent] + [lax.ppermute(sent, "head", pairs) for pairs in turns], axis=0)
        other = lax.ppermute(sent, "head", [(i, i ^ 1) for i in range(heads)])
        sent = jnp.concatenate([sent, other], axis=0)
        first_row = (h_i >> 1) + (h_i & 1) * chips
    else:
        sent = lax.all_gather(sent, "seq").reshape(-1)
        sent = lax.all_gather(jnp.concatenate([sent, halo.reshape(-1)]), "head")
        first_row = 0
    halo = lax.dynamic_index_in_dim(sent, first_row, 0, False)[seqs * size :].reshape(halo.shape)
    halo = jnp.pad(halo, ((0, 0), (LANES - EDGE, 0), (0, 0)))
    first = seq_gather(first)
    if swapped:
        all_of = lambda shape: (shape, lambda m: (0,) * len(shape))
        outs = [(seqs, width // seqs), (8, wide), (8, wide), (key_ch, LANES), (8, LANES)]
        gain_steps, chan, conv_par, key_par, params = kernel_call(
            glue_kernel,
            (1,),
            [scalar, all_of((heads, seqs * size))],
            [(shape, f32) + all_of(shape) for shape in outs],
            [pltpu.VMEM((LANES, LANES), f32)],
            (first, seg_rows, gate_p, halo),
        )(jnp.stack([s_i, h_i]), sent)
    else:
        sent = jnp.swapaxes(sent[:, : seqs * size].reshape(heads, seqs, -1), 0, 1).reshape(every, -1)
        at = 0

        def take(count):
            nonlocal at
            at += count
            return sent[:, at - count : at]

        gain_steps = from_steps(take(rows).reshape(seqs, heads * rows), s_i).astype(f32)
        conv_p = take((CONV_K + 1) * conv_share).reshape(every, CONV_K + 1, conv_share)
        conv_p = jnp.transpose(conv_p, (1, 0, 2)).reshape(CONV_K + 1, CONV_CH).astype(f32)
        gate_g = mine(take(gate_share).reshape(D_INNER), run_ch).astype(f32)
        par = jnp.sum(take(9 * head_share)[:heads].astype(f32).reshape(heads, 3, 3, head_share), axis=1)
        par = mine(jnp.swapaxes(par, 0, 1).reshape(3, HEADS), run_heads)
        params = fill(fill(jnp.stack([par[1], -jnp.exp(par[0])], axis=1), 0, 8), 1, LANES)
        chan = fill(jnp.stack([widen(jnp.repeat(par[2], HEADDIM)), widen(gate_g)]), 0, 8)
        conv_par = fill(widen(mine(conv_p[:, :D_INNER], run_ch)), 0, 8)
        key_par = lax.dynamic_slice_in_dim(conv_p[:, D_INNER:], h_i * key_ch, key_ch, 1).T
        key_par = fill(fill(key_par, 0, key_rows_n), 1, LANES)

    tile = lambda m, c: (m, c, 0)
    second = head_swap(after(gate_p, first[0]))

    def project(x, size, wait=()):
        many = x.shape[1]
        return kernel_call(
            proj_kernel,
            (micro, many // size),
            [scalar, ((1, size, width), tile), (gain_steps.shape, fixed)] + [(first[0].shape, fixed)] * seqs,
            [
                ((micro, many, width), bf16, (1, size, width), tile),
                ((micro, many, wide + LANES), bf16, (1, size, wide + LANES), tile),
                ((micro, LANES, many), bf16, (1, LANES, size), lambda m, c: (m, 0, c)),
                ((key_ch, width), bf16, (key_ch, width), fixed),
            ],
            (),
            wait,
        )(place, x, gain_steps, *first)

    normed_low, proj, small_in, key_rows = project(inputs, min(shard, 512), (second,))
    _, proj_rim, small_rim, _ = project(halo, LANES)
    grad_rows = lax.all_gather(after(out_grad, proj), "head", axis=1, tiled=True)

    w_gate = seq_gather(second.reshape(heads * rows, wide))
    if not swapped:
        w_out = lax.all_gather(out_weight, BOTH, axis=0, tiled=True)
        w_out = [widen(lax.dynamic_slice_in_dim(w_out, h_i * chans, chans, 0), 0)]
    gate_specs = [(w_gate[0].shape, fixed)] * seqs
    out_specs = [(part.shape, fixed) for part in w_out]


    whole = ((1, shard, wide), lambda m: (m, 0, 0))
    conv_ins = [
        whole,
        ((1, 16, wide), lambda m: (m, LANES // 16 - 1, 0)),
        by_micro(shard, LANES),
        ((8, wide), lambda m: (0, 0)),
    ]
    key_ins = [
        by_micro(LANES, shard),
        by_micro(LANES, LANES),
        by_micro(8, shard),
        ((key_rows_n, LANES), lambda m: (0, 0)),
    ]
    vals = kernel_call(conv_kernel, (micro,), conv_ins, [((micro, shard, wide), bf16) + whole])(
        proj, proj_rim, valid_cols, conv_par
    )[0]
    keys = kernel_call(
        key_conv_kernel, (micro,), key_ins, [((micro, key_rows_n, shard), bf16) + by_micro(key_rows_n, shard)]
    )(small_in, small_rim, valid, key_par)[0]
    keys = keys[:, :key_ch]
    keys = lax.all_gather(keys, "head", axis=1, tiled=True)

    grid = (micro, blocks)
    size = SCAN_BLOCK
    here = lambda m, c: (m, c, 0)
    along = lambda m, c: (m, 0, c)
    state_at = lambda m, c: (m, c, 0, 0)
    micro_at = lambda m, c: (m, 0, 0)
    row8 = (1, 8, size)
    tok_c, tok_l = (1, size, wide), (1, size, LANES)
    n_state = STATE + 16
    f_state = ((1, 1, STATE, wide), state_at)
    f_pre = ((1, 1, 8, wide), state_at)
    cols, rows_t, ktok, starts, prefix, payload = micro_call(
        prep_kernel,
        micro,
        blocks,
        [((1, 16, size), along), (row8, along), ((8, LANES), fixed), (tok_c, here), ((1, 2 * STATE, size), along)],
        [
            ((micro, shard, LANES), f32, tok_l, here),
            ((micro, 32, shard), f32, (1, 32, size), along),
            ((micro, shard, 2 * STATE), bf16, (1, size, 2 * STATE), here),
            ((micro, blocks, STATE, wide), f32) + f_state,
            ((micro, blocks, 8, wide), f32) + f_pre,
            ((micro, n_state, wide), bf16, (1, n_state, wide), micro_at),
        ],
        [(STATE, wide), (8, wide)],
        w_gate,
    )(small_in, seg_rows, params, vals, keys)
    key_rows = lax.all_gather(after(key_rows, payload), "head")
    size = min(shard, 512)
    gate_in, d_ynorm = kernel_call(
        functools.partial(fill_kernel, seqs),
        (micro, shard // size),
        [((1, size, width), tile)] * 2 + gate_specs + out_specs,
        [((micro, shard, wide), f32, (1, size, wide), tile)] * 2,
        [pltpu.VMEM((wide, width), bf16)],
        (payload,),
    )(normed_low, grad_rows, *w_gate, *w_out)
    size = SCAN_BLOCK
    state_in = linked(payload, False, gate_in)
    mixer, sums = micro_call(
        functools.partial(fwd_kernel, swapped, seqs - 1),
        micro,
        blocks,
        [
            scalar,
            (tok_c, here),
            ((1, size, 2 * STATE), here),
            (tok_l, here),
            ((1, 32, size), along),
            f_state,
            f_pre,
            (tok_c, here),
            (tok_c, here),
            ((8, wide), fixed),
        ]
        + [((1, n_state, wide), micro_at)] * (seqs - 1),
        [((micro, shard, wide), bf16, tok_c, here), ((micro, 8, shard), f32, row8, along)],
        [(STATE, wide)],
    )(place, vals, ktok, cols, rows_t, starts, prefix, gate_in, d_ynorm, chan, *state_in)

    sums = fill(lax.psum(sums[:, :2], "head"), 1, 8)
    back_here = lambda m, c: (m, blocks - 1 - c, 0)
    back_along = lambda m, c: (m, 0, blocks - 1 - c)
    back_state = lambda m, c: (m, blocks - 1 - c, 0, 0)
    b_state, b_pre = (f_state[0], back_state), (f_pre[0], back_state)
    ynorm_low, d_mix, d_gate, block_adj, payload = micro_call(
        functools.partial(norm_kernel, swapped),
        micro,
        blocks,
        [
            scalar,
            (tok_c, back_here),
            (tok_c, back_here),
            (tok_c, back_here),
            (row8, back_along),
            (tok_l, back_here),
            ((1, 2 * STATE, size), back_along),
            b_pre,
            ((8, wide), fixed),
            ((1, 16, wide), lambda m, c: (m, STATE // 16, 0)),
        ],
        [
            ((micro, shard, wide), bf16, tok_c, back_here),
            ((micro, shard, wide), bf16, tok_c, back_here),
            ((micro, shard, wide), bf16, tok_c, back_here),
            ((micro, blocks, STATE, wide), f32) + b_state,
            ((micro, n_state, wide), bf16, (1, n_state, wide), micro_at),
        ],
        [(STATE, wide)],
        (key_rows,),
    )(place, mixer, gate_in, d_ynorm, sums, cols, keys, prefix, chan, payload)
    wide_tile = min(shard, 512)
    out_part = kernel_call(
        out_kernel,
        (micro, shard // wide_tile),
        [((1, wide_tile, wide), here)] + out_specs,
        [((micro, shard, width), bf16, (1, wide_tile, width), here)],
        [pltpu.VMEM((wide, width), bf16)],
    )(ynorm_low, *w_out)[0]
    out_sum = lax.psum_scatter(out_part, "head", scatter_dimension=1, tiled=True)

    def weight_parts(a, count, *b, below=None, wait=(), us=None):
        run = a.shape[2] // count
        wide_b = sum(x.shape[2] for x in b)
        extra = [] if below is None else [below]
        out = (run + sum(x.shape[0] for x in extra), wide_b)
        return kernel_call(
            functools.partial(weight_kernel, len(b), below is not None),
            (count,),
            [((micro, shard, run), lambda k: (0, 0, k))]
            + [(x.shape, lambda k: (0, 0, 0)) for x in b]
            + [(x.shape, lambda k: (0, 0)) for x in extra],
            [(out, bf16, out, lambda k: (0, 0))] * count,
            [pltpu.VMEM(b[0].shape[:2] + (wide_b,), bf16)] * (len(b) > 1),
            wait,
            us,
        )(a, *b, *extra)

    if swapped:
        out = (wide, width)
        grad_out_part = kernel_call(
            rows_kernel,
            (runs,),
            [
                scalar,
                ((micro, shard, run_ch), lambda k: (0, 0, k)),
                (grad_rows.shape, lambda k: (0, 0, 0)),
            ],
            [(out, bf16, out, lambda k: (0, 0))],
        )(place, ynorm_low, grad_rows)[0]
    else:
        grad_out_part = ()
    grad_w_gate = weight_parts(normed_low, seqs, d_gate, us=0)
    adj_in = linked(payload, True, out_part, grad_w_gate, grad_out_part)

    by_heads = key_ch % 16 == 0
    key_shape = (heads, micro, key_ch, shard) if by_heads else (1, micro, 2 * STATE, shard)
    d_vals, d_keys, d_step, head_g, skip_g = micro_call(
        functools.partial(bwd_kernel, seqs - 1),
        micro,
        blocks,
        [
            (tok_c, back_here),
            ((1, 2 * STATE, size), back_along),
            ((1, size, 2 * STATE), back_here),
            (tok_l, back_here),
            ((1, 32, size), back_along),
            b_state,
            b_pre,
            (tok_c, back_here),
            b_state,
            ((8, wide), fixed),
            ((8, LANES), fixed),
        ]
        + [((1, n_state, wide), micro_at)] * (2 * seqs - 2),
        [
            ((micro, shard, wide), bf16, tok_c, back_here),
            (key_shape, bf16, (key_shape[0], 1, key_shape[2], size), lambda m, c: (0, 0, 0, blocks - 1 - c)),
            ((micro, shard, LANES), bf16, tok_l, back_here),
            ((8, LANES), f32, (8, LANES), fixed),
            ((8, wide), f32, (8, wide), fixed),
        ],
        [(STATE, wide)] * 2,
    )(
        vals, keys, ktok, cols, rows_t, starts, prefix, d_mix, block_adj, chan, params, *state_in, *adj_in
    )
    by_head = lambda x: x.astype(bf16).reshape(heads, rows, -1)
    gate_parts = seq_exchange([after(part, adj_in) for part in grad_w_gate])
    g_gate = by_head(total_of(gate_parts))
    d_val_in, val_back, conv_val_g = kernel_call(
        conv_back_kernel,
        (micro,),
        [whole] + conv_ins,
        [
            ((micro, shard, wide), bf16) + whole,
            ((micro, 8, wide), f32, (1, 8, wide), lambda m: (m, 0, 0)),
            ((8, wide), f32, (8, wide), lambda m: (0, 0)),
        ],
        (),
        gate_parts[1:],
    )(d_vals, proj, proj_rim, valid_cols, conv_par)
    if not by_heads:
        d_keys = jnp.swapaxes(d_keys.reshape(micro, heads, key_ch, shard), 0, 1)
    d_keys = head_swap(d_keys)
    g_gate_own = head_swap(after(g_gate, d_keys))
    val_back = lax.ppermute(val_back, "seq", backward)
    rim_sum = d_val_in[:, shard - 16 :].astype(f32) + jnp.pad(val_back, ((0, 0), (8, 0), (0, 0)))
    d_val_in = lax.dynamic_update_slice_in_dim(d_val_in, rim_sum.astype(bf16), shard - 16, 1)

    d_keys = jnp.pad(d_keys, ((0, 0), (0, 0), (0, key_rows_n - key_ch), (0, 0)))
    d_key_in, key_back, conv_key_g = kernel_call(
        key_back_kernel,
        (micro,),
        [((heads, 1, key_rows_n, shard), lambda m: (0, m, 0, 0))] + key_ins,
        [
            ((micro, key_rows_n, shard), f32) + by_micro(key_rows_n, shard),
            ((micro, key_rows_n, LANES), f32) + by_micro(key_rows_n, LANES),
            ((8, LANES), f32, (8, LANES), lambda m: (0, 0)),
        ],
        [pltpu.VMEM((LANES, LANES), f32)],
    )(d_keys, small_in, small_rim, valid, key_par)
    key_back = lax.ppermute(key_back, "seq", backward)

    size = min(shard, 512)
    tile = lambda m, c: (m, c, 0)
    tile_c, tile_l, tile_w = ((1, size, n) for n in (wide, LANES, width))
    d_normed = kernel_call(
        functools.partial(normed_back_kernel, seqs),
        (micro, shard // size),
        [(tile_c, tile), (tile_c, tile), (tile_l, tile)] + gate_specs + [(first[0].shape, fixed)] * seqs,
        [((micro, shard, width), bf16, tile_w, tile)],
        (),
        (out_sum, d_key_in),
    )(d_gate, d_val_in, d_step, *w_gate, *first)[0]
    d_normed_sum = lax.psum_scatter(d_normed, "head", scatter_dimension=1, tiled=True)

    fixed1 = lambda m: (0, 0)
    blocks8 = [(8, wide), (8, LANES), (8, LANES), (8, wide)]
    packed = (8, wide + LANES)
    small = kernel_call(
        pack_kernel,
        (1,),
        [(block, fixed1) for block in blocks8],
        [(packed, f32, packed, fixed1)],
    )(conv_val_g, conv_key_g, head_g, skip_g)[0]
    small = seq_reduce([small] * seqs)

    d_key_in, d_small = kernel_call(
        key_join_kernel,
        (micro,),
        [by_micro(key_rows_n, shard), by_micro(key_rows_n, LANES), by_micro(shard, LANES)],
        [
            ((micro, key_rows_n, shard), bf16) + by_micro(key_rows_n, shard),
            ((micro, shard, LANES), bf16) + by_micro(shard, LANES),
        ],
        (),
        (g_gate_own,),
    )(d_key_in, key_back, d_step)
    d_key_in = d_key_in[:, :key_ch]
    g_first = weight_parts(normed_low, seqs, d_val_in, d_small)
    if swapped:
        grad_out_weight = lax.psum_scatter(
            grad_out_part, "seq", scatter_dimension=0, tiled=True
        ).astype(f32)
    else:
        full = dot("mtk,mtd->kd", ynorm_low, grad_rows).astype(bf16)[:chans]
        full = lax.dynamic_update_slice_in_dim(jnp.zeros((D_INNER, width), bf16), full, h_i * chans, 0)
        grad_out_weight = lax.psum_scatter(full, BOTH, scatter_dimension=0, tiled=True).astype(f32)
    d_key_in, small = after((d_key_in, small), g_first)
    key_own = jnp.transpose(d_key_in.reshape(micro, key_ch, heads, tok), (2, 0, 1, 3))
    count = key_own.size // heads
    key_n = -(-count // (8 * (wide + LANES))) * 8
    key_own = fill(key_own.reshape(heads, count), 1, key_n * (wide + LANES)).reshape(heads, key_n, -1)
    small = [jnp.broadcast_to(part[None], (heads,) + part.shape) for part in three_parts(small)[:2]]
    small = head_swap(after(jnp.concatenate(small + [key_own], axis=1), g_first))
    key_own = small[:, 16:].reshape(heads, -1)[:, :count].reshape(heads, micro, key_ch, tok)

    hidden_out = (hidden_in.astype(f32) + after(out_sum, g_first).astype(f32)).astype(bf16)
    gate_gg = jnp.sum(after(grad_out_weight, g_first) * out_weight.astype(f32), axis=1) / gate_gain.astype(f32)

    if swapped:
        conv_g, head_g = kernel_call(
            unpack_kernel,
            (1,),
            [scalar, ((heads, 16, wide + LANES), lambda m: (0, 0, 0))],
            [
                ((8, 2 * LANES), f32, (8, 2 * LANES), lambda m: (0, 0)),
                ((8, LANES), f32, (8, LANES), lambda m: (0, 0)),
            ],
            [pltpu.VMEM((heads, 8, wide + LANES), f32)],
        )(jnp.stack([s_i, h_i]), small)
        conv_g = conv_g[: CONV_K + 1, :conv_share]
        head_g = head_g[CONV_K + 1 :, :head_share]
    else:
        sums = small[:, :8].astype(f32) + small[:, 8:16].astype(f32)
        conv_g = jnp.concatenate(
            [sums[:, : CONV_K + 1, :chans], sums[:, : CONV_K + 1, wide : wide + key_ch]], axis=2
        )
        head_g = sums[:, CONV_K + 1 : CONV_K + 4, :n_heads].reshape(heads, 3, runs, run_heads)
        conv_gv = jnp.transpose(conv_g[:, :, :chans].reshape(heads, CONV_K + 1, runs, run_ch), (1, 2, 0, 3))
        conv_gk = jnp.transpose(conv_g[:, :, chans:], (1, 0, 2))
        conv_g = jnp.concatenate(
            [conv_gv.reshape(CONV_K + 1, D_INNER), conv_gk.reshape(CONV_K + 1, 2 * STATE)], axis=1
        )
        head_g = jnp.transpose(head_g, (1, 2, 0, 3)).reshape(3, HEADS)
        conv_g = lax.dynamic_slice_in_dim(conv_g, linear * conv_share, conv_share, 1)
        head_g = lax.dynamic_slice_in_dim(head_g, h_i * head_share, head_share, 1)
    g_first = by_head(seq_reduce(g_first))
    g_first = head_swap(after(g_first, conv_g, head_g, key_own))
    if swapped:
        own_at = lambda m: (m, 0, 0)
        own = (1, tok, width)
        flat = lambda m: (0, 0)
        steps = (seqs, width // seqs)
        grad_in = kernel_call(
            grad_in_kernel,
            (micro,),
            [
                scalar,
                (own, own_at),
                ((heads, 1, key_ch, tok), lambda m: (0, m, 0, 0)),
                ((2 * STATE, width), flat),
                (own, own_at),
                (steps, flat),
                (own, own_at),
            ],
            [((micro, tok, width), bf16, own, own_at)],
            [pltpu.VMEM((tok, width), f32)],
            (hidden_out, gate_gg),
        )(place, d_normed_sum, key_own, key_rows.reshape(2 * STATE, width), hidden_in, gain_steps, out_grad)[0]
        whole3 = lambda shape: (shape, lambda m: (0,) * len(shape))
        grad_in_weight, norm_sum = kernel_call(
            weight_grad_kernel,
            (1,),
            [whole3(g_gate_own.shape), whole3(g_first.shape), whole3(in_weight.shape)],
            [
                (in_weight.shape, f32) + whole3(in_weight.shape),
                ((rows, LANES), f32) + whole3((rows, LANES)),
            ],
            (),
            (grad_in,),
        )(g_gate_own, g_first, in_weight)
        norm_sum = norm_sum[:, 0]
    else:
        key_part = dot("hmct,hcd->mtd", key_own, key_rows)
        d_normed = (d_normed_sum.astype(f32) + key_part).reshape(micro, tok, seqs, -1)
        d_normed = from_steps(jnp.moveaxis(d_normed, 2, 0), s_i)
        d_normed = jnp.moveaxis(d_normed, 0, 2).reshape(micro, tok, width)
        own = hidden_in.astype(f32)
        own_inv = lax.rsqrt(jnp.mean(own * own, axis=-1, keepdims=True) + EPS)
        d_unit = d_normed * from_steps(gain_steps, s_i).reshape(-1)
        shared = own_inv * own_inv * jnp.mean(d_unit * own, axis=-1, keepdims=True)
        grad_in = (out_grad.astype(f32) + own_inv * (d_unit - own * shared)).astype(bf16)

        def uncolumns(x, size):
            x = x.astype(f32).reshape(heads, rows, runs, size)
            return jnp.transpose(x, (1, 2, 0, 3)).reshape(rows, runs * heads * size)

        g_key = jnp.transpose(g_first[:, :rows, wide + 8 : wide + 8 + key_ch], (1, 0, 2))
        grad_in_weight = jnp.concatenate(
            [
                uncolumns(g_gate_own[:, :rows, :chans], run_ch),
                uncolumns(g_first[:, :rows, :chans], run_ch),
                g_key.astype(f32).reshape(rows, -1),
                uncolumns(g_first[:, :rows, wide : wide + n_heads], run_heads),
            ],
            axis=1,
        )
        norm_sum = jnp.sum(grad_in_weight * in_weight.astype(f32), axis=1)
    norm_g = norm_sum / norm_gain.astype(f32)

    return (
        hidden_out,
        grad_in,
        norm_g,
        grad_in_weight,
        conv_g[:CONV_K],
        conv_g[CONV_K],
        head_g[0],
        head_g[1],
        head_g[2],
        gate_gg,
        grad_out_weight,
    )


def solution(mesh):
    tokens = P(None, BOTH, None)
    by_rows = P(BOTH, None)
    return jax.shard_map(
        body,
        mesh=mesh,
        in_specs=(
            tokens,
            P(),
            P(BOTH),
            by_rows,
            P(None, BOTH),
            P(BOTH),
            P("head"),
            P("head"),
            P("head"),
            P(BOTH),
            by_rows,
            tokens,
        ),
        out_specs=(
            tokens,
            tokens,
            P(BOTH),
            by_rows,
            P(None, BOTH),
            P(BOTH),
            P("head"),
            P("head"),
            P("head"),
            P(BOTH),
            by_rows,
        ),
        check_vma=False,
    )
```
